32 devices in a mesh: runs: 2 (over x), gy: 16 (over z, y, core).
Axes of the slice: x: 2, y: 2, z: 4, core: 2. Of those that a mesh axis runs over, the one named last changes fastest.
Arguments:
- depth: float32 [1024, 1920], P(('runs', 'gy')), parts along dimension 0, may hold values from 0.02 to 3
- flux_east: float32 [1024, 1920], P(('runs', 'gy')), parts along dimension 0, may hold values from -2 to 2
- flux_south: float32 [1024, 1920], P(('runs', 'gy')), parts along dimension 0, may hold values from -2 to 2
- river_section: float32 [4096], P(('runs', 'gy')), parts along dimension 0, may hold values from 0 to 2
- bed_level: float32 [512, 1920], P('gy'), may hold values from -3 to 3
- rough_class: int32 [512, 1920], P('gy'), may hold values from 0 to 7
- manning_table: float32 [8], replicated, may hold values from 0.02 to 0.15
- bank_cell: int32 [4, 2048], P(None, 'gy'), may hold values from 0 to 983039, as said below
Outputs:
- depth_out: float32 [1024, 1920], P(('runs', 'gy')), parts along dimension 0
- east_out: float32 [1024, 1920], P(('runs', 'gy')), parts along dimension 0
- south_out: float32 [1024, 1920], P(('runs', 'gy')), parts along dimension 0
- section_out: float32 [4096], P(('runs', 'gy')), parts along dimension 0
The draws below stay inside these ranges and needn't reach their ends.
There are 2 independent parts, one for each index of `runs`. The reference program is written for one: setup_inputs(seed, part) draws one part's arguments, and reference() takes and returns one part's arrays. A program takes and returns all parts, laid end to end along the dimension named above; an argument that names none is the same for every part. Nothing has to cross between parts.
Inputs may be any that keep to these rules, and one draw needn't show every extreme that they name: `bank_cell`: the 4 corridor cells of a node are consecutive flat indices row * 1920 + column within one map row. Node n is owned by gy index o = n // 128, and all its corridor cells lie in map rows from max((o - 1) * 32, 0) to min((o + 2) * 32, 512) - 1.
All inputs are finite; a program needn't handle non-finite values.
Results may differ from the reference program's by a relative error of at most 0.00013.
Values sent between devices are 32-bit elements; how exact they have to be, the bound alone decides.
No kernel may reach another device: no remote copies, remote signals or barrier semaphores. Data moves between devices by JAX's collectives and lax.ppermute only.
A program may use at most 64 MiB of HBM per device.

```python
import math
import jax
import jax.numpy as jnp

RY = 32
NX = 1920
NODE_DEV = 128
K = 4
CLASSES = 8
STEPS = 4
NY = 512
NODES = 2048


def draw_bank_cell(key, part):
    tiles = NODES // NODE_DEV
    key_start, key_walk, key_jitter = jax.random.split(key, 3)
    node = jnp.arange(NODES, dtype=jnp.int32)
    owner = node // NODE_DEV
    place = node % NODE_DEV
    jitter = jax.random.randint(key_jitter, (NODES,), 0, 2).astype(jnp.int32)
    row = (owner - 1) * RY + place * 3 * RY // NODE_DEV + jitter
    row = jnp.clip(row, jnp.maximum((owner - 1) * RY, 0), jnp.minimum((owner + 2) * RY - 1, NY - 1))
    start = jax.random.randint(key_start, (tiles, 1), 0, NX - K + 1).astype(jnp.int32)
    moves = jax.random.randint(key_walk, (tiles, NODE_DEV), -2, 3).astype(jnp.int32)
    column = jnp.clip(start + jnp.cumsum(moves, axis=1), 0, NX - K).reshape(-1).astype(jnp.int32)
    row = row.at[0].set(0).at[NODES - 1].set(NY - 1)
    column = column.at[0].set(0).at[NODES - 1].set(NX - K)
    flat = row * NX + column
    return (flat[None, :] + jnp.arange(K, dtype=jnp.int32)[:, None]).astype(jnp.int32)


def plant(result, rng, low, top_value):
    dims = result.shape
    index_at = [jax.random.randint(jax.random.fold_in(rng, axis), (), 0, dims[axis]) for axis in range(len(dims))]
    result = result.at[tuple(index_at)].set(low)
    longest = dims.index(max(dims))
    index_at[longest] = (index_at[longest] + 1) % dims[longest]
    return result.at[tuple(index_at)].set(top_value)


def shard_levels(stream_key, dims, cuts, low, largest):
    def one(position, blocks):
        heights = jax.random.uniform(jax.random.fold_in(jax.random.fold_in(stream_key, 6), position), (blocks,), jnp.float32, low / len(cuts), largest / len(cuts))
        return jnp.repeat(jnp.exp(heights), dims[position] // blocks).reshape((-1,) + (1,) * (len(dims) - position - 1))

    factor_of = one(*cuts[0])
    for cut in cuts[1:]:
        factor_of = factor_of * one(*cut)
    return factor_of


def noise(rng, shape, scale, reach, cuts=(), held_as=jnp.bfloat16):
    level = shard_levels(rng, shape, cuts, -0.22, 0.18) if cuts else 1.0
    result = jax.random.normal(rng, shape, jnp.float32) * scale * level
    return jnp.minimum(jnp.maximum(result, -reach), reach).astype(held_as)


def setup_inputs(seed: int = 0, part: int = 0) -> dict:
    key_of = jax.random.split(jax.random.key(seed), 9)
    part_splits = jax.random.split(jax.random.fold_in(key_of[8], part), 9)
    return {
        "depth": jnp.clip(jnp.exp(math.log(3.0) - 5.0106353 * jax.random.uniform(part_splits[0], (NY, NX), jnp.float32) ** shard_levels(part_splits[0], (NY, NX), ((0, 16),), -0.2, 0.2)), 0.02, 3.0),
        "flux_east": noise(part_splits[1], (NY, NX), 0.3, 2.0, ((0, 16),), jnp.float32),
        "flux_south": noise(part_splits[2], (NY, NX), 0.3, 2.0, ((0, 16),), jnp.float32),
        "river_section": jnp.clip(2.0 * jax.random.uniform(part_splits[3], (NODES,), jnp.float32) ** shard_levels(part_splits[3], (NODES,), ((0, 16),), -0.2, 0.2), 0.0, 2.0),
        "bed_level": noise(key_of[4], (NY, NX), 0.5, 3.0, ((0, 16),), jnp.float32),
        "rough_class": plant(jax.random.randint(key_of[5], (NY, NX), 0, CLASSES), jax.random.fold_in(key_of[5], 1), 0, CLASSES - 1).astype(jnp.int32),
        "manning_table": jnp.clip(jnp.exp(jax.random.uniform(key_of[6], (CLASSES,), jnp.float32, math.log(0.02), math.log(0.15))), 0.02, 0.15),
        "bank_cell": draw_bank_cell(jax.random.fold_in(key_of[8], 71), part),
    }


GRAV = 9.81
TSTEP = 8.0
CELL = 90.0
FLOOR = 0.05
BANK_COEF = 200.0
CELL_AREA = 8100.0
NODE_AREA = 20000.0


def face_flux(flux, surf_a, surf_b, bed_a, bed_b, mann_a, mann_b):
    flow_depth = jnp.maximum(jnp.maximum(surf_a, surf_b) - jnp.maximum(bed_a, bed_b), FLOOR)
    mean_mann = 0.5 * (mann_a + mann_b)
    driven = flux - GRAV * flow_depth * TSTEP * (surf_b - surf_a) / CELL
    damping = 1.0 + GRAV * TSTEP * mean_mann * mean_mann * jnp.abs(flux) / jnp.power(flow_depth, 7.0 / 3.0)
    return driven / damping


def reference(depth, flux_east, flux_south, river_section, bed_level, rough_class, manning_table, bank_cell):
    manning = manning_table[rough_class]
    rows_all, cols_all = depth.shape
    for substep in range(STEPS):
        surface = depth + bed_level
        east_part = face_flux(flux_east[:, :-1], surface[:, :-1], surface[:, 1:], bed_level[:, :-1], bed_level[:, 1:], manning[:, :-1], manning[:, 1:])
        flux_east = jnp.concatenate([east_part, jnp.zeros((rows_all, 1), jnp.float32)], axis=1)
        south_part = face_flux(flux_south[:-1], surface[:-1], surface[1:], bed_level[:-1], bed_level[1:], manning[:-1], manning[1:])
        flux_south = jnp.concatenate([south_part, jnp.zeros((1, cols_all), jnp.float32)], axis=0)
        surf_flat = surface.reshape(-1)
        bank_flow = BANK_COEF * (river_section[None, :] - surf_flat[bank_cell])
        source = jnp.zeros((rows_all * cols_all,), jnp.float32).at[bank_cell.reshape(-1)].add(bank_flow.reshape(-1)).reshape(rows_all, cols_all)
        east_in = jnp.concatenate([jnp.zeros((rows_all, 1), jnp.float32), flux_east[:, :-1]], axis=1)
        south_in = jnp.concatenate([jnp.zeros((1, cols_all), jnp.float32), flux_south[:-1]], axis=0)
        depth = depth + TSTEP / CELL * (east_in - flux_east + south_in - flux_south) + TSTEP * source / CELL_AREA
        river_section = river_section - TSTEP * jnp.sum(bank_flow, axis=0) / NODE_AREA
    return depth, flux_east, flux_south, river_section
```

```python
import functools

import jax
import jax.numpy as jnp
from jax import lax
from jax.experimental import pallas as pl
from jax.experimental.pallas import tpu as pltpu
from jax.sharding import PartitionSpec as P

STEPS = 4

GRAV = 9.81
TSTEP = 8.0
CELL = 90.0
FLOOR = 0.05
BANK_COEF = 200.0
CELL_AREA = 8100.0
NODE_AREA = 20000.0

LANES = 128
HALO = 4
SLOPE = GRAV * TSTEP / CELL
SPREAD = TSTEP / CELL
FEED = TSTEP * BANK_COEF / CELL_AREA
DRAIN = TSTEP * BANK_COEF / NODE_AREA


def swapped(value, axis, first):
    count = lax.axis_size(axis)
    pairs = []
    for low in range(first, count - 1, 2):
        pairs += [(low, low + 1), (low + 1, low)]
    return lax.ppermute(value, axis, pairs)


def split3(value):
    high = value.astype(jnp.bfloat16)
    rest = value - high.astype(jnp.float32)
    middle = rest.astype(jnp.bfloat16)
    low = (rest - middle.astype(jnp.float32)).astype(jnp.bfloat16)
    return high, middle, low


def one_hot(count, key):
    rows = lax.broadcasted_iota(jnp.int32, (count, key.shape[1]), 0)
    return jnp.where(rows == key, 1.0, 0.0)


def pack_kernel(
    place, depth, east, south, bed, rough, own, partner, to_partner, to_other
):
    rows, columns = depth.shape
    even = place[0] % 2 == 0

    def put(target, start):
        for slot, source in enumerate((depth, bed, rough, east, south)):
            target[slot, :, :columns] = source[start : start + HALO, :].astype(jnp.float32)

    @pl.when(even)
    def _():
        put(to_partner, rows - HALO)
        put(to_other, 0)

    @pl.when(jnp.logical_not(even))
    def _():
        put(to_partner, 0)
        put(to_other, rows - HALO)

    for target in (to_partner, to_other):
        for slot in range(5):
            target[slot, :, columns:] = jnp.zeros((HALO, LANES), jnp.float32)
    to_other[0, 0:2, columns:] = own[...]
    to_other[0, 2:4, columns:] = partner[...]


def flow_kernel(
    corridor,
    tiles,
    place,
    table,
    depth_in,
    east_in,
    south_in,
    bed_in,
    rough_in,
    own,
    partner,
    by_partner,
    by_other,
    depth_out,
    east_out,
    south_out,
    terms,
    depth,
    east,
    south,
    bed,
    mann,
    bed_e,
    bed_s,
    drag_e,
    drag_s,
    count,
    covers,
    total,
    level,
    sems,
):
    rows, columns = depth_in.shape
    ext = rows + 2 * HALO
    chunks = columns // LANES
    position = place[0]
    even = position % 2 == 0
    lane = lax.broadcasted_iota(jnp.int32, (ext, LANES), 1)
    row = lax.broadcasted_iota(jnp.int32, (ext, LANES), 0)

    def cols(chunk):
        return slice(chunk * LANES, (chunk + 1) * LANES)

    for chunk in range(chunks):
        at = cols(chunk)
        halos = []
        for slot in range(5):
            a, b = by_partner[slot, :, at], by_other[slot, :, at]
            below = jnp.where(even, a, b)
            above = jnp.where(even, b, a)
            halos.append(jnp.concatenate([below, above], axis=0))
        depth[:rows, at] = depth_in[:, at]
        bed[:rows, at] = bed_in[:, at]
        east[:rows, at] = east_in[:, at]
        south[:rows, at] = south_in[:, at]
        depth[rows:, at] = halos[0]
        bed[rows:, at] = halos[1]
        east[rows:, at] = halos[3]
        south[rows:, at] = halos[4]
        klass = jnp.concatenate(
            [rough_in[:, at].astype(jnp.float32), halos[2]], axis=0
        )
        value = jnp.full(klass.shape, table[0], jnp.float32)
        for k in range(1, table.shape[0]):
            value = jnp.where(klass == float(k), table[k], value)
        mann[:, at] = value

    def left(value, following, by):
        return jnp.where(
            lane >= LANES - by,
            pltpu.roll(following, LANES - by, 1),
            pltpu.roll(value, LANES - by, 1),
        )

    def up(value):
        return pltpu.roll(value, ext - 1, 0)

    for chunk in range(chunks):
        at, then = cols(chunk), cols(min(chunk + 1, chunks - 1))
        b0, m0 = bed[:, at], mann[:, at]
        bed_e[:, at] = jnp.maximum(b0, left(b0, bed[:, then], 1))
        bed_s[:, at] = jnp.maximum(b0, up(b0))
        pair = m0 + left(m0, mann[:, then], 1)
        drag_e[:, at] = (0.25 * GRAV * TSTEP) * (pair * pair)
        pair = m0 + up(m0)
        drag_s[:, at] = (0.25 * GRAV * TSTEP) * (pair * pair)

    near = by_other[0, :, columns:]
    far = by_partner[0, :, columns:]
    sections = jnp.concatenate(
        [own[0:1, :], partner[0:1, :], near[0:1, :], near[2:3, :], far[0:1, :]], axis=1
    )
    cells = jnp.concatenate(
        [own[1:2, :], partner[1:2, :], near[1:2, :], near[3:4, :], far[1:2, :]], axis=1
    )
    base = (position * rows * columns + 1).astype(jnp.float32)
    offset = cells - base + float(HALO * columns)
    valid = (cells > 0.0) & (offset >= 0.0) & (offset < float(ext * columns))
    offset = jnp.where(valid, offset, 0.0)
    node_row = jnp.floor((offset + 0.5) * (1.0 / columns))
    node_col = (offset - node_row * float(columns)).astype(jnp.int32)
    node_row = node_row.astype(jnp.int32) - HALO
    node_row = jnp.where(node_row < 0, node_row + ext, node_row)
    node_chunk = node_col // LANES
    node_lane = node_col - node_chunk * LANES
    start_key = jnp.where(valid, node_chunk * ext + node_row, -1)
    at_lane = one_hot(LANES, node_lane)
    starts = one_hot(chunks * ext + 8, start_key).astype(jnp.bfloat16)
    parts = [at_lane] + [at_lane * part.astype(jnp.float32) for part in split3(sections)]
    grid = lax.dot_general(
        starts,
        jnp.concatenate(parts, axis=0).astype(jnp.bfloat16),
        (((1,), (1,)), ((), ())),
        preferred_element_type=jnp.float32,
    )

    def right_sum(value, state):
        once = pltpu.roll(value, 1, 1)
        pair = value + jnp.where(lane < 1, state[0], once)
        twice = pltpu.roll(pair, 2, 1)
        return pair + jnp.where(lane < 2, state[1], twice), (once, twice)

    zero = jnp.zeros((ext, LANES), jnp.float32)
    state = (zero, zero)
    for chunk in range(chunks):
        at = cols(chunk)
        block = grid[chunk * ext : (chunk + 1) * ext]
        number = block[:, :LANES]
        count[:, at] = DRAIN * number
        total[:, at] = (
            block[:, LANES : 2 * LANES] + block[:, 2 * LANES : 3 * LANES]
        ) + block[:, 3 * LANES :]
        covering, state = right_sum(number, state)
        covers[:, at] = FEED * covering
        level[:, at] = zero

    wall = ((row == ext - 1) & (position == 0)) | ((row == rows - 1) & (position == tiles - 1))

    def face(flux, surf_a, surf_b, bed_max, drag):
        flow_depth = jnp.maximum(jnp.maximum(surf_a, surf_b) - bed_max, FLOOR)
        power = jnp.exp2((-7.0 / 3.0) * jnp.log2(flow_depth))
        driven = flux - SLOPE * flow_depth * (surf_b - surf_a)
        return driven / (1.0 + drag * jnp.abs(flux) * power)

    def substep(step, carry):
        surf = depth[:, cols(0)] + bed[:, cols(0)]
        rolled = [pltpu.roll(surf, LANES - by, 1) for by in range(1, corridor)]
        east_last = zero
        state = (zero, zero)
        for chunk in range(chunks):
            at = cols(chunk)
            if chunk + 1 < chunks:
                then = cols(chunk + 1)
                surf_then = depth[:, then] + bed[:, then]
                rolled_then = [pltpu.roll(surf_then, LANES - by, 1) for by in range(1, corridor)]
            else:
                surf_then, rolled_then = surf, rolled
            moved = [
                jnp.where(lane >= LANES - 1 - by, rolled_then[by], rolled[by])
                for by in range(corridor - 1)
            ]
            new_east = face(east[:, at], surf, moved[0], bed_e[:, at], drag_e[:, at])
            if chunk + 1 == chunks:
                new_east = jnp.where(lane == LANES - 1, 0.0, new_east)
            new_south = face(south[:, at], surf, up(surf), bed_s[:, at], drag_s[:, at])
            new_south = jnp.where(wall, 0.0, new_south)
            east[:, at] = new_east
            south[:, at] = new_south
            window = surf
            for other in moved:
                window = window + other
            level[:, at] = (1.0 - corridor * DRAIN) * level[:, at] + DRAIN * window
            held = total[:, at]
            summed, state = right_sum(held, state)
            total[:, at] = (1.0 - corridor * DRAIN) * held + count[:, at] * window
            east_rolled = pltpu.roll(new_east, 1, 1)
            inflow = jnp.where(lane < 1, east_last, east_rolled) + pltpu.roll(new_south, 1, 0)
            east_last = east_rolled
            depth[:, at] = (
                depth[:, at]
                + SPREAD * (inflow - new_east - new_south)
                + (FEED * summed - covers[:, at] * surf)
            )
            surf, rolled = surf_then, rolled_then
        return carry

    lax.fori_loop(0, STEPS, substep, 0)

    copies = [
        pltpu.make_async_copy(source.at[pl.ds(0, rows), :], target, sems.at[slot])
        for slot, (source, target) in enumerate(
            ((depth, depth_out), (east, east_out), (south, south_out))
        )
    ]
    for copy in copies:
        copy.start()

    mine = 3 * own.shape[1]
    inside = valid & (node_row < rows)
    take_key = jnp.where(inside, node_chunk * rows + node_row, -1)[:, :mine]
    takes = one_hot(chunks * rows, take_key).astype(jnp.bfloat16)
    levels = jnp.concatenate([level[:rows, cols(chunk)] for chunk in range(chunks)], axis=0)
    picked = lax.dot_general(
        jnp.concatenate(split3(levels), axis=1),
        takes,
        (((0,), (0,)), ((), ())),
        preferred_element_type=jnp.float32,
    )
    picked = (picked[:LANES] + picked[LANES : 2 * LANES]) + picked[2 * LANES :]
    terms[...] = jnp.sum(picked * at_lane[:, :mine], axis=0, keepdims=True)
    for copy in copies:
        copy.wait()


def local(
    depth, flux_east, flux_south, river_section, bed_level, rough_class, manning_table, bank_cell
):
    rows, columns = depth.shape
    owned = river_section.shape[0]
    corridor = bank_cell.shape[0]
    tiles = lax.axis_size("gy")
    position = lax.axis_index("gy")
    ext = rows + 2 * HALO
    place = position.astype(jnp.int32).reshape(1)
    own = jnp.stack([river_section, (bank_cell[0] + 1).astype(jnp.float32)])
    partner = swapped(own, "gy", 0)
    smem = pl.BlockSpec(memory_space=pltpu.SMEM)
    vmem = pl.BlockSpec(memory_space=pltpu.VMEM)
    anywhere = pl.BlockSpec(memory_space=pl.ANY)
    held = [
        pltpu.with_memory_space_constraint(value, pltpu.VMEM)
        for value in (depth, flux_east, flux_south, bed_level, rough_class)
    ]
    packed = jax.ShapeDtypeStruct((5, HALO, columns + LANES), jnp.float32)
    to_partner, to_other = pl.pallas_call(
        pack_kernel,
        out_shape=(packed, packed),
        in_specs=[smem] + [vmem] * 7,
        out_specs=(vmem, vmem),
        name="pack",
    )(place, *held, own, partner)
    by_other = swapped(to_other, "gy", 1)
    to_partner = to_partner.at[0, 0:2, columns:].set(by_other[0, 0:2, columns:])
    by_partner = swapped(to_partner, "gy", 0)
    field = jax.ShapeDtypeStruct((rows, columns), jnp.float32)
    state = pltpu.VMEM((ext, columns), jnp.float32)
    depth, flux_east, flux_south, terms = pl.pallas_call(
        functools.partial(flow_kernel, corridor, tiles),
        out_shape=(field, field, field, jax.ShapeDtypeStruct((1, 3 * owned), jnp.float32)),
        in_specs=[smem, smem] + [vmem] * 9,
        out_specs=(anywhere, anywhere, anywhere, vmem),
        scratch_shapes=[state] * 13 + [pltpu.SemaphoreType.DMA((3,))],
        compiler_params=pltpu.CompilerParams(vmem_limit_bytes=32 * 1024 * 1024),
        name="flow",
    )(place, manning_table, *held, own, partner, by_partner, by_other)
    terms = terms.reshape(3, owned)
    from_partner = swapped(terms[1], "gy", 0)
    from_other = swapped(terms[2], "gy", 1)
    kept = (1.0 - corridor * DRAIN) ** STEPS
    river_section = kept * river_section + terms[0] + from_partner + from_other
    return (depth, flux_east, flux_south, river_section)


def solution(mesh):
    return jax.shard_map(
        local,
        mesh=mesh,
        in_specs=(
            P(("runs", "gy"), None),
            P(("runs", "gy"), None),
            P(("runs", "gy"), None),
            P(("runs", "gy")),
            P("gy", None),
            P("gy", None),
            P(),
            P(None, "gy"),
        ),
        out_specs=(
            P(("runs", "gy"), None),
            P(("runs", "gy"), None),
            P(("runs", "gy"), None),
            P(("runs", "gy")),
        ),
        check_vma=False,
    )
```

```python
import functools

import jax
import jax.numpy as jnp
from jax import lax
from jax.experimental import pallas as pl
from jax.experimental.pallas import tpu as pltpu
from jax.sharding import PartitionSpec as P

STEPS = 4

GRAV = 9.81
TSTEP = 8.0
CELL = 90.0
FLOOR = 0.05
BANK_COEF = 200.0
CELL_AREA = 8100.0
NODE_AREA = 20000.0

LANES = 128
HALO = 4
SLOPE = GRAV * TSTEP / CELL
SPREAD = TSTEP / CELL
FEED = TSTEP * BANK_COEF / CELL_AREA
DRAIN = TSTEP * BANK_COEF / NODE_AREA
VMEM_LIMIT = 32 * 1024 * 1024

SMEM_SPEC = pl.BlockSpec(memory_space=pltpu.SMEM)
VMEM_SPEC = pl.BlockSpec(memory_space=pltpu.VMEM)
HBM_SPEC = pl.BlockSpec(memory_space=pltpu.HBM)


def swapped(value, first):
    count = lax.axis_size("gy")
    pairs = []
    for low in range(first, count - 1, 2):
        pairs += [(low, low + 1), (low + 1, low)]
    return lax.ppermute(value, "gy", pairs)


def cols(chunk):
    return slice(chunk * LANES, (chunk + 1) * LANES)


def lanes_of(rows):
    return lax.broadcasted_iota(jnp.int32, (rows, LANES), 1)


def moved_left(value, following, by):
    return jnp.where(
        lanes_of(value.shape[0]) >= LANES - by,
        pltpu.roll(following, LANES - by, 1),
        pltpu.roll(value, LANES - by, 1),
    )


def moved_up(value):
    return pltpu.roll(value, value.shape[0] - 1, 0)


def split3(value):
    high = value.astype(jnp.bfloat16)
    rest = value - high.astype(jnp.float32)
    middle = rest.astype(jnp.bfloat16)
    low = (rest - middle.astype(jnp.float32)).astype(jnp.bfloat16)
    return high, middle, low


def one_hot(count, key):
    rows = lax.broadcasted_iota(jnp.int32, (count, key.shape[1]), 0)
    return jnp.where(rows == key, 1.0, 0.0)


def drag_of(mann_a, mann_b):
    pair = mann_a + mann_b
    return (0.25 * GRAV * TSTEP) * (pair * pair)


def looked_up(klass, entries):
    value = jnp.broadcast_to(entries[0], klass.shape)
    for k in range(1, len(entries)):
        value = jnp.where(klass == k, entries[k], value)
    return value


def face(flux, surf_a, surf_b, bed_max, drag):
    flow_depth = jnp.maximum(jnp.maximum(surf_a, surf_b) - bed_max, FLOOR)
    power = jnp.exp2((-7.0 / 3.0) * jnp.log2(flow_depth))
    driven = flux - SLOPE * flow_depth * (surf_b - surf_a)
    damping = 1.0 + drag * jnp.abs(flux) * power
    inverse = pl.reciprocal(damping, approx=True)
    inverse = inverse * (2.0 - damping * inverse)
    return driven * inverse


def right_sum(value, state):
    lane = lanes_of(value.shape[0])
    once = pltpu.roll(value, 1, 1)
    pair = value + jnp.where(lane < 1, state[0], once)
    twice = pltpu.roll(pair, 2, 1)
    return pair + jnp.where(lane < 2, state[1], twice), (once, twice)


def pack_kernel(depth, bed, rough, east, south, to_other, held, held_rough, sems):
    rows, columns = depth.shape
    even = lax.axis_index("gy") % 2 == 0
    start = pl.multiple_of(jnp.where(even, 0, rows - 8), 8)
    copies = [
        pltpu.make_async_copy(source.at[pl.ds(start, 8), :], target, sems.at[slot])
        for slot, (source, target) in enumerate(
            (
                (depth, held.at[0]),
                (bed, held.at[1]),
                (rough, held_rough),
                (east, held.at[2]),
                (south, held.at[3]),
            )
        )
    ]
    for copy in copies:
        copy.start()
    for slot, copy in enumerate(copies):
        copy.wait()
        block = (
            held_rough[...].astype(jnp.float32) if slot == 2 else held[slot - (slot > 2)]
        )
        to_other[slot] = jnp.where(even, block[:HALO], block[8 - HALO :])


def prepare_kernel(
    table,
    depth_in,
    east_in,
    south_in,
    bed_in,
    rough_in,
    to_partner,
    table_rows,
    depth,
    east,
    south,
    bed,
    mann,
    bed_e,
    bed_s,
    drag_e,
    drag_s,
    rough,
    sems,
):
    rows, columns = depth_in.shape
    chunks = columns // LANES
    even = lax.axis_index("gy") % 2 == 0
    own = pl.ds(0, rows)
    copies = [
        pltpu.make_async_copy(source, target, sems.at[slot])
        for slot, (source, target) in enumerate(
            (
                (rough_in, rough),
                (bed_in, bed.at[own, :]),
                (depth_in, depth.at[own, :]),
                (east_in, east.at[own, :]),
                (south_in, south.at[own, :]),
            )
        )
    ]
    for copy in copies:
        copy.start()
    entries = [table[k] for k in range(table.shape[0])]
    for k, entry in enumerate(entries):
        table_rows[k : k + 1, :] = jnp.full((1, LANES), entry, jnp.float32)
    copies[0].wait()
    copies[1].wait()
    for chunk in range(chunks):
        at = cols(chunk)
        mann[:rows, at] = looked_up(rough[:, at], entries)
    for chunk in range(chunks):
        at, then = cols(chunk), cols(min(chunk + 1, chunks - 1))
        b0, m0 = bed[:rows, at], mann[:rows, at]
        bed_e[:rows, at] = jnp.maximum(b0, moved_left(b0, bed[:rows, then], 1))
        bed_s[:rows, at] = jnp.maximum(b0, moved_up(b0))
        drag_e[:rows, at] = drag_of(m0, moved_left(m0, mann[:rows, then], 1))
        drag_s[:rows, at] = drag_of(m0, moved_up(m0))
    for copy in copies[2:]:
        copy.wait()
    for slot, source in enumerate((depth, bed, rough, east, south)):
        for chunk in range(chunks):
            at = cols(chunk)
            first = source[:8, at].astype(jnp.float32)
            last = source[rows - 8 : rows, at].astype(jnp.float32)
            to_partner[slot, :, at] = jnp.where(even, last[8 - HALO :], first[:HALO])


def substep(last, corridor, wall, refs):
    depth, east, south, bed, bed_e, bed_s, drag_e, drag_s, total, covers, count, level = refs[:12]
    ext, columns = depth.shape
    rows = ext - 2 * HALO
    chunks = columns // LANES
    tall = rows if last else ext
    lane = lanes_of(ext)
    zero = jnp.zeros((ext, LANES), jnp.float32)
    reach = 2 if last else corridor
    surf = depth[:, cols(0)] + bed[:, cols(0)]
    rolled = [pltpu.roll(surf, LANES - by, 1) for by in range(1, reach)]
    east_last = zero[:tall]
    state = (zero[:tall], zero[:tall])
    for chunk in range(chunks):
        at = cols(chunk)
        if chunk + 1 < chunks:
            then = cols(chunk + 1)
            surf_then = depth[:, then] + bed[:, then]
            rolled_then = [pltpu.roll(surf_then, LANES - by, 1) for by in range(1, reach)]
        else:
            surf_then, rolled_then = surf, rolled
        moved = [
            jnp.where(lane >= LANES - 1 - by, rolled_then[by], rolled[by])
            for by in range(reach - 1)
        ]
        new_east = face(
            east[:tall, at], surf[:tall], moved[0][:tall], bed_e[:tall, at], drag_e[:tall, at]
        )
        if chunk + 1 == chunks:
            new_east = jnp.where(lane[:tall] == LANES - 1, 0.0, new_east)
        new_south = face(south[:, at], surf, moved_up(surf), bed_s[:, at], drag_s[:, at])
        new_south = jnp.where(wall, 0.0, new_south)
        held = total[:tall, at]
        summed, state = right_sum(held, state)
        if not last:
            window = surf
            for other in moved:
                window = window + other
            level[:, at] = (1.0 - corridor * DRAIN) * level[:, at] + DRAIN * window
            total[:, at] = (1.0 - corridor * DRAIN) * held + count[:, at] * window
        east_rolled = pltpu.roll(new_east, 1, 1)
        north = pltpu.roll(new_south, 1, 0)
        inflow = jnp.where(lane[:tall] < 1, east_last, east_rolled) + north[:tall]
        east_last = east_rolled
        new_depth = (
            depth[:tall, at]
            + SPREAD * (inflow - new_east - new_south[:tall])
            + (FEED * summed - covers[:tall, at] * surf[:tall])
        )
        yield chunk, new_depth, new_east, new_south
        surf, rolled = surf_then, rolled_then


def wall_of(ext, tiles):
    position = lax.axis_index("gy")
    rows = ext - 2 * HALO
    row = lax.broadcasted_iota(jnp.int32, (ext, LANES), 0)
    return ((row == ext - 1) & (position == 0)) | ((row == rows - 1) & (position == tiles - 1))


def steps_kernel(corridor, tiles, by_partner, by_other, table_rows, sections, cells, *refs):
    held = refs[9:]
    own_term, partner_term, other_term = held[:3]
    depth, east, south, bed, mann, bed_e, bed_s, drag_e, drag_s, total, covers = held[3:14]
    count, level = held[14:]
    ext, columns = depth.shape
    rows = ext - 2 * HALO
    owned = sections.shape[1]
    chunks = columns // LANES
    position = lax.axis_index("gy")
    even = position % 2 == 0
    side = jnp.where(even, 1, -1)

    owners = [position, position + side, position - side, position - 2, position + 2]
    places = [jnp.clip(owner, 0, tiles - 1) for owner in owners]
    section = jnp.concatenate([sections[pl.ds(place, 1), :] for place in places], axis=1)
    cell = jnp.concatenate([cells[place, 0:1, :] for place in places], axis=1)
    real = jnp.concatenate(
        [
            jnp.full((1, owned), jnp.where(place == owner, 1, 0), jnp.int32)
            for place, owner in zip(places, owners)
        ],
        axis=1,
    )
    offset = cell - (position * rows - HALO) * columns
    valid = (real > 0) & (offset >= 0) & (offset < ext * columns)
    offset = jnp.where(valid, offset, 0).astype(jnp.float32)
    node_row = jnp.floor((offset + 0.5) * (1.0 / columns))
    node_col = (offset - node_row * float(columns)).astype(jnp.int32)
    node_row = node_row.astype(jnp.int32) - HALO
    node_row = jnp.where(node_row < 0, node_row + ext, node_row)
    node_chunk = node_col // LANES
    node_lane = node_col - node_chunk * LANES
    start_key = jnp.where(valid, node_chunk * ext + node_row, -1)
    at_lane = one_hot(LANES, node_lane)
    starts = one_hot(chunks * ext + 8, start_key).astype(jnp.bfloat16)
    parts = [at_lane] + [at_lane * part.astype(jnp.float32) for part in split3(section)]
    grid = lax.dot_general(
        starts,
        jnp.concatenate(parts, axis=0).astype(jnp.bfloat16),
        (((1,), (1,)), ((), ())),
        preferred_element_type=jnp.float32,
    )

    zero = jnp.zeros((ext, LANES), jnp.float32)
    state = (zero, zero)
    for chunk in range(chunks):
        at = cols(chunk)
        block = grid[chunk * ext : (chunk + 1) * ext]
        number = block[:, :LANES]
        count[:, at] = DRAIN * number
        total[:, at] = (
            block[:, LANES : 2 * LANES] + block[:, 2 * LANES : 3 * LANES]
        ) + block[:, 3 * LANES :]
        covering, state = right_sum(number, state)
        covers[:, at] = FEED * covering
        level[:, at] = zero

    entries = [table_rows[k : k + 1, :] for k in range(table_rows.shape[0])]
    for chunk in range(chunks):
        at = cols(chunk)
        halos = []
        for slot in range(5):
            a, b = by_partner[slot, :, at], by_other[slot, :, at]
            below = jnp.where(even, a, b)
            above = jnp.where(even, b, a)
            halos.append(jnp.concatenate([below, above], axis=0))
        depth[rows:, at] = halos[0]
        bed[rows:, at] = halos[1]
        mann[rows:, at] = looked_up(halos[2].astype(jnp.int32), entries)
        east[rows:, at] = halos[3]
        south[rows:, at] = halos[4]
    for chunk in range(chunks):
        at, then = cols(chunk), cols(min(chunk + 1, chunks - 1))
        b0, m0 = bed[rows:, at], mann[rows:, at]
        bed_e[rows:, at] = jnp.maximum(b0, moved_left(b0, bed[rows:, then], 1))
        drag_e[rows:, at] = drag_of(m0, moved_left(m0, mann[rows:, then], 1))
        b0, m0 = bed[rows - 8 :, at], mann[rows - 8 :, at]
        b_up = moved_up(bed[:, at])[rows - 8 :]
        m_up = moved_up(mann[:, at])[rows - 8 :]
        bed_s[rows - 8 :, at] = jnp.maximum(b0, b_up)
        drag_s[rows - 8 :, at] = drag_of(m0, m_up)

    wall = wall_of(ext, tiles)
    state_refs = (depth, east, south, bed, bed_e, bed_s, drag_e, drag_s, total, covers, count, level)

    def body(step, carry):
        for chunk, new_depth, new_east, new_south in substep(False, corridor, wall, state_refs):
            at = cols(chunk)
            depth[:, at] = new_depth
            east[:, at] = new_east
            south[:, at] = new_south
        return carry

    lax.fori_loop(0, STEPS - 1, body, 0)

    surf = depth[:rows, cols(0)] + bed[:rows, cols(0)]
    levels = []
    for chunk in range(chunks):
        then = cols(min(chunk + 1, chunks - 1))
        surf_then = depth[:rows, then] + bed[:rows, then]
        window = surf
        for by in range(1, corridor):
            window = window + moved_left(surf, surf_then, by)
        levels.append(
            (1.0 - corridor * DRAIN) * level[:rows, cols(chunk)] + DRAIN * window
        )
        surf = surf_then
    mine = 3 * owned
    inside = valid & (node_row < rows)
    take_key = jnp.where(inside, node_chunk * rows + node_row, -1)[:, :mine]
    takes = one_hot(chunks * rows, take_key).astype(jnp.bfloat16)
    picked = lax.dot_general(
        jnp.concatenate(split3(jnp.concatenate(levels, axis=0)), axis=1),
        takes,
        (((0,), (0,)), ((), ())),
        preferred_element_type=jnp.float32,
    )
    picked = (picked[:LANES] + picked[LANES : 2 * LANES]) + picked[2 * LANES :]
    terms = jnp.sum(picked * at_lane[:, :mine], axis=0, keepdims=True)
    kept = (1.0 - corridor * DRAIN) ** STEPS
    own_term[...] = kept * section[:, :owned] + terms[:, :owned]
    partner_term[...] = terms[:, owned : 2 * owned]
    other_term[...] = terms[:, 2 * owned :]


def last_kernel(corridor, tiles, *refs):
    state_refs = refs[:10]
    targets = refs[10:13]
    results = refs[13:16]
    sems = refs[16]
    ext, columns = state_refs[0].shape
    rows = ext - 2 * HALO
    chunks = columns // LANES
    group = 5
    copies = []
    steps = substep(True, corridor, wall_of(ext, tiles), state_refs + (None, None))
    for chunk, new_depth, new_east, new_south in steps:
        at = cols(chunk)
        for result, value in zip(results, (new_depth, new_east, new_south)):
            result[:, at] = value[:rows]
        if (chunk + 1) % group == 0 or chunk + 1 == chunks:
            first = chunk // group * group * LANES
            width = pl.ds(first, (chunk + 1) * LANES - first)
            for slot, (result, target) in enumerate(zip(results, targets)):
                copy = pltpu.make_async_copy(
                    result.at[:, width], target.at[:, width], sems.at[chunk // group, slot]
                )
                copy.start()
                copies.append(copy)
    for copy in copies:
        copy.wait()


def local(
    depth, flux_east, flux_south, river_section, bed_level, rough_class, manning_table, bank_cell
):
    rows, columns = depth.shape
    owned = river_section.shape[0]
    corridor = bank_cell.shape[0]
    tiles = lax.axis_size("gy")
    ext = rows + 2 * HALO
    chunks = columns // LANES
    sections = lax.all_gather(river_section, "gy")
    cells = lax.all_gather(bank_cell, "gy")

    def held(value):
        return pltpu.with_memory_space_constraint(value, pltpu.VMEM)

    def far(value):
        return pltpu.with_memory_space_constraint(value, pltpu.HBM)

    params = pltpu.CompilerParams(vmem_limit_bytes=VMEM_LIMIT)
    halo = pltpu.VMEM((5, HALO, columns), jnp.float32)
    field = pltpu.VMEM((ext, columns), jnp.float32)
    term = pltpu.VMEM((1, owned), jnp.float32)
    to_other = pl.pallas_call(
        pack_kernel,
        out_shape=halo,
        in_specs=[HBM_SPEC] * 5,
        out_specs=VMEM_SPEC,
        scratch_shapes=[
            pltpu.VMEM((4, 8, columns), jnp.float32),
            pltpu.VMEM((8, columns), jnp.int32),
            pltpu.SemaphoreType.DMA((5,)),
        ],
        compiler_params=params,
        name="pack",
    )(*[far(value) for value in (depth, bed_level, rough_class, flux_east, flux_south)])
    by_other = swapped(to_other, 1)
    prepared = pl.pallas_call(
        prepare_kernel,
        out_shape=[halo, pltpu.VMEM((manning_table.shape[0], LANES), jnp.float32)] + [field] * 9,
        in_specs=[SMEM_SPEC] + [HBM_SPEC] * 5,
        out_specs=[VMEM_SPEC] * 11,
        scratch_shapes=[
            pltpu.VMEM((rows, columns), jnp.int32),
            pltpu.SemaphoreType.DMA((5,)),
        ],
        compiler_params=params,
        name="prepare",
    )(
        manning_table,
        *[far(value) for value in (depth, flux_east, flux_south, bed_level, rough_class)],
    )
    by_partner = swapped(prepared[0], 0)
    stepped = pl.pallas_call(
        functools.partial(steps_kernel, corridor, tiles),
        out_shape=[term] * 3 + [field] * 11,
        in_specs=[VMEM_SPEC] * 14,
        out_specs=[VMEM_SPEC] * 14,
        scratch_shapes=[field] * 2,
        input_output_aliases={5 + slot: 3 + slot for slot in range(9)},
        compiler_params=params,
        name="steps",
    )(
        held(by_partner),
        held(by_other),
        held(prepared[1]),
        sections,
        cells,
        *[held(value) for value in prepared[2:]],
    )
    from_other = swapped(stepped[2].reshape(owned), 1)
    from_partner = swapped(stepped[1].reshape(owned), 0)
    fields = stepped[3:]
    result = pltpu.HBM((rows, columns), jnp.float32)
    depth, flux_east, flux_south = pl.pallas_call(
        functools.partial(last_kernel, corridor, tiles),
        out_shape=[result] * 3,
        in_specs=[VMEM_SPEC] * 10,
        out_specs=[HBM_SPEC] * 3,
        scratch_shapes=[pltpu.VMEM((rows, columns), jnp.float32)] * 3
        + [pltpu.SemaphoreType.DMA((-(-chunks // 5), 3))],
        compiler_params=params,
        name="last",
    )(*[held(value) for value in fields[:4] + fields[5:]])
    river_section = stepped[0].reshape(owned) + from_partner + from_other
    return (depth, flux_east, flux_south, river_section)


def solution(mesh):
    return jax.shard_map(
        local,
        mesh=mesh,
        in_specs=(
            P(("runs", "gy"), None),
            P(("runs", "gy"), None),
            P(("runs", "gy"), None),
            P(("runs", "gy")),
            P("gy", None),
            P("gy", None),
            P(),
            P(None, "gy"),
        ),
        out_specs=(
            P(("runs", "gy"), None),
            P(("runs", "gy"), None),
            P(("runs", "gy"), None),
            P(("runs", "gy")),
        ),
        check_vma=False,
    )
```

```python
import functools

import jax
import jax.numpy as jnp
from jax import lax
from jax.experimental import pallas as pl
from jax.experimental.pallas import tpu as pltpu
from jax.sharding import PartitionSpec as P

STEPS = 4

GRAV = 9.81
TSTEP = 8.0
CELL = 90.0
FLOOR = 0.05
BANK_COEF = 200.0
CELL_AREA = 8100.0
NODE_AREA = 20000.0

LANES = 128
HALO = 4
SLOPE = GRAV * TSTEP / CELL
SPREAD = TSTEP / CELL
FEED = TSTEP * BANK_COEF / CELL_AREA
DRAIN = TSTEP * BANK_COEF / NODE_AREA
VMEM_LIMIT = 32 * 1024 * 1024

SMEM_SPEC = pl.BlockSpec(memory_space=pltpu.SMEM)
VMEM_SPEC = pl.BlockSpec(memory_space=pltpu.VMEM)
HBM_SPEC = pl.BlockSpec(memory_space=pltpu.HBM)


def swapped(value, first):
    count = lax.axis_size("gy")
    pairs = []
    for low in range(first, count - 1, 2):
        pairs += [(low, low + 1), (low + 1, low)]
    return lax.ppermute(value, "gy", pairs)


def cols(chunk):
    return slice(chunk * LANES, (chunk + 1) * LANES)


def lanes_of(rows):
    return lax.broadcasted_iota(jnp.int32, (rows, LANES), 1)


def moved_left(value, following, by):
    return jnp.where(
        lanes_of(value.shape[0]) >= LANES - by,
        pltpu.roll(following, LANES - by, 1),
        pltpu.roll(value, LANES - by, 1),
    )


def moved_up(value):
    return pltpu.roll(value, value.shape[0] - 1, 0)


def split3(value):
    high = value.astype(jnp.bfloat16)
    rest = value - high.astype(jnp.float32)
    middle = rest.astype(jnp.bfloat16)
    low = (rest - middle.astype(jnp.float32)).astype(jnp.bfloat16)
    return high, middle, low


def one_hot(count, key):
    rows = lax.broadcasted_iota(jnp.int32, (count, key.shape[1]), 0)
    return jnp.where(rows == key, 1.0, 0.0)


def drag_of(mann_a, mann_b):
    pair = mann_a + mann_b
    return (0.25 * GRAV * TSTEP) * (pair * pair)


def looked_up(klass, entries):
    value = jnp.broadcast_to(entries[0], klass.shape)
    for k in range(1, len(entries)):
        value = jnp.where(klass == k, entries[k], value)
    return value


def face(flux, surf_a, surf_b, bed_max, drag):
    flow_depth = jnp.maximum(jnp.maximum(surf_a, surf_b) - bed_max, FLOOR)
    power = jnp.exp2((-7.0 / 3.0) * jnp.log2(flow_depth))
    driven = flux - SLOPE * flow_depth * (surf_b - surf_a)
    damping = 1.0 + drag * jnp.abs(flux) * power
    inverse = pl.reciprocal(damping, approx=True)
    inverse = inverse * (2.0 - damping * inverse)
    return driven * inverse


def right_sum(value, state):
    lane = lanes_of(value.shape[0])
    once = pltpu.roll(value, 1, 1)
    pair = value + jnp.where(lane < 1, state[0], once)
    twice = pltpu.roll(pair, 2, 1)
    return pair + jnp.where(lane < 2, state[1], twice), (once, twice)


def pack_kernel(
    depth, bed, rough, east, south, section, cells, to_other, own, held, held_rough, held_cells, sems
):
    rows, columns = depth.shape
    even = lax.axis_index("gy") % 2 == 0
    start = pl.multiple_of(jnp.where(even, 0, rows - 8), 8)
    copies = [
        pltpu.make_async_copy(source, target, sems.at[slot])
        for slot, (source, target) in enumerate(
            (
                (depth.at[pl.ds(start, 8), :], held.at[0]),
                (bed.at[pl.ds(start, 8), :], held.at[1]),
                (rough.at[pl.ds(start, 8), :], held_rough),
                (east.at[pl.ds(start, 8), :], held.at[2]),
                (south.at[pl.ds(start, 8), :], held.at[3]),
                (section, own.at[pl.ds(0, 1), :]),
                (cells, held_cells),
            )
        )
    ]
    for copy in copies:
        copy.start()
    for slot in range(5):
        copies[slot].wait()
        block = (
            held_rough[...].astype(jnp.float32) if slot == 2 else held[slot - (slot > 2)]
        )
        to_other[slot, :, :columns] = jnp.where(even, block[:HALO], block[8 - HALO :])
        to_other[slot, :, columns:] = jnp.zeros((HALO, LANES), jnp.float32)
    for copy in copies[5:]:
        copy.wait()
    own[1:2, :] = (held_cells[0:1, :] + 1).astype(jnp.float32)
    to_other[0, 0:2, columns:] = own[...]


def join_kernel(before, section, cells, to_other):
    columns = to_other.shape[2] - LANES
    to_other[0, 2:3, columns:] = section[...]
    to_other[0, 3:4, columns:] = (cells[0:1, :] + 1).astype(jnp.float32)


def prepare_kernel(
    table,
    depth_in,
    east_in,
    south_in,
    bed_in,
    rough_in,
    to_partner,
    table_rows,
    depth,
    east,
    south,
    bed,
    mann,
    bed_e,
    bed_s,
    drag_e,
    drag_s,
    rough,
    sems,
):
    rows, columns = depth_in.shape
    chunks = columns // LANES
    even = lax.axis_index("gy") % 2 == 0
    own = pl.ds(0, rows)
    copies = [
        pltpu.make_async_copy(source, target, sems.at[slot])
        for slot, (source, target) in enumerate(
            (
                (rough_in, rough),
                (bed_in, bed.at[own, :]),
                (depth_in, depth.at[own, :]),
                (east_in, east.at[own, :]),
                (south_in, south.at[own, :]),
            )
        )
    ]
    for copy in copies:
        copy.start()
    entries = [table[k] for k in range(table.shape[0])]
    for k, entry in enumerate(entries):
        table_rows[k : k + 1, :] = jnp.full((1, LANES), entry, jnp.float32)
    copies[0].wait()
    copies[1].wait()
    for chunk in range(chunks):
        at = cols(chunk)
        mann[:rows, at] = looked_up(rough[:, at], entries)
    for chunk in range(chunks):
        at, then = cols(chunk), cols(min(chunk + 1, chunks - 1))
        b0, m0 = bed[:rows, at], mann[:rows, at]
        bed_e[:rows, at] = jnp.maximum(b0, moved_left(b0, bed[:rows, then], 1))
        bed_s[:rows, at] = jnp.maximum(b0, moved_up(b0))
        drag_e[:rows, at] = drag_of(m0, moved_left(m0, mann[:rows, then], 1))
        drag_s[:rows, at] = drag_of(m0, moved_up(m0))
    for copy in copies[2:]:
        copy.wait()
    for slot, source in enumerate((depth, bed, rough, east, south)):
        for chunk in range(chunks):
            at = cols(chunk)
            first = source[:8, at].astype(jnp.float32)
            last = source[rows - 8 : rows, at].astype(jnp.float32)
            to_partner[slot, :, at] = jnp.where(even, last[8 - HALO :], first[:HALO])


def substep(last, corridor, wall, refs):
    depth, east, south, bed, bed_e, bed_s, drag_e, drag_s, total, covers, count, level = refs[:12]
    ext, columns = depth.shape
    rows = ext - 2 * HALO
    chunks = columns // LANES
    tall = rows if last else ext
    lane = lanes_of(ext)
    zero = jnp.zeros((ext, LANES), jnp.float32)
    reach = 2 if last else corridor
    surf = depth[:, cols(0)] + bed[:, cols(0)]
    rolled = [pltpu.roll(surf, LANES - by, 1) for by in range(1, reach)]
    east_last = zero[:tall]
    state = (zero[:tall], zero[:tall])
    for chunk in range(chunks):
        at = cols(chunk)
        if chunk + 1 < chunks:
            then = cols(chunk + 1)
            surf_then = depth[:, then] + bed[:, then]
            rolled_then = [pltpu.roll(surf_then, LANES - by, 1) for by in range(1, reach)]
        else:
            surf_then, rolled_then = surf, rolled
        moved = [
            jnp.where(lane >= LANES - 1 - by, rolled_then[by], rolled[by])
            for by in range(reach - 1)
        ]
        new_east = face(
            east[:tall, at], surf[:tall], moved[0][:tall], bed_e[:tall, at], drag_e[:tall, at]
        )
        if chunk + 1 == chunks:
            new_east = jnp.where(lane[:tall] == LANES - 1, 0.0, new_east)
        new_south = face(south[:, at], surf, moved_up(surf), bed_s[:, at], drag_s[:, at])
        new_south = jnp.where(wall, 0.0, new_south)
        held = total[:tall, at]
        summed, state = right_sum(held, state)
        if not last:
            window = surf
            for other in moved:
                window = window + other
            level[:, at] = (1.0 - corridor * DRAIN) * level[:, at] + DRAIN * window
            total[:, at] = (1.0 - corridor * DRAIN) * held + count[:, at] * window
        east_rolled = pltpu.roll(new_east, 1, 1)
        north = pltpu.roll(new_south, 1, 0)
        inflow = jnp.where(lane[:tall] < 1, east_last, east_rolled) + north[:tall]
        east_last = east_rolled
        new_depth = (
            depth[:tall, at]
            + SPREAD * (inflow - new_east - new_south[:tall])
            + (FEED * summed - covers[:tall, at] * surf[:tall])
        )
        yield chunk, new_depth, new_east, new_south
        surf, rolled = surf_then, rolled_then


def wall_of(ext, tiles):
    position = lax.axis_index("gy")
    rows = ext - 2 * HALO
    row = lax.broadcasted_iota(jnp.int32, (ext, LANES), 0)
    return ((row == ext - 1) & (position == 0)) | ((row == rows - 1) & (position == tiles - 1))


def steps_kernel(
    corridor, tiles, by_partner, by_other, table_rows, own, partner_section, partner_cells, far, *refs
):
    held = refs[9:]
    own_term, partner_term, other_term = held[:3]
    depth, east, south, bed, mann, bed_e, bed_s, drag_e, drag_s, total, covers = held[3:14]
    count, level = held[14:]
    ext, columns = depth.shape
    rows = ext - 2 * HALO
    owned = own.shape[1]
    chunks = columns // LANES
    position = lax.axis_index("gy")
    even = position % 2 == 0
    side = jnp.where(even, 1, -1)

    near = by_other[0, :, columns:]
    partner = jnp.where(position + side < tiles, partner_cells[0:1, :] + 1, 0).astype(jnp.float32)
    section = jnp.concatenate(
        [own[0:1, :], partner_section[...], near[0:1, :], near[2:3, :], far[0:1, :]], axis=1
    )
    cell = jnp.concatenate([own[1:2, :], partner, near[1:2, :], near[3:4, :], far[1:2, :]], axis=1)
    base = ((position * rows - HALO) * columns + 1).astype(jnp.float32)
    offset = cell - base
    valid = (cell > 0.0) & (offset >= 0.0) & (offset < float(ext * columns))
    offset = jnp.where(valid, offset, 0.0)
    node_row = jnp.floor((offset + 0.5) * (1.0 / columns))
    node_col = (offset - node_row * float(columns)).astype(jnp.int32)
    node_row = node_row.astype(jnp.int32) - HALO
    node_row = jnp.where(node_row < 0, node_row + ext, node_row)
    node_chunk = node_col // LANES
    node_lane = node_col - node_chunk * LANES
    start_key = jnp.where(valid, node_chunk * ext + node_row, -1)
    at_lane = one_hot(LANES, node_lane)
    starts = one_hot(chunks * ext + 8, start_key).astype(jnp.bfloat16)
    parts = [at_lane] + [at_lane * part.astype(jnp.float32) for part in split3(section)]
    grid = lax.dot_general(
        starts,
        jnp.concatenate(parts, axis=0).astype(jnp.bfloat16),
        (((1,), (1,)), ((), ())),
        preferred_element_type=jnp.float32,
    )

    zero = jnp.zeros((ext, LANES), jnp.float32)
    state = (zero, zero)
    for chunk in range(chunks):
        at = cols(chunk)
        block = grid[chunk * ext : (chunk + 1) * ext]
        number = block[:, :LANES]
        count[:, at] = DRAIN * number
        total[:, at] = (
            block[:, LANES : 2 * LANES] + block[:, 2 * LANES : 3 * LANES]
        ) + block[:, 3 * LANES :]
        covering, state = right_sum(number, state)
        covers[:, at] = FEED * covering
        level[:, at] = zero

    entries = [table_rows[k : k + 1, :] for k in range(table_rows.shape[0])]
    for chunk in range(chunks):
        at = cols(chunk)
        halos = []
        for slot in range(5):
            a, b = by_partner[slot, :, at], by_other[slot, :, at]
            below = jnp.where(even, a, b)
            above = jnp.where(even, b, a)
            halos.append(jnp.concatenate([below, above], axis=0))
        depth[rows:, at] = halos[0]
        bed[rows:, at] = halos[1]
        mann[rows:, at] = looked_up(halos[2].astype(jnp.int32), entries)
        east[rows:, at] = halos[3]
        south[rows:, at] = halos[4]
    for chunk in range(chunks):
        at, then = cols(chunk), cols(min(chunk + 1, chunks - 1))
        b0, m0 = bed[rows:, at], mann[rows:, at]
        bed_e[rows:, at] = jnp.maximum(b0, moved_left(b0, bed[rows:, then], 1))
        drag_e[rows:, at] = drag_of(m0, moved_left(m0, mann[rows:, then], 1))
        b0, m0 = bed[rows - 8 :, at], mann[rows - 8 :, at]
        b_up = moved_up(bed[:, at])[rows - 8 :]
        m_up = moved_up(mann[:, at])[rows - 8 :]
        bed_s[rows - 8 :, at] = jnp.maximum(b0, b_up)
        drag_s[rows - 8 :, at] = drag_of(m0, m_up)

    wall = wall_of(ext, tiles)
    state_refs = (depth, east, south, bed, bed_e, bed_s, drag_e, drag_s, total, covers, count, level)

    def body(step, carry):
        for chunk, new_depth, new_east, new_south in substep(False, corridor, wall, state_refs):
            at = cols(chunk)
            depth[:, at] = new_depth
            east[:, at] = new_east
            south[:, at] = new_south
        return carry

    lax.fori_loop(0, STEPS - 1, body, 0)

    surf = depth[:rows, cols(0)] + bed[:rows, cols(0)]
    levels = []
    for chunk in range(chunks):
        then = cols(min(chunk + 1, chunks - 1))
        surf_then = depth[:rows, then] + bed[:rows, then]
        window = surf
        for by in range(1, corridor):
            window = window + moved_left(surf, surf_then, by)
        levels.append(
            (1.0 - corridor * DRAIN) * level[:rows, cols(chunk)] + DRAIN * window
        )
        surf = surf_then
    mine = 3 * owned
    inside = valid & (node_row < rows)
    take_key = jnp.where(inside, node_chunk * rows + node_row, -1)[:, :mine]
    takes = one_hot(chunks * rows, take_key).astype(jnp.bfloat16)
    picked = lax.dot_general(
        jnp.concatenate(split3(jnp.concatenate(levels, axis=0)), axis=1),
        takes,
        (((0,), (0,)), ((), ())),
        preferred_element_type=jnp.float32,
    )
    picked = (picked[:LANES] + picked[LANES : 2 * LANES]) + picked[2 * LANES :]
    terms = jnp.sum(picked * at_lane[:, :mine], axis=0, keepdims=True)
    kept = (1.0 - corridor * DRAIN) ** STEPS
    own_term[...] = kept * section[:, :owned] + terms[:, :owned]
    partner_term[...] = terms[:, owned : 2 * owned]
    other_term[...] = terms[:, 2 * owned :]


def last_kernel(corridor, tiles, *refs):
    state_refs = refs[:10]
    targets = refs[10:13]
    results = refs[13:16]
    sems = refs[16]
    ext, columns = state_refs[0].shape
    rows = ext - 2 * HALO
    chunks = columns // LANES
    group = 5
    copies = []
    steps = substep(True, corridor, wall_of(ext, tiles), state_refs + (None, None))
    for chunk, new_depth, new_east, new_south in steps:
        at = cols(chunk)
        for result, value in zip(results, (new_depth, new_east, new_south)):
            result[:, at] = value[:rows]
        if (chunk + 1) % group == 0 or chunk + 1 == chunks:
            first = chunk // group * group * LANES
            width = pl.ds(first, (chunk + 1) * LANES - first)
            for slot, (result, target) in enumerate(zip(results, targets)):
                copy = pltpu.make_async_copy(
                    result.at[:, width], target.at[:, width], sems.at[chunk // group, slot]
                )
                copy.start()
                copies.append(copy)
    for copy in copies:
        copy.wait()


def local(
    depth, flux_east, flux_south, river_section, bed_level, rough_class, manning_table, bank_cell
):
    rows, columns = depth.shape
    owned = river_section.shape[0]
    corridor = bank_cell.shape[0]
    tiles = lax.axis_size("gy")
    ext = rows + 2 * HALO
    chunks = columns // LANES
    partner_section = swapped(river_section, 0).reshape(1, owned)
    partner_cells = swapped(bank_cell, 0)

    def held(value):
        return pltpu.with_memory_space_constraint(value, pltpu.VMEM)

    def far(value):
        return pltpu.with_memory_space_constraint(value, pltpu.HBM)

    params = pltpu.CompilerParams(vmem_limit_bytes=VMEM_LIMIT)
    halo = pltpu.VMEM((5, HALO, columns), jnp.float32)
    field = pltpu.VMEM((ext, columns), jnp.float32)
    term = pltpu.VMEM((1, owned), jnp.float32)
    wide = pltpu.VMEM((5, HALO, columns + LANES), jnp.float32)
    to_other, own = pl.pallas_call(
        pack_kernel,
        out_shape=[wide, pltpu.VMEM((2, owned), jnp.float32)],
        in_specs=[HBM_SPEC] * 7,
        out_specs=[VMEM_SPEC] * 2,
        scratch_shapes=[
            pltpu.VMEM((4, 8, columns), jnp.float32),
            pltpu.VMEM((8, columns), jnp.int32),
            pltpu.VMEM((corridor, owned), jnp.int32),
            pltpu.SemaphoreType.DMA((7,)),
        ],
        compiler_params=params,
        name="pack",
    )(
        *[far(value) for value in (depth, bed_level, rough_class, flux_east, flux_south)],
        far(river_section.reshape(1, owned)),
        far(bank_cell),
    )
    to_other = pl.pallas_call(
        join_kernel,
        out_shape=wide,
        in_specs=[VMEM_SPEC] * 3,
        out_specs=VMEM_SPEC,
        input_output_aliases={0: 0},
        compiler_params=params,
        name="join",
    )(held(to_other), held(partner_section), held(partner_cells))
    by_other = swapped(to_other, 1)
    from_far = swapped(by_other[0, 0:2, columns:], 0)
    prepared = pl.pallas_call(
        prepare_kernel,
        out_shape=[halo, pltpu.VMEM((manning_table.shape[0], LANES), jnp.float32)] + [field] * 9,
        in_specs=[SMEM_SPEC] + [HBM_SPEC] * 5,
        out_specs=[VMEM_SPEC] * 11,
        scratch_shapes=[
            pltpu.VMEM((rows, columns), jnp.int32),
            pltpu.SemaphoreType.DMA((5,)),
        ],
        compiler_params=params,
        name="prepare",
    )(
        manning_table,
        *[far(value) for value in (depth, flux_east, flux_south, bed_level, rough_class)],
    )
    by_partner = swapped(prepared[0], 0)
    stepped = pl.pallas_call(
        functools.partial(steps_kernel, corridor, tiles),
        out_shape=[term] * 3 + [field] * 11,
        in_specs=[VMEM_SPEC] * 16,
        out_specs=[VMEM_SPEC] * 14,
        scratch_shapes=[field] * 2,
        input_output_aliases={7 + slot: 3 + slot for slot in range(9)},
        compiler_params=params,
        name="steps",
    )(
        held(by_partner),
        held(by_other),
        held(prepared[1]),
        held(own),
        held(partner_section),
        held(partner_cells),
        held(from_far),
        *[held(value) for value in prepared[2:]],
    )
    from_other = swapped(stepped[2].reshape(owned), 1)
    from_partner = swapped(stepped[1].reshape(owned), 0)
    fields = stepped[3:]
    result = pltpu.HBM((rows, columns), jnp.float32)
    depth, flux_east, flux_south = pl.pallas_call(
        functools.partial(last_kernel, corridor, tiles),
        out_shape=[result] * 3,
        in_specs=[VMEM_SPEC] * 10,
        out_specs=[HBM_SPEC] * 3,
        scratch_shapes=[pltpu.VMEM((rows, columns), jnp.float32)] * 3
        + [pltpu.SemaphoreType.DMA((-(-chunks // 5), 3))],
        compiler_params=params,
        name="last",
    )(*[held(value) for value in fields[:4] + fields[5:]])
    river_section = stepped[0].reshape(owned) + from_partner + from_other
    return (depth, flux_east, flux_south, river_section)


def solution(mesh):
    return jax.shard_map(
        local,
        mesh=mesh,
        in_specs=(
            P(("runs", "gy"), None),
            P(("runs", "gy"), None),
            P(("runs", "gy"), None),
            P(("runs", "gy")),
            P("gy", None),
            P("gy", None),
            P(),
            P(None, "gy"),
        ),
        out_specs=(
            P(("runs", "gy"), None),
            P(("runs", "gy"), None),
            P(("runs", "gy"), None),
            P(("runs", "gy")),
        ),
        check_vma=False,
    )
```

```python
import functools

import jax
import jax.numpy as jnp
from jax import lax
from jax.experimental import pallas as pl
from jax.experimental.pallas import tpu as pltpu
from jax.sharding import PartitionSpec as P

STEPS = 4

GRAV = 9.81
TSTEP = 8.0
CELL = 90.0
FLOOR = 0.05
BANK_COEF = 200.0
CELL_AREA = 8100.0
NODE_AREA = 20000.0

LANES = 128
HALO = 4
SLOPE = GRAV * TSTEP / CELL
SPREAD = TSTEP / CELL
FEED = TSTEP * BANK_COEF / CELL_AREA
DRAIN = TSTEP * BANK_COEF / NODE_AREA
VMEM_LIMIT = 32 * 1024 * 1024

SMEM_SPEC = pl.BlockSpec(memory_space=pltpu.SMEM)
VMEM_SPEC = pl.BlockSpec(memory_space=pltpu.VMEM)
HBM_SPEC = pl.BlockSpec(memory_space=pltpu.HBM)


def swapped(value, first):
    count = lax.axis_size("gy")
    pairs = []
    for low in range(first, count - 1, 2):
        pairs += [(low, low + 1), (low + 1, low)]
    return lax.ppermute(value, "gy", pairs)


def cols(chunk):
    return slice(chunk * LANES, (chunk + 1) * LANES)


def lanes_of(rows):
    return lax.broadcasted_iota(jnp.int32, (rows, LANES), 1)


def moved_left(value, following, by):
    return jnp.where(
        lanes_of(value.shape[0]) >= LANES - by,
        pltpu.roll(following, LANES - by, 1),
        pltpu.roll(value, LANES - by, 1),
    )


def moved_up(value):
    return pltpu.roll(value, value.shape[0] - 1, 0)


def split3(value):
    high = value.astype(jnp.bfloat16)
    rest = value - high.astype(jnp.float32)
    middle = rest.astype(jnp.bfloat16)
    low = (rest - middle.astype(jnp.float32)).astype(jnp.bfloat16)
    return high, middle, low


def one_hot(count, key):
    rows = lax.broadcasted_iota(jnp.int32, (count, key.shape[1]), 0)
    return jnp.where(rows == key, 1.0, 0.0)


def drag_of(mann_a, mann_b):
    pair = mann_a + mann_b
    return (0.25 * GRAV * TSTEP) * (pair * pair)


def looked_up(klass, entries):
    value = jnp.broadcast_to(entries[0], klass.shape)
    for k in range(1, len(entries)):
        value = jnp.where(klass == k, entries[k], value)
    return value


def face(flux, surf_a, surf_b, bed_max, drag):
    flow_depth = jnp.maximum(jnp.maximum(surf_a, surf_b) - bed_max, FLOOR)
    power = jnp.exp2((-7.0 / 3.0) * jnp.log2(flow_depth))
    driven = flux - SLOPE * flow_depth * (surf_b - surf_a)
    damping = 1.0 + drag * jnp.abs(flux) * power
    return driven * pl.reciprocal(damping, approx=True)


def right_sum(value, state):
    lane = lanes_of(value.shape[0])
    once = pltpu.roll(value, 1, 1)
    pair = value + jnp.where(lane < 1, state[0], once)
    twice = pltpu.roll(pair, 2, 1)
    return pair + jnp.where(lane < 2, state[1], twice), (once, twice)


def east_walled(value, chunk, chunks):
    if chunk + 1 < chunks:
        return value
    return jnp.where(lanes_of(value.shape[0]) == LANES - 1, 0.0, value)


def located(cell, position, rows, ext, columns):
    base = ((position * rows - HALO) * columns + 1).astype(jnp.float32)
    offset = cell - base
    valid = (cell > 0.0) & (offset >= 0.0) & (offset < float(ext * columns))
    offset = jnp.where(valid, offset, 0.0)
    row = jnp.floor((offset + 0.5) * (1.0 / columns))
    column = (offset - row * float(columns)).astype(jnp.int32)
    row = row.astype(jnp.int32) - HALO
    row = jnp.where(row < 0, row + ext, row)
    chunk = column // LANES
    return valid, row, chunk, column - chunk * LANES


def scattered(section, key, lane, count):
    at_lane = one_hot(LANES, lane)
    parts = [at_lane] + [at_lane * part.astype(jnp.float32) for part in split3(section)]
    grid = lax.dot_general(
        one_hot(-(-count // 16) * 16, key).astype(jnp.bfloat16),
        jnp.concatenate(parts, axis=0).astype(jnp.bfloat16),
        (((1,), (1,)), ((), ())),
        preferred_element_type=jnp.float32,
    )
    number = grid[:, :LANES]
    total = (grid[:, LANES : 2 * LANES] + grid[:, 2 * LANES : 3 * LANES]) + grid[:, 3 * LANES :]
    return number, total


def pack_kernel(
    depth, bed, rough, east, south, section, cells, to_other, own, held, held_rough, held_cells, sems
):
    rows, columns = depth.shape
    even = lax.axis_index("gy") % 2 == 0
    start = pl.multiple_of(jnp.where(even, 0, rows - 8), 8)
    copies = [
        pltpu.make_async_copy(source, target, sems.at[slot])
        for slot, (source, target) in enumerate(
            (
                (depth.at[pl.ds(start, 8), :], held.at[0]),
                (bed.at[pl.ds(start, 8), :], held.at[1]),
                (rough.at[pl.ds(start, 8), :], held_rough),
                (east.at[pl.ds(start, 8), :], held.at[2]),
                (south.at[pl.ds(start, 8), :], held.at[3]),
                (section, own.at[pl.ds(0, 1), :]),
                (cells, held_cells),
            )
        )
    ]
    for copy in copies:
        copy.start()
    for slot in range(5):
        copies[slot].wait()
        block = (
            held_rough[...].astype(jnp.float32) if slot == 2 else held[slot - (slot > 2)]
        )
        to_other[slot, :, :columns] = jnp.where(even, block[:HALO], block[8 - HALO :])
        to_other[slot, :, columns:] = jnp.zeros((HALO, LANES), jnp.float32)
    for copy in copies[5:]:
        copy.wait()
    own[1:2, :] = (held_cells[0:1, :] + 1).astype(jnp.float32)
    to_other[0, 0:2, columns:] = own[...]


def join_kernel(before, section, cells, to_other):
    columns = to_other.shape[2] - LANES
    to_other[0, 2:3, columns:] = section[...]
    to_other[0, 3:4, columns:] = (cells[0:1, :] + 1).astype(jnp.float32)


def load_kernel(
    depth_in, east_in, south_in, bed_in, rough_in, to_partner, surf, east, south, bed, rough, sems
):
    rows, columns = depth_in.shape
    even = lax.axis_index("gy") % 2 == 0
    own = pl.ds(0, rows)
    copies = [
        pltpu.make_async_copy(source, target.at[own, :], sems.at[slot])
        for slot, (source, target) in enumerate(
            (
                (depth_in, surf),
                (bed_in, bed),
                (rough_in, rough),
                (east_in, east),
                (south_in, south),
            )
        )
    ]
    for copy in copies:
        copy.start()
    for slot, source in enumerate((surf, bed, rough, east, south)):
        copies[slot].wait()
        for chunk in range(columns // LANES):
            at = cols(chunk)
            first = source[:8, at].astype(jnp.float32)
            last = source[rows - 8 : rows, at].astype(jnp.float32)
            to_partner[slot, :, at] = jnp.where(even, last[8 - HALO :], first[:HALO])


def prepare_kernel(table, rough, own, partner_section, partner_cells, *refs):
    surf, east, south, bed = refs[4:8]
    mann, bed_e, bed_s, drag_e, drag_s, number, total, table_rows = refs[8:]
    ext, columns = surf.shape
    rows = ext - 2 * HALO
    chunks = columns // LANES
    tiles = lax.axis_size("gy")
    position = lax.axis_index("gy")
    side = jnp.where(position % 2 == 0, 1, -1)
    entries = [table[k] for k in range(table.shape[0])]
    for k, entry in enumerate(entries):
        table_rows[k : k + 1, :] = jnp.full((1, LANES), entry, jnp.float32)
    for chunk in range(chunks):
        at = cols(chunk)
        mann[:rows, at] = looked_up(rough[:, at], entries)
        surf[:rows, at] = surf[:rows, at] + bed[:rows, at]

    partner = jnp.where(position + side < tiles, partner_cells[0:1, :] + 1, 0).astype(jnp.float32)
    section = jnp.concatenate([own[0:1, :], partner_section[...]], axis=1)
    cell = jnp.concatenate([own[1:2, :], partner], axis=1)
    valid, node_row, node_chunk, node_lane = located(cell, position, rows, ext, columns)
    key = jnp.where(valid, node_chunk * ext + node_row, -1)
    starts, levels = scattered(section, key, node_lane, chunks * ext)
    for chunk in range(chunks):
        at = cols(chunk)
        number[:, at] = starts[chunk * ext : (chunk + 1) * ext]
        total[:, at] = levels[chunk * ext : (chunk + 1) * ext]

    kept = lax.broadcasted_iota(jnp.int32, (rows, LANES), 0) == rows - 1
    for chunk in range(chunks):
        at, then = cols(chunk), cols(min(chunk + 1, chunks - 1))
        s0, b0, m0 = surf[:rows, at], bed[:rows, at], mann[:rows, at]
        bed_max = jnp.maximum(b0, moved_left(b0, bed[:rows, then], 1))
        drag = drag_of(m0, moved_left(m0, mann[:rows, then], 1))
        bed_e[:rows, at] = bed_max
        drag_e[:rows, at] = drag
        new_east = face(
            east[:rows, at], s0, moved_left(s0, surf[:rows, then], 1), bed_max, drag
        )
        east[:rows, at] = east_walled(new_east, chunk, chunks)
        bed_max = jnp.maximum(b0, moved_up(b0))
        drag = drag_of(m0, moved_up(m0))
        bed_s[:rows, at] = bed_max
        drag_s[:rows, at] = drag
        q0 = south[:rows, at]
        south[:rows, at] = jnp.where(kept, q0, face(q0, s0, moved_up(s0), bed_max, drag))


def wall_of(ext, tiles):
    position = lax.axis_index("gy")
    rows = ext - 2 * HALO
    row = lax.broadcasted_iota(jnp.int32, (16, LANES), 0) + (ext - 16)
    return ((row == ext - 1) & (position == 0)) | ((row == rows - 1) & (position == tiles - 1))


def border_kernel(tiles, by_partner, by_other, table_rows, *refs):
    surf, east, south, bed, mann, bed_e, bed_s, drag_e, drag_s, number, total = refs[11:]
    ext, columns = surf.shape
    rows = ext - 2 * HALO
    chunks = columns // LANES
    position = lax.axis_index("gy")
    even = position % 2 == 0
    entries = [table_rows[k : k + 1, :] for k in range(table_rows.shape[0])]
    for chunk in range(chunks):
        at = cols(chunk)
        halos = []
        for slot in range(5):
            a, b = by_partner[slot, :, at], by_other[slot, :, at]
            below = jnp.where(even, a, b)
            above = jnp.where(even, b, a)
            halos.append(jnp.concatenate([below, above], axis=0))
        surf[rows:, at] = halos[0] + halos[1]
        bed[rows:, at] = halos[1]
        mann[rows:, at] = looked_up(halos[2].astype(jnp.int32), entries)
        east[rows:, at] = halos[3]
        south[rows:, at] = halos[4]

    near = by_other[0, :, columns:]
    section = jnp.concatenate([near[0:1, :], near[2:3, :]], axis=1)
    cell = jnp.concatenate([near[1:2, :], near[3:4, :]], axis=1)
    valid, node_row, node_chunk, node_lane = located(cell, position, rows, ext, columns)
    key = jnp.where(valid, node_chunk * ext + node_row, -1)
    starts, levels = scattered(section, key, node_lane, chunks * ext)

    wall = wall_of(ext, tiles)
    kept = lax.broadcasted_iota(jnp.int32, (16, LANES), 0) < 7
    for chunk in range(chunks):
        at, then = cols(chunk), cols(min(chunk + 1, chunks - 1))
        number[:, at] += starts[chunk * ext : (chunk + 1) * ext]
        total[:, at] += levels[chunk * ext : (chunk + 1) * ext]
        s0, b0, m0 = surf[rows:, at], bed[rows:, at], mann[rows:, at]
        bed_max = jnp.maximum(b0, moved_left(b0, bed[rows:, then], 1))
        drag = drag_of(m0, moved_left(m0, mann[rows:, then], 1))
        bed_e[rows:, at] = bed_max
        drag_e[rows:, at] = drag
        new_east = face(
            east[rows:, at], s0, moved_left(s0, surf[rows:, then], 1), bed_max, drag
        )
        east[rows:, at] = east_walled(new_east, chunk, chunks)

        def rolled_up(ref):
            value = jnp.concatenate([ref[rows - 8 :, at], ref[:8, at]], axis=0)
            return value[:16], moved_up(value)[:16]

        s0, s1 = rolled_up(surf)
        b0, b1 = rolled_up(bed)
        m0, m1 = rolled_up(mann)
        bed_max = jnp.maximum(b0, b1)
        drag = drag_of(m0, m1)
        bed_s[rows - 8 :, at] = bed_max
        drag_s[rows - 8 :, at] = drag
        q0 = south[rows - 8 :, at]
        new_south = jnp.where(wall, 0.0, face(q0, s0, s1, bed_max, drag))
        south[rows - 8 :, at] = jnp.where(kept, q0, new_south)


def substep(fluxes_done, last, corridor, wall, refs):
    surf, east, south, bed_e, bed_s, drag_e, drag_s, total, covers, count = refs
    ext, columns = surf.shape
    rows = ext - 2 * HALO
    chunks = columns // LANES
    tall = rows if last else ext
    lane = lanes_of(ext)
    zero = jnp.zeros((tall, LANES), jnp.float32)
    surfs, rolls, lefts, pairs, turned = {}, {}, {}, {}, {}

    def fetch(chunk):
        if chunk < chunks:
            surfs[chunk] = surf[:, cols(chunk)]
            rolls[chunk] = pltpu.roll(surfs[chunk], LANES - 1, 1)
        else:
            rolls[chunk] = rolls[chunks - 1]

    def join(chunk):
        if chunk < chunks:
            lefts[chunk] = jnp.where(lane >= LANES - 1, rolls[chunk + 1], rolls[chunk])
            if not last:
                pairs[chunk] = surfs[chunk] + lefts[chunk]
                turned[chunk] = pltpu.roll(pairs[chunk], LANES - 2, 1)
        else:
            turned[chunk] = turned.get(chunks - 1)

    fetch(0)
    fetch(1)
    join(0)
    east_last = zero
    state = (zero, zero)
    for chunk in range(chunks):
        at = cols(chunk)
        if not last:
            if chunk + 2 <= chunks:
                fetch(chunk + 2)
            join(chunk + 1)
        elif chunk > 0:
            fetch(chunk + 1)
            join(chunk)
        s0 = surfs[chunk]
        if fluxes_done:
            new_east, new_south = east[:, at], south[:, at]
        else:
            new_east = face(
                east[:tall, at], s0[:tall], lefts[chunk][:tall], bed_e[:tall, at], drag_e[:tall, at]
            )
            new_east = east_walled(new_east, chunk, chunks)
            new_south = face(south[:, at], s0, moved_up(s0), bed_s[:, at], drag_s[:, at])
            new_south = jnp.concatenate(
                [new_south[:-16], jnp.where(wall, 0.0, new_south[-16:])], axis=0
            )
        held = total[:tall, at]
        summed, state = right_sum(held, state)
        if not last:
            window = pairs[chunk] + jnp.where(
                lane >= LANES - 2, turned[chunk + 1], turned[chunk]
            )
            total[:, at] = (1.0 - corridor * DRAIN) * held + count[:, at] * window
        east_rolled = pltpu.roll(new_east, 1, 1)
        north = pltpu.roll(new_south, 1, 0)
        inflow = jnp.where(lane[:tall] < 1, east_last, east_rolled) + north[:tall]
        east_last = east_rolled
        new_surf = (
            s0[:tall]
            + SPREAD * (inflow - new_east - new_south[:tall])
            + (summed - covers[:tall, at] * s0[:tall])
        )
        yield chunk, new_surf, new_east, new_south


def steps_kernel(corridor, tiles, own, partner_cells, near, far, *refs):
    number = refs[7]
    own_term, partner_term, other_term = refs[9:12]
    surf, east, south, bed_e, bed_s, drag_e, drag_s, total, covers = refs[12:21]
    count, first_total = refs[21:]
    ext, columns = surf.shape
    rows = ext - 2 * HALO
    owned = own.shape[1]
    chunks = columns // LANES
    position = lax.axis_index("gy")
    side = jnp.where(position % 2 == 0, 1, -1)

    valid, node_row, node_chunk, node_lane = located(far[1:2, :], position, rows, ext, columns)
    key = jnp.where(valid & (node_row >= rows), node_chunk * 8 + (node_row - rows), -1)
    starts, levels = scattered(far[0:1, :], key, node_lane, chunks * 8)
    zero = jnp.zeros((ext, LANES), jnp.float32)
    state = (zero, zero)
    for chunk in range(chunks):
        at, mine = cols(chunk), slice(chunk * 8, chunk * 8 + 8)
        starting = number[:, at]
        starting = jnp.concatenate([starting[:rows], starting[rows:] + starts[mine]], axis=0)
        held = total[:, at]
        held = FEED * jnp.concatenate([held[:rows], held[rows:] + levels[mine]], axis=0)
        count[:, at] = (FEED * DRAIN) * starting
        total[:, at] = held
        first_total[:, at] = held[:rows]
        covering, state = right_sum(starting, state)
        covers[:, at] = FEED * covering

    wall = wall_of(ext, tiles)
    state_refs = (surf, east, south, bed_e, bed_s, drag_e, drag_s, total, covers, count)
    for chunk, new_surf, new_east, new_south in substep(True, False, corridor, wall, state_refs):
        surf[:, cols(chunk)] = new_surf

    def body(step, carry):
        for chunk, new_surf, new_east, new_south in substep(
            False, False, corridor, wall, state_refs
        ):
            at = cols(chunk)
            surf[:, at] = new_surf
            east[:, at] = new_east
            south[:, at] = new_south
        return carry

    lax.fori_loop(0, STEPS - 2, body, 0)

    kept = (1.0 - corridor * DRAIN) ** STEPS
    levels = []
    for chunk in range(chunks):
        at, then = cols(chunk), cols(min(chunk + 1, chunks - 1))
        window = surf[:rows, at]
        for by in range(1, corridor):
            window = window + moved_left(surf[:rows, at], surf[:rows, then], by)
        starting = count[:rows, at]
        held = (1.0 - corridor * DRAIN) * total[:rows, at] + starting * window
        gained = held - kept * first_total[:, at]
        weight = jnp.maximum(starting * (1.0 / DRAIN), FEED)
        levels.append(gained * pl.reciprocal(weight, approx=True))
    partner = jnp.where(position + side < tiles, partner_cells[0:1, :] + 1, 0).astype(jnp.float32)
    cell = jnp.concatenate([own[1:2, :], partner, near[1:2, :]], axis=1)
    valid, node_row, node_chunk, node_lane = located(cell, position, rows, ext, columns)
    take_key = jnp.where(valid & (node_row < rows), node_chunk * rows + node_row, -1)
    takes = one_hot(chunks * rows, take_key).astype(jnp.bfloat16)
    picked = lax.dot_general(
        jnp.concatenate(split3(jnp.concatenate(levels, axis=0)), axis=1),
        takes,
        (((0,), (0,)), ((), ())),
        preferred_element_type=jnp.float32,
    )
    picked = (picked[:LANES] + picked[LANES : 2 * LANES]) + picked[2 * LANES :]
    terms = jnp.sum(picked * one_hot(LANES, node_lane), axis=0, keepdims=True)
    own_term[...] = kept * own[0:1, :] + terms[:, :owned]
    partner_term[...] = terms[:, owned : 2 * owned]
    other_term[...] = terms[:, 2 * owned :]


def last_kernel(corridor, tiles, *refs):
    bed = refs[9]
    targets = refs[10:13]
    results = refs[13:16]
    sems = refs[16]
    ext, columns = bed.shape
    rows = ext - 2 * HALO
    chunks = columns // LANES
    group = 5
    copies = []
    steps = substep(False, True, corridor, wall_of(ext, tiles), refs[:9] + (None,))
    for chunk, new_surf, new_east, new_south in steps:
        at = cols(chunk)
        results[0][:, at] = new_surf - bed[:rows, at]
        results[1][:, at] = new_east
        results[2][:, at] = new_south[:rows]
        if (chunk + 1) % group == 0 or chunk + 1 == chunks:
            first = chunk // group * group * LANES
            width = pl.ds(first, (chunk + 1) * LANES - first)
            for slot, (result, target) in enumerate(zip(results, targets)):
                copy = pltpu.make_async_copy(
                    result.at[:, width], target.at[:, width], sems.at[chunk // group, slot]
                )
                copy.start()
                copies.append(copy)
    for copy in copies:
        copy.wait()


def local(
    depth, flux_east, flux_south, river_section, bed_level, rough_class, manning_table, bank_cell
):
    rows, columns = depth.shape
    owned = river_section.shape[0]
    corridor = bank_cell.shape[0]
    tiles = lax.axis_size("gy")
    ext = rows + 2 * HALO
    chunks = columns // LANES
    partner_section = swapped(river_section, 0).reshape(1, owned)
    partner_cells = swapped(bank_cell, 0)

    def held(value):
        return pltpu.with_memory_space_constraint(value, pltpu.VMEM)

    def far(value):
        return pltpu.with_memory_space_constraint(value, pltpu.HBM)

    params = pltpu.CompilerParams(vmem_limit_bytes=VMEM_LIMIT)
    halo = pltpu.VMEM((5, HALO, columns), jnp.float32)
    field = pltpu.VMEM((ext, columns), jnp.float32)
    term = pltpu.VMEM((1, owned), jnp.float32)
    wide = pltpu.VMEM((5, HALO, columns + LANES), jnp.float32)
    to_other, own = pl.pallas_call(
        pack_kernel,
        out_shape=[wide, pltpu.VMEM((2, owned), jnp.float32)],
        in_specs=[HBM_SPEC] * 7,
        out_specs=[VMEM_SPEC] * 2,
        scratch_shapes=[
            pltpu.VMEM((4, 8, columns), jnp.float32),
            pltpu.VMEM((8, columns), jnp.int32),
            pltpu.VMEM((corridor, owned), jnp.int32),
            pltpu.SemaphoreType.DMA((7,)),
        ],
        compiler_params=params,
        name="pack",
    )(
        *[far(value) for value in (depth, bed_level, rough_class, flux_east, flux_south)],
        far(river_section.reshape(1, owned)),
        far(bank_cell),
    )
    to_other = pl.pallas_call(
        join_kernel,
        out_shape=wide,
        in_specs=[VMEM_SPEC] * 3,
        out_specs=VMEM_SPEC,
        input_output_aliases={0: 0},
        compiler_params=params,
        name="join",
    )(held(to_other), held(partner_section), held(partner_cells))
    by_other = swapped(to_other, 1)
    from_far = swapped(by_other[0, 0:2, columns:], 0)
    to_partner, *loaded, rough = pl.pallas_call(
        load_kernel,
        out_shape=[halo] + [field] * 4 + [pltpu.VMEM((rows, columns), jnp.int32)],
        in_specs=[HBM_SPEC] * 5,
        out_specs=[VMEM_SPEC] * 6,
        scratch_shapes=[pltpu.SemaphoreType.DMA((5,))],
        compiler_params=params,
        name="load",
    )(*[far(value) for value in (depth, flux_east, flux_south, bed_level, rough_class)])
    by_partner = swapped(to_partner, 0)
    *fields, table_rows = pl.pallas_call(
        prepare_kernel,
        out_shape=[field] * 11 + [pltpu.VMEM((manning_table.shape[0], LANES), jnp.float32)],
        in_specs=[SMEM_SPEC] + [VMEM_SPEC] * 8,
        out_specs=[VMEM_SPEC] * 12,
        input_output_aliases={5 + slot: slot for slot in range(4)},
        compiler_params=params,
        name="prepare",
    )(
        manning_table,
        *[held(value) for value in (rough, own, partner_section, partner_cells, *loaded)],
    )
    near = by_other[0, 0:2, columns:]
    from_far = swapped(near, 0)
    fields = pl.pallas_call(
        functools.partial(border_kernel, tiles),
        out_shape=[field] * 11,
        in_specs=[VMEM_SPEC] * 14,
        out_specs=[VMEM_SPEC] * 11,
        input_output_aliases={3 + slot: slot for slot in range(11)},
        compiler_params=params,
        name="border",
    )(*[held(value) for value in (by_partner, by_other, table_rows, *fields)])
    surf, east, south, bed, _, bed_e, bed_s, drag_e, drag_s, number, total = fields
    stepped = pl.pallas_call(
        functools.partial(steps_kernel, corridor, tiles),
        out_shape=[term] * 3 + [field] * 9,
        in_specs=[VMEM_SPEC] * 13,
        out_specs=[VMEM_SPEC] * 12,
        scratch_shapes=[field, pltpu.VMEM((rows, columns), jnp.float32)],
        input_output_aliases={4 + slot: 3 + slot for slot in range(7)} | {12: 10},
        compiler_params=params,
        name="steps",
    )(
        *[held(value) for value in (own, partner_cells, near, from_far)],
        *[held(value) for value in (surf, east, south, bed_e, bed_s, drag_e, drag_s)],
        *[held(value) for value in (number, total)],
    )
    from_other = swapped(stepped[2].reshape(owned), 1)
    from_partner = swapped(stepped[1].reshape(owned), 0)
    result = pltpu.HBM((rows, columns), jnp.float32)
    depth, flux_east, flux_south = pl.pallas_call(
        functools.partial(last_kernel, corridor, tiles),
        out_shape=[result] * 3,
        in_specs=[VMEM_SPEC] * 10,
        out_specs=[HBM_SPEC] * 3,
        scratch_shapes=[pltpu.VMEM((rows, columns), jnp.float32)] * 3
        + [pltpu.SemaphoreType.DMA((-(-chunks // 5), 3))],
        compiler_params=params,
        name="last",
    )(*[held(value) for value in (*stepped[3:], bed)])
    river_section = stepped[0].reshape(owned) + from_partner + from_other
    return (depth, flux_east, flux_south, river_section)


def solution(mesh):
    return jax.shard_map(
        local,
        mesh=mesh,
        in_specs=(
            P(("runs", "gy"), None),
            P(("runs", "gy"), None),
            P(("runs", "gy"), None),
            P(("runs", "gy")),
            P("gy", None),
            P("gy", None),
            P(),
            P(None, "gy"),
        ),
        out_specs=(
            P(("runs", "gy"), None),
            P(("runs", "gy"), None),
            P(("runs", "gy"), None),
            P(("runs", "gy")),
        ),
        check_vma=False,
    )
```

```python
import functools

import jax
import jax.numpy as jnp
from jax import lax
from jax.experimental import pallas as pl
from jax.experimental.pallas import tpu as pltpu
from jax.sharding import PartitionSpec as P

STEPS = 4

GRAV = 9.81
TSTEP = 8.0
CELL = 90.0
FLOOR = 0.05
BANK_COEF = 200.0
CELL_AREA = 8100.0
NODE_AREA = 20000.0

LANES = 128
HALO = 4
SLOPE = GRAV * TSTEP / CELL
SPREAD = TSTEP / CELL
FEED = TSTEP * BANK_COEF / CELL_AREA
DRAIN = TSTEP * BANK_COEF / NODE_AREA
VMEM_LIMIT = 32 * 1024 * 1024

SMEM_SPEC = pl.BlockSpec(memory_space=pltpu.SMEM)
VMEM_SPEC = pl.BlockSpec(memory_space=pltpu.VMEM)
HBM_SPEC = pl.BlockSpec(memory_space=pltpu.HBM)


def swapped(value, first):
    count = lax.axis_size("gy")
    pairs = []
    for low in range(first, count - 1, 2):
        pairs += [(low, low + 1), (low + 1, low)]
    return lax.ppermute(value, "gy", pairs)


def cols(chunk):
    return slice(chunk * LANES, (chunk + 1) * LANES)


def lanes_of(rows):
    return lax.broadcasted_iota(jnp.int32, (rows, LANES), 1)


def moved_left(value, following, by):
    return jnp.where(
        lanes_of(value.shape[0]) >= LANES - by,
        pltpu.roll(following, LANES - by, 1),
        pltpu.roll(value, LANES - by, 1),
    )


def moved_up(value):
    return pltpu.roll(value, value.shape[0] - 1, 0)


def split3(value):
    high = value.astype(jnp.bfloat16)
    rest = value - high.astype(jnp.float32)
    middle = rest.astype(jnp.bfloat16)
    low = (rest - middle.astype(jnp.float32)).astype(jnp.bfloat16)
    return high, middle, low


def one_hot(count, key):
    rows = lax.broadcasted_iota(jnp.int32, (count, key.shape[1]), 0)
    return jnp.where(rows == key, 1.0, 0.0)


def drag_of(mann_a, mann_b):
    pair = mann_a + mann_b
    return (0.25 * GRAV * TSTEP) * (pair * pair)


def looked_up(klass, entries):
    value = jnp.broadcast_to(entries[0], klass.shape)
    for k in range(1, len(entries)):
        value = jnp.where(klass == k, entries[k], value)
    return value


def face(flux, surf_a, surf_b, bed_max, drag):
    flow_depth = jnp.maximum(jnp.maximum(surf_a, surf_b) - bed_max, FLOOR)
    power = jnp.exp2((-7.0 / 3.0) * jnp.log2(flow_depth))
    driven = flux - SLOPE * flow_depth * (surf_b - surf_a)
    damping = 1.0 + drag * jnp.abs(flux) * power
    return driven * pl.reciprocal(damping, approx=True)


def right_sum(value, state):
    lane = lanes_of(value.shape[0])
    once = pltpu.roll(value, 1, 1)
    pair = value + jnp.where(lane < 1, state[0], once)
    twice = pltpu.roll(pair, 2, 1)
    return pair + jnp.where(lane < 2, state[1], twice), (once, twice)


def east_walled(value, chunk, chunks):
    if chunk + 1 < chunks:
        return value
    return jnp.where(lanes_of(value.shape[0]) == LANES - 1, 0.0, value)


def located(cell, position, rows, ext, columns):
    base = ((position * rows - HALO) * columns + 1).astype(jnp.float32)
    offset = cell - base
    valid = (cell > 0.0) & (offset >= 0.0) & (offset < float(ext * columns))
    offset = jnp.where(valid, offset, 0.0)
    row = jnp.floor((offset + 0.5) * (1.0 / columns))
    column = (offset - row * float(columns)).astype(jnp.int32)
    row = row.astype(jnp.int32) - HALO
    row = jnp.where(row < 0, row + ext, row)
    chunk = column // LANES
    return valid, row, chunk, column - chunk * LANES


def scattered(section, key, lane, count):
    at_lane = one_hot(LANES, lane)
    parts = [at_lane] + [at_lane * part.astype(jnp.float32) for part in split3(section)]
    grid = lax.dot_general(
        one_hot(-(-count // 16) * 16, key).astype(jnp.bfloat16),
        jnp.concatenate(parts, axis=0).astype(jnp.bfloat16),
        (((1,), (1,)), ((), ())),
        preferred_element_type=jnp.float32,
    )
    number = grid[:, :LANES]
    total = (grid[:, LANES : 2 * LANES] + grid[:, 2 * LANES : 3 * LANES]) + grid[:, 3 * LANES :]
    return number, total


def pack_kernel(
    depth, bed, rough, east, south, section, cells, to_other, own, held, held_rough, held_cells, sems
):
    rows, columns = depth.shape
    even = lax.axis_index("gy") % 2 == 0
    start = pl.multiple_of(jnp.where(even, 0, rows - 8), 8)
    copies = [
        pltpu.make_async_copy(source, target, sems.at[slot])
        for slot, (source, target) in enumerate(
            (
                (depth.at[pl.ds(start, 8), :], held.at[0]),
                (bed.at[pl.ds(start, 8), :], held.at[1]),
                (rough.at[pl.ds(start, 8), :], held_rough),
                (east.at[pl.ds(start, 8), :], held.at[2]),
                (south.at[pl.ds(start, 8), :], held.at[3]),
                (section, own.at[pl.ds(0, 1), :]),
                (cells, held_cells),
            )
        )
    ]
    for copy in copies:
        copy.start()
    for slot in range(5):
        copies[slot].wait()
        block = (
            held_rough[...].astype(jnp.float32) if slot == 2 else held[slot - (slot > 2)]
        )
        to_other[slot, :, :columns] = jnp.where(even, block[:HALO], block[8 - HALO :])
        to_other[slot, :, columns:] = jnp.zeros((HALO, LANES), jnp.float32)
    for copy in copies[5:]:
        copy.wait()
    own[1:2, :] = (held_cells[0:1, :] + 1).astype(jnp.float32)
    to_other[0, 0:2, columns:] = own[...]


def join_kernel(before, section, cells, to_other):
    columns = to_other.shape[2] - LANES
    to_other[0, 2:3, columns:] = section[...]
    to_other[0, 3:4, columns:] = (cells[0:1, :] + 1).astype(jnp.float32)


def load_kernel(
    depth_in, east_in, south_in, bed_in, rough_in, to_partner, surf, east, south, bed, rough, sems
):
    rows, columns = depth_in.shape
    even = lax.axis_index("gy") % 2 == 0
    own = pl.ds(0, rows)
    copies = [
        pltpu.make_async_copy(source, target.at[own, :], sems.at[slot])
        for slot, (source, target) in enumerate(
            (
                (depth_in, surf),
                (bed_in, bed),
                (rough_in, rough),
                (east_in, east),
                (south_in, south),
            )
        )
    ]
    for copy in copies:
        copy.start()
    for slot, source in enumerate((surf, bed, rough, east, south)):
        copies[slot].wait()
        for chunk in range(columns // LANES):
            at = cols(chunk)
            first = source[:8, at].astype(jnp.float32)
            last = source[rows - 8 : rows, at].astype(jnp.float32)
            to_partner[slot, :, at] = jnp.where(even, last[8 - HALO :], first[:HALO])


def relay_kernel(by_other, prepared, near):
    del prepared
    columns = by_other.shape[2] - LANES
    near[...] = by_other[0, 0:2, columns:]


def prepare_kernel(table, rough, own, partner_section, partner_cells, *refs):
    surf, east, south, bed = refs[4:8]
    mann, bed_e, bed_s, drag_e, drag_s, number, total, table_rows = refs[8:]
    ext, columns = surf.shape
    rows = ext - 2 * HALO
    chunks = columns // LANES
    tiles = lax.axis_size("gy")
    position = lax.axis_index("gy")
    side = jnp.where(position % 2 == 0, 1, -1)
    entries = [table[k] for k in range(table.shape[0])]
    for k, entry in enumerate(entries):
        table_rows[k : k + 1, :] = jnp.full((1, LANES), entry, jnp.float32)
    for chunk in range(chunks):
        at = cols(chunk)
        mann[:rows, at] = looked_up(rough[:, at], entries)
        surf[:rows, at] = surf[:rows, at] + bed[:rows, at]

    partner = jnp.where(position + side < tiles, partner_cells[0:1, :] + 1, 0).astype(jnp.float32)
    section = jnp.concatenate([own[0:1, :], partner_section[...]], axis=1)
    cell = jnp.concatenate([own[1:2, :], partner], axis=1)
    valid, node_row, node_chunk, node_lane = located(cell, position, rows, ext, columns)
    key = jnp.where(valid, node_chunk * ext + node_row, -1)
    starts, levels = scattered(section, key, node_lane, chunks * ext)
    for chunk in range(chunks):
        at = cols(chunk)
        number[:, at] = starts[chunk * ext : (chunk + 1) * ext]
        total[:, at] = levels[chunk * ext : (chunk + 1) * ext]

    kept = lax.broadcasted_iota(jnp.int32, (rows, LANES), 0) == rows - 1
    for chunk in range(chunks):
        at, then = cols(chunk), cols(min(chunk + 1, chunks - 1))
        s0, b0, m0 = surf[:rows, at], bed[:rows, at], mann[:rows, at]
        bed_max = jnp.maximum(b0, moved_left(b0, bed[:rows, then], 1))
        drag = drag_of(m0, moved_left(m0, mann[:rows, then], 1))
        bed_e[:rows, at] = bed_max
        drag_e[:rows, at] = drag
        new_east = face(
            east[:rows, at], s0, moved_left(s0, surf[:rows, then], 1), bed_max, drag
        )
        east[:rows, at] = east_walled(new_east, chunk, chunks)
        bed_max = jnp.maximum(b0, moved_up(b0))
        drag = drag_of(m0, moved_up(m0))
        bed_s[:rows, at] = bed_max
        drag_s[:rows, at] = drag
        q0 = south[:rows, at]
        south[:rows, at] = jnp.where(kept, q0, face(q0, s0, moved_up(s0), bed_max, drag))


def wall_of(ext, tiles):
    position = lax.axis_index("gy")
    rows = ext - 2 * HALO
    row = lax.broadcasted_iota(jnp.int32, (16, LANES), 0) + (ext - 16)
    return ((row == ext - 1) & (position == 0)) | ((row == rows - 1) & (position == tiles - 1))


def border_kernel(tiles, by_partner, by_other, table_rows, *refs):
    surf, east, south, bed, mann, bed_e, bed_s, drag_e, drag_s, number, total = refs[11:]
    ext, columns = surf.shape
    rows = ext - 2 * HALO
    chunks = columns // LANES
    position = lax.axis_index("gy")
    even = position % 2 == 0
    entries = [table_rows[k : k + 1, :] for k in range(table_rows.shape[0])]
    for chunk in range(chunks):
        at = cols(chunk)
        halos = []
        for slot in range(5):
            a, b = by_partner[slot, :, at], by_other[slot, :, at]
            below = jnp.where(even, a, b)
            above = jnp.where(even, b, a)
            halos.append(jnp.concatenate([below, above], axis=0))
        surf[rows:, at] = halos[0] + halos[1]
        bed[rows:, at] = halos[1]
        mann[rows:, at] = looked_up(halos[2].astype(jnp.int32), entries)
        east[rows:, at] = halos[3]
        south[rows:, at] = halos[4]

    near = by_other[0, :, columns:]
    section = jnp.concatenate([near[0:1, :], near[2:3, :]], axis=1)
    cell = jnp.concatenate([near[1:2, :], near[3:4, :]], axis=1)
    valid, node_row, node_chunk, node_lane = located(cell, position, rows, ext, columns)
    key = jnp.where(valid, node_chunk * ext + node_row, -1)
    starts, levels = scattered(section, key, node_lane, chunks * ext)

    wall = wall_of(ext, tiles)
    kept = lax.broadcasted_iota(jnp.int32, (16, LANES), 0) < 7
    for chunk in range(chunks):
        at, then = cols(chunk), cols(min(chunk + 1, chunks - 1))
        number[:, at] += starts[chunk * ext : (chunk + 1) * ext]
        total[:, at] += levels[chunk * ext : (chunk + 1) * ext]
        s0, b0, m0 = surf[rows:, at], bed[rows:, at], mann[rows:, at]
        bed_max = jnp.maximum(b0, moved_left(b0, bed[rows:, then], 1))
        drag = drag_of(m0, moved_left(m0, mann[rows:, then], 1))
        bed_e[rows:, at] = bed_max
        drag_e[rows:, at] = drag
        new_east = face(
            east[rows:, at], s0, moved_left(s0, surf[rows:, then], 1), bed_max, drag
        )
        east[rows:, at] = east_walled(new_east, chunk, chunks)

        def rolled_up(ref):
            value = jnp.concatenate([ref[rows - 8 :, at], ref[:8, at]], axis=0)
            return value[:16], moved_up(value)[:16]

        s0, s1 = rolled_up(surf)
        b0, b1 = rolled_up(bed)
        m0, m1 = rolled_up(mann)
        bed_max = jnp.maximum(b0, b1)
        drag = drag_of(m0, m1)
        bed_s[rows - 8 :, at] = bed_max
        drag_s[rows - 8 :, at] = drag
        q0 = south[rows - 8 :, at]
        new_south = jnp.where(wall, 0.0, face(q0, s0, s1, bed_max, drag))
        south[rows - 8 :, at] = jnp.where(kept, q0, new_south)


def exchange(corridor, surf, total, covers, count, gain):
    ext, columns = surf.shape
    chunks = columns // LANES
    lane = lanes_of(ext)
    zero = jnp.zeros((ext, LANES), jnp.float32)
    state = (zero, zero)

    def paired(value, rolled, rolled_then):
        pair = value + jnp.where(lane >= LANES - 1, rolled_then, rolled)
        return pair, pltpu.roll(pair, LANES - 2, 1)

    values = [surf[:, cols(0)], surf[:, cols(1)]]
    rolls = [pltpu.roll(value, LANES - 1, 1) for value in values]
    pair, turned = paired(values[0], rolls[0], rolls[1])
    for chunk in range(chunks):
        at = cols(chunk)
        if chunk + 1 < chunks:
            if chunk + 2 < chunks:
                ahead = surf[:, cols(chunk + 2)]
                rolled_ahead = pltpu.roll(ahead, LANES - 1, 1)
            else:
                ahead, rolled_ahead = values[1], rolls[1]
            pair_then, turned_then = paired(values[1], rolls[1], rolled_ahead)
        else:
            pair_then, turned_then = pair, turned
        window = pair + jnp.where(lane >= LANES - 2, turned_then, turned)
        held = total[:, at]
        summed, state = right_sum(held, state)
        gain[:, at] = summed - covers[:, at] * values[0]
        total[:, at] = (1.0 - corridor * DRAIN) * held + count[:, at] * window
        values, rolls = [values[1], ahead], [rolls[1], rolled_ahead]
        pair, turned = pair_then, turned_then


def substep(fluxes_done, last, wall, gained, refs):
    surf, east, south, bed_e, bed_s, drag_e, drag_s = refs
    ext, columns = surf.shape
    rows = ext - 2 * HALO
    chunks = columns // LANES
    tall = rows if last else ext
    lane = lanes_of(tall)
    s0 = surf[:, cols(0)]
    rolled = pltpu.roll(s0[:tall], LANES - 1, 1)
    east_last = jnp.zeros((tall, LANES), jnp.float32)
    for chunk in range(chunks):
        at = cols(chunk)
        if chunk + 1 < chunks:
            s1 = surf[:, cols(chunk + 1)]
            rolled_then = pltpu.roll(s1[:tall], LANES - 1, 1)
        else:
            s1, rolled_then = s0, rolled
        if fluxes_done:
            new_east, new_south = east[:, at], south[:, at]
        else:
            left = jnp.where(lane >= LANES - 1, rolled_then, rolled)
            new_east = face(east[:tall, at], s0[:tall], left, bed_e[:tall, at], drag_e[:tall, at])
            new_east = east_walled(new_east, chunk, chunks)
            new_south = face(south[:, at], s0, moved_up(s0), bed_s[:, at], drag_s[:, at])
            new_south = jnp.concatenate(
                [new_south[:-16], jnp.where(wall, 0.0, new_south[-16:])], axis=0
            )
        east_rolled = pltpu.roll(new_east, 1, 1)
        north = pltpu.roll(new_south, 1, 0)
        inflow = jnp.where(lane < 1, east_last, east_rolled) + north[:tall]
        east_last = east_rolled
        outflow = new_east + new_south[:tall]
        new_surf = s0[:tall] + SPREAD * (inflow - outflow) + gained(chunk, s0)
        yield chunk, new_surf, new_east, new_south
        s0, rolled = s1, rolled_then


def steps_kernel(corridor, tiles, own, partner_cells, near, far, *refs):
    number = refs[7]
    own_term, partner_term, other_term = refs[9:12]
    surf, east, south, bed_e, bed_s, drag_e, drag_s, total, covers = refs[12:21]
    count, first_total, gain = refs[21:]
    ext, columns = surf.shape
    rows = ext - 2 * HALO
    owned = own.shape[1]
    chunks = columns // LANES
    position = lax.axis_index("gy")
    side = jnp.where(position % 2 == 0, 1, -1)

    valid, node_row, node_chunk, node_lane = located(far[1:2, :], position, rows, ext, columns)
    key = jnp.where(valid & (node_row >= rows), node_chunk * 8 + (node_row - rows), -1)
    starts, levels = scattered(far[0:1, :], key, node_lane, chunks * 8)
    zero = jnp.zeros((ext, LANES), jnp.float32)
    state = (zero, zero)
    for chunk in range(chunks):
        at, mine = cols(chunk), slice(chunk * 8, chunk * 8 + 8)
        starting = number[:, at]
        starting = jnp.concatenate([starting[:rows], starting[rows:] + starts[mine]], axis=0)
        held = total[:, at]
        held = FEED * jnp.concatenate([held[:rows], held[rows:] + levels[mine]], axis=0)
        count[:, at] = (FEED * DRAIN) * starting
        total[:, at] = held
        first_total[:, at] = held[:rows]
        covering, state = right_sum(starting, state)
        covers[:, at] = FEED * covering

    wall = wall_of(ext, tiles)
    state_refs = (surf, east, south, bed_e, bed_s, drag_e, drag_s)

    def gained(chunk, value):
        return gain[:, cols(chunk)]

    exchange(corridor, surf, total, covers, count, gain)
    for chunk, new_surf, _, _ in substep(True, False, wall, gained, state_refs):
        surf[:, cols(chunk)] = new_surf

    def body(step, carry):
        exchange(corridor, surf, total, covers, count, gain)
        for chunk, new_surf, new_east, new_south in substep(
            False, False, wall, gained, state_refs
        ):
            at = cols(chunk)
            surf[:, at] = new_surf
            east[:, at] = new_east
            south[:, at] = new_south
        return carry

    lax.fori_loop(0, STEPS - 2, body, 0)

    kept = (1.0 - corridor * DRAIN) ** STEPS
    levels = []
    for chunk in range(chunks):
        at, then = cols(chunk), cols(min(chunk + 1, chunks - 1))
        window = surf[:rows, at]
        for by in range(1, corridor):
            window = window + moved_left(surf[:rows, at], surf[:rows, then], by)
        starting = count[:rows, at]
        held = (1.0 - corridor * DRAIN) * total[:rows, at] + starting * window
        gained = held - kept * first_total[:, at]
        weight = jnp.maximum(starting * (1.0 / DRAIN), FEED)
        levels.append(gained * pl.reciprocal(weight, approx=True))
    partner = jnp.where(position + side < tiles, partner_cells[0:1, :] + 1, 0).astype(jnp.float32)
    cell = jnp.concatenate([own[1:2, :], partner, near[1:2, :]], axis=1)
    valid, node_row, node_chunk, node_lane = located(cell, position, rows, ext, columns)
    take_key = jnp.where(valid & (node_row < rows), node_chunk * rows + node_row, -1)
    takes = one_hot(chunks * rows, take_key).astype(jnp.bfloat16)
    picked = lax.dot_general(
        jnp.concatenate(split3(jnp.concatenate(levels, axis=0)), axis=1),
        takes,
        (((0,), (0,)), ((), ())),
        preferred_element_type=jnp.float32,
    )
    picked = (picked[:LANES] + picked[LANES : 2 * LANES]) + picked[2 * LANES :]
    terms = jnp.sum(picked * one_hot(LANES, node_lane), axis=0, keepdims=True)
    own_term[...] = kept * own[0:1, :] + terms[:, :owned]
    partner_term[...] = terms[:, owned : 2 * owned]
    other_term[...] = terms[:, 2 * owned :]


def last_kernel(tiles, *refs):
    total, covers, bed = refs[7:10]
    targets = refs[10:13]
    results = refs[13:16]
    sems = refs[16]
    ext, columns = bed.shape
    rows = ext - 2 * HALO
    chunks = columns // LANES
    group = 5
    copies = []
    zero = jnp.zeros((rows, LANES), jnp.float32)
    state = [(zero, zero)]

    def gained(chunk, value):
        at = cols(chunk)
        summed, state[0] = right_sum(total[:rows, at], state[0])
        return summed - covers[:rows, at] * value[:rows]

    steps = substep(False, True, wall_of(ext, tiles), gained, refs[:7])
    for chunk, new_surf, new_east, new_south in steps:
        at = cols(chunk)
        results[0][:, at] = new_surf - bed[:rows, at]
        results[1][:, at] = new_east
        results[2][:, at] = new_south[:rows]
        if (chunk + 1) % group == 0 or chunk + 1 == chunks:
            first = chunk // group * group * LANES
            width = pl.ds(first, (chunk + 1) * LANES - first)
            for slot, (result, target) in enumerate(zip(results, targets)):
                copy = pltpu.make_async_copy(
                    result.at[:, width], target.at[:, width], sems.at[chunk // group, slot]
                )
                copy.start()
                copies.append(copy)
    for copy in copies:
        copy.wait()


def local(
    depth, flux_east, flux_south, river_section, bed_level, rough_class, manning_table, bank_cell
):
    rows, columns = depth.shape
    owned = river_section.shape[0]
    corridor = bank_cell.shape[0]
    tiles = lax.axis_size("gy")
    ext = rows + 2 * HALO
    chunks = columns // LANES
    partner_section = swapped(river_section, 0).reshape(1, owned)
    partner_cells = swapped(bank_cell, 0)

    def held(value):
        return pltpu.with_memory_space_constraint(value, pltpu.VMEM)

    def far(value):
        return pltpu.with_memory_space_constraint(value, pltpu.HBM)

    params = pltpu.CompilerParams(vmem_limit_bytes=VMEM_LIMIT)
    halo = pltpu.VMEM((5, HALO, columns), jnp.float32)
    field = pltpu.VMEM((ext, columns), jnp.float32)
    term = pltpu.VMEM((1, owned), jnp.float32)
    wide = pltpu.VMEM((5, HALO, columns + LANES), jnp.float32)
    to_other, own = pl.pallas_call(
        pack_kernel,
        out_shape=[wide, pltpu.VMEM((2, owned), jnp.float32)],
        in_specs=[HBM_SPEC] * 7,
        out_specs=[VMEM_SPEC] * 2,
        scratch_shapes=[
            pltpu.VMEM((4, 8, columns), jnp.float32),
            pltpu.VMEM((8, columns), jnp.int32),
            pltpu.VMEM((corridor, owned), jnp.int32),
            pltpu.SemaphoreType.DMA((7,)),
        ],
        compiler_params=params,
        name="pack",
    )(
        *[far(value) for value in (depth, bed_level, rough_class, flux_east, flux_south)],
        far(river_section.reshape(1, owned)),
        far(bank_cell),
    )
    to_other = pl.pallas_call(
        join_kernel,
        out_shape=wide,
        in_specs=[VMEM_SPEC] * 3,
        out_specs=VMEM_SPEC,
        input_output_aliases={0: 0},
        compiler_params=params,
        name="join",
    )(held(to_other), held(partner_section), held(partner_cells))
    by_other = swapped(to_other, 1)
    from_far = swapped(by_other[0, 0:2, columns:], 0)
    to_partner, *loaded, rough = pl.pallas_call(
        load_kernel,
        out_shape=[halo] + [field] * 4 + [pltpu.VMEM((rows, columns), jnp.int32)],
        in_specs=[HBM_SPEC] * 5,
        out_specs=[VMEM_SPEC] * 6,
        scratch_shapes=[pltpu.SemaphoreType.DMA((5,))],
        compiler_params=params,
        name="load",
    )(*[far(value) for value in (depth, flux_east, flux_south, bed_level, rough_class)])
    by_partner = swapped(to_partner, 0)
    *fields, table_rows = pl.pallas_call(
        prepare_kernel,
        out_shape=[field] * 11 + [pltpu.VMEM((manning_table.shape[0], LANES), jnp.float32)],
        in_specs=[SMEM_SPEC] + [VMEM_SPEC] * 8,
        out_specs=[VMEM_SPEC] * 12,
        input_output_aliases={5 + slot: slot for slot in range(4)},
        compiler_params=params,
        name="prepare",
    )(
        manning_table,
        *[held(value) for value in (rough, own, partner_section, partner_cells, *loaded)],
    )
    near = pl.pallas_call(
        relay_kernel,
        out_shape=pltpu.VMEM((2, owned), jnp.float32),
        in_specs=[VMEM_SPEC] * 2,
        out_specs=VMEM_SPEC,
        compiler_params=params,
        name="relay",
    )(held(by_other), held(table_rows))
    from_far = swapped(near, 0)
    fields = pl.pallas_call(
        functools.partial(border_kernel, tiles),
        out_shape=[field] * 11,
        in_specs=[VMEM_SPEC] * 14,
        out_specs=[VMEM_SPEC] * 11,
        input_output_aliases={3 + slot: slot for slot in range(11)},
        compiler_params=params,
        name="border",
    )(*[held(value) for value in (by_partner, by_other, table_rows, *fields)])
    surf, east, south, bed, _, bed_e, bed_s, drag_e, drag_s, number, total = fields
    stepped = pl.pallas_call(
        functools.partial(steps_kernel, corridor, tiles),
        out_shape=[term] * 3 + [field] * 9,
        in_specs=[VMEM_SPEC] * 13,
        out_specs=[VMEM_SPEC] * 12,
        scratch_shapes=[field, pltpu.VMEM((rows, columns), jnp.float32), field],
        input_output_aliases={4 + slot: 3 + slot for slot in range(7)} | {12: 10},
        compiler_params=params,
        name="steps",
    )(
        *[held(value) for value in (own, partner_cells, near, from_far)],
        *[held(value) for value in (surf, east, south, bed_e, bed_s, drag_e, drag_s)],
        *[held(value) for value in (number, total)],
    )
    from_other = swapped(stepped[2].reshape(owned), 1)
    from_partner = swapped(stepped[1].reshape(owned), 0)
    result = pltpu.HBM((rows, columns), jnp.float32)
    depth, flux_east, flux_south = pl.pallas_call(
        functools.partial(last_kernel, tiles),
        out_shape=[result] * 3,
        in_specs=[VMEM_SPEC] * 10,
        out_specs=[HBM_SPEC] * 3,
        scratch_shapes=[pltpu.VMEM((rows, columns), jnp.float32)] * 3
        + [pltpu.SemaphoreType.DMA((-(-chunks // 5), 3))],
        compiler_params=params,
        name="last",
    )(*[held(value) for value in (*stepped[3:], bed)])
    river_section = stepped[0].reshape(owned) + from_partner + from_other
    return (depth, flux_east, flux_south, river_section)


def solution(mesh):
    return jax.shard_map(
        local,
        mesh=mesh,
        in_specs=(
            P(("runs", "gy"), None),
            P(("runs", "gy"), None),
            P(("runs", "gy"), None),
            P(("runs", "gy")),
            P("gy", None),
            P("gy", None),
            P(),
            P(None, "gy"),
        ),
        out_specs=(
            P(("runs", "gy"), None),
            P(("runs", "gy"), None),
            P(("runs", "gy"), None),
            P(("runs", "gy")),
        ),
        check_vma=False,
    )
```

```python
import functools

import jax
import jax.numpy as jnp
from jax import lax
from jax.experimental import pallas as pl
from jax.experimental.pallas import tpu as pltpu
from jax.sharding import PartitionSpec as P

STEPS = 4

GRAV = 9.81
TSTEP = 8.0
CELL = 90.0
FLOOR = 0.05
BANK_COEF = 200.0
CELL_AREA = 8100.0
NODE_AREA = 20000.0

LANES = 128
HALO = 4
SLOPE = GRAV * TSTEP / CELL
SPREAD = TSTEP / CELL
FEED = TSTEP * BANK_COEF / CELL_AREA
DRAIN = TSTEP * BANK_COEF / NODE_AREA
VMEM_LIMIT = 32 * 1024 * 1024

SMEM_SPEC = pl.BlockSpec(memory_space=pltpu.SMEM)
VMEM_SPEC = pl.BlockSpec(memory_space=pltpu.VMEM)
HBM_SPEC = pl.BlockSpec(memory_space=pltpu.HBM)


def swapped(value, first):
    count = lax.axis_size("gy")
    pairs = []
    for low in range(first, count - 1, 2):
        pairs += [(low, low + 1), (low + 1, low)]
    return lax.ppermute(value, "gy", pairs)


def cols(chunk):
    return slice(chunk * LANES, (chunk + 1) * LANES)


def lanes_of(rows):
    return lax.broadcasted_iota(jnp.int32, (rows, LANES), 1)


def moved_left(value, following, by):
    return jnp.where(
        lanes_of(value.shape[0]) >= LANES - by,
        pltpu.roll(following, LANES - by, 1),
        pltpu.roll(value, LANES - by, 1),
    )


def moved_up(value):
    return pltpu.roll(value, value.shape[0] - 1, 0)


def split3(value):
    high = value.astype(jnp.bfloat16)
    rest = value - high.astype(jnp.float32)
    middle = rest.astype(jnp.bfloat16)
    low = (rest - middle.astype(jnp.float32)).astype(jnp.bfloat16)
    return high, middle, low


def one_hot(count, key):
    rows = lax.broadcasted_iota(jnp.int32, (count, key.shape[1]), 0)
    return jnp.where(rows == key, 1.0, 0.0)


def drag_of(mann_a, mann_b):
    pair = mann_a + mann_b
    return (0.25 * GRAV * TSTEP) * (pair * pair)


def looked_up(klass, entries):
    value = jnp.broadcast_to(entries[0], klass.shape)
    for k in range(1, len(entries)):
        value = jnp.where(klass == k, entries[k], value)
    return value


def face(flux, surf_a, surf_b, bed_max, drag):
    flow_depth = jnp.maximum(jnp.maximum(surf_a, surf_b) - bed_max, FLOOR)
    power = jnp.exp2((-7.0 / 3.0) * jnp.log2(flow_depth))
    driven = flux - SLOPE * flow_depth * (surf_b - surf_a)
    damping = 1.0 + drag * jnp.abs(flux) * power
    return driven * pl.reciprocal(damping, approx=True)


def right_sum(value, state):
    lane = lanes_of(value.shape[0])
    once = pltpu.roll(value, 1, 1)
    pair = value + jnp.where(lane < 1, state[0], once)
    twice = pltpu.roll(pair, 2, 1)
    return pair + jnp.where(lane < 2, state[1], twice), (once, twice)


def east_walled(value, chunk, chunks):
    if chunk + 1 < chunks:
        return value
    return jnp.where(lanes_of(value.shape[0]) == LANES - 1, 0.0, value)


def located(cell, position, rows, ext, columns):
    base = ((position * rows - HALO) * columns + 1).astype(jnp.float32)
    offset = cell - base
    valid = (cell > 0.0) & (offset >= 0.0) & (offset < float(ext * columns))
    offset = jnp.where(valid, offset, 0.0)
    row = jnp.floor((offset + 0.5) * (1.0 / columns))
    column = (offset - row * float(columns)).astype(jnp.int32)
    row = row.astype(jnp.int32) - HALO
    row = jnp.where(row < 0, row + ext, row)
    chunk = column // LANES
    return valid, row, chunk, column - chunk * LANES


def scattered(section, key, lane, count):
    at_lane = one_hot(LANES, lane)
    parts = [at_lane] + [at_lane * part.astype(jnp.float32) for part in split3(section)]
    grid = lax.dot_general(
        one_hot(-(-count // 16) * 16, key).astype(jnp.bfloat16),
        jnp.concatenate(parts, axis=0).astype(jnp.bfloat16),
        (((1,), (1,)), ((), ())),
        preferred_element_type=jnp.float32,
    )
    number = grid[:, :LANES]
    total = (grid[:, LANES : 2 * LANES] + grid[:, 2 * LANES : 3 * LANES]) + grid[:, 3 * LANES :]
    return number, total


def pack_kernel(
    depth, bed, rough, east, south, section, cells, to_other, own, held, held_rough, held_cells, sems
):
    rows, columns = depth.shape
    even = lax.axis_index("gy") % 2 == 0
    start = pl.multiple_of(jnp.where(even, 0, rows - 8), 8)
    copies = [
        pltpu.make_async_copy(source, target, sems.at[slot])
        for slot, (source, target) in enumerate(
            (
                (depth.at[pl.ds(start, 8), :], held.at[0]),
                (bed.at[pl.ds(start, 8), :], held.at[1]),
                (rough.at[pl.ds(start, 8), :], held_rough),
                (east.at[pl.ds(start, 8), :], held.at[2]),
                (south.at[pl.ds(start, 8), :], held.at[3]),
                (section, own.at[pl.ds(0, 1), :]),
                (cells, held_cells),
            )
        )
    ]
    for copy in copies:
        copy.start()
    for slot in range(5):
        copies[slot].wait()
        block = (
            held_rough[...].astype(jnp.float32) if slot == 2 else held[slot - (slot > 2)]
        )
        to_other[slot, :, :columns] = jnp.where(even, block[:HALO], block[8 - HALO :])
        to_other[slot, :, columns:] = jnp.zeros((HALO, LANES), jnp.float32)
    for copy in copies[5:]:
        copy.wait()
    own[1:2, :] = (held_cells[0:1, :] + 1).astype(jnp.float32)
    to_other[0, 0:2, columns:] = own[...]


def join_kernel(before, section, cells, to_other):
    columns = to_other.shape[2] - LANES
    to_other[0, 2:3, columns:] = section[...]
    to_other[0, 3:4, columns:] = (cells[0:1, :] + 1).astype(jnp.float32)


def load_kernel(
    depth_in, east_in, south_in, bed_in, rough_in, to_partner, surf, east, south, bed, rough, sems
):
    rows, columns = depth_in.shape
    even = lax.axis_index("gy") % 2 == 0
    own = pl.ds(0, rows)
    copies = [
        pltpu.make_async_copy(source, target.at[own, :], sems.at[slot])
        for slot, (source, target) in enumerate(
            (
                (depth_in, surf),
                (bed_in, bed),
                (rough_in, rough),
                (east_in, east),
                (south_in, south),
            )
        )
    ]
    for copy in copies:
        copy.start()
    for slot, source in enumerate((surf, bed, rough, east, south)):
        copies[slot].wait()
        for chunk in range(columns // LANES):
            at = cols(chunk)
            first = source[:8, at].astype(jnp.float32)
            last = source[rows - 8 : rows, at].astype(jnp.float32)
            to_partner[slot, :, at] = jnp.where(even, last[8 - HALO :], first[:HALO])


def relay_kernel(by_other, prepared, near):
    del prepared
    columns = by_other.shape[2] - LANES
    near[...] = by_other[0, 0:2, columns:]


def prepare_kernel(table, rough, own, partner_section, partner_cells, *refs):
    surf, east, south, bed = refs[4:8]
    mann, bed_e, bed_s, drag_e, drag_s, number, total, table_rows = refs[8:]
    ext, columns = surf.shape
    rows = ext - 2 * HALO
    chunks = columns // LANES
    tiles = lax.axis_size("gy")
    position = lax.axis_index("gy")
    side = jnp.where(position % 2 == 0, 1, -1)
    entries = [table[k] for k in range(table.shape[0])]
    for k, entry in enumerate(entries):
        table_rows[k : k + 1, :] = jnp.full((1, LANES), entry, jnp.float32)
    for chunk in range(chunks):
        at = cols(chunk)
        mann[:rows, at] = looked_up(rough[:, at], entries)
        surf[:rows, at] = surf[:rows, at] + bed[:rows, at]

    partner = jnp.where(position + side < tiles, partner_cells[0:1, :] + 1, 0).astype(jnp.float32)
    section = jnp.concatenate([own[0:1, :], partner_section[...]], axis=1)
    cell = jnp.concatenate([own[1:2, :], partner], axis=1)
    valid, node_row, node_chunk, node_lane = located(cell, position, rows, ext, columns)
    key = jnp.where(valid, node_chunk * ext + node_row, -1)
    starts, levels = scattered(section, key, node_lane, chunks * ext)
    for chunk in range(chunks):
        at = cols(chunk)
        number[:, at] = starts[chunk * ext : (chunk + 1) * ext]
        total[:, at] = levels[chunk * ext : (chunk + 1) * ext]

    kept = lax.broadcasted_iota(jnp.int32, (rows, LANES), 0) == rows - 1
    for chunk in range(chunks):
        at, then = cols(chunk), cols(min(chunk + 1, chunks - 1))
        s0, b0, m0 = surf[:rows, at], bed[:rows, at], mann[:rows, at]
        bed_max = jnp.maximum(b0, moved_left(b0, bed[:rows, then], 1))
        drag = drag_of(m0, moved_left(m0, mann[:rows, then], 1))
        bed_e[:rows, at] = bed_max
        drag_e[:rows, at] = drag
        new_east = face(
            east[:rows, at], s0, moved_left(s0, surf[:rows, then], 1), bed_max, drag
        )
        east[:rows, at] = east_walled(new_east, chunk, chunks)
        bed_max = jnp.maximum(b0, moved_up(b0))
        drag = drag_of(m0, moved_up(m0))
        bed_s[:rows, at] = bed_max
        drag_s[:rows, at] = drag
        q0 = south[:rows, at]
        south[:rows, at] = jnp.where(kept, q0, face(q0, s0, moved_up(s0), bed_max, drag))


def wall_of(ext, tiles):
    position = lax.axis_index("gy")
    rows = ext - 2 * HALO
    row = lax.broadcasted_iota(jnp.int32, (16, LANES), 0) + (ext - 16)
    return ((row == ext - 1) & (position == 0)) | ((row == rows - 1) & (position == tiles - 1))


def border_kernel(tiles, by_partner, by_other, table_rows, *refs):
    surf, east, south, bed, mann, bed_e, bed_s, drag_e, drag_s, number, total = refs[11:]
    ext, columns = surf.shape
    rows = ext - 2 * HALO
    chunks = columns // LANES
    position = lax.axis_index("gy")
    even = position % 2 == 0
    entries = [table_rows[k : k + 1, :] for k in range(table_rows.shape[0])]
    for chunk in range(chunks):
        at = cols(chunk)
        halos = []
        for slot in range(5):
            a, b = by_partner[slot, :, at], by_other[slot, :, at]
            below = jnp.where(even, a, b)
            above = jnp.where(even, b, a)
            halos.append(jnp.concatenate([below, above], axis=0))
        surf[rows:, at] = halos[0] + halos[1]
        bed[rows:, at] = halos[1]
        mann[rows:, at] = looked_up(halos[2].astype(jnp.int32), entries)
        east[rows:, at] = halos[3]
        south[rows:, at] = halos[4]

    near = by_other[0, :, columns:]
    section = jnp.concatenate([near[0:1, :], near[2:3, :]], axis=1)
    cell = jnp.concatenate([near[1:2, :], near[3:4, :]], axis=1)
    valid, node_row, node_chunk, node_lane = located(cell, position, rows, ext, columns)
    key = jnp.where(valid, node_chunk * ext + node_row, -1)
    starts, levels = scattered(section, key, node_lane, chunks * ext)

    wall = wall_of(ext, tiles)
    kept = lax.broadcasted_iota(jnp.int32, (16, LANES), 0) < 7
    for chunk in range(chunks):
        at, then = cols(chunk), cols(min(chunk + 1, chunks - 1))
        number[:, at] += starts[chunk * ext : (chunk + 1) * ext]
        total[:, at] += levels[chunk * ext : (chunk + 1) * ext]
        s0, b0, m0 = surf[rows:, at], bed[rows:, at], mann[rows:, at]
        bed_max = jnp.maximum(b0, moved_left(b0, bed[rows:, then], 1))
        drag = drag_of(m0, moved_left(m0, mann[rows:, then], 1))
        bed_e[rows:, at] = bed_max
        drag_e[rows:, at] = drag
        new_east = face(
            east[rows:, at], s0, moved_left(s0, surf[rows:, then], 1), bed_max, drag
        )
        east[rows:, at] = east_walled(new_east, chunk, chunks)

        def rolled_up(ref):
            value = jnp.concatenate([ref[rows - 8 :, at], ref[:8, at]], axis=0)
            return value[:16], moved_up(value)[:16]

        s0, s1 = rolled_up(surf)
        b0, b1 = rolled_up(bed)
        m0, m1 = rolled_up(mann)
        bed_max = jnp.maximum(b0, b1)
        drag = drag_of(m0, m1)
        bed_s[rows - 8 :, at] = bed_max
        drag_s[rows - 8 :, at] = drag
        q0 = south[rows - 8 :, at]
        new_south = jnp.where(wall, 0.0, face(q0, s0, s1, bed_max, drag))
        south[rows - 8 :, at] = jnp.where(kept, q0, new_south)


def substep(fluxes_done, last, corridor, wall, refs):
    surf, east, south, bed_e, bed_s, drag_e, drag_s, total, covers, count = refs
    ext, columns = surf.shape
    rows = ext - 2 * HALO
    chunks = columns // LANES
    tall = rows if last else ext
    reach = 2 if last else corridor
    lane = lanes_of(tall)
    zero = jnp.zeros((tall, LANES), jnp.float32)

    def turned(value):
        return [pltpu.roll(value[:tall], LANES - by, 1) for by in range(1, reach)]

    s0 = surf[:, cols(0)]
    rolled = turned(s0)
    east_last = zero
    state = (zero, zero)
    for chunk in range(chunks):
        at = cols(chunk)
        if chunk + 1 < chunks:
            s1 = surf[:, cols(chunk + 1)]
            rolled_then = turned(s1)
        else:
            s1, rolled_then = s0, rolled
        moved = [
            jnp.where(lane >= LANES - 1 - by, rolled_then[by], rolled[by])
            for by in range(reach - 1)
        ]
        if fluxes_done:
            new_east, new_south = east[:, at], south[:, at]
        else:
            new_east = face(
                east[:tall, at], s0[:tall], moved[0], bed_e[:tall, at], drag_e[:tall, at]
            )
            new_east = east_walled(new_east, chunk, chunks)
            new_south = face(south[:, at], s0, moved_up(s0), bed_s[:, at], drag_s[:, at])
            new_south = jnp.concatenate(
                [new_south[:-16], jnp.where(wall, 0.0, new_south[-16:])], axis=0
            )
        held = total[:tall, at]
        summed, state = right_sum(held, state)
        new_total = None
        if not last:
            window = (s0 + moved[0]) + sum(moved[2:], moved[1])
            new_total = (1.0 - corridor * DRAIN) * held + count[:, at] * window
        east_rolled = pltpu.roll(new_east, 1, 1)
        north = pltpu.roll(new_south, 1, 0)
        inflow = jnp.where(lane < 1, east_last, east_rolled) + north[:tall]
        east_last = east_rolled
        outflow = new_east + new_south[:tall]
        gain = summed - covers[:tall, at] * s0[:tall]
        new_surf = s0[:tall] + (SPREAD * (inflow - outflow) + gain)
        yield chunk, new_surf, new_east, new_south, new_total
        s0, rolled = s1, rolled_then


def steps_kernel(corridor, tiles, own, partner_cells, near, far, *refs):
    number = refs[7]
    own_term, partner_term, other_term = refs[9:12]
    surf, east, south, bed_e, bed_s, drag_e, drag_s, total, covers = refs[12:21]
    count, first_total = refs[21:]
    ext, columns = surf.shape
    rows = ext - 2 * HALO
    owned = own.shape[1]
    chunks = columns // LANES
    position = lax.axis_index("gy")
    side = jnp.where(position % 2 == 0, 1, -1)

    valid, node_row, node_chunk, node_lane = located(far[1:2, :], position, rows, ext, columns)
    key = jnp.where(valid & (node_row >= rows), node_chunk * 8 + (node_row - rows), -1)
    starts, levels = scattered(far[0:1, :], key, node_lane, chunks * 8)
    zero = jnp.zeros((ext, LANES), jnp.float32)
    state = (zero, zero)
    for chunk in range(chunks):
        at, mine = cols(chunk), slice(chunk * 8, chunk * 8 + 8)
        starting = number[:, at]
        starting = jnp.concatenate([starting[:rows], starting[rows:] + starts[mine]], axis=0)
        held = total[:, at]
        held = FEED * jnp.concatenate([held[:rows], held[rows:] + levels[mine]], axis=0)
        count[:, at] = (FEED * DRAIN) * starting
        total[:, at] = held
        first_total[:, at] = held[:rows]
        covering, state = right_sum(starting, state)
        covers[:, at] = FEED * covering

    wall = wall_of(ext, tiles)
    state_refs = (surf, east, south, bed_e, bed_s, drag_e, drag_s, total, covers, count)
    for step in range(STEPS - 1):
        for chunk, new_surf, new_east, new_south, new_total in substep(
            step == 0, False, corridor, wall, state_refs
        ):
            at = cols(chunk)
            surf[:, at] = new_surf
            total[:, at] = new_total
            if step > 0:
                east[:, at] = new_east
                south[:, at] = new_south

    kept = (1.0 - corridor * DRAIN) ** STEPS
    levels = []
    for chunk in range(chunks):
        at, then = cols(chunk), cols(min(chunk + 1, chunks - 1))
        window = surf[:rows, at]
        for by in range(1, corridor):
            window = window + moved_left(surf[:rows, at], surf[:rows, then], by)
        starting = count[:rows, at]
        held = (1.0 - corridor * DRAIN) * total[:rows, at] + starting * window
        gained = held - kept * first_total[:, at]
        weight = jnp.maximum(starting * (1.0 / DRAIN), FEED)
        levels.append(gained * pl.reciprocal(weight, approx=True))
    partner = jnp.where(position + side < tiles, partner_cells[0:1, :] + 1, 0).astype(jnp.float32)
    cell = jnp.concatenate([own[1:2, :], partner, near[1:2, :]], axis=1)
    valid, node_row, node_chunk, node_lane = located(cell, position, rows, ext, columns)
    take_key = jnp.where(valid & (node_row < rows), node_chunk * rows + node_row, -1)
    takes = one_hot(chunks * rows, take_key).astype(jnp.bfloat16)
    picked = lax.dot_general(
        jnp.concatenate(split3(jnp.concatenate(levels, axis=0)), axis=1),
        takes,
        (((0,), (0,)), ((), ())),
        preferred_element_type=jnp.float32,
    )
    picked = (picked[:LANES] + picked[LANES : 2 * LANES]) + picked[2 * LANES :]
    terms = jnp.sum(picked * one_hot(LANES, node_lane), axis=0, keepdims=True)
    own_term[...] = kept * own[0:1, :] + terms[:, :owned]
    partner_term[...] = terms[:, owned : 2 * owned]
    other_term[...] = terms[:, 2 * owned :]


def last_kernel(corridor, tiles, *refs):
    bed = refs[9]
    targets = refs[10:13]
    results = refs[13:16]
    sems = refs[16]
    ext, columns = bed.shape
    rows = ext - 2 * HALO
    chunks = columns // LANES
    group = 5
    copies = []
    steps = substep(False, True, corridor, wall_of(ext, tiles), refs[:9] + (None,))
    for chunk, new_surf, new_east, new_south, _ in steps:
        at = cols(chunk)
        results[0][:, at] = new_surf - bed[:rows, at]
        results[1][:, at] = new_east
        results[2][:, at] = new_south[:rows]
        if (chunk + 1) % group == 0 or chunk + 1 == chunks:
            first = chunk // group * group * LANES
            width = pl.ds(first, (chunk + 1) * LANES - first)
            for slot, (result, target) in enumerate(zip(results, targets)):
                copy = pltpu.make_async_copy(
                    result.at[:, width], target.at[:, width], sems.at[chunk // group, slot]
                )
                copy.start()
                copies.append(copy)
    for copy in copies:
        copy.wait()


def local(
    depth, flux_east, flux_south, river_section, bed_level, rough_class, manning_table, bank_cell
):
    rows, columns = depth.shape
    owned = river_section.shape[0]
    corridor = bank_cell.shape[0]
    tiles = lax.axis_size("gy")
    ext = rows + 2 * HALO
    chunks = columns // LANES
    partner_section = swapped(river_section, 0).reshape(1, owned)
    partner_cells = swapped(bank_cell, 0)

    def held(value):
        return pltpu.with_memory_space_constraint(value, pltpu.VMEM)

    def far(value):
        return pltpu.with_memory_space_constraint(value, pltpu.HBM)

    params = pltpu.CompilerParams(vmem_limit_bytes=VMEM_LIMIT)
    halo = pltpu.VMEM((5, HALO, columns), jnp.float32)
    field = pltpu.VMEM((ext, columns), jnp.float32)
    term = pltpu.VMEM((1, owned), jnp.float32)
    wide = pltpu.VMEM((5, HALO, columns + LANES), jnp.float32)
    to_other, own = pl.pallas_call(
        pack_kernel,
        out_shape=[wide, pltpu.VMEM((2, owned), jnp.float32)],
        in_specs=[HBM_SPEC] * 7,
        out_specs=[VMEM_SPEC] * 2,
        scratch_shapes=[
            pltpu.VMEM((4, 8, columns), jnp.float32),
            pltpu.VMEM((8, columns), jnp.int32),
            pltpu.VMEM((corridor, owned), jnp.int32),
            pltpu.SemaphoreType.DMA((7,)),
        ],
        compiler_params=params,
        name="pack",
    )(
        *[far(value) for value in (depth, bed_level, rough_class, flux_east, flux_south)],
        far(river_section.reshape(1, owned)),
        far(bank_cell),
    )
    to_other = pl.pallas_call(
        join_kernel,
        out_shape=wide,
        in_specs=[VMEM_SPEC] * 3,
        out_specs=VMEM_SPEC,
        input_output_aliases={0: 0},
        compiler_params=params,
        name="join",
    )(held(to_other), held(partner_section), held(partner_cells))
    by_other = swapped(to_other, 1)
    from_far = swapped(by_other[0, 0:2, columns:], 0)
    to_partner, *loaded, rough = pl.pallas_call(
        load_kernel,
        out_shape=[halo] + [field] * 4 + [pltpu.VMEM((rows, columns), jnp.int32)],
        in_specs=[HBM_SPEC] * 5,
        out_specs=[VMEM_SPEC] * 6,
        scratch_shapes=[pltpu.SemaphoreType.DMA((5,))],
        compiler_params=params,
        name="load",
    )(*[far(value) for value in (depth, flux_east, flux_south, bed_level, rough_class)])
    by_partner = swapped(to_partner, 0)
    *fields, table_rows = pl.pallas_call(
        prepare_kernel,
        out_shape=[field] * 11 + [pltpu.VMEM((manning_table.shape[0], LANES), jnp.float32)],
        in_specs=[SMEM_SPEC] + [VMEM_SPEC] * 8,
        out_specs=[VMEM_SPEC] * 12,
        input_output_aliases={5 + slot: slot for slot in range(4)},
        compiler_params=params,
        name="prepare",
    )(
        manning_table,
        *[held(value) for value in (rough, own, partner_section, partner_cells, *loaded)],
    )
    near = pl.pallas_call(
        relay_kernel,
        out_shape=pltpu.VMEM((2, owned), jnp.float32),
        in_specs=[VMEM_SPEC] * 2,
        out_specs=VMEM_SPEC,
        compiler_params=params,
        name="relay",
    )(held(by_other), held(table_rows))
    from_far = swapped(near, 0)
    fields = pl.pallas_call(
        functools.partial(border_kernel, tiles),
        out_shape=[field] * 11,
        in_specs=[VMEM_SPEC] * 14,
        out_specs=[VMEM_SPEC] * 11,
        input_output_aliases={3 + slot: slot for slot in range(11)},
        compiler_params=params,
        name="border",
    )(*[held(value) for value in (by_partner, by_other, table_rows, *fields)])
    surf, east, south, bed, _, bed_e, bed_s, drag_e, drag_s, number, total = fields
    stepped = pl.pallas_call(
        functools.partial(steps_kernel, corridor, tiles),
        out_shape=[term] * 3 + [field] * 9,
        in_specs=[VMEM_SPEC] * 13,
        out_specs=[VMEM_SPEC] * 12,
        scratch_shapes=[field, pltpu.VMEM((rows, columns), jnp.float32)],
        input_output_aliases={4 + slot: 3 + slot for slot in range(7)} | {12: 10},
        compiler_params=params,
        name="steps",
    )(
        *[held(value) for value in (own, partner_cells, near, from_far)],
        *[held(value) for value in (surf, east, south, bed_e, bed_s, drag_e, drag_s)],
        *[held(value) for value in (number, total)],
    )
    from_other = swapped(stepped[2].reshape(owned), 1)
    from_partner = swapped(stepped[1].reshape(owned), 0)
    result = pltpu.HBM((rows, columns), jnp.float32)
    depth, flux_east, flux_south = pl.pallas_call(
        functools.partial(last_kernel, corridor, tiles),
        out_shape=[result] * 3,
        in_specs=[VMEM_SPEC] * 10,
        out_specs=[HBM_SPEC] * 3,
        scratch_shapes=[pltpu.VMEM((rows, columns), jnp.float32)] * 3
        + [pltpu.SemaphoreType.DMA((-(-chunks // 5), 3))],
        compiler_params=params,
        name="last",
    )(*[held(value) for value in (*stepped[3:], bed)])
    river_section = stepped[0].reshape(owned) + from_partner + from_other
    return (depth, flux_east, flux_south, river_section)


def solution(mesh):
    return jax.shard_map(
        local,
        mesh=mesh,
        in_specs=(
            P(("runs", "gy"), None),
            P(("runs", "gy"), None),
            P(("runs", "gy"), None),
            P(("runs", "gy")),
            P("gy", None),
            P("gy", None),
            P(),
            P(None, "gy"),
        ),
        out_specs=(
            P(("runs", "gy"), None),
            P(("runs", "gy"), None),
            P(("runs", "gy"), None),
            P(("runs", "gy")),
        ),
        check_vma=False,
    )
```

```python
import functools

import jax
import jax.numpy as jnp
from jax import lax
from jax.experimental import pallas as pl
from jax.experimental.pallas import tpu as pltpu
from jax.sharding import PartitionSpec as P

STEPS = 4

GRAV = 9.81
TSTEP = 8.0
CELL = 90.0
FLOOR = 0.05
BANK_COEF = 200.0
CELL_AREA = 8100.0
NODE_AREA = 20000.0

LANES = 128
HALO = 4
SLOPE = GRAV * TSTEP / CELL
SPREAD = TSTEP / CELL
FEED = TSTEP * BANK_COEF / CELL_AREA
DRAIN = TSTEP * BANK_COEF / NODE_AREA
VMEM_LIMIT = 32 * 1024 * 1024

SMEM_SPEC = pl.BlockSpec(memory_space=pltpu.SMEM)
VMEM_SPEC = pl.BlockSpec(memory_space=pltpu.VMEM)
HBM_SPEC = pl.BlockSpec(memory_space=pltpu.HBM)


def swapped(value, first):
    count = lax.axis_size("gy")
    pairs = []
    for low in range(first, count - 1, 2):
        pairs += [(low, low + 1), (low + 1, low)]
    return lax.ppermute(value, "gy", pairs)


def cols(chunk):
    return slice(chunk * LANES, (chunk + 1) * LANES)


def lanes_of(rows):
    return lax.broadcasted_iota(jnp.int32, (rows, LANES), 1)


def moved_left(value, following, by):
    return jnp.where(
        lanes_of(value.shape[0]) >= LANES - by,
        pltpu.roll(following, LANES - by, 1),
        pltpu.roll(value, LANES - by, 1),
    )


def moved_up(value):
    return pltpu.roll(value, value.shape[0] - 1, 0)


def split3(value):
    high = value.astype(jnp.bfloat16)
    rest = value - high.astype(jnp.float32)
    middle = rest.astype(jnp.bfloat16)
    low = (rest - middle.astype(jnp.float32)).astype(jnp.bfloat16)
    return high, middle, low


def one_hot(count, key):
    rows = lax.broadcasted_iota(jnp.int32, (count, key.shape[1]), 0)
    return jnp.where(rows == key, 1.0, 0.0)


def drag_of(mann_a, mann_b):
    pair = mann_a + mann_b
    return (0.25 * GRAV * TSTEP) * (pair * pair)


def looked_up(klass, entries):
    value = jnp.broadcast_to(entries[0], klass.shape)
    for k in range(1, len(entries)):
        value = jnp.where(klass == k, entries[k], value)
    return value


def face(flux, surf_a, surf_b, bed_max, drag):
    flow_depth = jnp.maximum(jnp.maximum(surf_a, surf_b) - bed_max, FLOOR)
    power = jnp.exp2((-7.0 / 3.0) * jnp.log2(flow_depth))
    driven = flux - SLOPE * flow_depth * (surf_b - surf_a)
    damping = 1.0 + drag * jnp.abs(flux) * power
    return driven * pl.reciprocal(damping, approx=True)


def right_sum(value, state):
    lane = lanes_of(value.shape[0])
    once = pltpu.roll(value, 1, 1)
    pair = value + jnp.where(lane < 1, state[0], once)
    twice = pltpu.roll(pair, 2, 1)
    return pair + jnp.where(lane < 2, state[1], twice), (once, twice)


def east_walled(value, chunk, chunks):
    if chunk + 1 < chunks:
        return value
    return jnp.where(lanes_of(value.shape[0]) == LANES - 1, 0.0, value)


def located(cell, position, rows, ext, columns):
    base = ((position * rows - HALO) * columns + 1).astype(jnp.float32)
    offset = cell - base
    valid = (cell > 0.0) & (offset >= 0.0) & (offset < float(ext * columns))
    offset = jnp.where(valid, offset, 0.0)
    row = jnp.floor((offset + 0.5) * (1.0 / columns))
    column = (offset - row * float(columns)).astype(jnp.int32)
    row = row.astype(jnp.int32) - HALO
    row = jnp.where(row < 0, row + ext, row)
    chunk = column // LANES
    return valid, row, chunk, column - chunk * LANES


def scattered(section, key, lane, count):
    at_lane = one_hot(LANES, lane)
    parts = [at_lane] + [at_lane * part.astype(jnp.float32) for part in split3(section)]
    grid = lax.dot_general(
        one_hot(-(-count // 16) * 16, key).astype(jnp.bfloat16),
        jnp.concatenate(parts, axis=0).astype(jnp.bfloat16),
        (((1,), (1,)), ((), ())),
        preferred_element_type=jnp.float32,
    )
    number = grid[:, :LANES]
    total = (grid[:, LANES : 2 * LANES] + grid[:, 2 * LANES : 3 * LANES]) + grid[:, 3 * LANES :]
    return number, total


def pack_kernel(
    depth, bed, rough, east, south, section, cells, to_other, own, held, held_rough, held_cells, sems
):
    rows, columns = depth.shape
    even = lax.axis_index("gy") % 2 == 0
    start = pl.multiple_of(jnp.where(even, 0, rows - 8), 8)
    copies = [
        pltpu.make_async_copy(source, target, sems.at[slot])
        for slot, (source, target) in enumerate(
            (
                (depth.at[pl.ds(start, 8), :], held.at[0]),
                (bed.at[pl.ds(start, 8), :], held.at[1]),
                (rough.at[pl.ds(start, 8), :], held_rough),
                (east.at[pl.ds(start, 8), :], held.at[2]),
                (south.at[pl.ds(start, 8), :], held.at[3]),
                (section, own.at[pl.ds(0, 1), :]),
                (cells, held_cells),
            )
        )
    ]
    for copy in copies:
        copy.start()
    for slot in range(5):
        copies[slot].wait()
        block = (
            held_rough[...].astype(jnp.float32) if slot == 2 else held[slot - (slot > 2)]
        )
        to_other[slot, :, :columns] = jnp.where(even, block[:HALO], block[8 - HALO :])
        to_other[slot, :, columns:] = jnp.zeros((HALO, LANES), jnp.float32)
    for copy in copies[5:]:
        copy.wait()
    own[1:2, :] = (held_cells[0:1, :] + 1).astype(jnp.float32)
    to_other[0, 0:2, columns:] = own[...]


def join_kernel(before, section, cells, to_other):
    columns = to_other.shape[2] - LANES
    to_other[0, 2:3, columns:] = section[...]
    to_other[0, 3:4, columns:] = (cells[0:1, :] + 1).astype(jnp.float32)


def picking(key, lane, takes, at_lane):
    for block in range(key.shape[1] // LANES):
        mine = slice(block * LANES, (block + 1) * LANES)

        def column(row):
            wide = jnp.broadcast_to(row[:, mine].astype(jnp.float32), (LANES, LANES))
            return jnp.transpose(wide).astype(jnp.int32)

        spread = lanes_of(LANES)
        at = column(key)
        for first in range(0, takes.shape[1], LANES):
            hit = jnp.where(spread + first == at, 1.0, 0.0)
            takes[mine, first : first + LANES] = hit.astype(jnp.bfloat16)
        at_lane[mine, :] = jnp.where(spread == column(lane), 1.0, 0.0)


def load_kernel(
    depth_in, east_in, south_in, bed_in, rough_in, to_partner, surf, east, south, bed, rough, sems
):
    rows, columns = depth_in.shape
    even = lax.axis_index("gy") % 2 == 0
    own = pl.ds(0, rows)
    copies = [
        pltpu.make_async_copy(source, target.at[own, :], sems.at[slot])
        for slot, (source, target) in enumerate(
            (
                (depth_in, surf),
                (bed_in, bed),
                (rough_in, rough),
                (east_in, east),
                (south_in, south),
            )
        )
    ]
    for copy in copies:
        copy.start()
    for slot, source in enumerate((surf, bed, rough, east, south)):
        copies[slot].wait()
        for chunk in range(columns // LANES):
            at = cols(chunk)
            first = source[:8, at].astype(jnp.float32)
            last = source[rows - 8 : rows, at].astype(jnp.float32)
            to_partner[slot, :, at] = jnp.where(even, last[8 - HALO :], first[:HALO])


def relay_kernel(by_other, prepared, near):
    del prepared
    columns = by_other.shape[2] - LANES
    near[...] = by_other[0, 0:2, columns:]


def prepare_kernel(table, rough, own, partner_section, partner_cells, *refs):
    surf, east, south, bed = refs[4:8]
    mann, bed_e, bed_s, drag_e, drag_s, number, total, table_rows, takes, at_lane = refs[8:]
    ext, columns = surf.shape
    rows = ext - 2 * HALO
    chunks = columns // LANES
    tiles = lax.axis_size("gy")
    position = lax.axis_index("gy")
    side = jnp.where(position % 2 == 0, 1, -1)
    entries = [table[k] for k in range(table.shape[0])]
    for k, entry in enumerate(entries):
        table_rows[k : k + 1, :] = jnp.full((1, LANES), entry, jnp.float32)
    for chunk in range(chunks):
        at = cols(chunk)
        mann[:rows, at] = looked_up(rough[:, at], entries)
        surf[:rows, at] = surf[:rows, at] + bed[:rows, at]

    partner = jnp.where(position + side < tiles, partner_cells[0:1, :] + 1, 0).astype(jnp.float32)
    section = jnp.concatenate([own[0:1, :], partner_section[...]], axis=1)
    cell = jnp.concatenate([own[1:2, :], partner], axis=1)
    valid, node_row, node_chunk, node_lane = located(cell, position, rows, ext, columns)
    key = jnp.where(valid, node_chunk * ext + node_row, -1)
    starts, levels = scattered(section, key, node_lane, chunks * ext)
    for chunk in range(chunks):
        at = cols(chunk)
        number[:, at] = starts[chunk * ext : (chunk + 1) * ext]
        total[:, at] = levels[chunk * ext : (chunk + 1) * ext]

    key = jnp.where(valid & (node_row < rows), node_chunk * rows + node_row, -1)
    picking(key, node_lane, takes, at_lane)

    kept = lax.broadcasted_iota(jnp.int32, (rows, LANES), 0) == rows - 1
    for chunk in range(chunks):
        at, then = cols(chunk), cols(min(chunk + 1, chunks - 1))
        s0, b0, m0 = surf[:rows, at], bed[:rows, at], mann[:rows, at]
        bed_max = jnp.maximum(b0, moved_left(b0, bed[:rows, then], 1))
        drag = drag_of(m0, moved_left(m0, mann[:rows, then], 1))
        bed_e[:rows, at] = bed_max
        drag_e[:rows, at] = drag
        new_east = face(
            east[:rows, at], s0, moved_left(s0, surf[:rows, then], 1), bed_max, drag
        )
        east[:rows, at] = east_walled(new_east, chunk, chunks)
        bed_max = jnp.maximum(b0, moved_up(b0))
        drag = drag_of(m0, moved_up(m0))
        bed_s[:rows, at] = bed_max
        drag_s[:rows, at] = drag
        q0 = south[:rows, at]
        south[:rows, at] = jnp.where(kept, q0, face(q0, s0, moved_up(s0), bed_max, drag))


def wall_of(ext, tiles):
    position = lax.axis_index("gy")
    rows = ext - 2 * HALO
    row = lax.broadcasted_iota(jnp.int32, (16, LANES), 0) + (ext - 16)
    return ((row == ext - 1) & (position == 0)) | ((row == rows - 1) & (position == tiles - 1))


def border_kernel(tiles, by_partner, by_other, table_rows, *refs):
    surf, east, south, bed, mann, bed_e, bed_s, drag_e, drag_s, number, total, takes, at_lane = refs[11:]
    ext, columns = surf.shape
    rows = ext - 2 * HALO
    chunks = columns // LANES
    position = lax.axis_index("gy")
    even = position % 2 == 0
    entries = [table_rows[k : k + 1, :] for k in range(table_rows.shape[0])]
    for chunk in range(chunks):
        at = cols(chunk)
        halos = []
        for slot in range(5):
            a, b = by_partner[slot, :, at], by_other[slot, :, at]
            below = jnp.where(even, a, b)
            above = jnp.where(even, b, a)
            halos.append(jnp.concatenate([below, above], axis=0))
        surf[rows:, at] = halos[0] + halos[1]
        bed[rows:, at] = halos[1]
        mann[rows:, at] = looked_up(halos[2].astype(jnp.int32), entries)
        east[rows:, at] = halos[3]
        south[rows:, at] = halos[4]

    near = by_other[0, :, columns:]
    section = jnp.concatenate([near[0:1, :], near[2:3, :]], axis=1)
    cell = jnp.concatenate([near[1:2, :], near[3:4, :]], axis=1)
    valid, node_row, node_chunk, node_lane = located(cell, position, rows, ext, columns)
    key = jnp.where(valid, node_chunk * ext + node_row, -1)
    starts, levels = scattered(section, key, node_lane, chunks * ext)

    key = jnp.where(valid & (node_row < rows), node_chunk * rows + node_row, -1)
    picking(key[:, :LANES], node_lane[:, :LANES], takes, at_lane)

    wall = wall_of(ext, tiles)
    kept = lax.broadcasted_iota(jnp.int32, (16, LANES), 0) < 7
    for chunk in range(chunks):
        at, then = cols(chunk), cols(min(chunk + 1, chunks - 1))
        number[:, at] += starts[chunk * ext : (chunk + 1) * ext]
        total[:, at] += levels[chunk * ext : (chunk + 1) * ext]
        s0, b0, m0 = surf[rows:, at], bed[rows:, at], mann[rows:, at]
        bed_max = jnp.maximum(b0, moved_left(b0, bed[rows:, then], 1))
        drag = drag_of(m0, moved_left(m0, mann[rows:, then], 1))
        bed_e[rows:, at] = bed_max
        drag_e[rows:, at] = drag
        new_east = face(
            east[rows:, at], s0, moved_left(s0, surf[rows:, then], 1), bed_max, drag
        )
        east[rows:, at] = east_walled(new_east, chunk, chunks)

        def rolled_up(ref):
            value = jnp.concatenate([ref[rows - 8 :, at], ref[:8, at]], axis=0)
            return value[:16], moved_up(value)[:16]

        s0, s1 = rolled_up(surf)
        b0, b1 = rolled_up(bed)
        m0, m1 = rolled_up(mann)
        bed_max = jnp.maximum(b0, b1)
        drag = drag_of(m0, m1)
        bed_s[rows - 8 :, at] = bed_max
        drag_s[rows - 8 :, at] = drag
        q0 = south[rows - 8 :, at]
        new_south = jnp.where(wall, 0.0, face(q0, s0, s1, bed_max, drag))
        south[rows - 8 :, at] = jnp.where(kept, q0, new_south)


def substep(fluxes_done, last, corridor, wall, refs):
    surf, east, south, bed_e, bed_s, drag_e, drag_s, total, covers, count = refs
    ext, columns = surf.shape
    rows = ext - 2 * HALO
    chunks = columns // LANES
    tall = rows if last else ext
    reach = 2 if last else corridor
    lane = lanes_of(tall)
    zero = jnp.zeros((tall, LANES), jnp.float32)

    def turned(value):
        return [pltpu.roll(value[:tall], LANES - by, 1) for by in range(1, reach)]

    s0 = surf[:, cols(0)]
    rolled = turned(s0)
    east_last = zero
    state = (zero, zero)
    for chunk in range(chunks):
        at = cols(chunk)
        if chunk + 1 < chunks:
            s1 = surf[:, cols(chunk + 1)]
            rolled_then = turned(s1)
        else:
            s1, rolled_then = s0, rolled
        moved = [
            jnp.where(lane >= LANES - 1 - by, rolled_then[by], rolled[by])
            for by in range(reach - 1)
        ]
        if fluxes_done:
            new_east, new_south = east[:, at], south[:, at]
        else:
            new_east = face(
                east[:tall, at], s0[:tall], moved[0], bed_e[:tall, at], drag_e[:tall, at]
            )
            new_east = east_walled(new_east, chunk, chunks)
            new_south = face(south[:, at], s0, moved_up(s0), bed_s[:, at], drag_s[:, at])
            new_south = jnp.concatenate(
                [new_south[:-16], jnp.where(wall, 0.0, new_south[-16:])], axis=0
            )
        held = total[:tall, at]
        summed, state = right_sum(held, state)
        new_total = None
        if not last:
            window = (s0 + moved[0]) + sum(moved[2:], moved[1])
            new_total = (1.0 - corridor * DRAIN) * held + count[:, at] * window
        east_rolled = pltpu.roll(new_east, 1, 1)
        north = pltpu.roll(new_south, 1, 0)
        inflow = jnp.where(lane < 1, east_last, east_rolled) + north[:tall]
        east_last = east_rolled
        outflow = new_east + new_south[:tall]
        gain = summed - covers[:tall, at] * s0[:tall]
        new_surf = s0[:tall] + (SPREAD * (inflow - outflow) + gain)
        yield chunk, new_surf, new_east, new_south, new_total
        s0, rolled = s1, rolled_then


def steps_kernel(corridor, tiles, own, far, *refs):
    surf, east, south, bed_e, bed_s, drag_e, drag_s, number, total = refs[:9]
    takes, at_lane, takes_near, at_lane_near = refs[9:13]
    own_term, partner_term, other_term = refs[13:16]
    surf_out, east_out, south_out, total_out, covers = refs[16:21]
    count, total_0, total_1, total_2, surf_1, surf_2, east_1, south_1 = refs[21:]
    ext, columns = surf.shape
    rows = ext - 2 * HALO
    owned = own.shape[1]
    chunks = columns // LANES
    position = lax.axis_index("gy")

    valid, node_row, node_chunk, node_lane = located(far[1:2, :], position, rows, ext, columns)
    key = jnp.where(valid & (node_row >= rows), node_chunk * 8 + (node_row - rows), -1)
    starts, levels = scattered(far[0:1, :], key, node_lane, chunks * 8)
    zero = jnp.zeros((ext, LANES), jnp.float32)
    state = (zero, zero)
    for chunk in range(chunks):
        at, mine = cols(chunk), slice(chunk * 8, chunk * 8 + 8)
        starting = number[:, at]
        starting = jnp.concatenate([starting[:rows], starting[rows:] + starts[mine]], axis=0)
        held = total[:, at]
        held = FEED * jnp.concatenate([held[:rows], held[rows:] + levels[mine]], axis=0)
        count[:, at] = (FEED * DRAIN) * starting
        total_0[:, at] = held
        covering, state = right_sum(starting, state)
        covers[:, at] = FEED * covering

    wall = wall_of(ext, tiles)
    faces = (bed_e, bed_s, drag_e, drag_s)
    befores = (
        (surf, east, south, total_0),
        (surf_1, east, south, total_1),
        (surf_2, east_1, south_1, total_2),
    )
    afters = (
        (surf_1, None, None, total_1),
        (surf_2, east_1, south_1, total_2),
        (surf_out, east_out, south_out, total_out),
    )
    for step in range(STEPS - 1):
        before, after = befores[step], afters[step]
        state_refs = (*before[:3], *faces, before[3], covers, count)
        for chunk, *results in substep(step == 0, False, corridor, wall, state_refs):
            for target, result in zip(after, results):
                if target is not None:
                    target[:, cols(chunk)] = result

    kept = (1.0 - corridor * DRAIN) ** STEPS
    lane = lanes_of(rows)

    def turned(value):
        return [pltpu.roll(value, LANES - by, 1) for by in range(1, corridor)]

    s0 = surf_out[:rows, cols(0)]
    rolled = turned(s0)
    levels = []
    for chunk in range(chunks):
        at = cols(chunk)
        if chunk + 1 < chunks:
            s1 = surf_out[:rows, cols(chunk + 1)]
            rolled_then = turned(s1)
        else:
            s1, rolled_then = s0, rolled
        window = s0
        for by in range(corridor - 1):
            window = window + jnp.where(lane >= LANES - 1 - by, rolled_then[by], rolled[by])
        starting = count[:rows, at]
        held = (1.0 - corridor * DRAIN) * total_out[:rows, at] + starting * window
        gained = held - kept * total_0[:rows, at]
        weight = jnp.maximum(starting * (1.0 / DRAIN), FEED)
        levels.append(gained * pl.reciprocal(weight, approx=True))
        s0, rolled = s1, rolled_then
    spare = takes.shape[1] - chunks * rows
    if spare:
        levels.append(jnp.zeros((spare, LANES), jnp.float32))
    picked = jnp.dot(
        jnp.concatenate([takes[...], takes_near[...]], axis=0),
        jnp.concatenate(split3(jnp.concatenate(levels, axis=0)), axis=1),
        preferred_element_type=jnp.float32,
    )
    hit = jnp.concatenate([at_lane[...], at_lane_near[...]], axis=0)
    picked = (picked * jnp.concatenate([hit] * 3, axis=1)).astype(jnp.bfloat16)
    terms = lax.dot_general(
        jnp.ones((8, 3 * LANES), jnp.bfloat16),
        picked,
        (((1,), (1,)), ((), ())),
        preferred_element_type=jnp.float32,
    )[0:1]
    own_term[...] = kept * own[0:1, :] + terms[:, :owned]
    partner_term[...] = terms[:, owned : 2 * owned]
    other_term[...] = terms[:, 2 * owned :]


def last_kernel(corridor, tiles, *refs):
    bed = refs[9]
    targets = refs[10:13]
    results = refs[13:16]
    sems = refs[16]
    ext, columns = bed.shape
    rows = ext - 2 * HALO
    chunks = columns // LANES
    group = 5
    copies = []
    steps = substep(False, True, corridor, wall_of(ext, tiles), refs[:9] + (None,))
    for chunk, new_surf, new_east, new_south, _ in steps:
        at = cols(chunk)
        results[0][:, at] = new_surf - bed[:rows, at]
        results[1][:, at] = new_east
        results[2][:, at] = new_south[:rows]
        if (chunk + 1) % group == 0 or chunk + 1 == chunks:
            first = chunk // group * group * LANES
            width = pl.ds(first, (chunk + 1) * LANES - first)
            for slot, (result, target) in enumerate(zip(results, targets)):
                copy = pltpu.make_async_copy(
                    result.at[:, width], target.at[:, width], sems.at[chunk // group, slot]
                )
                copy.start()
                copies.append(copy)
    for copy in copies:
        copy.wait()


def local(
    depth, flux_east, flux_south, river_section, bed_level, rough_class, manning_table, bank_cell
):
    rows, columns = depth.shape
    owned = river_section.shape[0]
    corridor = bank_cell.shape[0]
    tiles = lax.axis_size("gy")
    ext = rows + 2 * HALO
    chunks = columns // LANES
    partner_section = swapped(river_section, 0).reshape(1, owned)
    partner_cells = swapped(bank_cell, 0)

    def held(value):
        return pltpu.with_memory_space_constraint(value, pltpu.VMEM)

    def far(value):
        return pltpu.with_memory_space_constraint(value, pltpu.HBM)

    params = pltpu.CompilerParams(vmem_limit_bytes=VMEM_LIMIT)
    halo = pltpu.VMEM((5, HALO, columns), jnp.float32)
    field = pltpu.VMEM((ext, columns), jnp.float32)
    term = pltpu.VMEM((1, owned), jnp.float32)
    cells = -(-chunks * rows // LANES) * LANES
    wide = pltpu.VMEM((5, HALO, columns + LANES), jnp.float32)
    to_other, own = pl.pallas_call(
        pack_kernel,
        out_shape=[wide, pltpu.VMEM((2, owned), jnp.float32)],
        in_specs=[HBM_SPEC] * 7,
        out_specs=[VMEM_SPEC] * 2,
        scratch_shapes=[
            pltpu.VMEM((4, 8, columns), jnp.float32),
            pltpu.VMEM((8, columns), jnp.int32),
            pltpu.VMEM((corridor, owned), jnp.int32),
            pltpu.SemaphoreType.DMA((7,)),
        ],
        compiler_params=params,
        name="pack",
    )(
        *[far(value) for value in (depth, bed_level, rough_class, flux_east, flux_south)],
        far(river_section.reshape(1, owned)),
        far(bank_cell),
    )
    to_other = pl.pallas_call(
        join_kernel,
        out_shape=wide,
        in_specs=[VMEM_SPEC] * 3,
        out_specs=VMEM_SPEC,
        input_output_aliases={0: 0},
        compiler_params=params,
        name="join",
    )(held(to_other), held(partner_section), held(partner_cells))
    by_other = swapped(to_other, 1)
    from_far = swapped(by_other[0, 0:2, columns:], 0)
    to_partner, *loaded, rough = pl.pallas_call(
        load_kernel,
        out_shape=[halo] + [field] * 4 + [pltpu.VMEM((rows, columns), jnp.int32)],
        in_specs=[HBM_SPEC] * 5,
        out_specs=[VMEM_SPEC] * 6,
        scratch_shapes=[pltpu.SemaphoreType.DMA((5,))],
        compiler_params=params,
        name="load",
    )(*[far(value) for value in (depth, flux_east, flux_south, bed_level, rough_class)])
    by_partner = swapped(to_partner, 0)
    *fields, table_rows, takes, at_lane = pl.pallas_call(
        prepare_kernel,
        out_shape=[field] * 11
        + [
            pltpu.VMEM((manning_table.shape[0], LANES), jnp.float32),
            pltpu.VMEM((2 * owned, cells), jnp.bfloat16),
            pltpu.VMEM((2 * owned, LANES), jnp.float32),
        ],
        in_specs=[SMEM_SPEC] + [VMEM_SPEC] * 8,
        out_specs=[VMEM_SPEC] * 14,
        input_output_aliases={5 + slot: slot for slot in range(4)},
        compiler_params=params,
        name="prepare",
    )(
        manning_table,
        *[held(value) for value in (rough, own, partner_section, partner_cells, *loaded)],
    )
    near = pl.pallas_call(
        relay_kernel,
        out_shape=pltpu.VMEM((2, owned), jnp.float32),
        in_specs=[VMEM_SPEC] * 2,
        out_specs=VMEM_SPEC,
        compiler_params=params,
        name="relay",
    )(held(by_other), held(table_rows))
    from_far = swapped(near, 0)
    *fields, takes_near, at_lane_near = pl.pallas_call(
        functools.partial(border_kernel, tiles),
        out_shape=[field] * 11
        + [pltpu.VMEM((owned, cells), jnp.bfloat16), pltpu.VMEM((owned, LANES), jnp.float32)],
        in_specs=[VMEM_SPEC] * 14,
        out_specs=[VMEM_SPEC] * 13,
        input_output_aliases={3 + slot: slot for slot in range(11)},
        compiler_params=params,
        name="border",
    )(*[held(value) for value in (by_partner, by_other, table_rows, *fields)])
    surf, east, south, bed, _, *faces, number, total = fields
    stepped = pl.pallas_call(
        functools.partial(steps_kernel, corridor, tiles),
        out_shape=[term] * 3 + [field] * 5,
        in_specs=[VMEM_SPEC] * 15,
        out_specs=[VMEM_SPEC] * 8,
        scratch_shapes=[field] * 8,
        compiler_params=params,
        name="steps",
    )(
        *[
            held(value)
            for value in (
                *(own, from_far, surf, east, south, *faces, number, total),
                *(takes, at_lane, takes_near, at_lane_near),
            )
        ]
    )
    surf, east, south, total, covers = stepped[3:]
    from_other = swapped(stepped[2].reshape(owned), 1)
    from_partner = swapped(stepped[1].reshape(owned), 0)
    result = pltpu.HBM((rows, columns), jnp.float32)
    depth, flux_east, flux_south = pl.pallas_call(
        functools.partial(last_kernel, corridor, tiles),
        out_shape=[result] * 3,
        in_specs=[VMEM_SPEC] * 10,
        out_specs=[HBM_SPEC] * 3,
        scratch_shapes=[pltpu.VMEM((rows, columns), jnp.float32)] * 3
        + [pltpu.SemaphoreType.DMA((-(-chunks // 5), 3))],
        compiler_params=params,
        name="last",
    )(*[held(value) for value in (surf, east, south, *faces, total, covers, bed)])
    river_section = stepped[0].reshape(owned) + from_partner + from_other
    return (depth, flux_east, flux_south, river_section)


def solution(mesh):
    return jax.shard_map(
        local,
        mesh=mesh,
        in_specs=(
            P(("runs", "gy"), None),
            P(("runs", "gy"), None),
            P(("runs", "gy"), None),
            P(("runs", "gy")),
            P("gy", None),
            P("gy", None),
            P(),
            P(None, "gy"),
        ),
        out_specs=(
            P(("runs", "gy"), None),
            P(("runs", "gy"), None),
            P(("runs", "gy"), None),
            P(("runs", "gy")),
        ),
        check_vma=False,
    )
```

```python
import functools

import jax
import jax.numpy as jnp
from jax import lax
from jax.experimental import pallas as pl
from jax.experimental.pallas import tpu as pltpu
from jax.sharding import PartitionSpec as P

STEPS = 4

GRAV = 9.81
TSTEP = 8.0
CELL = 90.0
FLOOR = 0.05
BANK_COEF = 200.0
CELL_AREA = 8100.0
NODE_AREA = 20000.0

LANES = 128
HALO = 4
SLOPE = GRAV * TSTEP / CELL
SPREAD = TSTEP / CELL
FEED = TSTEP * BANK_COEF / CELL_AREA
DRAIN = TSTEP * BANK_COEF / NODE_AREA
VMEM_LIMIT = 32 * 1024 * 1024

SMEM_SPEC = pl.BlockSpec(memory_space=pltpu.SMEM)
VMEM_SPEC = pl.BlockSpec(memory_space=pltpu.VMEM)
HBM_SPEC = pl.BlockSpec(memory_space=pltpu.HBM)


def swapped(value, first):
    count = lax.axis_size("gy")
    pairs = []
    for low in range(first, count - 1, 2):
        pairs += [(low, low + 1), (low + 1, low)]
    return lax.ppermute(value, "gy", pairs)


def cols(chunk):
    return slice(chunk * LANES, (chunk + 1) * LANES)


def lanes_of(rows):
    return lax.broadcasted_iota(jnp.int32, (rows, LANES), 1)


def moved_left(value, following, by):
    return jnp.where(
        lanes_of(value.shape[0]) >= LANES - by,
        pltpu.roll(following, LANES - by, 1),
        pltpu.roll(value, LANES - by, 1),
    )


def moved_up(value):
    return pltpu.roll(value, value.shape[0] - 1, 0)


def split3(value):
    high = value.astype(jnp.bfloat16)
    rest = value - high.astype(jnp.float32)
    middle = rest.astype(jnp.bfloat16)
    low = (rest - middle.astype(jnp.float32)).astype(jnp.bfloat16)
    return high, middle, low


def one_hot(count, key):
    rows = lax.broadcasted_iota(jnp.int32, (count, key.shape[1]), 0)
    return jnp.where(rows == key, 1.0, 0.0)


def drag_of(mann_a, mann_b):
    pair = mann_a + mann_b
    return (0.25 * GRAV * TSTEP) * (pair * pair)


def looked_up(klass, entries):
    value = jnp.broadcast_to(entries[0], klass.shape)
    for k in range(1, len(entries)):
        value = jnp.where(klass == k, entries[k], value)
    return value


def face(flux, surf_a, surf_b, bed_max, drag):
    flow_depth = jnp.maximum(jnp.maximum(surf_a, surf_b) - bed_max, FLOOR)
    power = jnp.exp2((-7.0 / 3.0) * jnp.log2(flow_depth))
    driven = flux - SLOPE * flow_depth * (surf_b - surf_a)
    damping = 1.0 + drag * jnp.abs(flux) * power
    return driven * pl.reciprocal(damping, approx=True)


def right_sum(value, state):
    lane = lanes_of(value.shape[0])
    once = pltpu.roll(value, 1, 1)
    pair = value + jnp.where(lane < 1, state[0], once)
    twice = pltpu.roll(pair, 2, 1)
    return pair + jnp.where(lane < 2, state[1], twice), (once, twice)


def east_walled(value, chunk, chunks):
    if chunk + 1 < chunks:
        return value
    return jnp.where(lanes_of(value.shape[0]) == LANES - 1, 0.0, value)


def located(cell, position, rows, ext, columns):
    base = ((position * rows - HALO) * columns + 1).astype(jnp.float32)
    offset = cell - base
    valid = (cell > 0.0) & (offset >= 0.0) & (offset < float(ext * columns))
    offset = jnp.where(valid, offset, 0.0)
    row = jnp.floor((offset + 0.5) * (1.0 / columns))
    column = (offset - row * float(columns)).astype(jnp.int32)
    row = row.astype(jnp.int32) - HALO
    row = jnp.where(row < 0, row + ext, row)
    chunk = column // LANES
    return valid, row, chunk, column - chunk * LANES


def scattered(section, key, lane, count):
    at_lane = one_hot(LANES, lane)
    parts = [at_lane] + [at_lane * part.astype(jnp.float32) for part in split3(section)]
    grid = lax.dot_general(
        one_hot(-(-count // 16) * 16, key).astype(jnp.bfloat16),
        jnp.concatenate(parts, axis=0).astype(jnp.bfloat16),
        (((1,), (1,)), ((), ())),
        preferred_element_type=jnp.float32,
    )
    number = grid[:, :LANES]
    total = (grid[:, LANES : 2 * LANES] + grid[:, 2 * LANES : 3 * LANES]) + grid[:, 3 * LANES :]
    return number, total


def pack_kernel(
    depth, bed, rough, east, south, section, cells, to_other, own, held, held_rough, held_cells, sems
):
    rows, columns = depth.shape
    even = lax.axis_index("gy") % 2 == 0
    start = pl.multiple_of(jnp.where(even, 0, rows - 8), 8)
    copies = [
        pltpu.make_async_copy(source, target, sems.at[slot])
        for slot, (source, target) in enumerate(
            (
                (depth.at[pl.ds(start, 8), :], held.at[0]),
                (bed.at[pl.ds(start, 8), :], held.at[1]),
                (rough.at[pl.ds(start, 8), :], held_rough),
                (east.at[pl.ds(start, 8), :], held.at[2]),
                (south.at[pl.ds(start, 8), :], held.at[3]),
                (section, own.at[pl.ds(0, 1), :]),
                (cells, held_cells),
            )
        )
    ]
    for copy in copies:
        copy.start()
    for slot in range(5):
        copies[slot].wait()
        block = (
            held_rough[...].astype(jnp.float32) if slot == 2 else held[slot - (slot > 2)]
        )
        to_other[slot, :, :columns] = jnp.where(even, block[:HALO], block[8 - HALO :])
        to_other[slot, :, columns:] = jnp.zeros((HALO, LANES), jnp.float32)
    for copy in copies[5:]:
        copy.wait()
    own[1:2, :] = (held_cells[0:1, :] + 1).astype(jnp.float32)
    to_other[0, 0:2, columns:] = own[...]


def join_kernel(before, section, cells, to_other):
    columns = to_other.shape[2] - LANES
    to_other[0, 2:3, columns:] = section[...]
    to_other[0, 3:4, columns:] = (cells[0:1, :] + 1).astype(jnp.float32)


def picking(key, lane, takes, at_lane):
    for block in range(key.shape[1] // LANES):
        mine = slice(block * LANES, (block + 1) * LANES)

        def column(row):
            wide = jnp.broadcast_to(row[:, mine].astype(jnp.float32), (LANES, LANES))
            return jnp.transpose(wide).astype(jnp.int32)

        spread = lanes_of(LANES)
        at = column(key)
        for first in range(0, takes.shape[1], LANES):
            hit = jnp.where(spread + first == at, 1.0, 0.0)
            takes[mine, first : first + LANES] = hit.astype(jnp.bfloat16)
        at_lane[mine, :] = jnp.where(spread == column(lane), 1.0, 0.0)


def load_kernel(
    depth_in, east_in, south_in, bed_in, rough_in, to_partner, surf, east, south, bed, rough, sems
):
    rows, columns = depth_in.shape
    even = lax.axis_index("gy") % 2 == 0
    own = pl.ds(0, rows)
    copies = [
        pltpu.make_async_copy(source, target.at[own, :], sems.at[slot])
        for slot, (source, target) in enumerate(
            (
                (depth_in, surf),
                (bed_in, bed),
                (rough_in, rough),
                (east_in, east),
                (south_in, south),
            )
        )
    ]
    for copy in copies:
        copy.start()
    for slot, source in enumerate((surf, bed, rough, east, south)):
        copies[slot].wait()
        for chunk in range(columns // LANES):
            at = cols(chunk)
            first = source[:8, at].astype(jnp.float32)
            last = source[rows - 8 : rows, at].astype(jnp.float32)
            to_partner[slot, :, at] = jnp.where(even, last[8 - HALO :], first[:HALO])


def relay_kernel(by_other, prepared, near):
    del prepared
    columns = by_other.shape[2] - LANES
    near[...] = by_other[0, 0:2, columns:]


def prepare_kernel(table, rough, own, partner_section, partner_cells, *refs):
    surf, east, south, bed = refs[4:8]
    mann, bed_e, bed_s, drag_e, drag_s, number, total, table_rows, takes, at_lane = refs[8:]
    ext, columns = surf.shape
    rows = ext - 2 * HALO
    chunks = columns // LANES
    tiles = lax.axis_size("gy")
    position = lax.axis_index("gy")
    side = jnp.where(position % 2 == 0, 1, -1)
    entries = [table[k] for k in range(table.shape[0])]
    for k, entry in enumerate(entries):
        table_rows[k : k + 1, :] = jnp.full((1, LANES), entry, jnp.float32)
    for chunk in range(chunks):
        at = cols(chunk)
        mann[:rows, at] = looked_up(rough[:, at], entries)
        surf[:rows, at] = surf[:rows, at] + bed[:rows, at]

    partner = jnp.where(position + side < tiles, partner_cells[0:1, :] + 1, 0).astype(jnp.float32)
    section = jnp.concatenate([own[0:1, :], partner_section[...]], axis=1)
    cell = jnp.concatenate([own[1:2, :], partner], axis=1)
    valid, node_row, node_chunk, node_lane = located(cell, position, rows, ext, columns)
    key = jnp.where(valid, node_chunk * ext + node_row, -1)
    starts, levels = scattered(section, key, node_lane, chunks * ext)
    for chunk in range(chunks):
        at = cols(chunk)
        number[:, at] = starts[chunk * ext : (chunk + 1) * ext]
        total[:, at] = levels[chunk * ext : (chunk + 1) * ext]

    key = jnp.where(valid & (node_row < rows), node_chunk * rows + node_row, -1)
    picking(key, node_lane, takes, at_lane)

    kept = lax.broadcasted_iota(jnp.int32, (rows, LANES), 0) == rows - 1
    for chunk in range(chunks):
        at, then = cols(chunk), cols(min(chunk + 1, chunks - 1))
        s0, b0, m0 = surf[:rows, at], bed[:rows, at], mann[:rows, at]
        bed_max = jnp.maximum(b0, moved_left(b0, bed[:rows, then], 1))
        drag = drag_of(m0, moved_left(m0, mann[:rows, then], 1))
        bed_e[:rows, at] = bed_max
        drag_e[:rows, at] = drag
        new_east = face(
            east[:rows, at], s0, moved_left(s0, surf[:rows, then], 1), bed_max, drag
        )
        east[:rows, at] = east_walled(new_east, chunk, chunks)
        bed_max = jnp.maximum(b0, moved_up(b0))
        drag = drag_of(m0, moved_up(m0))
        bed_s[:rows, at] = bed_max
        drag_s[:rows, at] = drag
        q0 = south[:rows, at]
        south[:rows, at] = jnp.where(kept, q0, face(q0, s0, moved_up(s0), bed_max, drag))


def wall_of(ext, tiles):
    position = lax.axis_index("gy")
    rows = ext - 2 * HALO
    row = lax.broadcasted_iota(jnp.int32, (16, LANES), 0) + (ext - 16)
    return ((row == ext - 1) & (position == 0)) | ((row == rows - 1) & (position == tiles - 1))


def border_kernel(tiles, by_partner, by_other, table_rows, *refs):
    surf, east, south, bed, mann, bed_e, bed_s, drag_e, drag_s, number, total, takes, at_lane = refs[11:]
    ext, columns = surf.shape
    rows = ext - 2 * HALO
    chunks = columns // LANES
    position = lax.axis_index("gy")
    even = position % 2 == 0
    entries = [table_rows[k : k + 1, :] for k in range(table_rows.shape[0])]
    for chunk in range(chunks):
        at = cols(chunk)
        halos = []
        for slot in range(5):
            a, b = by_partner[slot, :, at], by_other[slot, :, at]
            below = jnp.where(even, a, b)
            above = jnp.where(even, b, a)
            halos.append(jnp.concatenate([below, above], axis=0))
        surf[rows:, at] = halos[0] + halos[1]
        bed[rows:, at] = halos[1]
        mann[rows:, at] = looked_up(halos[2].astype(jnp.int32), entries)
        east[rows:, at] = halos[3]
        south[rows:, at] = halos[4]

    near = by_other[0, :, columns:]
    section = jnp.concatenate([near[0:1, :], near[2:3, :]], axis=1)
    cell = jnp.concatenate([near[1:2, :], near[3:4, :]], axis=1)
    valid, node_row, node_chunk, node_lane = located(cell, position, rows, ext, columns)
    key = jnp.where(valid, node_chunk * ext + node_row, -1)
    starts, levels = scattered(section, key, node_lane, chunks * ext)

    key = jnp.where(valid & (node_row < rows), node_chunk * rows + node_row, -1)
    picking(key[:, :LANES], node_lane[:, :LANES], takes, at_lane)

    wall = wall_of(ext, tiles)
    kept = lax.broadcasted_iota(jnp.int32, (16, LANES), 0) < 7
    for chunk in range(chunks):
        at, then = cols(chunk), cols(min(chunk + 1, chunks - 1))
        number[:, at] += starts[chunk * ext : (chunk + 1) * ext]
        total[:, at] += levels[chunk * ext : (chunk + 1) * ext]
        s0, b0, m0 = surf[rows:, at], bed[rows:, at], mann[rows:, at]
        bed_max = jnp.maximum(b0, moved_left(b0, bed[rows:, then], 1))
        drag = drag_of(m0, moved_left(m0, mann[rows:, then], 1))
        bed_e[rows:, at] = bed_max
        drag_e[rows:, at] = drag
        new_east = face(
            east[rows:, at], s0, moved_left(s0, surf[rows:, then], 1), bed_max, drag
        )
        east[rows:, at] = east_walled(new_east, chunk, chunks)

        def rolled_up(ref):
            value = jnp.concatenate([ref[rows - 8 :, at], ref[:8, at]], axis=0)
            return value[:16], moved_up(value)[:16]

        s0, s1 = rolled_up(surf)
        b0, b1 = rolled_up(bed)
        m0, m1 = rolled_up(mann)
        bed_max = jnp.maximum(b0, b1)
        drag = drag_of(m0, m1)
        bed_s[rows - 8 :, at] = bed_max
        drag_s[rows - 8 :, at] = drag
        q0 = south[rows - 8 :, at]
        new_south = jnp.where(wall, 0.0, face(q0, s0, s1, bed_max, drag))
        south[rows - 8 :, at] = jnp.where(kept, q0, new_south)


def substep(fluxes_done, tall, windows, corridor, wall, refs):
    surf, east, south, bed_e, bed_s, drag_e, drag_s, total, covers, count = refs
    ext, columns = surf.shape
    chunks = columns // LANES
    reach = corridor if windows else 2
    lane = lanes_of(tall)
    zero = jnp.zeros((tall, LANES), jnp.float32)

    def turned(value):
        return [pltpu.roll(value[:tall], LANES - by, 1) for by in range(1, reach)]

    s0 = surf[:, cols(0)]
    rolled = turned(s0)
    east_last = zero
    state = (zero, zero)
    for chunk in range(chunks):
        at = cols(chunk)
        if chunk + 1 < chunks:
            s1 = surf[:, cols(chunk + 1)]
            rolled_then = turned(s1)
        else:
            s1, rolled_then = s0, rolled
        moved = [
            jnp.where(lane >= LANES - 1 - by, rolled_then[by], rolled[by])
            for by in range(reach - 1)
        ]
        if fluxes_done:
            new_east, new_south = east[:tall, at], south[:, at]
        else:
            new_east = face(
                east[:tall, at], s0[:tall], moved[0], bed_e[:tall, at], drag_e[:tall, at]
            )
            new_east = east_walled(new_east, chunk, chunks)
            new_south = face(south[:, at], s0, moved_up(s0), bed_s[:, at], drag_s[:, at])
            new_south = jnp.concatenate(
                [new_south[:-16], jnp.where(wall, 0.0, new_south[-16:])], axis=0
            )
        held = total[:tall, at]
        summed, state = right_sum(held, state)
        new_total = None
        if windows:
            window = (s0[:tall] + moved[0]) + sum(moved[2:], moved[1])
            new_total = (1.0 - corridor * DRAIN) * held + count[:tall, at] * window
        east_rolled = pltpu.roll(new_east, 1, 1)
        north = pltpu.roll(new_south, 1, 0)
        inflow = jnp.where(lane < 1, east_last, east_rolled) + north[:tall]
        east_last = east_rolled
        outflow = new_east + new_south[:tall]
        gain = summed - covers[:tall, at] * s0[:tall]
        new_surf = s0[:tall] + (SPREAD * (inflow - outflow) + gain)
        yield chunk, new_surf, new_east, new_south, new_total
        s0, rolled = s1, rolled_then


def first_kernel(corridor, surf, east, south, number, total, *refs):
    surf_1, total_0, total_1, count, covers = refs
    ext, columns = surf.shape
    rows = ext - 2 * HALO
    chunks = columns // LANES
    zero = jnp.zeros((rows, LANES), jnp.float32)
    state = (zero, zero)
    for chunk in range(chunks):
        at = cols(chunk)
        starting = number[:rows, at]
        count[:rows, at] = (FEED * DRAIN) * starting
        total_0[:rows, at] = FEED * total[:rows, at]
        summed, state = right_sum(starting, state)
        covers[:rows, at] = FEED * summed
    own = pl.ds(0, rows)
    refs = (surf, east, south, None, None, None, None, total_0, covers, count)
    for chunk, new_surf, _, _, new_total in substep(True, rows, True, corridor, None, refs):
        surf_1[own, cols(chunk)] = new_surf
        total_1[own, cols(chunk)] = new_total


def second_kernel(corridor, tiles, far, surf, east, south, *refs):
    bed_e, bed_s, drag_e, drag_s, number, total = refs[:6]
    surf_1, total_1, count, covers = refs[10:14]
    surf_2, east_2, south_2, total_2 = refs[14:18]
    ext, columns = surf.shape
    rows = ext - 2 * HALO
    chunks = columns // LANES
    position = lax.axis_index("gy")
    tail = slice(rows, ext)

    valid, node_row, node_chunk, node_lane = located(far[1:2, :], position, rows, ext, columns)
    key = jnp.where(valid & (node_row >= rows), node_chunk * 8 + (node_row - rows), -1)
    starts, levels = scattered(far[0:1, :], key, node_lane, chunks * 8)
    zero = jnp.zeros((ext - rows, LANES), jnp.float32)
    lane = lanes_of(ext - rows)
    state, state_levels = (zero, zero), (zero, zero)
    east_last = zero
    for chunk in range(chunks):
        at, mine = cols(chunk), slice(chunk * 8, chunk * 8 + 8)
        then = cols(min(chunk + 1, chunks - 1))
        starting = number[tail, at] + starts[mine]
        held = FEED * (total[tail, at] + levels[mine])
        starting_sum, state = right_sum(starting, state)
        summed, state_levels = right_sum(held, state_levels)
        s0 = surf[tail, at]
        window = s0
        for by in range(1, corridor):
            window = window + moved_left(s0, surf[tail, then], by)
        count_here = (FEED * DRAIN) * starting
        covers_here = FEED * starting_sum
        count[tail, at] = count_here
        covers[tail, at] = covers_here
        total_1[tail, at] = (1.0 - corridor * DRAIN) * held + count_here * window
        new_east, new_south = east[tail, at], south[tail, at]
        east_rolled = pltpu.roll(new_east, 1, 1)
        north = pltpu.roll(south[rows - 8 :, at], 1, 0)[8:]
        inflow = jnp.where(lane < 1, east_last, east_rolled) + north
        east_last = east_rolled
        gain = summed - covers_here * s0
        surf_1[tail, at] = s0 + (SPREAD * (inflow - (new_east + new_south)) + gain)

    refs = (surf_1, east, south, bed_e, bed_s, drag_e, drag_s, total_1, covers, count)
    after = (surf_2, east_2, south_2, total_2)
    steps = substep(False, ext, True, corridor, wall_of(ext, tiles), refs)
    for chunk, *results in steps:
        for target, result in zip(after, results):
            target[:, cols(chunk)] = result


def third_kernel(corridor, tiles, *refs):
    after = refs[10:]
    for chunk, *results in substep(
        False, refs[0].shape[0], True, corridor, wall_of(refs[0].shape[0], tiles), refs[:10]
    ):
        for target, result in zip(after, results):
            target[:, cols(chunk)] = result


def terms_kernel(corridor, own, surf, total, total_0, count, *refs):
    takes, at_lane, takes_near, at_lane_near, own_term, partner_term, other_term = refs
    ext, columns = surf.shape
    rows = ext - 2 * HALO
    owned = own.shape[1]
    chunks = columns // LANES
    kept = (1.0 - corridor * DRAIN) ** STEPS
    lane = lanes_of(rows)

    def turned(value):
        return [pltpu.roll(value, LANES - by, 1) for by in range(1, corridor)]

    s0 = surf[:rows, cols(0)]
    rolled = turned(s0)
    levels = []
    for chunk in range(chunks):
        at = cols(chunk)
        if chunk + 1 < chunks:
            s1 = surf[:rows, cols(chunk + 1)]
            rolled_then = turned(s1)
        else:
            s1, rolled_then = s0, rolled
        window = s0
        for by in range(corridor - 1):
            window = window + jnp.where(lane >= LANES - 1 - by, rolled_then[by], rolled[by])
        starting = count[:rows, at]
        held = (1.0 - corridor * DRAIN) * total[:rows, at] + starting * window
        gained = held - kept * total_0[:rows, at]
        weight = jnp.maximum(starting * (1.0 / DRAIN), FEED)
        levels.append(gained * pl.reciprocal(weight, approx=True))
        s0, rolled = s1, rolled_then
    spare = takes.shape[1] - chunks * rows
    if spare:
        levels.append(jnp.zeros((spare, LANES), jnp.float32))
    picked = jnp.dot(
        jnp.concatenate([takes[...], takes_near[...]], axis=0),
        jnp.concatenate(split3(jnp.concatenate(levels, axis=0)), axis=1),
        preferred_element_type=jnp.float32,
    )
    hit = jnp.concatenate([at_lane[...], at_lane_near[...]], axis=0)
    picked = (picked * jnp.concatenate([hit] * 3, axis=1)).astype(jnp.bfloat16)
    terms = lax.dot_general(
        jnp.ones((8, 3 * LANES), jnp.bfloat16),
        picked,
        (((1,), (1,)), ((), ())),
        preferred_element_type=jnp.float32,
    )[0:1]
    own_term[...] = kept * own[0:1, :] + terms[:, :owned]
    partner_term[...] = terms[:, owned : 2 * owned]
    other_term[...] = terms[:, 2 * owned :]


def last_kernel(corridor, tiles, *refs):
    bed = refs[9]
    targets = refs[10:13]
    results = refs[13:16]
    sems = refs[16]
    ext, columns = bed.shape
    rows = ext - 2 * HALO
    chunks = columns // LANES
    group = 5
    copies = []
    steps = substep(False, rows, False, corridor, wall_of(ext, tiles), refs[:9] + (None,))
    for chunk, new_surf, new_east, new_south, _ in steps:
        at = cols(chunk)
        results[0][:, at] = new_surf - bed[:rows, at]
        results[1][:, at] = new_east
        results[2][:, at] = new_south[:rows]
        if (chunk + 1) % group == 0 or chunk + 1 == chunks:
            first = chunk // group * group * LANES
            width = pl.ds(first, (chunk + 1) * LANES - first)
            for slot, (result, target) in enumerate(zip(results, targets)):
                copy = pltpu.make_async_copy(
                    result.at[:, width], target.at[:, width], sems.at[chunk // group, slot]
                )
                copy.start()
                copies.append(copy)
    for copy in copies:
        copy.wait()


def local(
    depth, flux_east, flux_south, river_section, bed_level, rough_class, manning_table, bank_cell
):
    rows, columns = depth.shape
    owned = river_section.shape[0]
    corridor = bank_cell.shape[0]
    tiles = lax.axis_size("gy")
    ext = rows + 2 * HALO
    chunks = columns // LANES
    partner_section = swapped(river_section, 0).reshape(1, owned)
    partner_cells = swapped(bank_cell, 0)

    def held(value):
        return pltpu.with_memory_space_constraint(value, pltpu.VMEM)

    def far(value):
        return pltpu.with_memory_space_constraint(value, pltpu.HBM)

    params = pltpu.CompilerParams(vmem_limit_bytes=VMEM_LIMIT)
    halo = pltpu.VMEM((5, HALO, columns), jnp.float32)
    field = pltpu.VMEM((ext, columns), jnp.float32)
    term = pltpu.VMEM((1, owned), jnp.float32)
    cells = -(-chunks * rows // LANES) * LANES
    wide = pltpu.VMEM((5, HALO, columns + LANES), jnp.float32)
    to_other, own = pl.pallas_call(
        pack_kernel,
        out_shape=[wide, pltpu.VMEM((2, owned), jnp.float32)],
        in_specs=[HBM_SPEC] * 7,
        out_specs=[VMEM_SPEC] * 2,
        scratch_shapes=[
            pltpu.VMEM((4, 8, columns), jnp.float32),
            pltpu.VMEM((8, columns), jnp.int32),
            pltpu.VMEM((corridor, owned), jnp.int32),
            pltpu.SemaphoreType.DMA((7,)),
        ],
        compiler_params=params,
        name="pack",
    )(
        *[far(value) for value in (depth, bed_level, rough_class, flux_east, flux_south)],
        far(river_section.reshape(1, owned)),
        far(bank_cell),
    )
    to_other = pl.pallas_call(
        join_kernel,
        out_shape=wide,
        in_specs=[VMEM_SPEC] * 3,
        out_specs=VMEM_SPEC,
        input_output_aliases={0: 0},
        compiler_params=params,
        name="join",
    )(held(to_other), held(partner_section), held(partner_cells))
    by_other = swapped(to_other, 1)
    from_far = swapped(by_other[0, 0:2, columns:], 0)
    to_partner, *loaded, rough = pl.pallas_call(
        load_kernel,
        out_shape=[halo] + [field] * 4 + [pltpu.VMEM((rows, columns), jnp.int32)],
        in_specs=[HBM_SPEC] * 5,
        out_specs=[VMEM_SPEC] * 6,
        scratch_shapes=[pltpu.SemaphoreType.DMA((5,))],
        compiler_params=params,
        name="load",
    )(*[far(value) for value in (depth, flux_east, flux_south, bed_level, rough_class)])
    by_partner = swapped(to_partner, 0)
    *fields, table_rows, takes, at_lane = pl.pallas_call(
        prepare_kernel,
        out_shape=[field] * 11
        + [
            pltpu.VMEM((manning_table.shape[0], LANES), jnp.float32),
            pltpu.VMEM((2 * owned, cells), jnp.bfloat16),
            pltpu.VMEM((2 * owned, LANES), jnp.float32),
        ],
        in_specs=[SMEM_SPEC] + [VMEM_SPEC] * 8,
        out_specs=[VMEM_SPEC] * 14,
        input_output_aliases={5 + slot: slot for slot in range(4)},
        compiler_params=params,
        name="prepare",
    )(
        manning_table,
        *[held(value) for value in (rough, own, partner_section, partner_cells, *loaded)],
    )
    near = pl.pallas_call(
        relay_kernel,
        out_shape=pltpu.VMEM((2, owned), jnp.float32),
        in_specs=[VMEM_SPEC] * 2,
        out_specs=VMEM_SPEC,
        compiler_params=params,
        name="relay",
    )(held(by_other), held(table_rows))
    from_far = swapped(near, 0)
    *fields, takes_near, at_lane_near = pl.pallas_call(
        functools.partial(border_kernel, tiles),
        out_shape=[field] * 11
        + [pltpu.VMEM((owned, cells), jnp.bfloat16), pltpu.VMEM((owned, LANES), jnp.float32)],
        in_specs=[VMEM_SPEC] * 14,
        out_specs=[VMEM_SPEC] * 13,
        input_output_aliases={3 + slot: slot for slot in range(11)},
        compiler_params=params,
        name="border",
    )(*[held(value) for value in (by_partner, by_other, table_rows, *fields)])
    surf, east, south, bed, _, *faces, number, total = fields
    surf_1, total_0, total_1, count, covers = pl.pallas_call(
        functools.partial(first_kernel, corridor),
        out_shape=[field] * 5,
        in_specs=[VMEM_SPEC] * 5,
        out_specs=[VMEM_SPEC] * 5,
        compiler_params=params,
        name="first",
    )(*[held(value) for value in (surf, east, south, number, total)])
    surf_1, total_1, count, covers, surf_2, east_2, south_2, total_2 = pl.pallas_call(
        functools.partial(second_kernel, corridor, tiles),
        out_shape=[field] * 8,
        in_specs=[VMEM_SPEC] * 14,
        out_specs=[VMEM_SPEC] * 8,
        input_output_aliases={10 + slot: slot for slot in range(4)},
        compiler_params=params,
        name="second",
    )(
        *[
            held(value)
            for value in (
                *(from_far, surf, east, south, *faces, number, total),
                *(surf_1, total_1, count, covers),
            )
        ]
    )
    surf, east, south, total = pl.pallas_call(
        functools.partial(third_kernel, corridor, tiles),
        out_shape=[field] * 4,
        in_specs=[VMEM_SPEC] * 10,
        out_specs=[VMEM_SPEC] * 4,
        compiler_params=params,
        name="third",
    )(*[held(value) for value in (surf_2, east_2, south_2, *faces, total_2, covers, count)])
    stepped = pl.pallas_call(
        functools.partial(terms_kernel, corridor),
        out_shape=[term] * 3,
        in_specs=[VMEM_SPEC] * 9,
        out_specs=[VMEM_SPEC] * 3,
        compiler_params=params,
        name="terms",
    )(
        *[
            held(value)
            for value in (
                *(own, surf, total, total_0, count),
                *(takes, at_lane, takes_near, at_lane_near),
            )
        ]
    )
    from_other = swapped(stepped[2].reshape(owned), 1)
    from_partner = swapped(stepped[1].reshape(owned), 0)
    result = pltpu.HBM((rows, columns), jnp.float32)
    depth, flux_east, flux_south = pl.pallas_call(
        functools.partial(last_kernel, corridor, tiles),
        out_shape=[result] * 3,
        in_specs=[VMEM_SPEC] * 10,
        out_specs=[HBM_SPEC] * 3,
        scratch_shapes=[pltpu.VMEM((rows, columns), jnp.float32)] * 3
        + [pltpu.SemaphoreType.DMA((-(-chunks // 5), 3))],
        compiler_params=params,
        name="last",
    )(*[held(value) for value in (surf, east, south, *faces, total, covers, bed)])
    river_section = stepped[0].reshape(owned) + from_partner + from_other
    return (depth, flux_east, flux_south, river_section)


def solution(mesh):
    return jax.shard_map(
        local,
        mesh=mesh,
        in_specs=(
            P(("runs", "gy"), None),
            P(("runs", "gy"), None),
            P(("runs", "gy"), None),
            P(("runs", "gy")),
            P("gy", None),
            P("gy", None),
            P(),
            P(None, "gy"),
        ),
        out_specs=(
            P(("runs", "gy"), None),
            P(("runs", "gy"), None),
            P(("runs", "gy"), None),
            P(("runs", "gy")),
        ),
        check_vma=False,
    )
```

```python
import functools

import jax
import jax.numpy as jnp
from jax import lax
from jax.experimental import pallas as pl
from jax.experimental.pallas import tpu as pltpu
from jax.sharding import PartitionSpec as P

STEPS = 4

GRAV = 9.81
TSTEP = 8.0
CELL = 90.0
FLOOR = 0.05
BANK_COEF = 200.0
CELL_AREA = 8100.0
NODE_AREA = 20000.0

LANES = 128
HALO = 4
SLOPE = GRAV * TSTEP / CELL
SPREAD = TSTEP / CELL
FEED = TSTEP * BANK_COEF / CELL_AREA
DRAIN = TSTEP * BANK_COEF / NODE_AREA
VMEM_LIMIT = 32 * 1024 * 1024

SMEM_SPEC = pl.BlockSpec(memory_space=pltpu.SMEM)
VMEM_SPEC = pl.BlockSpec(memory_space=pltpu.VMEM)
HBM_SPEC = pl.BlockSpec(memory_space=pltpu.HBM)


def swapped(value, first):
    count = lax.axis_size("gy")
    pairs = []
    for low in range(first, count - 1, 2):
        pairs += [(low, low + 1), (low + 1, low)]
    return lax.ppermute(value, "gy", pairs)


def cols(chunk):
    return slice(chunk * LANES, (chunk + 1) * LANES)


def lanes_of(rows):
    return lax.broadcasted_iota(jnp.int32, (rows, LANES), 1)


def moved_left(value, following, by):
    return jnp.where(
        lanes_of(value.shape[0]) >= LANES - by,
        pltpu.roll(following, LANES - by, 1),
        pltpu.roll(value, LANES - by, 1),
    )


def moved_up(value):
    return pltpu.roll(value, value.shape[0] - 1, 0)


def split3(value):
    high = value.astype(jnp.bfloat16)
    rest = value - high.astype(jnp.float32)
    middle = rest.astype(jnp.bfloat16)
    low = (rest - middle.astype(jnp.float32)).astype(jnp.bfloat16)
    return high, middle, low


def one_hot(count, key):
    rows = lax.broadcasted_iota(jnp.int32, (count, key.shape[1]), 0)
    return jnp.where(rows == key, 1.0, 0.0)


def drag_of(mann_a, mann_b):
    pair = mann_a + mann_b
    return (0.25 * GRAV * TSTEP) * (pair * pair)


def looked_up(klass, entries):
    value = jnp.broadcast_to(entries[0], klass.shape)
    for k in range(1, len(entries)):
        value = jnp.where(klass == k, entries[k], value)
    return value


def face(flux, surf_a, surf_b, bed_max, drag):
    flow_depth = jnp.maximum(jnp.maximum(surf_a, surf_b) - bed_max, FLOOR)
    power = jnp.exp2((-7.0 / 3.0) * jnp.log2(flow_depth))
    driven = flux - SLOPE * flow_depth * (surf_b - surf_a)
    damping = 1.0 + drag * jnp.abs(flux) * power
    return driven * pl.reciprocal(damping, approx=True)


def window_sums(blocks, reach, forward):
    height = blocks[0].shape[0]
    count = len(blocks)
    spare = -(count * height) % 16
    whole = blocks + ([jnp.zeros((spare, LANES), jnp.float32)] if spare else [])
    whole = jnp.concatenate(whole, axis=0)
    high = whole.astype(jnp.bfloat16)
    low = (whole - high.astype(jnp.float32)).astype(jnp.bfloat16)
    source = lax.broadcasted_iota(jnp.int32, (2 * LANES, 2 * LANES), 0) % LANES
    target = lax.broadcasted_iota(jnp.int32, (2 * LANES, 2 * LANES), 1)
    spill = target >= LANES
    target = target % LANES
    if forward:
        ahead = source - target + jnp.where(spill, LANES, 0)
    else:
        ahead = target - source + jnp.where(spill, LANES, 0)
    band = jnp.where((ahead >= 0) & (ahead < reach), 1.0, 0.0).astype(jnp.bfloat16)
    sums = jnp.dot(
        jnp.concatenate([high, low], axis=1), band, preferred_element_type=jnp.float32
    )
    results = []
    for block in range(count):
        result = sums[block * height : (block + 1) * height, :LANES]
        beside = block + 1 if forward else block - 1
        if 0 <= beside < count:
            result = result + sums[beside * height : (beside + 1) * height, LANES:]
        results.append(result)
    return results


def east_walled(value, chunk, chunks):
    if chunk + 1 < chunks:
        return value
    return jnp.where(lanes_of(value.shape[0]) == LANES - 1, 0.0, value)


def located(cell, position, rows, ext, columns):
    base = ((position * rows - HALO) * columns + 1).astype(jnp.float32)
    offset = cell - base
    valid = (cell > 0.0) & (offset >= 0.0) & (offset < float(ext * columns))
    offset = jnp.where(valid, offset, 0.0)
    row = jnp.floor((offset + 0.5) * (1.0 / columns))
    column = (offset - row * float(columns)).astype(jnp.int32)
    row = row.astype(jnp.int32) - HALO
    row = jnp.where(row < 0, row + ext, row)
    chunk = column // LANES
    return valid, row, chunk, column - chunk * LANES


def scattered(section, key, lane, count):
    at_lane = one_hot(LANES, lane)
    parts = [at_lane] + [at_lane * part.astype(jnp.float32) for part in split3(section)]
    grid = lax.dot_general(
        one_hot(-(-count // 16) * 16, key).astype(jnp.bfloat16),
        jnp.concatenate(parts, axis=0).astype(jnp.bfloat16),
        (((1,), (1,)), ((), ())),
        preferred_element_type=jnp.float32,
    )
    number = grid[:, :LANES]
    total = (grid[:, LANES : 2 * LANES] + grid[:, 2 * LANES : 3 * LANES]) + grid[:, 3 * LANES :]
    return number, total


def pack_kernel(
    depth, bed, rough, east, south, section, cells, to_other, own, held, held_rough, held_cells, sems
):
    rows, columns = depth.shape
    even = lax.axis_index("gy") % 2 == 0
    start = pl.multiple_of(jnp.where(even, 0, rows - 8), 8)
    copies = [
        pltpu.make_async_copy(source, target, sems.at[slot])
        for slot, (source, target) in enumerate(
            (
                (depth.at[pl.ds(start, 8), :], held.at[0]),
                (bed.at[pl.ds(start, 8), :], held.at[1]),
                (rough.at[pl.ds(start, 8), :], held_rough),
                (east.at[pl.ds(start, 8), :], held.at[2]),
                (south.at[pl.ds(start, 8), :], held.at[3]),
                (section, own.at[pl.ds(0, 1), :]),
                (cells, held_cells),
            )
        )
    ]
    for copy in copies:
        copy.start()
    for slot in range(5):
        copies[slot].wait()
        block = (
            held_rough[...].astype(jnp.float32) if slot == 2 else held[slot - (slot > 2)]
        )
        to_other[slot, :, :columns] = jnp.where(even, block[:HALO], block[8 - HALO :])
        to_other[slot, :, columns:] = jnp.zeros((HALO, LANES), jnp.float32)
    for copy in copies[5:]:
        copy.wait()
    own[1:2, :] = (held_cells[0:1, :] + 1).astype(jnp.float32)
    to_other[0, 0:2, columns:] = own[...]


def join_kernel(before, section, cells, to_other):
    columns = to_other.shape[2] - LANES
    to_other[0, 2:3, columns:] = section[...]
    to_other[0, 3:4, columns:] = (cells[0:1, :] + 1).astype(jnp.float32)


def picking(key, lane, takes, at_lane):
    for block in range(key.shape[1] // LANES):
        mine = slice(block * LANES, (block + 1) * LANES)

        def column(row):
            wide = jnp.broadcast_to(row[:, mine].astype(jnp.float32), (LANES, LANES))
            return jnp.transpose(wide).astype(jnp.int32)

        spread = lanes_of(LANES)
        at = column(key)
        for first in range(0, takes.shape[1], LANES):
            hit = jnp.where(spread + first == at, 1.0, 0.0)
            takes[mine, first : first + LANES] = hit.astype(jnp.bfloat16)
        at_lane[mine, :] = jnp.where(spread == column(lane), 1.0, 0.0)


def load_kernel(
    depth_in, east_in, south_in, bed_in, rough_in, to_partner, surf, east, south, bed, rough, sems
):
    rows, columns = depth_in.shape
    even = lax.axis_index("gy") % 2 == 0
    own = pl.ds(0, rows)
    copies = [
        pltpu.make_async_copy(source, target.at[own, :], sems.at[slot])
        for slot, (source, target) in enumerate(
            (
                (depth_in, surf),
                (bed_in, bed),
                (rough_in, rough),
                (east_in, east),
                (south_in, south),
            )
        )
    ]
    for copy in copies:
        copy.start()
    for slot, source in enumerate((surf, bed, rough, east, south)):
        copies[slot].wait()
        for chunk in range(columns // LANES):
            at = cols(chunk)
            first = source[:8, at].astype(jnp.float32)
            last = source[rows - 8 : rows, at].astype(jnp.float32)
            to_partner[slot, :, at] = jnp.where(even, last[8 - HALO :], first[:HALO])


def relay_kernel(by_other, prepared, near):
    del prepared
    columns = by_other.shape[2] - LANES
    near[...] = by_other[0, 0:2, columns:]


def prepare_kernel(table, rough, own, partner_section, partner_cells, *refs):
    surf, east, south, bed = refs[4:8]
    mann, bed_e, bed_s, drag_e, drag_s, number, total, table_rows, takes, at_lane = refs[8:]
    ext, columns = surf.shape
    rows = ext - 2 * HALO
    chunks = columns // LANES
    tiles = lax.axis_size("gy")
    position = lax.axis_index("gy")
    side = jnp.where(position % 2 == 0, 1, -1)
    entries = [table[k] for k in range(table.shape[0])]
    for k, entry in enumerate(entries):
        table_rows[k : k + 1, :] = jnp.full((1, LANES), entry, jnp.float32)
    for chunk in range(chunks):
        at = cols(chunk)
        mann[:rows, at] = looked_up(rough[:, at], entries)
        surf[:rows, at] = surf[:rows, at] + bed[:rows, at]

    partner = jnp.where(position + side < tiles, partner_cells[0:1, :] + 1, 0).astype(jnp.float32)
    section = jnp.concatenate([own[0:1, :], partner_section[...]], axis=1)
    cell = jnp.concatenate([own[1:2, :], partner], axis=1)
    valid, node_row, node_chunk, node_lane = located(cell, position, rows, ext, columns)
    key = jnp.where(valid, node_chunk * ext + node_row, -1)
    starts, levels = scattered(section, key, node_lane, chunks * ext)
    for chunk in range(chunks):
        at = cols(chunk)
        number[:, at] = starts[chunk * ext : (chunk + 1) * ext]
        total[:, at] = levels[chunk * ext : (chunk + 1) * ext]

    key = jnp.where(valid & (node_row < rows), node_chunk * rows + node_row, -1)
    picking(key, node_lane, takes, at_lane)

    kept = lax.broadcasted_iota(jnp.int32, (rows, LANES), 0) == rows - 1
    for chunk in range(chunks):
        at, then = cols(chunk), cols(min(chunk + 1, chunks - 1))
        s0, b0, m0 = surf[:rows, at], bed[:rows, at], mann[:rows, at]
        bed_max = jnp.maximum(b0, moved_left(b0, bed[:rows, then], 1))
        drag = drag_of(m0, moved_left(m0, mann[:rows, then], 1))
        bed_e[:rows, at] = bed_max
        drag_e[:rows, at] = drag
        new_east = face(
            east[:rows, at], s0, moved_left(s0, surf[:rows, then], 1), bed_max, drag
        )
        east[:rows, at] = east_walled(new_east, chunk, chunks)
        bed_max = jnp.maximum(b0, moved_up(b0))
        drag = drag_of(m0, moved_up(m0))
        bed_s[:rows, at] = bed_max
        drag_s[:rows, at] = drag
        q0 = south[:rows, at]
        south[:rows, at] = jnp.where(kept, q0, face(q0, s0, moved_up(s0), bed_max, drag))


def wall_of(ext, tiles):
    position = lax.axis_index("gy")
    rows = ext - 2 * HALO
    row = lax.broadcasted_iota(jnp.int32, (16, LANES), 0) + (ext - 16)
    return ((row == ext - 1) & (position == 0)) | ((row == rows - 1) & (position == tiles - 1))


def border_kernel(tiles, by_partner, by_other, table_rows, *refs):
    surf, east, south, bed, mann, bed_e, bed_s, drag_e, drag_s, number, total, takes, at_lane = refs[11:]
    ext, columns = surf.shape
    rows = ext - 2 * HALO
    chunks = columns // LANES
    position = lax.axis_index("gy")
    even = position % 2 == 0
    entries = [table_rows[k : k + 1, :] for k in range(table_rows.shape[0])]
    for chunk in range(chunks):
        at = cols(chunk)
        halos = []
        for slot in range(5):
            a, b = by_partner[slot, :, at], by_other[slot, :, at]
            below = jnp.where(even, a, b)
            above = jnp.where(even, b, a)
            halos.append(jnp.concatenate([below, above], axis=0))
        surf[rows:, at] = halos[0] + halos[1]
        bed[rows:, at] = halos[1]
        mann[rows:, at] = looked_up(halos[2].astype(jnp.int32), entries)
        east[rows:, at] = halos[3]
        south[rows:, at] = halos[4]

    near = by_other[0, :, columns:]
    section = jnp.concatenate([near[0:1, :], near[2:3, :]], axis=1)
    cell = jnp.concatenate([near[1:2, :], near[3:4, :]], axis=1)
    valid, node_row, node_chunk, node_lane = located(cell, position, rows, ext, columns)
    key = jnp.where(valid, node_chunk * ext + node_row, -1)
    starts, levels = scattered(section, key, node_lane, chunks * ext)

    key = jnp.where(valid & (node_row < rows), node_chunk * rows + node_row, -1)
    picking(key[:, :LANES], node_lane[:, :LANES], takes, at_lane)

    wall = wall_of(ext, tiles)
    kept = lax.broadcasted_iota(jnp.int32, (16, LANES), 0) < 7
    for chunk in range(chunks):
        at, then = cols(chunk), cols(min(chunk + 1, chunks - 1))
        number[:, at] += starts[chunk * ext : (chunk + 1) * ext]
        total[:, at] += levels[chunk * ext : (chunk + 1) * ext]
        s0, b0, m0 = surf[rows:, at], bed[rows:, at], mann[rows:, at]
        bed_max = jnp.maximum(b0, moved_left(b0, bed[rows:, then], 1))
        drag = drag_of(m0, moved_left(m0, mann[rows:, then], 1))
        bed_e[rows:, at] = bed_max
        drag_e[rows:, at] = drag
        new_east = face(
            east[rows:, at], s0, moved_left(s0, surf[rows:, then], 1), bed_max, drag
        )
        east[rows:, at] = east_walled(new_east, chunk, chunks)

        def rolled_up(ref):
            value = jnp.concatenate([ref[rows - 8 :, at], ref[:8, at]], axis=0)
            return value[:16], moved_up(value)[:16]

        s0, s1 = rolled_up(surf)
        b0, b1 = rolled_up(bed)
        m0, m1 = rolled_up(mann)
        bed_max = jnp.maximum(b0, b1)
        drag = drag_of(m0, m1)
        bed_s[rows - 8 :, at] = bed_max
        drag_s[rows - 8 :, at] = drag
        q0 = south[rows - 8 :, at]
        new_south = jnp.where(wall, 0.0, face(q0, s0, s1, bed_max, drag))
        south[rows - 8 :, at] = jnp.where(kept, q0, new_south)


def fluxes(tall, wall, before, faces, after):
    surf, east, south = before
    bed_e, bed_s, drag_e, drag_s = faces
    east_out, south_out = after
    chunks = surf.shape[1] // LANES
    for chunk in range(chunks):
        at, then = cols(chunk), cols(min(chunk + 1, chunks - 1))
        s0 = surf[:, at]
        left = moved_left(s0[:tall], surf[:tall, then], 1)
        new_east = face(east[:tall, at], s0[:tall], left, bed_e[:tall, at], drag_e[:tall, at])
        east_out[:tall, at] = east_walled(new_east, chunk, chunks)
        new_south = face(south[:, at], s0, moved_up(s0), bed_s[:, at], drag_s[:, at])
        south_out[:, at] = jnp.concatenate(
            [new_south[:-16], jnp.where(wall, 0.0, new_south[-16:])], axis=0
        )


def settled(mine, surf, east, south, gain):
    ext, columns = surf.shape
    for chunk in range(columns // LANES):
        at = cols(chunk)
        new_east = east[mine, at]
        new_south = south[:, at]
        lane = lanes_of(new_east.shape[0])
        west = pltpu.roll(new_east, 1, 1)
        if chunk > 0:
            west = jnp.where(lane < 1, pltpu.roll(east[mine, cols(chunk - 1)], 1, 1), west)
        else:
            west = jnp.where(lane < 1, 0.0, west)
        north = pltpu.roll(new_south, 1, 0)[mine]
        inflow = west + north
        s0 = surf[mine, at]
        outflow = new_east + new_south[mine]
        yield chunk, s0 + (SPREAD * (inflow - outflow) + gain(chunk, s0))


def exchange(corridor, mine, surf, total, count, covers, total_out):
    chunks = surf.shape[1] // LANES
    windows = window_sums([surf[mine, cols(chunk)] for chunk in range(chunks)], corridor, True)
    sums = window_sums([total[mine, cols(chunk)] for chunk in range(chunks)], corridor, False)
    for chunk in range(chunks):
        at = cols(chunk)
        total_out[mine, at] = (1.0 - corridor * DRAIN) * total[mine, at] + count[
            mine, at
        ] * windows[chunk]

    def gain(chunk, value):
        return sums[chunk] - covers[mine, cols(chunk)] * value

    return gain


def first_kernel(corridor, surf, east, south, number, total, *refs):
    surf_1, total_0, total_1, count, covers = refs
    rows = surf.shape[0] - 2 * HALO
    chunks = surf.shape[1] // LANES
    own = slice(0, rows)
    covering = window_sums([number[own, cols(chunk)] for chunk in range(chunks)], corridor, False)
    for chunk in range(chunks):
        at = cols(chunk)
        count[own, at] = (FEED * DRAIN) * number[own, at]
        covers[own, at] = FEED * covering[chunk]
        total_0[own, at] = FEED * total[own, at]
    gain = exchange(corridor, own, surf, total_0, count, covers, total_1)
    for chunk, new_surf in settled(own, surf, east, south, gain):
        surf_1[own, cols(chunk)] = new_surf


def second_kernel(corridor, tiles, far, surf, east, south, *refs):
    faces = refs[:4]
    number, total = refs[4:6]
    surf_1, total_1, count, covers = refs[10:14]
    surf_2, east_2, south_2, total_2 = refs[14:18]
    total_0 = refs[18]
    ext, columns = surf.shape
    rows = ext - 2 * HALO
    chunks = columns // LANES
    position = lax.axis_index("gy")
    tail = slice(rows, ext)

    valid, node_row, node_chunk, node_lane = located(far[1:2, :], position, rows, ext, columns)
    key = jnp.where(valid & (node_row >= rows), node_chunk * 8 + (node_row - rows), -1)
    starts, levels = scattered(far[0:1, :], key, node_lane, chunks * 8)
    starting = [
        number[tail, cols(chunk)] + starts[chunk * 8 : chunk * 8 + 8] for chunk in range(chunks)
    ]
    covering = window_sums(starting, corridor, False)
    for chunk in range(chunks):
        at = cols(chunk)
        count[tail, at] = (FEED * DRAIN) * starting[chunk]
        covers[tail, at] = FEED * covering[chunk]
        total_0[tail, at] = FEED * (total[tail, at] + levels[chunk * 8 : chunk * 8 + 8])
    gain = exchange(corridor, tail, surf, total_0, count, covers, total_1)
    for chunk, new_surf in settled(tail, surf, east, south, gain):
        surf_1[tail, cols(chunk)] = new_surf

    every = slice(0, ext)
    gain = exchange(corridor, every, surf_1, total_1, count, covers, total_2)
    fluxes(ext, wall_of(ext, tiles), (surf_1, east, south), faces, (east_2, south_2))
    for chunk, new_surf in settled(every, surf_1, east_2, south_2, gain):
        surf_2[:, cols(chunk)] = new_surf


def third_kernel(corridor, tiles, surf, east, south, *refs):
    faces = refs[:4]
    total, covers, count, surf_3, east_3, south_3, total_3 = refs[4:]
    ext = surf.shape[0]
    every = slice(0, ext)
    gain = exchange(corridor, every, surf, total, count, covers, total_3)
    fluxes(ext, wall_of(ext, tiles), (surf, east, south), faces, (east_3, south_3))
    for chunk, new_surf in settled(every, surf, east_3, south_3, gain):
        surf_3[:, cols(chunk)] = new_surf


def terms_kernel(corridor, own, surf, total, total_0, count, *refs):
    takes, at_lane, takes_near, at_lane_near, own_term, partner_term, other_term = refs
    ext, columns = surf.shape
    rows = ext - 2 * HALO
    owned = own.shape[1]
    chunks = columns // LANES
    kept = (1.0 - corridor * DRAIN) ** STEPS
    windows = window_sums([surf[:rows, cols(chunk)] for chunk in range(chunks)], corridor, True)
    levels = []
    for chunk in range(chunks):
        at = cols(chunk)
        starting = count[:rows, at]
        held = (1.0 - corridor * DRAIN) * total[:rows, at] + starting * windows[chunk]
        gained = held - kept * total_0[:rows, at]
        weight = jnp.maximum(starting * (1.0 / DRAIN), FEED)
        levels.append(gained * pl.reciprocal(weight, approx=True))
    spare = takes.shape[1] - chunks * rows
    if spare:
        levels.append(jnp.zeros((spare, LANES), jnp.float32))
    picked = jnp.dot(
        jnp.concatenate([takes[...], takes_near[...]], axis=0),
        jnp.concatenate(split3(jnp.concatenate(levels, axis=0)), axis=1),
        preferred_element_type=jnp.float32,
    )
    hit = jnp.concatenate([at_lane[...], at_lane_near[...]], axis=0)
    picked = (picked * jnp.concatenate([hit] * 3, axis=1)).astype(jnp.bfloat16)
    terms = lax.dot_general(
        jnp.ones((8, 3 * LANES), jnp.bfloat16),
        picked,
        (((1,), (1,)), ((), ())),
        preferred_element_type=jnp.float32,
    )[0:1]
    own_term[...] = kept * own[0:1, :] + terms[:, :owned]
    partner_term[...] = terms[:, owned : 2 * owned]
    other_term[...] = terms[:, 2 * owned :]


def last_kernel(corridor, tiles, surf, east, south, *refs):
    faces = refs[:4]
    total, covers, bed, depth_out, east_out, south_out = refs[4:10]
    depth_new, east_new, south_new, sems = refs[10:]
    ext, columns = surf.shape
    rows = ext - 2 * HALO
    own = slice(0, rows)
    copies = [
        pltpu.make_async_copy(source.at[pl.ds(0, rows), :], target, sems.at[slot])
        for slot, (source, target) in enumerate(
            ((east_new, east_out), (south_new, south_out), (depth_new, depth_out))
        )
    ]
    fluxes(rows, wall_of(ext, tiles), (surf, east, south), faces, (east_new, south_new))
    copies[0].start()
    copies[1].start()
    chunks = columns // LANES
    sums = window_sums([total[own, cols(chunk)] for chunk in range(chunks)], corridor, False)

    def gain(chunk, value):
        return sums[chunk] - covers[own, cols(chunk)] * value

    for chunk, new_surf in settled(own, surf, east_new, south_new, gain):
        at = cols(chunk)
        depth_new[:, at] = new_surf - bed[own, at]
    copies[2].start()
    for copy in copies:
        copy.wait()


def local(
    depth, flux_east, flux_south, river_section, bed_level, rough_class, manning_table, bank_cell
):
    rows, columns = depth.shape
    owned = river_section.shape[0]
    corridor = bank_cell.shape[0]
    tiles = lax.axis_size("gy")
    ext = rows + 2 * HALO
    chunks = columns // LANES
    partner_section = swapped(river_section, 0).reshape(1, owned)
    partner_cells = swapped(bank_cell, 0)

    def held(value):
        return pltpu.with_memory_space_constraint(value, pltpu.VMEM)

    def far(value):
        return pltpu.with_memory_space_constraint(value, pltpu.HBM)

    params = pltpu.CompilerParams(vmem_limit_bytes=VMEM_LIMIT)
    halo = pltpu.VMEM((5, HALO, columns), jnp.float32)
    field = pltpu.VMEM((ext, columns), jnp.float32)
    term = pltpu.VMEM((1, owned), jnp.float32)
    cells = -(-chunks * rows // LANES) * LANES
    wide = pltpu.VMEM((5, HALO, columns + LANES), jnp.float32)
    to_other, own = pl.pallas_call(
        pack_kernel,
        out_shape=[wide, pltpu.VMEM((2, owned), jnp.float32)],
        in_specs=[HBM_SPEC] * 7,
        out_specs=[VMEM_SPEC] * 2,
        scratch_shapes=[
            pltpu.VMEM((4, 8, columns), jnp.float32),
            pltpu.VMEM((8, columns), jnp.int32),
            pltpu.VMEM((corridor, owned), jnp.int32),
            pltpu.SemaphoreType.DMA((7,)),
        ],
        compiler_params=params,
        name="pack",
    )(
        *[far(value) for value in (depth, bed_level, rough_class, flux_east, flux_south)],
        far(river_section.reshape(1, owned)),
        far(bank_cell),
    )
    to_other = pl.pallas_call(
        join_kernel,
        out_shape=wide,
        in_specs=[VMEM_SPEC] * 3,
        out_specs=VMEM_SPEC,
        input_output_aliases={0: 0},
        compiler_params=params,
        name="join",
    )(held(to_other), held(partner_section), held(partner_cells))
    by_other = swapped(to_other, 1)
    from_far = swapped(by_other[0, 0:2, columns:], 0)
    to_partner, *loaded, rough = pl.pallas_call(
        load_kernel,
        out_shape=[halo] + [field] * 4 + [pltpu.VMEM((rows, columns), jnp.int32)],
        in_specs=[HBM_SPEC] * 5,
        out_specs=[VMEM_SPEC] * 6,
        scratch_shapes=[pltpu.SemaphoreType.DMA((5,))],
        compiler_params=params,
        name="load",
    )(*[far(value) for value in (depth, flux_east, flux_south, bed_level, rough_class)])
    by_partner = swapped(to_partner, 0)
    *fields, table_rows, takes, at_lane = pl.pallas_call(
        prepare_kernel,
        out_shape=[field] * 11
        + [
            pltpu.VMEM((manning_table.shape[0], LANES), jnp.float32),
            pltpu.VMEM((2 * owned, cells), jnp.bfloat16),
            pltpu.VMEM((2 * owned, LANES), jnp.float32),
        ],
        in_specs=[SMEM_SPEC] + [VMEM_SPEC] * 8,
        out_specs=[VMEM_SPEC] * 14,
        input_output_aliases={5 + slot: slot for slot in range(4)},
        compiler_params=params,
        name="prepare",
    )(
        manning_table,
        *[held(value) for value in (rough, own, partner_section, partner_cells, *loaded)],
    )
    near = pl.pallas_call(
        relay_kernel,
        out_shape=pltpu.VMEM((2, owned), jnp.float32),
        in_specs=[VMEM_SPEC] * 2,
        out_specs=VMEM_SPEC,
        compiler_params=params,
        name="relay",
    )(held(by_other), held(table_rows))
    from_far = swapped(near, 0)
    *fields, takes_near, at_lane_near = pl.pallas_call(
        functools.partial(border_kernel, tiles),
        out_shape=[field] * 11
        + [pltpu.VMEM((owned, cells), jnp.bfloat16), pltpu.VMEM((owned, LANES), jnp.float32)],
        in_specs=[VMEM_SPEC] * 14,
        out_specs=[VMEM_SPEC] * 13,
        input_output_aliases={3 + slot: slot for slot in range(11)},
        compiler_params=params,
        name="border",
    )(*[held(value) for value in (by_partner, by_other, table_rows, *fields)])
    surf, east, south, bed, _, *faces, number, total = fields
    surf_1, total_0, total_1, count, covers = pl.pallas_call(
        functools.partial(first_kernel, corridor),
        out_shape=[field] * 5,
        in_specs=[VMEM_SPEC] * 5,
        out_specs=[VMEM_SPEC] * 5,
        compiler_params=params,
        name="first",
    )(*[held(value) for value in (surf, east, south, number, total)])
    surf_1, total_1, count, covers, surf_2, east_2, south_2, total_2 = pl.pallas_call(
        functools.partial(second_kernel, corridor, tiles),
        out_shape=[field] * 8,
        in_specs=[VMEM_SPEC] * 14,
        out_specs=[VMEM_SPEC] * 8,
        scratch_shapes=[field],
        input_output_aliases={10 + slot: slot for slot in range(4)},
        compiler_params=params,
        name="second",
    )(
        *[
            held(value)
            for value in (
                *(from_far, surf, east, south, *faces, number, total),
                *(surf_1, total_1, count, covers),
            )
        ]
    )
    surf, east, south, total = pl.pallas_call(
        functools.partial(third_kernel, corridor, tiles),
        out_shape=[field] * 4,
        in_specs=[VMEM_SPEC] * 10,
        out_specs=[VMEM_SPEC] * 4,
        compiler_params=params,
        name="third",
    )(*[held(value) for value in (surf_2, east_2, south_2, *faces, total_2, covers, count)])
    stepped = pl.pallas_call(
        functools.partial(terms_kernel, corridor),
        out_shape=[term] * 3,
        in_specs=[VMEM_SPEC] * 9,
        out_specs=[VMEM_SPEC] * 3,
        compiler_params=params,
        name="terms",
    )(
        *[
            held(value)
            for value in (
                *(own, surf, total, total_0, count),
                *(takes, at_lane, takes_near, at_lane_near),
            )
        ]
    )
    from_other = swapped(stepped[2].reshape(owned), 1)
    from_partner = swapped(stepped[1].reshape(owned), 0)
    result = pltpu.HBM((rows, columns), jnp.float32)
    depth, flux_east, flux_south = pl.pallas_call(
        functools.partial(last_kernel, corridor, tiles),
        out_shape=[result] * 3,
        in_specs=[VMEM_SPEC] * 10,
        out_specs=[HBM_SPEC] * 3,
        scratch_shapes=[pltpu.VMEM((rows, columns), jnp.float32)] * 2
        + [field, pltpu.SemaphoreType.DMA((3,))],
        compiler_params=params,
        name="last",
    )(*[held(value) for value in (surf, east, south, *faces, total, covers, bed)])
    river_section = stepped[0].reshape(owned) + from_partner + from_other
    return (depth, flux_east, flux_south, river_section)


def solution(mesh):
    return jax.shard_map(
        local,
        mesh=mesh,
        in_specs=(
            P(("runs", "gy"), None),
            P(("runs", "gy"), None),
            P(("runs", "gy"), None),
            P(("runs", "gy")),
            P("gy", None),
            P("gy", None),
            P(),
            P(None, "gy"),
        ),
        out_specs=(
            P(("runs", "gy"), None),
            P(("runs", "gy"), None),
            P(("runs", "gy"), None),
            P(("runs", "gy")),
        ),
        check_vma=False,
    )
```

```python
import functools

import jax
import jax.numpy as jnp
from jax import lax
from jax.experimental import pallas as pl
from jax.experimental.pallas import tpu as pltpu
from jax.sharding import PartitionSpec as P

STEPS = 4

GRAV = 9.81
TSTEP = 8.0
CELL = 90.0
FLOOR = 0.05
BANK_COEF = 200.0
CELL_AREA = 8100.0
NODE_AREA = 20000.0

LANES = 128
HALO = 4
SLOPE = GRAV * TSTEP / CELL
SPREAD = TSTEP / CELL
FEED = TSTEP * BANK_COEF / CELL_AREA
DRAIN = TSTEP * BANK_COEF / NODE_AREA
VMEM_LIMIT = 32 * 1024 * 1024

SMEM_SPEC = pl.BlockSpec(memory_space=pltpu.SMEM)
VMEM_SPEC = pl.BlockSpec(memory_space=pltpu.VMEM)
HBM_SPEC = pl.BlockSpec(memory_space=pltpu.HBM)


def swapped(value, first):
    count = lax.axis_size("gy")
    pairs = []
    for low in range(first, count - 1, 2):
        pairs += [(low, low + 1), (low + 1, low)]
    return lax.ppermute(value, "gy", pairs)


def cols(chunk):
    return slice(chunk * LANES, (chunk + 1) * LANES)


def lanes_of(rows):
    return lax.broadcasted_iota(jnp.int32, (rows, LANES), 1)


def moved_left(value, following, by):
    return jnp.where(
        lanes_of(value.shape[0]) >= LANES - by,
        pltpu.roll(following, LANES - by, 1),
        pltpu.roll(value, LANES - by, 1),
    )


def moved_up(value):
    return pltpu.roll(value, value.shape[0] - 1, 0)


def split3(value):
    high = value.astype(jnp.bfloat16)
    rest = value - high.astype(jnp.float32)
    middle = rest.astype(jnp.bfloat16)
    low = (rest - middle.astype(jnp.float32)).astype(jnp.bfloat16)
    return high, middle, low


def one_hot(count, key):
    rows = lax.broadcasted_iota(jnp.int32, (count, key.shape[1]), 0)
    return jnp.where(rows == key, 1.0, 0.0)


def drag_of(mann_a, mann_b):
    pair = mann_a + mann_b
    return (0.25 * GRAV * TSTEP) * (pair * pair)


def looked_up(klass, entries):
    value = jnp.broadcast_to(entries[0], klass.shape)
    for k in range(1, len(entries)):
        value = jnp.where(klass == k, entries[k], value)
    return value


def face(flux, surf_a, surf_b, bed_max, drag):
    flow_depth = jnp.maximum(jnp.maximum(surf_a, surf_b) - bed_max, FLOOR)
    power = jnp.exp2((-7.0 / 3.0) * jnp.log2(flow_depth))
    driven = flux - SLOPE * flow_depth * (surf_b - surf_a)
    damping = 1.0 + drag * jnp.abs(flux) * power
    return driven * pl.reciprocal(damping, approx=True)


def window_sums(blocks, reach, forward):
    height = blocks[0].shape[0]
    count = len(blocks)
    spare = -(count * height) % 16
    whole = blocks + ([jnp.zeros((spare, LANES), jnp.float32)] if spare else [])
    whole = jnp.concatenate(whole, axis=0)
    high = whole.astype(jnp.bfloat16)
    low = (whole - high.astype(jnp.float32)).astype(jnp.bfloat16)
    source = lax.broadcasted_iota(jnp.int32, (2 * LANES, 2 * LANES), 0) % LANES
    target = lax.broadcasted_iota(jnp.int32, (2 * LANES, 2 * LANES), 1)
    spill = target >= LANES
    target = target % LANES
    if forward:
        ahead = source - target + jnp.where(spill, LANES, 0)
    else:
        ahead = target - source + jnp.where(spill, LANES, 0)
    band = jnp.where((ahead >= 0) & (ahead < reach), 1.0, 0.0).astype(jnp.bfloat16)
    sums = jnp.dot(
        jnp.concatenate([high, low], axis=1), band, preferred_element_type=jnp.float32
    )
    results = []
    for block in range(count):
        result = sums[block * height : (block + 1) * height, :LANES]
        beside = block + 1 if forward else block - 1
        if 0 <= beside < count:
            result = result + sums[beside * height : (beside + 1) * height, LANES:]
        results.append(result)
    return results


def east_walled(value, chunk, chunks):
    if chunk + 1 < chunks:
        return value
    return jnp.where(lanes_of(value.shape[0]) == LANES - 1, 0.0, value)


def located(cell, position, rows, ext, columns):
    base = ((position * rows - HALO) * columns + 1).astype(jnp.float32)
    offset = cell - base
    valid = (cell > 0.0) & (offset >= 0.0) & (offset < float(ext * columns))
    offset = jnp.where(valid, offset, 0.0)
    row = jnp.floor((offset + 0.5) * (1.0 / columns))
    column = (offset - row * float(columns)).astype(jnp.int32)
    row = row.astype(jnp.int32) - HALO
    row = jnp.where(row < 0, row + ext, row)
    chunk = column // LANES
    return valid, row, chunk, column - chunk * LANES


def scattered(section, key, lane, count):
    at_lane = one_hot(LANES, lane)
    parts = [at_lane] + [at_lane * part.astype(jnp.float32) for part in split3(section)]
    grid = lax.dot_general(
        one_hot(-(-count // 16) * 16, key).astype(jnp.bfloat16),
        jnp.concatenate(parts, axis=0).astype(jnp.bfloat16),
        (((1,), (1,)), ((), ())),
        preferred_element_type=jnp.float32,
    )
    number = grid[:, :LANES]
    total = (grid[:, LANES : 2 * LANES] + grid[:, 2 * LANES : 3 * LANES]) + grid[:, 3 * LANES :]
    return number, total


def pack_kernel(
    depth, bed, rough, east, south, section, cells, to_other, own, held, held_rough, held_cells, sems
):
    rows, columns = depth.shape
    even = lax.axis_index("gy") % 2 == 0
    start = pl.multiple_of(jnp.where(even, 0, rows - 8), 8)
    copies = [
        pltpu.make_async_copy(source, target, sems.at[slot])
        for slot, (source, target) in enumerate(
            (
                (depth.at[pl.ds(start, 8), :], held.at[0]),
                (bed.at[pl.ds(start, 8), :], held.at[1]),
                (rough.at[pl.ds(start, 8), :], held_rough),
                (east.at[pl.ds(start, 8), :], held.at[2]),
                (south.at[pl.ds(start, 8), :], held.at[3]),
                (section, own.at[pl.ds(0, 1), :]),
                (cells, held_cells),
            )
        )
    ]
    for copy in copies:
        copy.start()
    for slot in range(5):
        copies[slot].wait()
        block = (
            held_rough[...].astype(jnp.float32) if slot == 2 else held[slot - (slot > 2)]
        )
        to_other[slot] = jnp.where(even, block[:HALO], block[8 - HALO :])
    for copy in copies[5:]:
        copy.wait()
    own[1:2, :] = (held_cells[0:1, :] + 1).astype(jnp.float32)


def join_kernel(before, own, section, cells, to_other):
    even = lax.axis_index("gy") % 2 == 0
    owned = own.shape[1]
    rows = (own[0:1, :], own[1:2, :], section[...], (cells[0:1, :] + 1).astype(jnp.float32))

    def put(spare):
        for slot, row in enumerate(rows):
            to_other[3, spare : spare + 1, slot * owned : (slot + 1) * owned] = row

    @pl.when(even)
    def _():
        put(HALO - 1)

    @pl.when(jnp.logical_not(even))
    def _():
        put(0)


def picking(reach, rows, key, lane, takes, masks):
    for block in range(key.shape[1] // LANES):
        mine = slice(block * LANES, (block + 1) * LANES)

        def column(row):
            wide = jnp.broadcast_to(row[:, mine].astype(jnp.float32), (LANES, LANES))
            return jnp.transpose(wide).astype(jnp.int32)

        spread = lanes_of(LANES)
        at = column(key)
        after = jnp.where(at < 0, at, at + rows)
        for first in range(0, takes.shape[2], LANES):
            for half, place in enumerate((at, after)):
                hit = jnp.where(spread + first == place, 1.0, 0.0)
                takes[half, mine, first : first + LANES] = hit.astype(jnp.bfloat16)
        ahead = spread - column(lane)
        masks[0, mine, :] = jnp.where((ahead >= 0) & (ahead < reach), 1.0, 0.0)
        masks[1, mine, :] = jnp.where(ahead + LANES < reach, 1.0, 0.0)


def load_kernel(
    depth_in, east_in, south_in, bed_in, rough_in, to_partner, surf, east, south, bed, rough, sems
):
    rows, columns = depth_in.shape
    even = lax.axis_index("gy") % 2 == 0
    own = pl.ds(0, rows)
    copies = [
        pltpu.make_async_copy(source, target.at[own, :], sems.at[slot])
        for slot, (source, target) in enumerate(
            (
                (depth_in, surf),
                (bed_in, bed),
                (rough_in, rough),
                (east_in, east),
                (south_in, south),
            )
        )
    ]
    for copy in copies:
        copy.start()
    for slot, source in enumerate((surf, bed, rough, east, south)):
        copies[slot].wait()
        for chunk in range(columns // LANES):
            at = cols(chunk)
            first = source[:8, at].astype(jnp.float32)
            last = source[rows - 8 : rows, at].astype(jnp.float32)
            to_partner[slot, :, at] = jnp.where(even, last[8 - HALO :], first[:HALO])


def relay_kernel(by_other, prepared, near, beyond):
    del prepared
    even = lax.axis_index("gy") % 2 == 0
    owned = near.shape[1]
    for target, first in ((near, 0), (beyond, 2)):
        for slot in range(2):
            mine = slice((first + slot) * owned, (first + slot + 1) * owned)
            target[slot : slot + 1, :] = jnp.where(
                even, by_other[3, 0:1, mine], by_other[3, HALO - 1 : HALO, mine]
            )


def prepare_kernel(reach, table, rough, own, partner_section, partner_cells, *refs):
    surf, east, south, bed = refs[4:8]
    mann, bed_e, bed_s, drag_e, drag_s, number, total, table_rows, takes, masks = refs[8:]
    ext, columns = surf.shape
    rows = ext - 2 * HALO
    chunks = columns // LANES
    tiles = lax.axis_size("gy")
    position = lax.axis_index("gy")
    side = jnp.where(position % 2 == 0, 1, -1)
    entries = [table[k] for k in range(table.shape[0])]
    for k, entry in enumerate(entries):
        table_rows[k : k + 1, :] = jnp.full((1, LANES), entry, jnp.float32)
    for chunk in range(chunks):
        at = cols(chunk)
        mann[:rows, at] = looked_up(rough[:, at], entries)
        surf[:rows, at] = surf[:rows, at] + bed[:rows, at]

    partner = jnp.where(position + side < tiles, partner_cells[0:1, :] + 1, 0).astype(jnp.float32)
    section = jnp.concatenate([own[0:1, :], partner_section[...]], axis=1)
    cell = jnp.concatenate([own[1:2, :], partner], axis=1)
    valid, node_row, node_chunk, node_lane = located(cell, position, rows, ext, columns)
    key = jnp.where(valid, node_chunk * ext + node_row, -1)
    starts, levels = scattered(section, key, node_lane, chunks * ext)
    for chunk in range(chunks):
        at = cols(chunk)
        number[:, at] = starts[chunk * ext : (chunk + 1) * ext]
        total[:, at] = levels[chunk * ext : (chunk + 1) * ext]

    key = jnp.where(valid & (node_row < rows), node_chunk * rows + node_row, -1)
    picking(reach, rows, key, node_lane, takes, masks)

    kept = lax.broadcasted_iota(jnp.int32, (rows, LANES), 0) == rows - 1
    for chunk in range(chunks):
        at, then = cols(chunk), cols(min(chunk + 1, chunks - 1))
        s0, b0, m0 = surf[:rows, at], bed[:rows, at], mann[:rows, at]
        bed_max = jnp.maximum(b0, moved_left(b0, bed[:rows, then], 1))
        drag = drag_of(m0, moved_left(m0, mann[:rows, then], 1))
        bed_e[:rows, at] = bed_max
        drag_e[:rows, at] = drag
        new_east = face(
            east[:rows, at], s0, moved_left(s0, surf[:rows, then], 1), bed_max, drag
        )
        east[:rows, at] = east_walled(new_east, chunk, chunks)
        bed_max = jnp.maximum(b0, moved_up(b0))
        drag = drag_of(m0, moved_up(m0))
        bed_s[:rows, at] = bed_max
        drag_s[:rows, at] = drag
        q0 = south[:rows, at]
        south[:rows, at] = jnp.where(kept, q0, face(q0, s0, moved_up(s0), bed_max, drag))


def wall_of(ext, tiles):
    position = lax.axis_index("gy")
    rows = ext - 2 * HALO
    row = lax.broadcasted_iota(jnp.int32, (16, LANES), 0) + (ext - 16)
    return ((row == ext - 1) & (position == 0)) | ((row == rows - 1) & (position == tiles - 1))


def border_kernel(reach, tiles, by_partner, by_other, table_rows, near, beyond, *refs):
    surf, east, south, bed, mann, bed_e, bed_s, drag_e, drag_s, number, total, takes, masks = refs[11:]
    ext, columns = surf.shape
    rows = ext - 2 * HALO
    chunks = columns // LANES
    position = lax.axis_index("gy")
    even = position % 2 == 0
    entries = [table_rows[k : k + 1, :] for k in range(table_rows.shape[0])]
    row = lax.broadcasted_iota(jnp.int32, (2 * HALO, LANES), 0)
    spare = jnp.where(even, HALO, HALO - 1)
    for chunk in range(chunks):
        at = cols(chunk)
        halos = []
        for slot in range(5):
            a, b = by_partner[slot, :, at], by_other[slot, :, at]
            below = jnp.where(even, a, b)
            above = jnp.where(even, b, a)
            halos.append(jnp.concatenate([below, above], axis=0))
        surf[rows:, at] = halos[0] + halos[1]
        bed[rows:, at] = halos[1]
        mann[rows:, at] = looked_up(halos[2].astype(jnp.int32), entries)
        east[rows:, at] = jnp.where(row == spare, 0.0, halos[3])
        south[rows:, at] = halos[4]

    section = jnp.concatenate([near[0:1, :], beyond[0:1, :]], axis=1)
    cell = jnp.concatenate([near[1:2, :], beyond[1:2, :]], axis=1)
    valid, node_row, node_chunk, node_lane = located(cell, position, rows, ext, columns)
    key = jnp.where(valid, node_chunk * ext + node_row, -1)
    starts, levels = scattered(section, key, node_lane, chunks * ext)

    key = jnp.where(valid & (node_row < rows), node_chunk * rows + node_row, -1)
    owned = near.shape[1]
    picking(reach, rows, key[:, :owned], node_lane[:, :owned], takes, masks)

    wall = wall_of(ext, tiles)
    kept = lax.broadcasted_iota(jnp.int32, (16, LANES), 0) < 7
    for chunk in range(chunks):
        at, then = cols(chunk), cols(min(chunk + 1, chunks - 1))
        number[:, at] += starts[chunk * ext : (chunk + 1) * ext]
        total[:, at] += levels[chunk * ext : (chunk + 1) * ext]
        s0, b0, m0 = surf[rows:, at], bed[rows:, at], mann[rows:, at]
        bed_max = jnp.maximum(b0, moved_left(b0, bed[rows:, then], 1))
        drag = drag_of(m0, moved_left(m0, mann[rows:, then], 1))
        bed_e[rows:, at] = bed_max
        drag_e[rows:, at] = drag
        new_east = face(
            east[rows:, at], s0, moved_left(s0, surf[rows:, then], 1), bed_max, drag
        )
        east[rows:, at] = east_walled(new_east, chunk, chunks)

        def rolled_up(ref):
            value = jnp.concatenate([ref[rows - 8 :, at], ref[:8, at]], axis=0)
            return value[:16], moved_up(value)[:16]

        s0, s1 = rolled_up(surf)
        b0, b1 = rolled_up(bed)
        m0, m1 = rolled_up(mann)
        bed_max = jnp.maximum(b0, b1)
        drag = drag_of(m0, m1)
        bed_s[rows - 8 :, at] = bed_max
        drag_s[rows - 8 :, at] = drag
        q0 = south[rows - 8 :, at]
        new_south = jnp.where(wall, 0.0, face(q0, s0, s1, bed_max, drag))
        south[rows - 8 :, at] = jnp.where(kept, q0, new_south)


def fluxes(mine, wall, before, faces, east_out, south_out=None):
    surf, east, south = before
    bed_e, bed_s, drag_e, drag_s = faces
    chunks = surf.shape[1] // LANES
    for chunk in range(chunks):
        at, then = cols(chunk), cols(min(chunk + 1, chunks - 1))
        s0 = surf[mine, at]
        left = moved_left(s0, surf[mine, then], 1)
        new_east = face(east[mine, at], s0, left, bed_e[mine, at], drag_e[mine, at])
        east_out[mine, at] = east_walled(new_east, chunk, chunks)
        if south_out is not None:
            s0 = surf[:, at]
            new_south = face(south[:, at], s0, moved_up(s0), bed_s[:, at], drag_s[:, at])
            south_out[:, at] = jnp.concatenate(
                [new_south[:-16], jnp.where(wall, 0.0, new_south[-16:])], axis=0
            )


def settled(mine, surf, east, south, gain):
    ext, columns = surf.shape
    for chunk in range(columns // LANES):
        at = cols(chunk)
        new_east = east[mine, at]
        new_south = south[:, at]
        lane = lanes_of(new_east.shape[0])
        west = pltpu.roll(new_east, 1, 1)
        if chunk > 0:
            west = jnp.where(lane < 1, pltpu.roll(east[mine, cols(chunk - 1)], 1, 1), west)
        else:
            west = jnp.where(lane < 1, 0.0, west)
        north = pltpu.roll(new_south, 1, 0)[mine]
        inflow = west + north
        s0 = surf[mine, at]
        outflow = new_east + new_south[mine]
        yield chunk, s0 + (SPREAD * (inflow - outflow) + gain(chunk, s0))


def exchange(corridor, mine, surf, total, count, covers, total_out):
    chunks = surf.shape[1] // LANES
    sums = window_sums([total[mine, cols(chunk)] for chunk in range(chunks)], corridor, False)
    if total_out is not None:
        windows = window_sums([surf[mine, cols(chunk)] for chunk in range(chunks)], corridor, True)
        for chunk in range(chunks):
            at = cols(chunk)
            kept = (1.0 - corridor * DRAIN) * total[mine, at]
            total_out[mine, at] = kept + count[mine, at] * windows[chunk]

    def gain(chunk, value):
        return sums[chunk] - covers[mine, cols(chunk)] * value

    return gain


def given(corridor, surf, before, after):
    rows = surf.shape[0] - 2 * HALO
    for chunk in range(surf.shape[1] // LANES):
        at = cols(chunk)
        value = (DRAIN * (1.0 - corridor * DRAIN)) * surf[:rows, at]
        if before is not None:
            value = (1.0 - corridor * DRAIN) * before[:, at] + value
        after[:, at] = value


def first_kernel(corridor, surf, east, south, number, total, *refs):
    surf_1, total_1, count, covers, given_1, total_0 = refs
    rows = surf.shape[0] - 2 * HALO
    chunks = surf.shape[1] // LANES
    own = slice(0, rows)
    covering = window_sums([number[own, cols(chunk)] for chunk in range(chunks)], corridor, False)
    for chunk in range(chunks):
        at = cols(chunk)
        count[own, at] = (FEED * DRAIN) * number[own, at]
        covers[own, at] = FEED * covering[chunk]
        total_0[own, at] = FEED * total[own, at]
    gain = exchange(corridor, own, surf, total_0, count, covers, total_1)
    for chunk, new_surf in settled(own, surf, east, south, gain):
        surf_1[own, cols(chunk)] = new_surf
    given(corridor, surf, None, given_1)


def second_kernel(corridor, tiles, far, surf, east, south, *refs):
    faces = refs[:4]
    number, total, given_1 = refs[4:7]
    surf_1, total_1, count, covers = refs[11:15]
    surf_2, east_2, south_2, total_2, given_2, total_0 = refs[15:]
    ext, columns = surf.shape
    rows = ext - 2 * HALO
    chunks = columns // LANES
    position = lax.axis_index("gy")
    tail = slice(rows, ext)

    valid, node_row, node_chunk, node_lane = located(far[1:2, :], position, rows, ext, columns)
    key = jnp.where(valid & (node_row >= rows), node_chunk * 8 + (node_row - rows), -1)
    starts, levels = scattered(far[0:1, :], key, node_lane, chunks * 8)
    starting = [
        number[tail, cols(chunk)] + starts[chunk * 8 : chunk * 8 + 8] for chunk in range(chunks)
    ]
    covering = window_sums(starting, corridor, False)
    for chunk in range(chunks):
        at = cols(chunk)
        count[tail, at] = (FEED * DRAIN) * starting[chunk]
        covers[tail, at] = FEED * covering[chunk]
        total_0[tail, at] = FEED * (total[tail, at] + levels[chunk * 8 : chunk * 8 + 8])
    gain = exchange(corridor, tail, surf, total_0, count, covers, total_1)
    for chunk, new_surf in settled(tail, surf, east, south, gain):
        surf_1[tail, cols(chunk)] = new_surf

    every = slice(0, ext)
    gain = exchange(corridor, every, surf_1, total_1, count, covers, total_2)
    fluxes(every, wall_of(ext, tiles), (surf_1, east, south), faces, east_2, south_2)
    for chunk, new_surf in settled(every, surf_1, east_2, south_2, gain):
        surf_2[:, cols(chunk)] = new_surf
    given(corridor, surf_1, given_1, given_2)


def third_kernel(corridor, tiles, surf, east, south, *refs):
    faces = refs[:4]
    total, covers, count, given_2, surf_3, east_3, south_3, total_3, given_3 = refs[4:]
    ext = surf.shape[0]
    own = slice(0, ext - 2 * HALO)
    gain = exchange(corridor, own, surf, total, count, covers, total_3)
    fluxes(own, wall_of(ext, tiles), (surf, east, south), faces, east_3, south_3)
    for chunk, new_surf in settled(own, surf, east_3, south_3, gain):
        surf_3[own, cols(chunk)] = new_surf
    given(corridor, surf, given_2, given_3)


def terms_kernel(corridor, own, surf, given_3, *refs):
    takes, masks, takes_near, masks_near, own_term, partner_term, other_term = refs
    rows, columns = given_3.shape
    owned = own.shape[1]
    chunks = columns // LANES
    levels = [
        given_3[:, cols(chunk)] + DRAIN * surf[:rows, cols(chunk)] for chunk in range(chunks)
    ]
    spare = takes.shape[2] - chunks * rows
    if spare:
        levels.append(jnp.zeros((spare, LANES), jnp.float32))
    levels = jnp.concatenate(levels, axis=0)
    high = levels.astype(jnp.bfloat16)
    low = (levels - high.astype(jnp.float32)).astype(jnp.bfloat16)
    picked = jnp.dot(
        jnp.concatenate([takes[0], takes_near[0], takes[1], takes_near[1]], axis=0),
        jnp.concatenate([high, low], axis=1),
        preferred_element_type=jnp.float32,
    )
    hit = jnp.concatenate([masks[0], masks_near[0], masks[1], masks_near[1]], axis=0)
    picked = (picked * jnp.concatenate([hit, hit], axis=1)).astype(jnp.bfloat16)
    picked = jnp.concatenate([picked[: 3 * owned], picked[3 * owned :]], axis=1)
    terms = lax.dot_general(
        jnp.ones((8, 4 * LANES), jnp.bfloat16),
        picked,
        (((1,), (1,)), ((), ())),
        preferred_element_type=jnp.float32,
    )[0:1]
    own_term[...] = (1.0 - corridor * DRAIN) ** STEPS * own[0:1, :] + terms[:, :owned]
    partner_term[...] = terms[:, owned : 2 * owned]
    other_term[...] = terms[:, 2 * owned :]


def turn_kernel(corridor, tiles, surf_2, east_2, south_3, *refs):
    faces = refs[:4]
    total, covers = refs[4:6]
    east_3 = refs[7]
    surf_3, east_4, south_4, east_out, south_out, east_tail, sems = refs[8:]
    ext = surf_2.shape[0]
    rows = ext - 2 * HALO
    tail = slice(rows, ext)
    gain = exchange(corridor, tail, surf_2, total, None, covers, None)
    fluxes(tail, None, (surf_2, east_2, None), faces, east_tail)
    for chunk, new_surf in settled(tail, surf_2, east_tail, south_3, gain):
        surf_3[tail, cols(chunk)] = new_surf
    copies = [
        pltpu.make_async_copy(source.at[pl.ds(0, rows), :], target, sems.at[slot])
        for slot, (source, target) in enumerate(((east_4, east_out), (south_4, south_out)))
    ]
    own = slice(0, rows)
    fluxes(own, wall_of(ext, tiles), (surf_3, east_3, south_3), faces, east_4, south_4)
    for copy in copies:
        copy.start()
    for copy in copies:
        copy.wait()


def last_kernel(corridor, surf, east, south, total, covers, bed, depth_out, depth_new, sem):
    rows, columns = depth_new.shape
    own = slice(0, rows)
    gain = exchange(corridor, own, surf, total, None, covers, None)
    for chunk, new_surf in settled(own, surf, east, south, gain):
        at = cols(chunk)
        depth_new[:, at] = new_surf - bed[own, at]
    copy = pltpu.make_async_copy(depth_new, depth_out, sem)
    copy.start()
    copy.wait()


def local(
    depth, flux_east, flux_south, river_section, bed_level, rough_class, manning_table, bank_cell
):
    rows, columns = depth.shape
    owned = river_section.shape[0]
    corridor = bank_cell.shape[0]
    tiles = lax.axis_size("gy")
    ext = rows + 2 * HALO
    chunks = columns // LANES
    partner_section = swapped(river_section, 0).reshape(1, owned)
    partner_cells = swapped(bank_cell, 0)

    def held(value):
        return pltpu.with_memory_space_constraint(value, pltpu.VMEM)

    def far(value):
        return pltpu.with_memory_space_constraint(value, pltpu.HBM)

    params = pltpu.CompilerParams(vmem_limit_bytes=VMEM_LIMIT)
    halo = pltpu.VMEM((5, HALO, columns), jnp.float32)
    field = pltpu.VMEM((ext, columns), jnp.float32)
    small = pltpu.VMEM((rows, columns), jnp.float32)
    term = pltpu.VMEM((1, owned), jnp.float32)
    pair = pltpu.VMEM((2, owned), jnp.float32)
    result = pltpu.HBM((rows, columns), jnp.float32)
    cells = -(-chunks * rows // LANES) * LANES

    def call(kernel, name, outs, values, scratch=(), aliases=None, first_spec=VMEM_SPEC):
        return pl.pallas_call(
            kernel,
            out_shape=outs,
            in_specs=[first_spec] + [VMEM_SPEC] * (len(values) - 1),
            out_specs=[HBM_SPEC if out is result else VMEM_SPEC for out in outs],
            scratch_shapes=scratch,
            input_output_aliases=aliases or {},
            compiler_params=params,
            name=name,
        )(
            *[
                value if slot == 0 and first_spec is SMEM_SPEC else held(value)
                for slot, value in enumerate(values)
            ]
        )

    def picks(nodes):
        return [
            pltpu.VMEM((2, nodes, cells), jnp.bfloat16),
            pltpu.VMEM((2, nodes, LANES), jnp.float32),
        ]

    to_other, own = pl.pallas_call(
        pack_kernel,
        out_shape=[halo, pair],
        in_specs=[HBM_SPEC] * 7,
        out_specs=[VMEM_SPEC] * 2,
        scratch_shapes=[
            pltpu.VMEM((4, 8, columns), jnp.float32),
            pltpu.VMEM((8, columns), jnp.int32),
            pltpu.VMEM((corridor, owned), jnp.int32),
            pltpu.SemaphoreType.DMA((7,)),
        ],
        compiler_params=params,
        name="pack",
    )(
        *[far(value) for value in (depth, bed_level, rough_class, flux_east, flux_south)],
        far(river_section.reshape(1, owned)),
        far(bank_cell),
    )
    (to_other,) = call(
        join_kernel,
        "join",
        [halo],
        (to_other, own, partner_section, partner_cells),
        aliases={0: 0},
    )
    by_other = swapped(to_other, 1)
    to_partner, *loaded, rough = pl.pallas_call(
        load_kernel,
        out_shape=[halo] + [field] * 4 + [pltpu.VMEM((rows, columns), jnp.int32)],
        in_specs=[HBM_SPEC] * 5,
        out_specs=[VMEM_SPEC] * 6,
        scratch_shapes=[pltpu.SemaphoreType.DMA((5,))],
        compiler_params=params,
        name="load",
    )(*[far(value) for value in (depth, flux_east, flux_south, bed_level, rough_class)])
    by_partner = swapped(to_partner, 0)
    *fields, table_rows, takes, masks = call(
        functools.partial(prepare_kernel, corridor),
        "prepare",
        [field] * 11
        + [pltpu.VMEM((manning_table.shape[0], LANES), jnp.float32)]
        + picks(2 * owned),
        (manning_table, rough, own, partner_section, partner_cells, *loaded),
        aliases={5 + slot: slot for slot in range(4)},
        first_spec=SMEM_SPEC,
    )
    near, beyond = call(relay_kernel, "relay", [pair, pair], (by_other, table_rows))
    from_far = swapped(near, 0)
    *fields, takes_near, masks_near = call(
        functools.partial(border_kernel, corridor, tiles),
        "border",
        [field] * 11 + picks(owned),
        (by_partner, by_other, table_rows, near, beyond, *fields),
        aliases={5 + slot: slot for slot in range(11)},
    )
    surf, east, south, bed, _, *faces, number, total = fields
    surf_1, total_1, count, covers, given_1 = call(
        functools.partial(first_kernel, corridor),
        "first",
        [field] * 4 + [small],
        (surf, east, south, number, total),
        scratch=[field],
    )
    surf_1, total_1, count, covers, surf_2, east_2, south_2, total_2, given_2 = call(
        functools.partial(second_kernel, corridor, tiles),
        "second",
        [field] * 8 + [small],
        (
            *(from_far, surf, east, south, *faces, number, total, given_1),
            *(surf_1, total_1, count, covers),
        ),
        scratch=[field],
        aliases={11 + slot: slot for slot in range(4)},
    )
    surf_3, east_3, south_3, total_3, given_3 = call(
        functools.partial(third_kernel, corridor, tiles),
        "third",
        [field] * 4 + [small],
        (surf_2, east_2, south_2, *faces, total_2, covers, count, given_2),
    )
    own_term, partner_term, other_term = call(
        functools.partial(terms_kernel, corridor),
        "terms",
        [term] * 3,
        (own, surf_3, given_3, takes, masks, takes_near, masks_near),
    )
    from_other = swapped(other_term.reshape(owned), 1)
    surf_3, east_4, south_4, flux_east, flux_south = call(
        functools.partial(turn_kernel, corridor, tiles),
        "turn",
        [field, small, field, result, result],
        (surf_2, east_2, south_3, *faces, total_2, covers, surf_3, east_3),
        scratch=[field, pltpu.SemaphoreType.DMA((2,))],
        aliases={9: 0},
    )
    from_partner = swapped(partner_term.reshape(owned), 0)
    (depth,) = call(
        functools.partial(last_kernel, corridor),
        "last",
        [result],
        (surf_3, east_4, south_4, total_3, covers, bed),
        scratch=[small, pltpu.SemaphoreType.DMA(())],
    )
    river_section = own_term.reshape(owned) + from_other + from_partner
    return (depth, flux_east, flux_south, river_section)


def solution(mesh):
    return jax.shard_map(
        local,
        mesh=mesh,
        in_specs=(
            P(("runs", "gy"), None),
            P(("runs", "gy"), None),
            P(("runs", "gy"), None),
            P(("runs", "gy")),
            P("gy", None),
            P("gy", None),
            P(),
            P(None, "gy"),
        ),
        out_specs=(
            P(("runs", "gy"), None),
            P(("runs", "gy"), None),
            P(("runs", "gy"), None),
            P(("runs", "gy")),
        ),
        check_vma=False,
    )
```

```python
import functools

import jax
import jax.numpy as jnp
from jax import lax
from jax.experimental import pallas as pl
from jax.experimental.pallas import tpu as pltpu
from jax.sharding import PartitionSpec as P

STEPS = 4

GRAV = 9.81
TSTEP = 8.0
CELL = 90.0
FLOOR = 0.05
BANK_COEF = 200.0
CELL_AREA = 8100.0
NODE_AREA = 20000.0

LANES = 128
HALO = 4
SLOPE = GRAV * TSTEP / CELL
SPREAD = TSTEP / CELL
FEED = TSTEP * BANK_COEF / CELL_AREA
DRAIN = TSTEP * BANK_COEF / NODE_AREA
VMEM_LIMIT = 32 * 1024 * 1024

VMEM_SPEC = pl.BlockSpec(memory_space=pltpu.VMEM)
HBM_SPEC = pl.BlockSpec(memory_space=pltpu.HBM)


def swapped(value, first):
    count = lax.axis_size("gy")
    pairs = []
    for low in range(first, count - 1, 2):
        pairs += [(low, low + 1), (low + 1, low)]
    return lax.ppermute(value, "gy", pairs)


def cols(chunk):
    return slice(chunk * LANES, (chunk + 1) * LANES)


def lanes_of(rows):
    return lax.broadcasted_iota(jnp.int32, (rows, LANES), 1)


def moved_left(value, following, by):
    return jnp.where(
        lanes_of(value.shape[0]) >= LANES - by,
        pltpu.roll(following, LANES - by, 1),
        pltpu.roll(value, LANES - by, 1),
    )


def moved_up(value):
    return pltpu.roll(value, value.shape[0] - 1, 0)


def split3(value):
    high = value.astype(jnp.bfloat16)
    rest = value - high.astype(jnp.float32)
    middle = rest.astype(jnp.bfloat16)
    low = (rest - middle.astype(jnp.float32)).astype(jnp.bfloat16)
    return high, middle, low


def one_hot(count, key):
    rows = lax.broadcasted_iota(jnp.int32, (count, key.shape[1]), 0)
    return jnp.where(rows == key, 1.0, 0.0)


def drag_of(mann_a, mann_b):
    pair = mann_a + mann_b
    return (0.25 * GRAV * TSTEP) * (pair * pair)


def looked_up(klass, entries):
    value = jnp.broadcast_to(entries[0], klass.shape)
    for k in range(1, len(entries)):
        value = jnp.where(klass == k, entries[k], value)
    return value


def face(flux, surf_a, surf_b, bed_max, drag):
    flow_depth = jnp.maximum(jnp.maximum(surf_a, surf_b) - bed_max, FLOOR)
    power = jnp.exp2((-7.0 / 3.0) * jnp.log2(flow_depth))
    driven = flux - SLOPE * flow_depth * (surf_b - surf_a)
    damping = 1.0 + drag * jnp.abs(flux) * power
    return driven * pl.reciprocal(damping, approx=True)


def window_sums(blocks, reach, forward):
    height = blocks[0].shape[0]
    count = len(blocks)
    spare = -(count * height) % 16
    whole = blocks + ([jnp.zeros((spare, LANES), jnp.float32)] if spare else [])
    whole = jnp.concatenate(whole, axis=0)
    high = whole.astype(jnp.bfloat16)
    low = (whole - high.astype(jnp.float32)).astype(jnp.bfloat16)
    source = lax.broadcasted_iota(jnp.int32, (2 * LANES, 2 * LANES), 0) % LANES
    target = lax.broadcasted_iota(jnp.int32, (2 * LANES, 2 * LANES), 1)
    spill = target >= LANES
    target = target % LANES
    if forward:
        ahead = source - target + jnp.where(spill, LANES, 0)
    else:
        ahead = target - source + jnp.where(spill, LANES, 0)
    band = jnp.where((ahead >= 0) & (ahead < reach), 1.0, 0.0).astype(jnp.bfloat16)
    sums = jnp.dot(
        jnp.concatenate([high, low], axis=1), band, preferred_element_type=jnp.float32
    )
    results = []
    for block in range(count):
        result = sums[block * height : (block + 1) * height, :LANES]
        beside = block + 1 if forward else block - 1
        if 0 <= beside < count:
            result = result + sums[beside * height : (beside + 1) * height, LANES:]
        results.append(result)
    return results


def east_walled(value, chunk, chunks):
    if chunk + 1 < chunks:
        return value
    return jnp.where(lanes_of(value.shape[0]) == LANES - 1, 0.0, value)


def located(cell, position, rows, ext, columns):
    base = ((position * rows - HALO) * columns + 1).astype(jnp.float32)
    offset = cell - base
    valid = (cell > 0.0) & (offset >= 0.0) & (offset < float(ext * columns))
    offset = jnp.where(valid, offset, 0.0)
    row = jnp.floor((offset + 0.5) * (1.0 / columns))
    column = (offset - row * float(columns)).astype(jnp.int32)
    row = row.astype(jnp.int32) - HALO
    row = jnp.where(row < 0, row + ext, row)
    chunk = column // LANES
    return valid, row, chunk, column - chunk * LANES


def scattered(section, key, lane, count):
    at_lane = one_hot(LANES, lane)
    parts = [at_lane] + [at_lane * part.astype(jnp.float32) for part in split3(section)]
    grid = lax.dot_general(
        one_hot(-(-count // 16) * 16, key).astype(jnp.bfloat16),
        jnp.concatenate(parts, axis=0).astype(jnp.bfloat16),
        (((1,), (1,)), ((), ())),
        preferred_element_type=jnp.float32,
    )
    number = grid[:, :LANES]
    total = (grid[:, LANES : 2 * LANES] + grid[:, 2 * LANES : 3 * LANES]) + grid[:, 3 * LANES :]
    return number, total


def pack_kernel(
    depth, bed, rough, east, south, section, cells, to_other, own, held, held_rough, held_cells, sems
):
    rows, columns = depth.shape
    even = lax.axis_index("gy") % 2 == 0
    start = pl.multiple_of(jnp.where(even, 0, rows - 8), 8)
    copies = [
        pltpu.make_async_copy(source, target, sems.at[slot])
        for slot, (source, target) in enumerate(
            (
                (depth.at[pl.ds(start, 8), :], held.at[0]),
                (bed.at[pl.ds(start, 8), :], held.at[1]),
                (rough.at[pl.ds(start, 8), :], held_rough),
                (east.at[pl.ds(start, 8), :], held.at[2]),
                (south.at[pl.ds(start, 8), :], held.at[3]),
                (section, own.at[pl.ds(0, 1), :]),
                (cells, held_cells),
            )
        )
    ]
    for copy in copies:
        copy.start()
    for slot in range(5):
        copies[slot].wait()
        block = (
            held_rough[...].astype(jnp.float32) if slot == 2 else held[slot - (slot > 2)]
        )
        to_other[slot] = jnp.where(even, block[:HALO], block[8 - HALO :])
    for copy in copies[5:]:
        copy.wait()
    own[1:2, :] = (held_cells[0:1, :] + 1).astype(jnp.float32)


def join_kernel(before, own, section, cells, to_other):
    even = lax.axis_index("gy") % 2 == 0
    owned = own.shape[1]
    rows = (own[0:1, :], own[1:2, :], section[...], (cells[0:1, :] + 1).astype(jnp.float32))

    def put(spare):
        for slot, row in enumerate(rows):
            to_other[3, spare : spare + 1, slot * owned : (slot + 1) * owned] = row

    @pl.when(even)
    def _():
        put(HALO - 1)

    @pl.when(jnp.logical_not(even))
    def _():
        put(0)


def picking(reach, rows, key, lane, takes, masks):
    for block in range(key.shape[1] // LANES):
        mine = slice(block * LANES, (block + 1) * LANES)

        def column(row):
            wide = jnp.broadcast_to(row[:, mine].astype(jnp.float32), (LANES, LANES))
            return jnp.transpose(wide).astype(jnp.int32)

        spread = lanes_of(LANES)
        at = column(key)
        after = jnp.where(at < 0, at, at + rows)
        for first in range(0, takes.shape[2], LANES):
            for half, place in enumerate((at, after)):
                hit = jnp.where(spread + first == place, 1.0, 0.0)
                takes[half, mine, first : first + LANES] = hit.astype(jnp.bfloat16)
        ahead = spread - column(lane)
        masks[0, mine, :] = jnp.where((ahead >= 0) & (ahead < reach), 1.0, 0.0)
        masks[1, mine, :] = jnp.where(ahead + LANES < reach, 1.0, 0.0)


def load_kernel(
    depth_in, east_in, south_in, bed_in, rough_in, table_in, *refs
):
    to_partner, surf, east, south, bed, rough, table_rows, table, sems = refs
    rows, columns = depth_in.shape
    even = lax.axis_index("gy") % 2 == 0
    own = pl.ds(0, rows)
    copies = [
        pltpu.make_async_copy(source, target.at[own, :], sems.at[slot])
        for slot, (source, target) in enumerate(
            (
                (depth_in, surf),
                (bed_in, bed),
                (rough_in, rough),
                (east_in, east),
                (south_in, south),
            )
        )
    ]
    copies.append(pltpu.make_async_copy(table_in, table, sems.at[5]))
    for copy in copies:
        copy.start()
    copies[5].wait()
    for k in range(table_rows.shape[0]):
        table_rows[k : k + 1, :] = jnp.broadcast_to(table[:, k : k + 1], (1, LANES))
    for slot, source in enumerate((surf, bed, rough, east, south)):
        copies[slot].wait()
        for chunk in range(columns // LANES):
            at = cols(chunk)
            first = source[:8, at].astype(jnp.float32)
            last = source[rows - 8 : rows, at].astype(jnp.float32)
            to_partner[slot, :, at] = jnp.where(even, last[8 - HALO :], first[:HALO])


def relay_kernel(by_other, prepared, near, beyond):
    del prepared
    even = lax.axis_index("gy") % 2 == 0
    owned = near.shape[1]
    for target, first in ((near, 0), (beyond, 2)):
        for slot in range(2):
            mine = slice((first + slot) * owned, (first + slot + 1) * owned)
            target[slot : slot + 1, :] = jnp.where(
                even, by_other[3, 0:1, mine], by_other[3, HALO - 1 : HALO, mine]
            )


def prepare_kernel(reach, table_rows, rough, own, partner_section, partner_cells, *refs):
    surf, east, south, bed = refs[4:8]
    mann, bed_e, bed_s, drag_e, drag_s, number, total, takes, masks = refs[8:]
    ext, columns = surf.shape
    rows = ext - 2 * HALO
    chunks = columns // LANES
    tiles = lax.axis_size("gy")
    position = lax.axis_index("gy")
    side = jnp.where(position % 2 == 0, 1, -1)
    entries = [table_rows[k : k + 1, :] for k in range(table_rows.shape[0])]
    for chunk in range(chunks):
        at = cols(chunk)
        mann[:rows, at] = looked_up(rough[:, at], entries)
        surf[:rows, at] = surf[:rows, at] + bed[:rows, at]

    partner = jnp.where(position + side < tiles, partner_cells[0:1, :] + 1, 0).astype(jnp.float32)
    section = jnp.concatenate([own[0:1, :], partner_section[...]], axis=1)
    cell = jnp.concatenate([own[1:2, :], partner], axis=1)
    valid, node_row, node_chunk, node_lane = located(cell, position, rows, ext, columns)
    key = jnp.where(valid, node_chunk * ext + node_row, -1)
    starts, levels = scattered(section, key, node_lane, chunks * ext)
    for chunk in range(chunks):
        at = cols(chunk)
        number[:, at] = starts[chunk * ext : (chunk + 1) * ext]
        total[:, at] = levels[chunk * ext : (chunk + 1) * ext]

    key = jnp.where(valid & (node_row < rows), node_chunk * rows + node_row, -1)
    picking(reach, rows, key, node_lane, takes, masks)

    kept = lax.broadcasted_iota(jnp.int32, (rows, LANES), 0) == rows - 1
    for chunk in range(chunks):
        at, then = cols(chunk), cols(min(chunk + 1, chunks - 1))
        s0, b0, m0 = surf[:rows, at], bed[:rows, at], mann[:rows, at]
        bed_max = jnp.maximum(b0, moved_left(b0, bed[:rows, then], 1))
        drag = drag_of(m0, moved_left(m0, mann[:rows, then], 1))
        bed_e[:rows, at] = bed_max
        drag_e[:rows, at] = drag
        new_east = face(
            east[:rows, at], s0, moved_left(s0, surf[:rows, then], 1), bed_max, drag
        )
        east[:rows, at] = east_walled(new_east, chunk, chunks)
        bed_max = jnp.maximum(b0, moved_up(b0))
        drag = drag_of(m0, moved_up(m0))
        bed_s[:rows, at] = bed_max
        drag_s[:rows, at] = drag
        q0 = south[:rows, at]
        south[:rows, at] = jnp.where(kept, q0, face(q0, s0, moved_up(s0), bed_max, drag))


def wall_of(ext, tiles):
    position = lax.axis_index("gy")
    rows = ext - 2 * HALO
    row = lax.broadcasted_iota(jnp.int32, (16, LANES), 0) + (ext - 16)
    return ((row == ext - 1) & (position == 0)) | ((row == rows - 1) & (position == tiles - 1))


def border_kernel(reach, tiles, by_partner, by_other, table_rows, near, beyond, *refs):
    surf, east, south, bed, mann, bed_e, bed_s, drag_e, drag_s, number, total, takes, masks = refs[11:]
    ext, columns = surf.shape
    rows = ext - 2 * HALO
    chunks = columns // LANES
    position = lax.axis_index("gy")
    even = position % 2 == 0
    entries = [table_rows[k : k + 1, :] for k in range(table_rows.shape[0])]
    row = lax.broadcasted_iota(jnp.int32, (2 * HALO, LANES), 0)
    spare = jnp.where(even, HALO, HALO - 1)
    for chunk in range(chunks):
        at = cols(chunk)
        halos = []
        for slot in range(5):
            a, b = by_partner[slot, :, at], by_other[slot, :, at]
            below = jnp.where(even, a, b)
            above = jnp.where(even, b, a)
            halos.append(jnp.concatenate([below, above], axis=0))
        surf[rows:, at] = halos[0] + halos[1]
        bed[rows:, at] = halos[1]
        mann[rows:, at] = looked_up(halos[2].astype(jnp.int32), entries)
        east[rows:, at] = jnp.where(row == spare, 0.0, halos[3])
        south[rows:, at] = halos[4]

    section = jnp.concatenate([near[0:1, :], beyond[0:1, :]], axis=1)
    cell = jnp.concatenate([near[1:2, :], beyond[1:2, :]], axis=1)
    valid, node_row, node_chunk, node_lane = located(cell, position, rows, ext, columns)
    key = jnp.where(valid, node_chunk * ext + node_row, -1)
    starts, levels = scattered(section, key, node_lane, chunks * ext)

    key = jnp.where(valid & (node_row < rows), node_chunk * rows + node_row, -1)
    owned = near.shape[1]
    picking(reach, rows, key[:, :owned], node_lane[:, :owned], takes, masks)

    wall = wall_of(ext, tiles)
    kept = lax.broadcasted_iota(jnp.int32, (16, LANES), 0) < 7
    for chunk in range(chunks):
        at, then = cols(chunk), cols(min(chunk + 1, chunks - 1))
        number[:, at] += starts[chunk * ext : (chunk + 1) * ext]
        total[:, at] += levels[chunk * ext : (chunk + 1) * ext]
        s0, b0, m0 = surf[rows:, at], bed[rows:, at], mann[rows:, at]
        bed_max = jnp.maximum(b0, moved_left(b0, bed[rows:, then], 1))
        drag = drag_of(m0, moved_left(m0, mann[rows:, then], 1))
        bed_e[rows:, at] = bed_max
        drag_e[rows:, at] = drag
        new_east = face(
            east[rows:, at], s0, moved_left(s0, surf[rows:, then], 1), bed_max, drag
        )
        east[rows:, at] = east_walled(new_east, chunk, chunks)

        def rolled_up(ref):
            value = jnp.concatenate([ref[rows - 8 :, at], ref[:8, at]], axis=0)
            return value[:16], moved_up(value)[:16]

        s0, s1 = rolled_up(surf)
        b0, b1 = rolled_up(bed)
        m0, m1 = rolled_up(mann)
        bed_max = jnp.maximum(b0, b1)
        drag = drag_of(m0, m1)
        bed_s[rows - 8 :, at] = bed_max
        drag_s[rows - 8 :, at] = drag
        q0 = south[rows - 8 :, at]
        new_south = jnp.where(wall, 0.0, face(q0, s0, s1, bed_max, drag))
        south[rows - 8 :, at] = jnp.where(kept, q0, new_south)


def fluxes(mine, wall, before, faces, east_out, south_out=None):
    surf, east, south = before
    bed_e, bed_s, drag_e, drag_s = faces
    chunks = surf.shape[1] // LANES
    rolled = pltpu.roll(surf[mine, cols(0)], LANES - 1, 1)
    lane = lanes_of(rolled.shape[0])
    for chunk in range(chunks):
        at = cols(chunk)
        s0 = surf[mine, at]
        rolled_then = rolled
        if chunk + 1 < chunks:
            rolled_then = pltpu.roll(surf[mine, cols(chunk + 1)], LANES - 1, 1)
        left = jnp.where(lane >= LANES - 1, rolled_then, rolled)
        rolled = rolled_then
        new_east = face(east[mine, at], s0, left, bed_e[mine, at], drag_e[mine, at])
        east_out[mine, at] = east_walled(new_east, chunk, chunks)
        if south_out is not None:
            s0 = surf[:, at]
            new_south = face(south[:, at], s0, moved_up(s0), bed_s[:, at], drag_s[:, at])
            south_out[:, at] = jnp.concatenate(
                [new_south[:-16], jnp.where(wall, 0.0, new_south[-16:])], axis=0
            )


def settled(mine, surf, east, south, gain):
    ext, columns = surf.shape
    rolled = 0.0
    for chunk in range(columns // LANES):
        at = cols(chunk)
        new_east = east[mine, at]
        new_south = south[:, at]
        lane = lanes_of(new_east.shape[0])
        rolled_before, rolled = rolled, pltpu.roll(new_east, 1, 1)
        west = jnp.where(lane < 1, rolled_before, rolled)
        north = pltpu.roll(new_south, 1, 0)[mine]
        inflow = west + north
        s0 = surf[mine, at]
        outflow = new_east + new_south[mine]
        yield chunk, s0 + (SPREAD * (inflow - outflow) + gain(chunk, s0))


def exchange(corridor, mine, surf, total, count, covers, total_out):
    chunks = surf.shape[1] // LANES
    sums = window_sums([total[mine, cols(chunk)] for chunk in range(chunks)], corridor, False)
    if total_out is not None:
        windows = window_sums([surf[mine, cols(chunk)] for chunk in range(chunks)], corridor, True)
        for chunk in range(chunks):
            at = cols(chunk)
            kept = (1.0 - corridor * DRAIN) * total[mine, at]
            total_out[mine, at] = kept + count[mine, at] * windows[chunk]

    def gain(chunk, value):
        return sums[chunk] - covers[mine, cols(chunk)] * value

    return gain


def given(corridor, surf, before, after):
    rows = surf.shape[0] - 2 * HALO
    for chunk in range(surf.shape[1] // LANES):
        at = cols(chunk)
        value = (DRAIN * (1.0 - corridor * DRAIN)) * surf[:rows, at]
        if before is not None:
            value = (1.0 - corridor * DRAIN) * before[:, at] + value
        after[:, at] = value


def first_kernel(corridor, surf, east, south, number, total, *refs):
    surf_1, total_1, count, covers, given_1, total_0 = refs
    rows = surf.shape[0] - 2 * HALO
    chunks = surf.shape[1] // LANES
    own = slice(0, rows)
    covering = window_sums([number[own, cols(chunk)] for chunk in range(chunks)], corridor, False)
    for chunk in range(chunks):
        at = cols(chunk)
        count[own, at] = (FEED * DRAIN) * number[own, at]
        covers[own, at] = FEED * covering[chunk]
        total_0[own, at] = FEED * total[own, at]
    gain = exchange(corridor, own, surf, total_0, count, covers, total_1)
    for chunk, new_surf in settled(own, surf, east, south, gain):
        surf_1[own, cols(chunk)] = new_surf
    given(corridor, surf, None, given_1)


def second_kernel(corridor, tiles, far, surf, east, south, *refs):
    faces = refs[:4]
    number, total, given_1 = refs[4:7]
    surf_1, total_1, count, covers = refs[11:15]
    surf_2, east_2, south_2, total_2, given_2, total_0 = refs[15:]
    ext, columns = surf.shape
    rows = ext - 2 * HALO
    chunks = columns // LANES
    position = lax.axis_index("gy")
    tail = slice(rows, ext)

    valid, node_row, node_chunk, node_lane = located(far[1:2, :], position, rows, ext, columns)
    key = jnp.where(valid & (node_row >= rows), node_chunk * 8 + (node_row - rows), -1)
    starts, levels = scattered(far[0:1, :], key, node_lane, chunks * 8)
    starting = [
        number[tail, cols(chunk)] + starts[chunk * 8 : chunk * 8 + 8] for chunk in range(chunks)
    ]
    covering = window_sums(starting, corridor, False)
    for chunk in range(chunks):
        at = cols(chunk)
        count[tail, at] = (FEED * DRAIN) * starting[chunk]
        covers[tail, at] = FEED * covering[chunk]
        total_0[tail, at] = FEED * (total[tail, at] + levels[chunk * 8 : chunk * 8 + 8])
    gain = exchange(corridor, tail, surf, total_0, count, covers, total_1)
    for chunk, new_surf in settled(tail, surf, east, south, gain):
        surf_1[tail, cols(chunk)] = new_surf

    every = slice(0, ext)
    gain = exchange(corridor, every, surf_1, total_1, count, covers, total_2)
    fluxes(every, wall_of(ext, tiles), (surf_1, east, south), faces, east_2, south_2)
    for chunk, new_surf in settled(every, surf_1, east_2, south_2, gain):
        surf_2[:, cols(chunk)] = new_surf
    given(corridor, surf_1, given_1, given_2)


def third_kernel(corridor, tiles, surf, east, south, *refs):
    faces = refs[:4]
    total, covers, count, given_2, surf_3, east_3, south_3, total_3, given_3 = refs[4:]
    ext = surf.shape[0]
    own = slice(0, ext - 2 * HALO)
    gain = exchange(corridor, own, surf, total, count, covers, total_3)
    fluxes(own, wall_of(ext, tiles), (surf, east, south), faces, east_3, south_3)
    for chunk, new_surf in settled(own, surf, east_3, south_3, gain):
        surf_3[own, cols(chunk)] = new_surf
    given(corridor, surf, given_2, given_3)


def terms_kernel(corridor, own, surf, given_3, *refs):
    takes, masks, takes_near, masks_near, own_term, partner_term, other_term = refs
    rows, columns = given_3.shape
    owned = own.shape[1]
    chunks = columns // LANES
    levels = [
        given_3[:, cols(chunk)] + DRAIN * surf[:rows, cols(chunk)] for chunk in range(chunks)
    ]
    spare = takes.shape[2] - chunks * rows
    if spare:
        levels.append(jnp.zeros((spare, LANES), jnp.float32))
    levels = jnp.concatenate(levels, axis=0)
    high = levels.astype(jnp.bfloat16)
    low = (levels - high.astype(jnp.float32)).astype(jnp.bfloat16)
    picked = jnp.dot(
        jnp.concatenate([takes[0], takes_near[0], takes[1], takes_near[1]], axis=0),
        jnp.concatenate([high, low], axis=1),
        preferred_element_type=jnp.float32,
    )
    hit = jnp.concatenate([masks[0], masks_near[0], masks[1], masks_near[1]], axis=0)
    picked = (picked * jnp.concatenate([hit, hit], axis=1)).astype(jnp.bfloat16)
    picked = jnp.concatenate([picked[: 3 * owned], picked[3 * owned :]], axis=1)
    terms = lax.dot_general(
        jnp.ones((8, 4 * LANES), jnp.bfloat16),
        picked,
        (((1,), (1,)), ((), ())),
        preferred_element_type=jnp.float32,
    )[0:1]
    own_term[...] = (1.0 - corridor * DRAIN) ** STEPS * own[0:1, :] + terms[:, :owned]
    partner_term[...] = terms[:, owned : 2 * owned]
    other_term[...] = terms[:, 2 * owned :]


def last_kernel(corridor, tiles, surf_2, east_2, south_3, *refs):
    faces = refs[:4]
    total_2, total_3, covers, bed, _, east_3 = refs[4:10]
    surf_3, depth_out, east_out, south_out, depth_4, east_4, south_4, east_tail, sems = refs[10:]
    ext, columns = surf_2.shape
    rows = ext - 2 * HALO
    own, tail = slice(0, rows), slice(rows, ext)
    gain = exchange(corridor, tail, surf_2, total_2, None, covers, None)
    fluxes(tail, None, (surf_2, east_2, None), faces, east_tail)
    for chunk, new_surf in settled(tail, surf_2, east_tail, south_3, gain):
        surf_3[tail, cols(chunk)] = new_surf
    copies = [
        pltpu.make_async_copy(source.at[pl.ds(0, rows), :], target, sems.at[slot])
        for slot, (source, target) in enumerate(
            ((east_4, east_out), (south_4, south_out), (depth_4, depth_out))
        )
    ]
    fluxes(own, wall_of(ext, tiles), (surf_3, east_3, south_3), faces, east_4, south_4)
    copies[0].start()
    copies[1].start()
    gain = exchange(corridor, own, surf_3, total_3, None, covers, None)
    for chunk, new_surf in settled(own, surf_3, east_4, south_4, gain):
        at = cols(chunk)
        depth_4[:, at] = new_surf - bed[own, at]
    copies[2].start()
    for copy in copies:
        copy.wait()


def local(
    depth, flux_east, flux_south, river_section, bed_level, rough_class, manning_table, bank_cell
):
    rows, columns = depth.shape
    owned = river_section.shape[0]
    corridor = bank_cell.shape[0]
    tiles = lax.axis_size("gy")
    ext = rows + 2 * HALO
    chunks = columns // LANES
    partner_section = swapped(river_section, 0).reshape(1, owned)
    partner_cells = swapped(bank_cell, 0)

    def held(value):
        return pltpu.with_memory_space_constraint(value, pltpu.VMEM)

    def far(value):
        return pltpu.with_memory_space_constraint(value, pltpu.HBM)

    params = pltpu.CompilerParams(vmem_limit_bytes=VMEM_LIMIT)
    halo = pltpu.VMEM((5, HALO, columns), jnp.float32)
    field = pltpu.VMEM((ext, columns), jnp.float32)
    small = pltpu.VMEM((rows, columns), jnp.float32)
    term = pltpu.VMEM((1, owned), jnp.float32)
    pair = pltpu.VMEM((2, owned), jnp.float32)
    result = pltpu.HBM((rows, columns), jnp.float32)
    cells = -(-chunks * rows // LANES) * LANES

    def call(kernel, name, outs, values, scratch=(), aliases=None):
        return pl.pallas_call(
            kernel,
            out_shape=outs,
            in_specs=[VMEM_SPEC] * len(values),
            out_specs=[HBM_SPEC if out is result else VMEM_SPEC for out in outs],
            scratch_shapes=scratch,
            input_output_aliases=aliases or {},
            compiler_params=params,
            name=name,
        )(*[held(value) for value in values])

    def picks(nodes):
        return [
            pltpu.VMEM((2, nodes, cells), jnp.bfloat16),
            pltpu.VMEM((2, nodes, LANES), jnp.float32),
        ]

    to_other, own = pl.pallas_call(
        pack_kernel,
        out_shape=[halo, pair],
        in_specs=[HBM_SPEC] * 7,
        out_specs=[VMEM_SPEC] * 2,
        scratch_shapes=[
            pltpu.VMEM((4, 8, columns), jnp.float32),
            pltpu.VMEM((8, columns), jnp.int32),
            pltpu.VMEM((corridor, owned), jnp.int32),
            pltpu.SemaphoreType.DMA((7,)),
        ],
        compiler_params=params,
        name="pack",
    )(
        *[far(value) for value in (depth, bed_level, rough_class, flux_east, flux_south)],
        far(river_section.reshape(1, owned)),
        far(bank_cell),
    )
    (to_other,) = call(
        join_kernel,
        "join",
        [halo],
        (to_other, own, partner_section, partner_cells),
        aliases={0: 0},
    )
    by_other = swapped(to_other, 1)
    classes = manning_table.shape[0]
    to_partner, *loaded, rough, table_rows = pl.pallas_call(
        load_kernel,
        out_shape=[halo]
        + [field] * 4
        + [pltpu.VMEM((rows, columns), jnp.int32), pltpu.VMEM((classes, LANES), jnp.float32)],
        in_specs=[HBM_SPEC] * 6,
        out_specs=[VMEM_SPEC] * 7,
        scratch_shapes=[pltpu.VMEM((1, classes), jnp.float32), pltpu.SemaphoreType.DMA((6,))],
        compiler_params=params,
        name="load",
    )(
        *[far(value) for value in (depth, flux_east, flux_south, bed_level, rough_class)],
        far(manning_table.reshape(1, classes)),
    )
    by_partner = swapped(to_partner, 0)
    *fields, takes, masks = call(
        functools.partial(prepare_kernel, corridor),
        "prepare",
        [field] * 11 + picks(2 * owned),
        (table_rows, rough, own, partner_section, partner_cells, *loaded),
        aliases={5 + slot: slot for slot in range(4)},
    )
    near, beyond = call(relay_kernel, "relay", [pair, pair], (by_other, masks))
    from_far = swapped(near, 0)
    *fields, takes_near, masks_near = call(
        functools.partial(border_kernel, corridor, tiles),
        "border",
        [field] * 11 + picks(owned),
        (by_partner, by_other, table_rows, near, beyond, *fields),
        aliases={5 + slot: slot for slot in range(11)},
    )
    surf, east, south, bed, _, *faces, number, total = fields
    surf_1, total_1, count, covers, given_1 = call(
        functools.partial(first_kernel, corridor),
        "first",
        [field] * 4 + [small],
        (surf, east, south, number, total),
        scratch=[field],
    )
    surf_1, total_1, count, covers, surf_2, east_2, south_2, total_2, given_2 = call(
        functools.partial(second_kernel, corridor, tiles),
        "second",
        [field] * 8 + [small],
        (
            *(from_far, surf, east, south, *faces, number, total, given_1),
            *(surf_1, total_1, count, covers),
        ),
        scratch=[field],
        aliases={11 + slot: slot for slot in range(4)},
    )
    surf_3, east_3, south_3, total_3, given_3 = call(
        functools.partial(third_kernel, corridor, tiles),
        "third",
        [field] * 4 + [small],
        (surf_2, east_2, south_2, *faces, total_2, covers, count, given_2),
    )
    own_term, partner_term, other_term = call(
        functools.partial(terms_kernel, corridor),
        "terms",
        [term] * 3,
        (own, surf_3, given_3, takes, masks, takes_near, masks_near),
    )
    from_other = swapped(other_term.reshape(owned), 1)
    from_partner = swapped(partner_term.reshape(owned), 0)
    _, depth, flux_east, flux_south = call(
        functools.partial(last_kernel, corridor, tiles),
        "last",
        [field, result, result, result],
        (surf_2, east_2, south_3, *faces, total_2, total_3, covers, bed, surf_3, east_3),
        scratch=[small, small, field, field, pltpu.SemaphoreType.DMA((3,))],
        aliases={11: 0},
    )
    river_section = own_term.reshape(owned) + from_other + from_partner
    return (depth, flux_east, flux_south, river_section)


def solution(mesh):
    return jax.shard_map(
        local,
        mesh=mesh,
        in_specs=(
            P(("runs", "gy"), None),
            P(("runs", "gy"), None),
            P(("runs", "gy"), None),
            P(("runs", "gy")),
            P("gy", None),
            P("gy", None),
            P(),
            P(None, "gy"),
        ),
        out_specs=(
            P(("runs", "gy"), None),
            P(("runs", "gy"), None),
            P(("runs", "gy"), None),
            P(("runs", "gy")),
        ),
        check_vma=False,
    )
```

```python
import functools

import jax
import jax.numpy as jnp
from jax import lax
from jax.experimental import pallas as pl
from jax.experimental.pallas import tpu as pltpu
from jax.sharding import PartitionSpec as P

STEPS = 4

GRAV = 9.81
TSTEP = 8.0
CELL = 90.0
FLOOR = 0.05
BANK_COEF = 200.0
CELL_AREA = 8100.0
NODE_AREA = 20000.0

LANES = 128
HALO = 4
SLOPE = GRAV * TSTEP / CELL
SPREAD = TSTEP / CELL
FEED = TSTEP * BANK_COEF / CELL_AREA
DRAIN = TSTEP * BANK_COEF / NODE_AREA
VMEM_LIMIT = 32 * 1024 * 1024

VMEM_SPEC = pl.BlockSpec(memory_space=pltpu.VMEM)
HBM_SPEC = pl.BlockSpec(memory_space=pltpu.HBM)


def swapped(value, first):
    count = lax.axis_size("gy")
    pairs = []
    for low in range(first, count - 1, 2):
        pairs += [(low, low + 1), (low + 1, low)]
    return lax.ppermute(value, "gy", pairs)


def cols(chunk):
    return slice(chunk * LANES, (chunk + 1) * LANES)


def lanes_of(rows):
    return lax.broadcasted_iota(jnp.int32, (rows, LANES), 1)


def moved_left(value, following, by):
    return jnp.where(
        lanes_of(value.shape[0]) >= LANES - by,
        pltpu.roll(following, LANES - by, 1),
        pltpu.roll(value, LANES - by, 1),
    )


def moved_up(value):
    return pltpu.roll(value, value.shape[0] - 1, 0)


def split3(value):
    high = value.astype(jnp.bfloat16)
    rest = value - high.astype(jnp.float32)
    middle = rest.astype(jnp.bfloat16)
    low = (rest - middle.astype(jnp.float32)).astype(jnp.bfloat16)
    return high, middle, low


def one_hot(count, key):
    rows = lax.broadcasted_iota(jnp.int32, (count, key.shape[1]), 0)
    return jnp.where(rows == key, 1.0, 0.0)


def drag_of(mann_a, mann_b):
    pair = mann_a + mann_b
    return (0.25 * GRAV * TSTEP) * (pair * pair)


def looked_up(klass, entries):
    value = jnp.broadcast_to(entries[0], klass.shape)
    for k in range(1, len(entries)):
        value = jnp.where(klass == k, entries[k], value)
    return value


def face(flux, surf_a, surf_b, bed_max, drag):
    flow_depth = jnp.maximum(jnp.maximum(surf_a, surf_b) - bed_max, FLOOR)
    power = jnp.exp2((-7.0 / 3.0) * jnp.log2(flow_depth))
    driven = flux - SLOPE * flow_depth * (surf_b - surf_a)
    damping = 1.0 + drag * jnp.abs(flux) * power
    return driven * pl.reciprocal(damping, approx=True)


def window_sums(blocks, reach, forward):
    height = blocks[0].shape[0]
    count = len(blocks)
    spare = -(count * height) % 16
    whole = blocks + ([jnp.zeros((spare, LANES), jnp.float32)] if spare else [])
    whole = jnp.concatenate(whole, axis=0)
    high = whole.astype(jnp.bfloat16)
    low = (whole - high.astype(jnp.float32)).astype(jnp.bfloat16)
    source = lax.broadcasted_iota(jnp.int32, (2 * LANES, 2 * LANES), 0) % LANES
    target = lax.broadcasted_iota(jnp.int32, (2 * LANES, 2 * LANES), 1)
    spill = target >= LANES
    target = target % LANES
    if forward:
        ahead = source - target + jnp.where(spill, LANES, 0)
    else:
        ahead = target - source + jnp.where(spill, LANES, 0)
    band = jnp.where((ahead >= 0) & (ahead < reach), 1.0, 0.0).astype(jnp.bfloat16)
    sums = jnp.dot(
        jnp.concatenate([high, low], axis=1), band, preferred_element_type=jnp.float32
    )
    results = []
    for block in range(count):
        result = sums[block * height : (block + 1) * height, :LANES]
        beside = block + 1 if forward else block - 1
        if 0 <= beside < count:
            result = result + sums[beside * height : (beside + 1) * height, LANES:]
        results.append(result)
    return results


def east_walled(value, chunk, chunks):
    if chunk + 1 < chunks:
        return value
    return jnp.where(lanes_of(value.shape[0]) == LANES - 1, 0.0, value)


def located(cell, position, rows, ext, columns):
    base = ((position * rows - HALO) * columns + 1).astype(jnp.float32)
    offset = cell - base
    valid = (cell > 0.0) & (offset >= 0.0) & (offset < float(ext * columns))
    offset = jnp.where(valid, offset, 0.0)
    row = jnp.floor((offset + 0.5) * (1.0 / columns))
    column = (offset - row * float(columns)).astype(jnp.int32)
    row = row.astype(jnp.int32) - HALO
    row = jnp.where(row < 0, row + ext, row)
    chunk = column // LANES
    return valid, row, chunk, column - chunk * LANES


def scattered(section, key, lane, count):
    at_lane = one_hot(LANES, lane)
    parts = [at_lane] + [at_lane * part.astype(jnp.float32) for part in split3(section)]
    grid = lax.dot_general(
        one_hot(-(-count // 16) * 16, key).astype(jnp.bfloat16),
        jnp.concatenate(parts, axis=0).astype(jnp.bfloat16),
        (((1,), (1,)), ((), ())),
        preferred_element_type=jnp.float32,
    )
    number = grid[:, :LANES]
    total = (grid[:, LANES : 2 * LANES] + grid[:, 2 * LANES : 3 * LANES]) + grid[:, 3 * LANES :]
    return number, total


def border_rows(first, last, put):
    row = lax.broadcasted_iota(jnp.int32, (HALO, LANES), 0)

    def low(fields, south):
        for slot, value in enumerate(fields):
            put(slot, jnp.where(row == HALO - 1, south[slot : slot + 1], value[:HALO]))

    def high(fields, south):
        for slot, value in enumerate(fields):
            flux = south[HALO + slot : HALO + slot + 1]
            put(slot, jnp.where(row == 0, flux, value[HALO:]))

    if first is not None:
        low(*first)
    if last is not None:
        high(*last)


def pack_kernel(
    depth, bed, rough, east, south, section, cells, table_in, to_other, own, *refs
):
    held, held_rough, held_cells, table, sems = refs
    rows, columns = depth.shape
    chunks = columns // LANES
    even = lax.axis_index("gy") % 2 == 0
    start = pl.multiple_of(jnp.where(even, 0, rows - 8), 8)
    near = pl.ds(start, 8)
    copies = [
        pltpu.make_async_copy(source, target, sems.at[slot])
        for slot, (source, target) in enumerate(
            (
                (rough.at[near, :], held_rough),
                (bed.at[near, :], held.at[1]),
                (depth.at[near, :], held.at[0]),
                (east.at[near, :], held.at[2]),
                (south.at[near, :], held.at[3]),
                (section, own.at[pl.ds(0, 1), :]),
                (cells, held_cells),
                (table_in, table),
            )
        )
    ]
    for copy in copies:
        copy.start()
    for copy in copies:
        copy.wait()
    own[1:2, :] = (held_cells[0:1, :] + 1).astype(jnp.float32)
    entries = [
        jnp.broadcast_to(table[:, k : k + 1], (1, LANES)) for k in range(table.shape[1])
    ]
    manns = [looked_up(held_rough[:, cols(chunk)], entries) for chunk in range(chunks)]
    row = lax.broadcasted_iota(jnp.int32, (8, LANES), 0)
    for chunk in range(chunks):
        at, then = cols(chunk), cols(min(chunk + 1, chunks - 1))
        m0, b0 = manns[chunk], held[1, :, at]
        s0 = held[0, :, at] + b0
        m1, b1 = manns[min(chunk + 1, chunks - 1)], held[1, :, then]
        s1 = held[0, :, then] + b1
        bed_max = jnp.maximum(b0, moved_left(b0, b1, 1))
        drag = drag_of(m0, moved_left(m0, m1, 1))
        new_east = face(held[2, :, at], s0, moved_left(s0, s1, 1), bed_max, drag)
        new_east = east_walled(new_east, chunk, chunks)
        bed_max = jnp.maximum(b0, moved_up(b0))
        drag = drag_of(m0, moved_up(m0))
        q0 = held[3, :, at]
        new_south = jnp.where(row == 7, q0, face(q0, s0, moved_up(s0), bed_max, drag))
        fields = (s0, b0, held_rough[:, at].astype(jnp.float32), new_east)
        lower, upper = {}, {}
        border_rows((fields, new_south), None, lower.__setitem__)
        border_rows(None, (fields, new_south), upper.__setitem__)
        for slot in range(4):
            to_other[slot, :, at] = jnp.where(even, lower[slot], upper[slot])
    for slot in range(1, 4):
        to_other[slot, :, columns:] = jnp.zeros((HALO, LANES), jnp.float32)
    to_other[0, 0:2, columns:] = own[...]


def join_kernel(before, section, cells, to_other):
    columns = to_other.shape[2] - LANES
    to_other[0, 2:3, columns:] = section[...]
    to_other[0, 3:4, columns:] = (cells[0:1, :] + 1).astype(jnp.float32)


def relay_kernel(by_other, prepared, near):
    del prepared
    columns = by_other.shape[2] - LANES
    near[...] = by_other[0, 0:2, columns:]


def picking(reach, rows, key, lane, takes, masks):
    for block in range(key.shape[1] // LANES):
        mine = slice(block * LANES, (block + 1) * LANES)

        def column(row):
            wide = jnp.broadcast_to(row[:, mine].astype(jnp.float32), (LANES, LANES))
            return jnp.transpose(wide).astype(jnp.int32)

        spread = lanes_of(LANES)
        at = column(key)
        after = jnp.where(at < 0, at, at + rows)
        for first in range(0, takes.shape[2], LANES):
            for half, place in enumerate((at, after)):
                hit = jnp.where(spread + first == place, 1.0, 0.0)
                takes[half, mine, first : first + LANES] = hit.astype(jnp.bfloat16)
        ahead = spread - column(lane)
        masks[0, mine, :] = jnp.where((ahead >= 0) & (ahead < reach), 1.0, 0.0)
        masks[1, mine, :] = jnp.where(ahead + LANES < reach, 1.0, 0.0)


def load_kernel(
    depth_in, east_in, south_in, bed_in, rough_in, table_in, *refs
):
    surf, east, south, bed, rough, table_rows, table, sems = refs
    rows, columns = depth_in.shape
    own = pl.ds(0, rows)
    copies = [
        pltpu.make_async_copy(source, target.at[own, :], sems.at[slot])
        for slot, (source, target) in enumerate(
            (
                (depth_in, surf),
                (bed_in, bed),
                (rough_in, rough),
                (east_in, east),
                (south_in, south),
            )
        )
    ]
    copies.append(pltpu.make_async_copy(table_in, table, sems.at[5]))
    for copy in copies:
        copy.start()
    copies[5].wait()
    for k in range(table_rows.shape[0]):
        table_rows[k : k + 1, :] = jnp.broadcast_to(table[:, k : k + 1], (1, LANES))
    for copy in copies[:5]:
        copy.wait()


def prepare_kernel(reach, table_rows, rough, own, partner_section, partner_cells, *refs):
    surf, east, south, bed = refs[4:8]
    mann, bed_e, bed_s, drag_e, drag_s, number, total, takes, masks, to_partner = refs[8:]
    ext, columns = surf.shape
    rows = ext - 2 * HALO
    chunks = columns // LANES
    tiles = lax.axis_size("gy")
    position = lax.axis_index("gy")
    side = jnp.where(position % 2 == 0, 1, -1)
    entries = [table_rows[k : k + 1, :] for k in range(table_rows.shape[0])]
    for chunk in range(chunks):
        at = cols(chunk)
        mann[:rows, at] = looked_up(rough[:, at], entries)
        surf[:rows, at] = surf[:rows, at] + bed[:rows, at]

    partner = jnp.where(position + side < tiles, partner_cells[0:1, :] + 1, 0).astype(jnp.float32)
    section = jnp.concatenate([own[0:1, :], partner_section[...]], axis=1)
    cell = jnp.concatenate([own[1:2, :], partner], axis=1)
    valid, node_row, node_chunk, node_lane = located(cell, position, rows, ext, columns)
    key = jnp.where(valid, node_chunk * ext + node_row, -1)
    starts, levels = scattered(section, key, node_lane, chunks * ext)
    for chunk in range(chunks):
        at = cols(chunk)
        number[:, at] = starts[chunk * ext : (chunk + 1) * ext]
        total[:, at] = levels[chunk * ext : (chunk + 1) * ext]

    key = jnp.where(valid & (node_row < rows), node_chunk * rows + node_row, -1)
    picking(reach, rows, key, node_lane, takes, masks)

    kept = lax.broadcasted_iota(jnp.int32, (rows, LANES), 0) == rows - 1
    for chunk in range(chunks):
        at, then = cols(chunk), cols(min(chunk + 1, chunks - 1))
        s0, b0, m0 = surf[:rows, at], bed[:rows, at], mann[:rows, at]
        bed_max = jnp.maximum(b0, moved_left(b0, bed[:rows, then], 1))
        drag = drag_of(m0, moved_left(m0, mann[:rows, then], 1))
        bed_e[:rows, at] = bed_max
        drag_e[:rows, at] = drag
        new_east = face(
            east[:rows, at], s0, moved_left(s0, surf[:rows, then], 1), bed_max, drag
        )
        east[:rows, at] = east_walled(new_east, chunk, chunks)
        bed_max = jnp.maximum(b0, moved_up(b0))
        drag = drag_of(m0, moved_up(m0))
        bed_s[:rows, at] = bed_max
        drag_s[:rows, at] = drag
        q0 = south[:rows, at]
        south[:rows, at] = jnp.where(kept, q0, face(q0, s0, moved_up(s0), bed_max, drag))

    even = position % 2 == 0
    for chunk in range(chunks):
        at = cols(chunk)

        def tile(part):
            fields = (surf[part, at], bed[part, at], rough[part, at].astype(jnp.float32))
            return (*fields, east[part, at]), south[part, at]

        lower, upper = {}, {}
        border_rows(tile(slice(0, 8)), None, lower.__setitem__)
        border_rows(None, tile(slice(rows - 8, rows)), upper.__setitem__)
        for slot in range(4):
            to_partner[slot, :, at] = jnp.where(even, upper[slot], lower[slot])


def wall_of(ext, tiles):
    position = lax.axis_index("gy")
    rows = ext - 2 * HALO
    row = lax.broadcasted_iota(jnp.int32, (16, LANES), 0) + (ext - 16)
    return ((row == ext - 1) & (position == 0)) | ((row == rows - 1) & (position == tiles - 1))


def border_kernel(reach, tiles, by_partner, by_other, table_rows, near, *refs):
    surf, east, south, bed, mann, bed_e, bed_s, drag_e, drag_s, number, total, takes, masks = refs[11:]
    ext, columns = surf.shape
    rows = ext - 2 * HALO
    chunks = columns // LANES
    position = lax.axis_index("gy")
    even = position % 2 == 0
    entries = [table_rows[k : k + 1, :] for k in range(table_rows.shape[0])]
    row = lax.broadcasted_iota(jnp.int32, (2 * HALO, LANES), 0)
    for chunk in range(chunks):
        at = cols(chunk)
        halos = []
        flux = jnp.zeros((2 * HALO, LANES), jnp.float32)
        for slot in range(4):
            a, b = by_partner[slot, :, at], by_other[slot, :, at]
            below = jnp.where(even, a, b)
            above = jnp.where(even, b, a)
            halos.append(jnp.concatenate([below, above], axis=0))
            flux = jnp.where(row == slot, below[HALO - 1 :], flux)
            flux = jnp.where(row == HALO + slot, above[:1], flux)
        surf[rows:, at] = halos[0]
        bed[rows:, at] = halos[1]
        mann[rows:, at] = looked_up(halos[2].astype(jnp.int32), entries)
        east[rows:, at] = halos[3]
        south[rows:, at] = flux

    beyond = by_other[0, 2:4, columns:]
    section = jnp.concatenate([near[0:1, :], beyond[0:1, :]], axis=1)
    cell = jnp.concatenate([near[1:2, :], beyond[1:2, :]], axis=1)
    valid, node_row, node_chunk, node_lane = located(cell, position, rows, ext, columns)
    key = jnp.where(valid, node_chunk * ext + node_row, -1)
    starts, levels = scattered(section, key, node_lane, chunks * ext)

    key = jnp.where(valid & (node_row < rows), node_chunk * rows + node_row, -1)
    owned = near.shape[1]
    picking(reach, rows, key[:, :owned], node_lane[:, :owned], takes, masks)

    wall = wall_of(ext, tiles)
    kept = lax.broadcasted_iota(jnp.int32, (16, LANES), 0) % 8 < 7
    for chunk in range(chunks):
        at, then = cols(chunk), cols(min(chunk + 1, chunks - 1))
        number[:, at] += starts[chunk * ext : (chunk + 1) * ext]
        total[:, at] += levels[chunk * ext : (chunk + 1) * ext]
        b0, m0 = bed[rows:, at], mann[rows:, at]
        bed_e[rows:, at] = jnp.maximum(b0, moved_left(b0, bed[rows:, then], 1))
        drag_e[rows:, at] = drag_of(m0, moved_left(m0, mann[rows:, then], 1))

        def rolled_up(ref):
            value = jnp.concatenate([ref[rows - 8 :, at], ref[:8, at]], axis=0)
            return value[:16], moved_up(value)[:16]

        s0, s1 = rolled_up(surf)
        b0, b1 = rolled_up(bed)
        m0, m1 = rolled_up(mann)
        bed_max = jnp.maximum(b0, b1)
        drag = drag_of(m0, m1)
        bed_s[rows - 8 :, at] = bed_max
        drag_s[rows - 8 :, at] = drag
        q0 = south[rows - 8 :, at]
        new_south = jnp.where(kept, q0, face(q0, s0, s1, bed_max, drag))
        south[rows - 8 :, at] = jnp.where(wall, 0.0, new_south)


def fluxes(mine, wall, before, faces, east_out, south_out=None):
    surf, east, south = before
    bed_e, bed_s, drag_e, drag_s = faces
    chunks = surf.shape[1] // LANES
    rolled = pltpu.roll(surf[mine, cols(0)], LANES - 1, 1)
    lane = lanes_of(rolled.shape[0])
    for chunk in range(chunks):
        at = cols(chunk)
        s0 = surf[mine, at]
        rolled_then = rolled
        if chunk + 1 < chunks:
            rolled_then = pltpu.roll(surf[mine, cols(chunk + 1)], LANES - 1, 1)
        left = jnp.where(lane >= LANES - 1, rolled_then, rolled)
        rolled = rolled_then
        new_east = face(east[mine, at], s0, left, bed_e[mine, at], drag_e[mine, at])
        east_out[mine, at] = east_walled(new_east, chunk, chunks)
        if south_out is not None:
            s0 = surf[:, at]
            new_south = face(south[:, at], s0, moved_up(s0), bed_s[:, at], drag_s[:, at])
            south_out[:, at] = jnp.concatenate(
                [new_south[:-16], jnp.where(wall, 0.0, new_south[-16:])], axis=0
            )


def settled(mine, surf, east, south, gain):
    ext, columns = surf.shape
    rolled = 0.0
    for chunk in range(columns // LANES):
        at = cols(chunk)
        new_east = east[mine, at]
        new_south = south[:, at]
        lane = lanes_of(new_east.shape[0])
        rolled_before, rolled = rolled, pltpu.roll(new_east, 1, 1)
        west = jnp.where(lane < 1, rolled_before, rolled)
        north = pltpu.roll(new_south, 1, 0)[mine]
        inflow = west + north
        s0 = surf[mine, at]
        outflow = new_east + new_south[mine]
        yield chunk, s0 + (SPREAD * (inflow - outflow) + gain(chunk, s0))


def exchange(corridor, mine, surf, total, count, covers, total_out):
    chunks = surf.shape[1] // LANES
    sums = window_sums([total[mine, cols(chunk)] for chunk in range(chunks)], corridor, False)
    if total_out is not None:
        windows = window_sums([surf[mine, cols(chunk)] for chunk in range(chunks)], corridor, True)
        for chunk in range(chunks):
            at = cols(chunk)
            kept = (1.0 - corridor * DRAIN) * total[mine, at]
            total_out[mine, at] = kept + count[mine, at] * windows[chunk]

    def gain(chunk, value):
        return sums[chunk] - covers[mine, cols(chunk)] * value

    return gain


def given(corridor, surf, before, after):
    rows = surf.shape[0] - 2 * HALO
    for chunk in range(surf.shape[1] // LANES):
        at = cols(chunk)
        value = (DRAIN * (1.0 - corridor * DRAIN)) * surf[:rows, at]
        if before is not None:
            value = (1.0 - corridor * DRAIN) * before[:, at] + value
        after[:, at] = value


def first_kernel(corridor, surf, east, south, number, total, *refs):
    surf_1, total_1, count, covers, given_1, total_0 = refs
    rows = surf.shape[0] - 2 * HALO
    chunks = surf.shape[1] // LANES
    own = slice(0, rows)
    covering = window_sums([number[own, cols(chunk)] for chunk in range(chunks)], corridor, False)
    for chunk in range(chunks):
        at = cols(chunk)
        count[own, at] = (FEED * DRAIN) * number[own, at]
        covers[own, at] = FEED * covering[chunk]
        total_0[own, at] = FEED * total[own, at]
    gain = exchange(corridor, own, surf, total_0, count, covers, total_1)
    for chunk, new_surf in settled(own, surf, east, south, gain):
        surf_1[own, cols(chunk)] = new_surf
    given(corridor, surf, None, given_1)


def second_kernel(corridor, tiles, far, surf, east, south, *refs):
    faces = refs[:4]
    number, total, given_1 = refs[4:7]
    surf_1, total_1, count, covers = refs[11:15]
    surf_2, east_2, south_2, total_2, given_2, total_0 = refs[15:]
    ext, columns = surf.shape
    rows = ext - 2 * HALO
    chunks = columns // LANES
    position = lax.axis_index("gy")
    tail = slice(rows, ext)

    valid, node_row, node_chunk, node_lane = located(far[1:2, :], position, rows, ext, columns)
    key = jnp.where(valid & (node_row >= rows), node_chunk * 8 + (node_row - rows), -1)
    starts, levels = scattered(far[0:1, :], key, node_lane, chunks * 8)
    starting = [
        number[tail, cols(chunk)] + starts[chunk * 8 : chunk * 8 + 8] for chunk in range(chunks)
    ]
    covering = window_sums(starting, corridor, False)
    for chunk in range(chunks):
        at = cols(chunk)
        count[tail, at] = (FEED * DRAIN) * starting[chunk]
        covers[tail, at] = FEED * covering[chunk]
        total_0[tail, at] = FEED * (total[tail, at] + levels[chunk * 8 : chunk * 8 + 8])
    gain = exchange(corridor, tail, surf, total_0, count, covers, total_1)
    for chunk, new_surf in settled(tail, surf, east, south, gain):
        surf_1[tail, cols(chunk)] = new_surf

    every = slice(0, ext)
    gain = exchange(corridor, every, surf_1, total_1, count, covers, total_2)
    fluxes(every, wall_of(ext, tiles), (surf_1, east, south), faces, east_2, south_2)
    for chunk, new_surf in settled(every, surf_1, east_2, south_2, gain):
        surf_2[:, cols(chunk)] = new_surf
    given(corridor, surf_1, given_1, given_2)


def third_kernel(corridor, tiles, surf, east, south, *refs):
    faces = refs[:4]
    total, covers, count, given_2, surf_3, east_3, south_3, total_3, given_3 = refs[4:]
    ext = surf.shape[0]
    own = slice(0, ext - 2 * HALO)
    gain = exchange(corridor, own, surf, total, count, covers, total_3)
    fluxes(own, wall_of(ext, tiles), (surf, east, south), faces, east_3, south_3)
    for chunk, new_surf in settled(own, surf, east_3, south_3, gain):
        surf_3[own, cols(chunk)] = new_surf
    given(corridor, surf, given_2, given_3)


def terms_kernel(corridor, own, surf, given_3, *refs):
    takes, masks, takes_near, masks_near, own_term, partner_term, other_term = refs
    rows, columns = given_3.shape
    owned = own.shape[1]
    chunks = columns // LANES
    levels = [
        given_3[:, cols(chunk)] + DRAIN * surf[:rows, cols(chunk)] for chunk in range(chunks)
    ]
    spare = takes.shape[2] - chunks * rows
    if spare:
        levels.append(jnp.zeros((spare, LANES), jnp.float32))
    levels = jnp.concatenate(levels, axis=0)
    high = levels.astype(jnp.bfloat16)
    low = (levels - high.astype(jnp.float32)).astype(jnp.bfloat16)
    picked = jnp.dot(
        jnp.concatenate([takes[0], takes_near[0], takes[1], takes_near[1]], axis=0),
        jnp.concatenate([high, low], axis=1),
        preferred_element_type=jnp.float32,
    )
    hit = jnp.concatenate([masks[0], masks_near[0], masks[1], masks_near[1]], axis=0)
    picked = (picked * jnp.concatenate([hit, hit], axis=1)).astype(jnp.bfloat16)
    picked = jnp.concatenate([picked[: 3 * owned], picked[3 * owned :]], axis=1)
    terms = lax.dot_general(
        jnp.ones((8, 4 * LANES), jnp.bfloat16),
        picked,
        (((1,), (1,)), ((), ())),
        preferred_element_type=jnp.float32,
    )[0:1]
    own_term[...] = (1.0 - corridor * DRAIN) ** STEPS * own[0:1, :] + terms[:, :owned]
    partner_term[...] = terms[:, owned : 2 * owned]
    other_term[...] = terms[:, 2 * owned :]


def last_kernel(corridor, tiles, surf_2, east_2, south_3, *refs):
    faces = refs[:4]
    total_2, total_3, covers, bed, _, east_3 = refs[4:10]
    surf_3, depth_out, east_out, south_out, depth_4, east_4, south_4, east_tail, sems = refs[10:]
    ext, columns = surf_2.shape
    rows = ext - 2 * HALO
    own, tail = slice(0, rows), slice(rows, ext)
    gain = exchange(corridor, tail, surf_2, total_2, None, covers, None)
    fluxes(tail, None, (surf_2, east_2, None), faces, east_tail)
    for chunk, new_surf in settled(tail, surf_2, east_tail, south_3, gain):
        surf_3[tail, cols(chunk)] = new_surf
    copies = [
        pltpu.make_async_copy(source.at[pl.ds(0, rows), :], target, sems.at[slot])
        for slot, (source, target) in enumerate(
            ((east_4, east_out), (south_4, south_out), (depth_4, depth_out))
        )
    ]
    fluxes(own, wall_of(ext, tiles), (surf_3, east_3, south_3), faces, east_4, south_4)
    copies[0].start()
    copies[1].start()
    gain = exchange(corridor, own, surf_3, total_3, None, covers, None)
    for chunk, new_surf in settled(own, surf_3, east_4, south_4, gain):
        at = cols(chunk)
        depth_4[:, at] = new_surf - bed[own, at]
    copies[2].start()
    for copy in copies:
        copy.wait()


def local(
    depth, flux_east, flux_south, river_section, bed_level, rough_class, manning_table, bank_cell
):
    rows, columns = depth.shape
    owned = river_section.shape[0]
    corridor = bank_cell.shape[0]
    tiles = lax.axis_size("gy")
    ext = rows + 2 * HALO
    chunks = columns // LANES
    partner_section = swapped(river_section, 0).reshape(1, owned)
    partner_cells = swapped(bank_cell, 0)

    def held(value):
        return pltpu.with_memory_space_constraint(value, pltpu.VMEM)

    def far(value):
        return pltpu.with_memory_space_constraint(value, pltpu.HBM)

    params = pltpu.CompilerParams(vmem_limit_bytes=VMEM_LIMIT)
    halo = pltpu.VMEM((4, HALO, columns), jnp.float32)
    wide = pltpu.VMEM((4, HALO, columns + LANES), jnp.float32)
    field = pltpu.VMEM((ext, columns), jnp.float32)
    small = pltpu.VMEM((rows, columns), jnp.float32)
    term = pltpu.VMEM((1, owned), jnp.float32)
    pair = pltpu.VMEM((2, owned), jnp.float32)
    result = pltpu.HBM((rows, columns), jnp.float32)
    cells = -(-chunks * rows // LANES) * LANES

    def call(kernel, name, outs, values, scratch=(), aliases=None):
        return pl.pallas_call(
            kernel,
            out_shape=outs,
            in_specs=[VMEM_SPEC] * len(values),
            out_specs=[HBM_SPEC if out is result else VMEM_SPEC for out in outs],
            scratch_shapes=scratch,
            input_output_aliases=aliases or {},
            compiler_params=params,
            name=name,
        )(*[held(value) for value in values])

    def picks(nodes):
        return [
            pltpu.VMEM((2, nodes, cells), jnp.bfloat16),
            pltpu.VMEM((2, nodes, LANES), jnp.float32),
        ]

    classes = manning_table.shape[0]
    table = far(manning_table.reshape(1, classes))
    table_held = pltpu.VMEM((1, classes), jnp.float32)
    to_other, own = pl.pallas_call(
        pack_kernel,
        out_shape=[wide, pair],
        in_specs=[HBM_SPEC] * 8,
        out_specs=[VMEM_SPEC] * 2,
        scratch_shapes=[
            pltpu.VMEM((4, 8, columns), jnp.float32),
            pltpu.VMEM((8, columns), jnp.int32),
            pltpu.VMEM((corridor, owned), jnp.int32),
            table_held,
            pltpu.SemaphoreType.DMA((8,)),
        ],
        compiler_params=params,
        name="pack",
    )(
        *[far(value) for value in (depth, bed_level, rough_class, flux_east, flux_south)],
        far(river_section.reshape(1, owned)),
        far(bank_cell),
        table,
    )
    (to_other,) = call(
        join_kernel,
        "join",
        [wide],
        (to_other, partner_section, partner_cells),
        aliases={0: 0},
    )
    by_other = swapped(to_other, 1)
    *loaded, rough, table_rows = pl.pallas_call(
        load_kernel,
        out_shape=[field] * 4
        + [pltpu.VMEM((rows, columns), jnp.int32), pltpu.VMEM((classes, LANES), jnp.float32)],
        in_specs=[HBM_SPEC] * 6,
        out_specs=[VMEM_SPEC] * 6,
        scratch_shapes=[table_held, pltpu.SemaphoreType.DMA((6,))],
        compiler_params=params,
        name="load",
    )(
        *[far(value) for value in (depth, flux_east, flux_south, bed_level, rough_class)],
        table,
    )
    *fields, takes, masks, to_partner = call(
        functools.partial(prepare_kernel, corridor),
        "prepare",
        [field] * 11 + picks(2 * owned) + [halo],
        (table_rows, rough, own, partner_section, partner_cells, *loaded),
        aliases={5 + slot: slot for slot in range(4)},
    )
    by_partner = swapped(to_partner, 0)
    (near,) = call(relay_kernel, "relay", [pair], (by_other, masks))
    from_far = swapped(near, 0)
    *fields, takes_near, masks_near = call(
        functools.partial(border_kernel, corridor, tiles),
        "border",
        [field] * 11 + picks(owned),
        (by_partner, by_other, table_rows, near, *fields),
        aliases={4 + slot: slot for slot in range(11)},
    )
    surf, east, south, bed, _, *faces, number, total = fields
    surf_1, total_1, count, covers, given_1 = call(
        functools.partial(first_kernel, corridor),
        "first",
        [field] * 4 + [small],
        (surf, east, south, number, total),
        scratch=[field],
    )
    surf_1, total_1, count, covers, surf_2, east_2, south_2, total_2, given_2 = call(
        functools.partial(second_kernel, corridor, tiles),
        "second",
        [field] * 8 + [small],
        (
            *(from_far, surf, east, south, *faces, number, total, given_1),
            *(surf_1, total_1, count, covers),
        ),
        scratch=[field],
        aliases={11 + slot: slot for slot in range(4)},
    )
    surf_3, east_3, south_3, total_3, given_3 = call(
        functools.partial(third_kernel, corridor, tiles),
        "third",
        [field] * 4 + [small],
        (surf_2, east_2, south_2, *faces, total_2, covers, count, given_2),
    )
    own_term, partner_term, other_term = call(
        functools.partial(terms_kernel, corridor),
        "terms",
        [term] * 3,
        (own, surf_3, given_3, takes, masks, takes_near, masks_near),
    )
    from_other = swapped(other_term.reshape(owned), 1)
    from_partner = swapped(partner_term.reshape(owned), 0)
    _, depth, flux_east, flux_south = call(
        functools.partial(last_kernel, corridor, tiles),
        "last",
        [field, result, result, result],
        (surf_2, east_2, south_3, *faces, total_2, total_3, covers, bed, surf_3, east_3),
        scratch=[small, small, field, field, pltpu.SemaphoreType.DMA((3,))],
        aliases={11: 0},
    )
    river_section = own_term.reshape(owned) + from_other + from_partner
    return (depth, flux_east, flux_south, river_section)


def solution(mesh):
    return jax.shard_map(
        local,
        mesh=mesh,
        in_specs=(
            P(("runs", "gy"), None),
            P(("runs", "gy"), None),
            P(("runs", "gy"), None),
            P(("runs", "gy")),
            P("gy", None),
            P("gy", None),
            P(),
            P(None, "gy"),
        ),
        out_specs=(
            P(("runs", "gy"), None),
            P(("runs", "gy"), None),
            P(("runs", "gy"), None),
            P(("runs", "gy")),
        ),
        check_vma=False,
    )
```

```python
import functools

import jax
import jax.numpy as jnp
from jax import lax
from jax.experimental import pallas as pl
from jax.experimental.pallas import tpu as pltpu
from jax.sharding import PartitionSpec as P

STEPS = 4

GRAV = 9.81
TSTEP = 8.0
CELL = 90.0
FLOOR = 0.05
BANK_COEF = 200.0
CELL_AREA = 8100.0
NODE_AREA = 20000.0

LANES = 128
HALO = 4
SLOPE = GRAV * TSTEP / CELL
SPREAD = TSTEP / CELL
FEED = TSTEP * BANK_COEF / CELL_AREA
DRAIN = TSTEP * BANK_COEF / NODE_AREA
VMEM_LIMIT = 32 * 1024 * 1024

VMEM_SPEC = pl.BlockSpec(memory_space=pltpu.VMEM)
HBM_SPEC = pl.BlockSpec(memory_space=pltpu.HBM)


def swapped(value, first):
    count = lax.axis_size("gy")
    pairs = []
    for low in range(first, count - 1, 2):
        pairs += [(low, low + 1), (low + 1, low)]
    return lax.ppermute(value, "gy", pairs)


def cols(chunk):
    return slice(chunk * LANES, (chunk + 1) * LANES)


def lanes_of(rows):
    return lax.broadcasted_iota(jnp.int32, (rows, LANES), 1)


def moved_left(value, following, by):
    return jnp.where(
        lanes_of(value.shape[0]) >= LANES - by,
        pltpu.roll(following, LANES - by, 1),
        pltpu.roll(value, LANES - by, 1),
    )


def moved_up(value):
    return pltpu.roll(value, value.shape[0] - 1, 0)


def split3(value):
    high = value.astype(jnp.bfloat16)
    rest = value - high.astype(jnp.float32)
    middle = rest.astype(jnp.bfloat16)
    low = (rest - middle.astype(jnp.float32)).astype(jnp.bfloat16)
    return high, middle, low


def one_hot(count, key):
    rows = lax.broadcasted_iota(jnp.int32, (count, key.shape[1]), 0)
    return jnp.where(rows == key, 1.0, 0.0)


def drag_of(mann_a, mann_b):
    pair = mann_a + mann_b
    return (0.25 * GRAV * TSTEP) * (pair * pair)


def looked_up(klass, entries):
    value = jnp.broadcast_to(entries[0], klass.shape)
    for k in range(1, len(entries)):
        value = jnp.where(klass == k, entries[k], value)
    return value


def face(flux, surf_a, surf_b, bed_max, drag):
    flow_depth = jnp.maximum(jnp.maximum(surf_a, surf_b) - bed_max, FLOOR)
    power = jnp.exp2((-7.0 / 3.0) * jnp.log2(flow_depth))
    driven = flux - SLOPE * flow_depth * (surf_b - surf_a)
    damping = 1.0 + drag * jnp.abs(flux) * power
    return driven * pl.reciprocal(damping, approx=True)


def window_sums(blocks, reach, forward):
    height = blocks[0].shape[0]
    count = len(blocks)
    spare = -(count * height) % 16
    whole = blocks + ([jnp.zeros((spare, LANES), jnp.float32)] if spare else [])
    whole = jnp.concatenate(whole, axis=0)
    high = whole.astype(jnp.bfloat16)
    low = (whole - high.astype(jnp.float32)).astype(jnp.bfloat16)
    source = lax.broadcasted_iota(jnp.int32, (2 * LANES, 2 * LANES), 0) % LANES
    target = lax.broadcasted_iota(jnp.int32, (2 * LANES, 2 * LANES), 1)
    spill = target >= LANES
    target = target % LANES
    if forward:
        ahead = source - target + jnp.where(spill, LANES, 0)
    else:
        ahead = target - source + jnp.where(spill, LANES, 0)
    band = jnp.where((ahead >= 0) & (ahead < reach), 1.0, 0.0).astype(jnp.bfloat16)
    sums = jnp.dot(
        jnp.concatenate([high, low], axis=1), band, preferred_element_type=jnp.float32
    )
    results = []
    for block in range(count):
        result = sums[block * height : (block + 1) * height, :LANES]
        beside = block + 1 if forward else block - 1
        if 0 <= beside < count:
            result = result + sums[beside * height : (beside + 1) * height, LANES:]
        results.append(result)
    return results


def east_walled(value, chunk, chunks):
    if chunk + 1 < chunks:
        return value
    return jnp.where(lanes_of(value.shape[0]) == LANES - 1, 0.0, value)


def located(cell, position, rows, ext, columns):
    base = ((position * rows - HALO) * columns + 1).astype(jnp.float32)
    offset = cell - base
    valid = (cell > 0.0) & (offset >= 0.0) & (offset < float(ext * columns))
    offset = jnp.where(valid, offset, 0.0)
    row = jnp.floor((offset + 0.5) * (1.0 / columns))
    column = (offset - row * float(columns)).astype(jnp.int32)
    row = row.astype(jnp.int32) - HALO
    row = jnp.where(row < 0, row + ext, row)
    chunk = column // LANES
    return valid, row, chunk, column - chunk * LANES


def scattered(section, key, lane, count):
    at_lane = one_hot(LANES, lane)
    parts = [at_lane] + [at_lane * part.astype(jnp.float32) for part in split3(section)]
    grid = lax.dot_general(
        one_hot(-(-count // 16) * 16, key).astype(jnp.bfloat16),
        jnp.concatenate(parts, axis=0).astype(jnp.bfloat16),
        (((1,), (1,)), ((), ())),
        preferred_element_type=jnp.float32,
    )
    number = grid[:, :LANES]
    total = (grid[:, LANES : 2 * LANES] + grid[:, 2 * LANES : 3 * LANES]) + grid[:, 3 * LANES :]
    return number, total


def border_rows(of_first, fields, south):
    outer = lax.broadcasted_iota(jnp.int32, (HALO, LANES), 0) == jnp.where(of_first, HALO - 1, 0)
    flux = jnp.where(of_first, south[:HALO], south[HALO:])
    return [
        jnp.where(outer, flux[slot : slot + 1], jnp.where(of_first, value[:HALO], value[HALO:]))
        for slot, value in enumerate(fields)
    ]


def pack_kernel(
    depth, bed, rough, east, south, section, cells, table_in, to_other, own, *refs
):
    held, held_rough, held_cells, table, sems = refs
    rows, columns = depth.shape
    chunks = columns // LANES
    even = lax.axis_index("gy") % 2 == 0
    start = pl.multiple_of(jnp.where(even, 0, rows - 8), 8)
    near = pl.ds(start, 8)
    copies = [
        pltpu.make_async_copy(source, target, sems.at[slot])
        for slot, (source, target) in enumerate(
            (
                (rough.at[near, :], held_rough),
                (bed.at[near, :], held.at[1]),
                (depth.at[near, :], held.at[0]),
                (east.at[near, :], held.at[2]),
                (south.at[near, :], held.at[3]),
                (section, own.at[pl.ds(0, 1), :]),
                (cells, held_cells),
                (table_in, table),
            )
        )
    ]
    for copy in copies:
        copy.start()
    for copy in copies:
        copy.wait()
    own[1:2, :] = (held_cells[0:1, :] + 1).astype(jnp.float32)
    entries = [
        jnp.broadcast_to(table[:, k : k + 1], (1, LANES)) for k in range(table.shape[1])
    ]
    manns = [looked_up(held_rough[:, cols(chunk)], entries) for chunk in range(chunks)]
    row = lax.broadcasted_iota(jnp.int32, (8, LANES), 0)
    beds = [held[1, :, cols(chunk)] for chunk in range(chunks)]
    surfs = [held[0, :, cols(chunk)] + beds[chunk] for chunk in range(chunks)]

    def moved(values):
        rolled = [pltpu.roll(value, LANES - 1, 1) for value in values]
        rolled.append(rolled[-1])
        edge = lanes_of(8) == LANES - 1
        return [jnp.where(edge, rolled[c + 1], rolled[c]) for c in range(chunks)]

    beds_left, surfs_left, manns_left = moved(beds), moved(surfs), moved(manns)
    for chunk in range(chunks):
        at = cols(chunk)
        m0, b0, s0 = manns[chunk], beds[chunk], surfs[chunk]
        bed_max = jnp.maximum(b0, beds_left[chunk])
        drag = drag_of(m0, manns_left[chunk])
        new_east = face(held[2, :, at], s0, surfs_left[chunk], bed_max, drag)
        new_east = east_walled(new_east, chunk, chunks)
        bed_max = jnp.maximum(b0, moved_up(b0))
        drag = drag_of(m0, moved_up(m0))
        q0 = held[3, :, at]
        new_south = jnp.where(row == 7, q0, face(q0, s0, moved_up(s0), bed_max, drag))
        fields = (s0, b0, held_rough[:, at].astype(jnp.float32), new_east)
        for slot, block in enumerate(border_rows(even, fields, new_south)):
            to_other[slot * chunks + chunk] = block
    to_other[4 * chunks, 0:2, :] = own[...]


def join_kernel(before, section, cells, to_other):
    nodes = to_other.shape[0] - 1
    to_other[nodes, 2:3, :] = section[...]
    to_other[nodes, 3:4, :] = (cells[0:1, :] + 1).astype(jnp.float32)


def relay_kernel(by_other, prepared, near):
    del prepared
    near[...] = by_other[by_other.shape[0] - 1, 0:2, :]


def picking(reach, rows, key, lane, takes, masks):
    for block in range(key.shape[1] // LANES):
        mine = slice(block * LANES, (block + 1) * LANES)

        def column(row):
            wide = jnp.broadcast_to(row[:, mine].astype(jnp.float32), (LANES, LANES))
            return jnp.transpose(wide).astype(jnp.int32)

        spread = lanes_of(LANES)
        at = column(key)
        after = jnp.where(at < 0, at, at + rows)
        for first in range(0, takes.shape[2], LANES):
            for half, place in enumerate((at, after)):
                hit = jnp.where(spread + first == place, 1.0, 0.0)
                takes[half, mine, first : first + LANES] = hit.astype(jnp.bfloat16)
        ahead = spread - column(lane)
        masks[0, mine, :] = jnp.where((ahead >= 0) & (ahead < reach), 1.0, 0.0)
        masks[1, mine, :] = jnp.where(ahead + LANES < reach, 1.0, 0.0)


def load_kernel(
    depth_in, east_in, south_in, bed_in, rough_in, table_in, *refs
):
    surf, east, south, bed, rough, table_rows, table, sems = refs
    rows, columns = depth_in.shape
    own = pl.ds(0, rows)
    copies = [
        pltpu.make_async_copy(source, target.at[own, :], sems.at[slot])
        for slot, (source, target) in enumerate(
            (
                (depth_in, surf),
                (bed_in, bed),
                (rough_in, rough),
                (east_in, east),
                (south_in, south),
            )
        )
    ]
    copies.append(pltpu.make_async_copy(table_in, table, sems.at[5]))
    for copy in copies:
        copy.start()
    copies[5].wait()
    for k in range(table_rows.shape[0]):
        table_rows[k : k + 1, :] = jnp.broadcast_to(table[:, k : k + 1], (1, LANES))
    for copy in copies[:5]:
        copy.wait()


def prepare_kernel(table_rows, rough, *refs):
    surf, east, south, bed = refs[4:8]
    mann, bed_e, bed_s, drag_e, drag_s, to_partner = refs[8:]
    ext, columns = surf.shape
    rows = ext - 2 * HALO
    chunks = columns // LANES
    even = lax.axis_index("gy") % 2 == 0
    entries = [table_rows[k : k + 1, :] for k in range(table_rows.shape[0])]
    for chunk in range(chunks):
        at = cols(chunk)
        mann[:rows, at] = looked_up(rough[:, at], entries)
        surf[:rows, at] = surf[:rows, at] + bed[:rows, at]

    kept = lax.broadcasted_iota(jnp.int32, (rows, LANES), 0) == rows - 1
    for chunk in range(chunks):
        at, then = cols(chunk), cols(min(chunk + 1, chunks - 1))
        s0, b0, m0 = surf[:rows, at], bed[:rows, at], mann[:rows, at]
        bed_max = jnp.maximum(b0, moved_left(b0, bed[:rows, then], 1))
        drag = drag_of(m0, moved_left(m0, mann[:rows, then], 1))
        bed_e[:rows, at] = bed_max
        drag_e[:rows, at] = drag
        new_east = face(
            east[:rows, at], s0, moved_left(s0, surf[:rows, then], 1), bed_max, drag
        )
        new_east = east_walled(new_east, chunk, chunks)
        east[:rows, at] = new_east
        bed_max = jnp.maximum(b0, moved_up(b0))
        drag = drag_of(m0, moved_up(m0))
        bed_s[:rows, at] = bed_max
        drag_s[:rows, at] = drag
        q0 = south[:rows, at]
        new_south = jnp.where(kept, q0, face(q0, s0, moved_up(s0), bed_max, drag))
        south[:rows, at] = new_south

        def ends(value):
            return jnp.where(even, value[rows - 8 :], value[:8])

        fields = (ends(s0), ends(b0), ends(rough[:, at].astype(jnp.float32)), ends(new_east))
        blocks = border_rows(jnp.logical_not(even), fields, ends(new_south))
        for slot, block in enumerate(blocks):
            to_partner[slot * chunks + chunk] = block


def nodes_kernel(reach, rows, own, partner_section, partner_cells, number, total, takes, masks):
    ext, columns = number.shape
    chunks = columns // LANES
    tiles = lax.axis_size("gy")
    position = lax.axis_index("gy")
    side = jnp.where(position % 2 == 0, 1, -1)
    partner = jnp.where(position + side < tiles, partner_cells[0:1, :] + 1, 0).astype(jnp.float32)
    section = jnp.concatenate([own[0:1, :], partner_section[...]], axis=1)
    cell = jnp.concatenate([own[1:2, :], partner], axis=1)
    valid, node_row, node_chunk, node_lane = located(cell, position, rows, ext, columns)
    key = jnp.where(valid, node_chunk * ext + node_row, -1)
    starts, levels = scattered(section, key, node_lane, chunks * ext)
    for chunk in range(chunks):
        at = cols(chunk)
        number[:, at] = starts[chunk * ext : (chunk + 1) * ext]
        total[:, at] = levels[chunk * ext : (chunk + 1) * ext]
    key = jnp.where(valid & (node_row < rows), node_chunk * rows + node_row, -1)
    picking(reach, rows, key, node_lane, takes, masks)


def wall_of(ext, tiles):
    position = lax.axis_index("gy")
    rows = ext - 2 * HALO
    row = lax.broadcasted_iota(jnp.int32, (16, LANES), 0) + (ext - 16)
    return ((row == ext - 1) & (position == 0)) | ((row == rows - 1) & (position == tiles - 1))


def border_kernel(reach, tiles, by_partner, by_other, table_rows, near, *refs):
    surf, east, south, bed, mann, bed_e, bed_s, drag_e, drag_s, number, total, takes, masks = refs[11:]
    ext, columns = surf.shape
    rows = ext - 2 * HALO
    chunks = columns // LANES
    position = lax.axis_index("gy")
    even = position % 2 == 0
    entries = [table_rows[k : k + 1, :] for k in range(table_rows.shape[0])]
    row = lax.broadcasted_iota(jnp.int32, (2 * HALO, LANES), 0)
    for chunk in range(chunks):
        at = cols(chunk)
        halos = []
        flux = jnp.zeros((2 * HALO, LANES), jnp.float32)
        for slot in range(4):
            a, b = by_partner[slot * chunks + chunk], by_other[slot * chunks + chunk]
            below = jnp.where(even, a, b)
            above = jnp.where(even, b, a)
            halos.append(jnp.concatenate([below, above], axis=0))
            flux = jnp.where(row == slot, below[HALO - 1 :], flux)
            flux = jnp.where(row == HALO + slot, above[:1], flux)
        surf[rows:, at] = halos[0]
        bed[rows:, at] = halos[1]
        mann[rows:, at] = looked_up(halos[2].astype(jnp.int32), entries)
        east[rows:, at] = halos[3]
        south[rows:, at] = flux

    beyond = by_other[4 * chunks, 2:4, :]
    section = jnp.concatenate([near[0:1, :], beyond[0:1, :]], axis=1)
    cell = jnp.concatenate([near[1:2, :], beyond[1:2, :]], axis=1)
    valid, node_row, node_chunk, node_lane = located(cell, position, rows, ext, columns)
    key = jnp.where(valid, node_chunk * ext + node_row, -1)
    starts, levels = scattered(section, key, node_lane, chunks * ext)

    key = jnp.where(valid & (node_row < rows), node_chunk * rows + node_row, -1)
    owned = near.shape[1]
    picking(reach, rows, key[:, :owned], node_lane[:, :owned], takes, masks)

    wall = wall_of(ext, tiles)
    kept = lax.broadcasted_iota(jnp.int32, (16, LANES), 0) % 8 < 7
    for chunk in range(chunks):
        at, then = cols(chunk), cols(min(chunk + 1, chunks - 1))
        number[:, at] += starts[chunk * ext : (chunk + 1) * ext]
        total[:, at] += levels[chunk * ext : (chunk + 1) * ext]
        b0, m0 = bed[rows:, at], mann[rows:, at]
        bed_e[rows:, at] = jnp.maximum(b0, moved_left(b0, bed[rows:, then], 1))
        drag_e[rows:, at] = drag_of(m0, moved_left(m0, mann[rows:, then], 1))

        def rolled_up(ref):
            value = jnp.concatenate([ref[rows - 8 :, at], ref[:8, at]], axis=0)
            return value[:16], moved_up(value)[:16]

        s0, s1 = rolled_up(surf)
        b0, b1 = rolled_up(bed)
        m0, m1 = rolled_up(mann)
        bed_max = jnp.maximum(b0, b1)
        drag = drag_of(m0, m1)
        bed_s[rows - 8 :, at] = bed_max
        drag_s[rows - 8 :, at] = drag
        q0 = south[rows - 8 :, at]
        new_south = jnp.where(kept, q0, face(q0, s0, s1, bed_max, drag))
        south[rows - 8 :, at] = jnp.where(wall, 0.0, new_south)


def fluxes(mine, wall, before, faces, east_out, south_out=None):
    surf, east, south = before
    bed_e, bed_s, drag_e, drag_s = faces
    chunks = surf.shape[1] // LANES
    rolled = pltpu.roll(surf[mine, cols(0)], LANES - 1, 1)
    lane = lanes_of(rolled.shape[0])
    for chunk in range(chunks):
        at = cols(chunk)
        s0 = surf[mine, at]
        rolled_then = rolled
        if chunk + 1 < chunks:
            rolled_then = pltpu.roll(surf[mine, cols(chunk + 1)], LANES - 1, 1)
        left = jnp.where(lane >= LANES - 1, rolled_then, rolled)
        rolled = rolled_then
        new_east = face(east[mine, at], s0, left, bed_e[mine, at], drag_e[mine, at])
        east_out[mine, at] = east_walled(new_east, chunk, chunks)
        if south_out is not None:
            s0 = surf[:, at]
            new_south = face(south[:, at], s0, moved_up(s0), bed_s[:, at], drag_s[:, at])
            south_out[:, at] = jnp.concatenate(
                [new_south[:-16], jnp.where(wall, 0.0, new_south[-16:])], axis=0
            )


def settled(mine, surf, east, south, gain):
    ext, columns = surf.shape
    rolled = 0.0
    for chunk in range(columns // LANES):
        at = cols(chunk)
        new_east = east[mine, at]
        new_south = south[:, at]
        lane = lanes_of(new_east.shape[0])
        rolled_before, rolled = rolled, pltpu.roll(new_east, 1, 1)
        west = jnp.where(lane < 1, rolled_before, rolled)
        north = pltpu.roll(new_south, 1, 0)[mine]
        inflow = west + north
        s0 = surf[mine, at]
        outflow = new_east + new_south[mine]
        yield chunk, s0 + (SPREAD * (inflow - outflow) + gain(chunk, s0))


def exchange(corridor, mine, surf, total, count, covers, total_out):
    chunks = surf.shape[1] // LANES
    sums = window_sums([total[mine, cols(chunk)] for chunk in range(chunks)], corridor, False)
    if total_out is not None:
        windows = window_sums([surf[mine, cols(chunk)] for chunk in range(chunks)], corridor, True)
        for chunk in range(chunks):
            at = cols(chunk)
            kept = (1.0 - corridor * DRAIN) * total[mine, at]
            total_out[mine, at] = kept + count[mine, at] * windows[chunk]

    def gain(chunk, value):
        return sums[chunk] - covers[mine, cols(chunk)] * value

    return gain


def given(corridor, surf, before, after):
    rows = surf.shape[0] - 2 * HALO
    for chunk in range(surf.shape[1] // LANES):
        at = cols(chunk)
        value = (DRAIN * (1.0 - corridor * DRAIN)) * surf[:rows, at]
        if before is not None:
            value = (1.0 - corridor * DRAIN) * before[:, at] + value
        after[:, at] = value


def first_kernel(corridor, surf, east, south, number, total, *refs):
    surf_1, total_1, count, covers, given_1, total_0 = refs
    rows = surf.shape[0] - 2 * HALO
    chunks = surf.shape[1] // LANES
    own = slice(0, rows)
    covering = window_sums([number[own, cols(chunk)] for chunk in range(chunks)], corridor, False)
    for chunk in range(chunks):
        at = cols(chunk)
        count[own, at] = (FEED * DRAIN) * number[own, at]
        covers[own, at] = FEED * covering[chunk]
        total_0[own, at] = FEED * total[own, at]
    gain = exchange(corridor, own, surf, total_0, count, covers, total_1)
    for chunk, new_surf in settled(own, surf, east, south, gain):
        surf_1[own, cols(chunk)] = new_surf
    given(corridor, surf, None, given_1)


def second_kernel(corridor, tiles, far, surf, east, south, *refs):
    faces = refs[:4]
    number, total, given_1 = refs[4:7]
    surf_1, total_1, count, covers = refs[11:15]
    surf_2, east_2, south_2, total_2, given_2, total_0 = refs[15:]
    ext, columns = surf.shape
    rows = ext - 2 * HALO
    chunks = columns // LANES
    position = lax.axis_index("gy")
    tail = slice(rows, ext)

    valid, node_row, node_chunk, node_lane = located(far[1:2, :], position, rows, ext, columns)
    key = jnp.where(valid & (node_row >= rows), node_chunk * 8 + (node_row - rows), -1)
    starts, levels = scattered(far[0:1, :], key, node_lane, chunks * 8)
    starting = [
        number[tail, cols(chunk)] + starts[chunk * 8 : chunk * 8 + 8] for chunk in range(chunks)
    ]
    covering = window_sums(starting, corridor, False)
    for chunk in range(chunks):
        at = cols(chunk)
        count[tail, at] = (FEED * DRAIN) * starting[chunk]
        covers[tail, at] = FEED * covering[chunk]
        total_0[tail, at] = FEED * (total[tail, at] + levels[chunk * 8 : chunk * 8 + 8])
    gain = exchange(corridor, tail, surf, total_0, count, covers, total_1)
    for chunk, new_surf in settled(tail, surf, east, south, gain):
        surf_1[tail, cols(chunk)] = new_surf

    every = slice(0, ext)
    gain = exchange(corridor, every, surf_1, total_1, count, covers, total_2)
    fluxes(every, wall_of(ext, tiles), (surf_1, east, south), faces, east_2, south_2)
    for chunk, new_surf in settled(every, surf_1, east_2, south_2, gain):
        surf_2[:, cols(chunk)] = new_surf
    given(corridor, surf_1, given_1, given_2)


def third_kernel(corridor, tiles, surf, east, south, *refs):
    faces = refs[:4]
    total, covers, count, given_2, surf_3, east_3, south_3, total_3, given_3 = refs[4:]
    ext = surf.shape[0]
    own = slice(0, ext - 2 * HALO)
    gain = exchange(corridor, own, surf, total, count, covers, total_3)
    fluxes(own, wall_of(ext, tiles), (surf, east, south), faces, east_3, south_3)
    for chunk, new_surf in settled(own, surf, east_3, south_3, gain):
        surf_3[own, cols(chunk)] = new_surf
    given(corridor, surf, given_2, given_3)


def terms_kernel(corridor, own, surf, given_3, *refs):
    takes, masks, takes_near, masks_near, own_term, partner_term, other_term = refs
    rows, columns = given_3.shape
    owned = own.shape[1]
    chunks = columns // LANES
    levels = [
        given_3[:, cols(chunk)] + DRAIN * surf[:rows, cols(chunk)] for chunk in range(chunks)
    ]
    spare = takes.shape[2] - chunks * rows
    if spare:
        levels.append(jnp.zeros((spare, LANES), jnp.float32))
    levels = jnp.concatenate(levels, axis=0)
    high = levels.astype(jnp.bfloat16)
    low = (levels - high.astype(jnp.float32)).astype(jnp.bfloat16)
    picked = jnp.dot(
        jnp.concatenate([takes[0], takes_near[0], takes[1], takes_near[1]], axis=0),
        jnp.concatenate([high, low], axis=1),
        preferred_element_type=jnp.float32,
    )
    hit = jnp.concatenate([masks[0], masks_near[0], masks[1], masks_near[1]], axis=0)
    picked = (picked * jnp.concatenate([hit, hit], axis=1)).astype(jnp.bfloat16)
    picked = jnp.concatenate([picked[: 3 * owned], picked[3 * owned :]], axis=1)
    terms = lax.dot_general(
        jnp.ones((8, 4 * LANES), jnp.bfloat16),
        picked,
        (((1,), (1,)), ((), ())),
        preferred_element_type=jnp.float32,
    )[0:1]
    own_term[...] = (1.0 - corridor * DRAIN) ** STEPS * own[0:1, :] + terms[:, :owned]
    partner_term[...] = terms[:, owned : 2 * owned]
    other_term[...] = terms[:, 2 * owned :]


def last_kernel(corridor, tiles, surf_2, east_2, south_3, *refs):
    faces = refs[:4]
    total_2, total_3, covers, bed, _, east_3 = refs[4:10]
    surf_3, depth_out, east_out, south_out, depth_4, east_4, south_4, east_tail, sems = refs[10:]
    ext, columns = surf_2.shape
    rows = ext - 2 * HALO
    own, tail = slice(0, rows), slice(rows, ext)
    gain = exchange(corridor, tail, surf_2, total_2, None, covers, None)
    fluxes(tail, None, (surf_2, east_2, None), faces, east_tail)
    for chunk, new_surf in settled(tail, surf_2, east_tail, south_3, gain):
        surf_3[tail, cols(chunk)] = new_surf
    copies = [
        pltpu.make_async_copy(source.at[pl.ds(0, rows), :], target, sems.at[slot])
        for slot, (source, target) in enumerate(
            ((east_4, east_out), (south_4, south_out), (depth_4, depth_out))
        )
    ]
    fluxes(own, wall_of(ext, tiles), (surf_3, east_3, south_3), faces, east_4, south_4)
    copies[0].start()
    copies[1].start()
    gain = exchange(corridor, own, surf_3, total_3, None, covers, None)
    for chunk, new_surf in settled(own, surf_3, east_4, south_4, gain):
        at = cols(chunk)
        depth_4[:, at] = new_surf - bed[own, at]
    copies[2].start()
    for copy in copies:
        copy.wait()


def local(
    depth, flux_east, flux_south, river_section, bed_level, rough_class, manning_table, bank_cell
):
    rows, columns = depth.shape
    owned = river_section.shape[0]
    corridor = bank_cell.shape[0]
    tiles = lax.axis_size("gy")
    ext = rows + 2 * HALO
    chunks = columns // LANES
    partner_section = swapped(river_section, 0).reshape(1, owned)
    partner_cells = swapped(bank_cell, 0)

    def held(value):
        return pltpu.with_memory_space_constraint(value, pltpu.VMEM)

    def far(value):
        return pltpu.with_memory_space_constraint(value, pltpu.HBM)

    params = pltpu.CompilerParams(vmem_limit_bytes=VMEM_LIMIT)
    halo = pltpu.VMEM((4 * chunks, HALO, LANES), jnp.float32)
    wide = pltpu.VMEM((4 * chunks + 1, HALO, LANES), jnp.float32)
    field = pltpu.VMEM((ext, columns), jnp.float32)
    small = pltpu.VMEM((rows, columns), jnp.float32)
    term = pltpu.VMEM((1, owned), jnp.float32)
    pair = pltpu.VMEM((2, owned), jnp.float32)
    result = pltpu.HBM((rows, columns), jnp.float32)
    cells = -(-chunks * rows // LANES) * LANES

    def call(kernel, name, outs, values, scratch=(), aliases=None):
        return pl.pallas_call(
            kernel,
            out_shape=outs,
            in_specs=[VMEM_SPEC] * len(values),
            out_specs=[HBM_SPEC if out is result else VMEM_SPEC for out in outs],
            scratch_shapes=scratch,
            input_output_aliases=aliases or {},
            compiler_params=params,
            name=name,
        )(*[held(value) for value in values])

    def picks(nodes):
        return [
            pltpu.VMEM((2, nodes, cells), jnp.bfloat16),
            pltpu.VMEM((2, nodes, LANES), jnp.float32),
        ]

    classes = manning_table.shape[0]
    table = far(manning_table.reshape(1, classes))
    table_held = pltpu.VMEM((1, classes), jnp.float32)
    to_other, own = pl.pallas_call(
        pack_kernel,
        out_shape=[wide, pair],
        in_specs=[HBM_SPEC] * 8,
        out_specs=[VMEM_SPEC] * 2,
        scratch_shapes=[
            pltpu.VMEM((4, 8, columns), jnp.float32),
            pltpu.VMEM((8, columns), jnp.int32),
            pltpu.VMEM((corridor, owned), jnp.int32),
            table_held,
            pltpu.SemaphoreType.DMA((8,)),
        ],
        compiler_params=params,
        name="pack",
    )(
        *[far(value) for value in (depth, bed_level, rough_class, flux_east, flux_south)],
        far(river_section.reshape(1, owned)),
        far(bank_cell),
        table,
    )
    (to_other,) = call(
        join_kernel,
        "join",
        [wide],
        (to_other, partner_section, partner_cells),
        aliases={0: 0},
    )
    by_other = swapped(to_other, 1)
    *loaded, rough, table_rows = pl.pallas_call(
        load_kernel,
        out_shape=[field] * 4
        + [pltpu.VMEM((rows, columns), jnp.int32), pltpu.VMEM((classes, LANES), jnp.float32)],
        in_specs=[HBM_SPEC] * 6,
        out_specs=[VMEM_SPEC] * 6,
        scratch_shapes=[table_held, pltpu.SemaphoreType.DMA((6,))],
        compiler_params=params,
        name="load",
    )(
        *[far(value) for value in (depth, flux_east, flux_south, bed_level, rough_class)],
        table,
    )
    *fields, to_partner = call(
        prepare_kernel,
        "prepare",
        [field] * 9 + [halo],
        (table_rows, rough, *loaded),
        aliases={2 + slot: slot for slot in range(4)},
    )
    by_partner = swapped(to_partner, 0)
    number, total, takes, masks = call(
        functools.partial(nodes_kernel, corridor, rows),
        "nodes",
        [field] * 2 + picks(2 * owned),
        (own, partner_section, partner_cells),
    )
    (near,) = call(relay_kernel, "relay", [pair], (by_other, masks))
    from_far = swapped(near, 0)
    *fields, takes_near, masks_near = call(
        functools.partial(border_kernel, corridor, tiles),
        "border",
        [field] * 11 + picks(owned),
        (by_partner, by_other, table_rows, near, *fields, number, total),
        aliases={4 + slot: slot for slot in range(11)},
    )
    surf, east, south, bed, _, *faces, number, total = fields
    surf_1, total_1, count, covers, given_1 = call(
        functools.partial(first_kernel, corridor),
        "first",
        [field] * 4 + [small],
        (surf, east, south, number, total),
        scratch=[field],
    )
    surf_1, total_1, count, covers, surf_2, east_2, south_2, total_2, given_2 = call(
        functools.partial(second_kernel, corridor, tiles),
        "second",
        [field] * 8 + [small],
        (
            *(from_far, surf, east, south, *faces, number, total, given_1),
            *(surf_1, total_1, count, covers),
        ),
        scratch=[field],
        aliases={11 + slot: slot for slot in range(4)},
    )
    surf_3, east_3, south_3, total_3, given_3 = call(
        functools.partial(third_kernel, corridor, tiles),
        "third",
        [field] * 4 + [small],
        (surf_2, east_2, south_2, *faces, total_2, covers, count, given_2),
    )
    own_term, partner_term, other_term = call(
        functools.partial(terms_kernel, corridor),
        "terms",
        [term] * 3,
        (own, surf_3, given_3, takes, masks, takes_near, masks_near),
    )
    from_other = swapped(other_term.reshape(owned), 1)
    from_partner = swapped(partner_term.reshape(owned), 0)
    _, depth, flux_east, flux_south = call(
        functools.partial(last_kernel, corridor, tiles),
        "last",
        [field, result, result, result],
        (surf_2, east_2, south_3, *faces, total_2, total_3, covers, bed, surf_3, east_3),
        scratch=[small, small, field, field, pltpu.SemaphoreType.DMA((3,))],
        aliases={11: 0},
    )
    river_section = own_term.reshape(owned) + from_other + from_partner
    return (depth, flux_east, flux_south, river_section)


def solution(mesh):
    return jax.shard_map(
        local,
        mesh=mesh,
        in_specs=(
            P(("runs", "gy"), None),
            P(("runs", "gy"), None),
            P(("runs", "gy"), None),
            P(("runs", "gy")),
            P("gy", None),
            P("gy", None),
            P(),
            P(None, "gy"),
        ),
        out_specs=(
            P(("runs", "gy"), None),
            P(("runs", "gy"), None),
            P(("runs", "gy"), None),
            P(("runs", "gy")),
        ),
        check_vma=False,
    )
```

```python
import functools

import jax
import jax.numpy as jnp
from jax import lax
from jax.experimental import pallas as pl
from jax.experimental.pallas import tpu as pltpu
from jax.sharding import PartitionSpec as P

STEPS = 4

GRAV = 9.81
TSTEP = 8.0
CELL = 90.0
FLOOR = 0.05
BANK_COEF = 200.0
CELL_AREA = 8100.0
NODE_AREA = 20000.0

LANES = 128
HALO = 4
SLOPE = GRAV * TSTEP / CELL
SPREAD = TSTEP / CELL
FEED = TSTEP * BANK_COEF / CELL_AREA
DRAIN = TSTEP * BANK_COEF / NODE_AREA
VMEM_LIMIT = 32 * 1024 * 1024

VMEM_SPEC = pl.BlockSpec(memory_space=pltpu.VMEM)
HBM_SPEC = pl.BlockSpec(memory_space=pltpu.HBM)


def swapped(value, first):
    count = lax.axis_size("gy")
    pairs = []
    for low in range(first, count - 1, 2):
        pairs += [(low, low + 1), (low + 1, low)]
    return lax.ppermute(value, "gy", pairs)


def cols(chunk):
    return slice(chunk * LANES, (chunk + 1) * LANES)


def lanes_of(rows):
    return lax.broadcasted_iota(jnp.int32, (rows, LANES), 1)


def moved_left(value, following, by):
    return jnp.where(
        lanes_of(value.shape[0]) >= LANES - by,
        pltpu.roll(following, LANES - by, 1),
        pltpu.roll(value, LANES - by, 1),
    )


def moved_up(value):
    return pltpu.roll(value, value.shape[0] - 1, 0)


def split3(value):
    high = value.astype(jnp.bfloat16)
    rest = value - high.astype(jnp.float32)
    middle = rest.astype(jnp.bfloat16)
    low = (rest - middle.astype(jnp.float32)).astype(jnp.bfloat16)
    return high, middle, low


def one_hot(count, key):
    rows = lax.broadcasted_iota(jnp.int32, (count, key.shape[1]), 0)
    return jnp.where(rows == key, 1.0, 0.0)


def drag_of(mann_a, mann_b):
    pair = mann_a + mann_b
    return (0.25 * GRAV * TSTEP * SLOPE) * (pair * pair)


def looked_up(klass, entries):
    value = jnp.broadcast_to(entries[0], klass.shape)
    for k in range(1, len(entries)):
        value = jnp.where(klass == k, entries[k], value)
    return value


def face(flux, surf_a, surf_b, bed_max, drag):
    flow_depth = jnp.maximum(jnp.maximum(surf_a, surf_b) - bed_max, FLOOR)
    power = jnp.exp2((-7.0 / 3.0) * jnp.log2(flow_depth))
    driven = flux - flow_depth * (surf_b - surf_a)
    damping = 1.0 + drag * jnp.abs(flux) * power
    return driven * pl.reciprocal(damping, approx=True)


def window_sums(blocks, reach, forward):
    height = blocks[0].shape[0]
    count = len(blocks)
    spare = -(count * height) % 16
    whole = blocks + ([jnp.zeros((spare, LANES), jnp.float32)] if spare else [])
    whole = jnp.concatenate(whole, axis=0)
    high = whole.astype(jnp.bfloat16)
    low = (whole - high.astype(jnp.float32)).astype(jnp.bfloat16)
    source = lax.broadcasted_iota(jnp.int32, (2 * LANES, 2 * LANES), 0) % LANES
    target = lax.broadcasted_iota(jnp.int32, (2 * LANES, 2 * LANES), 1)
    spill = target >= LANES
    target = target % LANES
    if forward:
        ahead = source - target + jnp.where(spill, LANES, 0)
    else:
        ahead = target - source + jnp.where(spill, LANES, 0)
    band = jnp.where((ahead >= 0) & (ahead < reach), 1.0, 0.0).astype(jnp.bfloat16)
    sums = jnp.dot(
        jnp.concatenate([high, low], axis=1), band, preferred_element_type=jnp.float32
    )
    results = []
    for block in range(count):
        result = sums[block * height : (block + 1) * height, :LANES]
        beside = block + 1 if forward else block - 1
        if 0 <= beside < count:
            result = result + sums[beside * height : (beside + 1) * height, LANES:]
        results.append(result)
    return results


def east_walled(value, chunk, chunks):
    if chunk + 1 < chunks:
        return value
    return jnp.where(lanes_of(value.shape[0]) == LANES - 1, 0.0, value)


def located(cell, position, rows, ext, columns):
    base = ((position * rows - HALO) * columns + 1).astype(jnp.float32)
    offset = cell - base
    valid = (cell > 0.0) & (offset >= 0.0) & (offset < float(ext * columns))
    offset = jnp.where(valid, offset, 0.0)
    row = jnp.floor((offset + 0.5) * (1.0 / columns))
    column = (offset - row * float(columns)).astype(jnp.int32)
    row = row.astype(jnp.int32) - HALO
    row = jnp.where(row < 0, row + ext, row)
    chunk = column // LANES
    return valid, row, chunk, column - chunk * LANES


def scattered(section, key, lane, count):
    at_lane = one_hot(LANES, lane)
    parts = [at_lane] + [at_lane * part.astype(jnp.float32) for part in split3(section)]
    grid = lax.dot_general(
        one_hot(-(-count // 16) * 16, key).astype(jnp.bfloat16),
        jnp.concatenate(parts, axis=0).astype(jnp.bfloat16),
        (((1,), (1,)), ((), ())),
        preferred_element_type=jnp.float32,
    )
    number = grid[:, :LANES]
    total = (grid[:, LANES : 2 * LANES] + grid[:, 2 * LANES : 3 * LANES]) + grid[:, 3 * LANES :]
    return number, total


def border_rows(of_first, fields, south):
    outer = lax.broadcasted_iota(jnp.int32, (HALO, LANES), 0) == jnp.where(of_first, HALO - 1, 0)
    flux = jnp.where(of_first, south[:HALO], south[HALO:])
    return [
        jnp.where(outer, flux[slot : slot + 1], jnp.where(of_first, value[:HALO], value[HALO:]))
        for slot, value in enumerate(fields)
    ]


def pack_kernel(
    depth, bed, rough, east, south, section, cells, table_in, to_other, own, *refs
):
    held, held_rough, held_cells, table, sems = refs
    rows, columns = depth.shape
    chunks = columns // LANES
    even = lax.axis_index("gy") % 2 == 0
    start = pl.multiple_of(jnp.where(even, 0, rows - 8), 8)
    near = pl.ds(start, 8)
    copies = [
        pltpu.make_async_copy(source, target, sems.at[slot])
        for slot, (source, target) in enumerate(
            (
                (rough.at[near, :], held_rough),
                (bed.at[near, :], held.at[1]),
                (depth.at[near, :], held.at[0]),
                (east.at[near, :], held.at[2]),
                (south.at[near, :], held.at[3]),
                (section, own.at[pl.ds(0, 1), :]),
                (cells, held_cells),
                (table_in, table),
            )
        )
    ]
    for copy in copies:
        copy.start()
    for copy in copies:
        copy.wait()
    own[1:2, :] = (held_cells[0:1, :] + 1).astype(jnp.float32)
    entries = [
        jnp.broadcast_to(table[:, k : k + 1], (1, LANES)) for k in range(table.shape[1])
    ]
    manns = [looked_up(held_rough[:, cols(chunk)], entries) for chunk in range(chunks)]
    row = lax.broadcasted_iota(jnp.int32, (8, LANES), 0)
    beds = [held[1, :, cols(chunk)] for chunk in range(chunks)]
    surfs = [held[0, :, cols(chunk)] + beds[chunk] for chunk in range(chunks)]

    def moved(values):
        rolled = [pltpu.roll(value, LANES - 1, 1) for value in values]
        rolled.append(rolled[-1])
        edge = lanes_of(8) == LANES - 1
        return [jnp.where(edge, rolled[c + 1], rolled[c]) for c in range(chunks)]

    beds_left, surfs_left, manns_left = moved(beds), moved(surfs), moved(manns)
    for chunk in range(chunks):
        at = cols(chunk)
        m0, b0, s0 = manns[chunk], beds[chunk], surfs[chunk]
        bed_max = jnp.maximum(b0, beds_left[chunk])
        drag = drag_of(m0, manns_left[chunk])
        q0 = (1.0 / SLOPE) * held[2, :, at]
        new_east = face(q0, s0, surfs_left[chunk], bed_max, drag)
        new_east = east_walled(new_east, chunk, chunks)
        bed_max = jnp.maximum(b0, moved_up(b0))
        drag = drag_of(m0, moved_up(m0))
        q0 = (1.0 / SLOPE) * held[3, :, at]
        new_south = jnp.where(row == 7, q0, face(q0, s0, moved_up(s0), bed_max, drag))
        fields = (s0, b0, held_rough[:, at].astype(jnp.float32), new_east)
        for slot, block in enumerate(border_rows(even, fields, new_south)):
            to_other[slot * chunks + chunk] = block
    to_other[4 * chunks, 0:2, :] = own[...]


def join_kernel(before, section, cells, to_other):
    nodes = to_other.shape[0] - 1
    to_other[nodes, 2:3, :] = section[...]
    to_other[nodes, 3:4, :] = (cells[0:1, :] + 1).astype(jnp.float32)


def relay_kernel(by_other, prepared, near):
    del prepared
    near[...] = by_other[by_other.shape[0] - 1, 0:2, :]


def picking(reach, rows, key, lane, takes, masks):
    for block in range(key.shape[1] // LANES):
        mine = slice(block * LANES, (block + 1) * LANES)

        def column(row):
            wide = jnp.broadcast_to(row[:, mine].astype(jnp.float32), (LANES, LANES))
            return jnp.transpose(wide).astype(jnp.int32)

        spread = lanes_of(LANES)
        at = column(key)
        after = jnp.where(at < 0, at, at + rows)
        for first in range(0, takes.shape[2], LANES):
            for half, place in enumerate((at, after)):
                hit = jnp.where(spread + first == place, 1.0, 0.0)
                takes[half, mine, first : first + LANES] = hit.astype(jnp.bfloat16)
        ahead = spread - column(lane)
        masks[0, mine, :] = jnp.where((ahead >= 0) & (ahead < reach), 1.0, 0.0)
        masks[1, mine, :] = jnp.where(ahead + LANES < reach, 1.0, 0.0)


def load_kernel(
    depth_in, east_in, south_in, bed_in, rough_in, table_in, *refs
):
    surf, east, south, bed, rough, table_rows, table, sems = refs
    rows, columns = depth_in.shape
    own = pl.ds(0, rows)
    copies = [
        pltpu.make_async_copy(source, target.at[own, :], sems.at[slot])
        for slot, (source, target) in enumerate(
            (
                (depth_in, surf),
                (bed_in, bed),
                (rough_in, rough),
                (east_in, east),
                (south_in, south),
            )
        )
    ]
    copies.append(pltpu.make_async_copy(table_in, table, sems.at[5]))
    for copy in copies:
        copy.start()
    copies[5].wait()
    for k in range(table_rows.shape[0]):
        table_rows[k : k + 1, :] = jnp.broadcast_to(table[:, k : k + 1], (1, LANES))
    for copy in copies[:5]:
        copy.wait()


def prepare_kernel(table_rows, rough, *refs):
    surf, east, south, bed = refs[4:8]
    mann, bed_e, bed_s, drag_e, drag_s, to_partner = refs[8:]
    ext, columns = surf.shape
    rows = ext - 2 * HALO
    chunks = columns // LANES
    even = lax.axis_index("gy") % 2 == 0
    entries = [table_rows[k : k + 1, :] for k in range(table_rows.shape[0])]
    for chunk in range(chunks):
        at = cols(chunk)
        mann[:rows, at] = looked_up(rough[:, at], entries)
        surf[:rows, at] = surf[:rows, at] + bed[:rows, at]

    kept = lax.broadcasted_iota(jnp.int32, (rows, LANES), 0) == rows - 1
    for chunk in range(chunks):
        at, then = cols(chunk), cols(min(chunk + 1, chunks - 1))
        s0, b0, m0 = surf[:rows, at], bed[:rows, at], mann[:rows, at]
        bed_max = jnp.maximum(b0, moved_left(b0, bed[:rows, then], 1))
        drag = drag_of(m0, moved_left(m0, mann[:rows, then], 1))
        bed_e[:rows, at] = bed_max
        drag_e[:rows, at] = drag
        q0 = (1.0 / SLOPE) * east[:rows, at]
        new_east = face(q0, s0, moved_left(s0, surf[:rows, then], 1), bed_max, drag)
        new_east = east_walled(new_east, chunk, chunks)
        east[:rows, at] = new_east
        bed_max = jnp.maximum(b0, moved_up(b0))
        drag = drag_of(m0, moved_up(m0))
        bed_s[:rows, at] = bed_max
        drag_s[:rows, at] = drag
        q0 = (1.0 / SLOPE) * south[:rows, at]
        new_south = jnp.where(kept, q0, face(q0, s0, moved_up(s0), bed_max, drag))
        south[:rows, at] = new_south

        def ends(value):
            return jnp.where(even, value[rows - 8 :], value[:8])

        fields = (ends(s0), ends(b0), ends(rough[:, at].astype(jnp.float32)), ends(new_east))
        blocks = border_rows(jnp.logical_not(even), fields, ends(new_south))
        for slot, block in enumerate(blocks):
            to_partner[slot * chunks + chunk] = block


def nodes_kernel(reach, surf, own, partner_section, partner_cells, *refs):
    number, total, takes, masks, windows, given_1 = refs
    rows = surf.shape[0] - 2 * HALO
    ext, columns = number.shape
    chunks = columns // LANES
    tiles = lax.axis_size("gy")
    position = lax.axis_index("gy")
    side = jnp.where(position % 2 == 0, 1, -1)
    partner = jnp.where(position + side < tiles, partner_cells[0:1, :] + 1, 0).astype(jnp.float32)
    section = jnp.concatenate([own[0:1, :], partner_section[...]], axis=1)
    cell = jnp.concatenate([own[1:2, :], partner], axis=1)
    valid, node_row, node_chunk, node_lane = located(cell, position, rows, ext, columns)
    key = jnp.where(valid, node_chunk * ext + node_row, -1)
    starts, levels = scattered(section, key, node_lane, chunks * ext)
    for chunk in range(chunks):
        at = cols(chunk)
        number[:, at] = starts[chunk * ext : (chunk + 1) * ext]
        total[:, at] = levels[chunk * ext : (chunk + 1) * ext]
    key = jnp.where(valid & (node_row < rows), node_chunk * rows + node_row, -1)
    picking(reach, rows, key, node_lane, takes, masks)
    sums = window_sums([surf[:rows, cols(chunk)] for chunk in range(chunks)], reach, True)
    for chunk in range(chunks):
        windows[:, cols(chunk)] = sums[chunk]
    give(reach, 0, surf, None, given_1)


def wall_of(ext, tiles):
    position = lax.axis_index("gy")
    rows = ext - 2 * HALO
    row = lax.broadcasted_iota(jnp.int32, (16, LANES), 0) + (ext - 16)
    return ((row == ext - 1) & (position == 0)) | ((row == rows - 1) & (position == tiles - 1))


def border_kernel(reach, tiles, by_partner, by_other, table_rows, near, *refs):
    surf, east, south, bed, mann, bed_e, bed_s, drag_e, drag_s, number, total, takes, masks = refs[11:]
    ext, columns = surf.shape
    rows = ext - 2 * HALO
    chunks = columns // LANES
    position = lax.axis_index("gy")
    even = position % 2 == 0
    entries = [table_rows[k : k + 1, :] for k in range(table_rows.shape[0])]
    row = lax.broadcasted_iota(jnp.int32, (2 * HALO, LANES), 0)
    for chunk in range(chunks):
        at = cols(chunk)
        halos = []
        flux = jnp.zeros((2 * HALO, LANES), jnp.float32)
        for slot in range(4):
            a, b = by_partner[slot * chunks + chunk], by_other[slot * chunks + chunk]
            below = jnp.where(even, a, b)
            above = jnp.where(even, b, a)
            halos.append(jnp.concatenate([below, above], axis=0))
            flux = jnp.where(row == slot, below[HALO - 1 :], flux)
            flux = jnp.where(row == HALO + slot, above[:1], flux)
        surf[rows:, at] = halos[0]
        bed[rows:, at] = halos[1]
        mann[rows:, at] = looked_up(halos[2].astype(jnp.int32), entries)
        east[rows:, at] = halos[3]
        south[rows:, at] = flux

    beyond = by_other[4 * chunks, 2:4, :]
    section = jnp.concatenate([near[0:1, :], beyond[0:1, :]], axis=1)
    cell = jnp.concatenate([near[1:2, :], beyond[1:2, :]], axis=1)
    valid, node_row, node_chunk, node_lane = located(cell, position, rows, ext, columns)
    key = jnp.where(valid, node_chunk * ext + node_row, -1)
    starts, levels = scattered(section, key, node_lane, chunks * ext)

    key = jnp.where(valid & (node_row < rows), node_chunk * rows + node_row, -1)
    owned = near.shape[1]
    picking(reach, rows, key[:, :owned], node_lane[:, :owned], takes, masks)

    wall = wall_of(ext, tiles)
    kept = lax.broadcasted_iota(jnp.int32, (16, LANES), 0) % 8 < 7
    for chunk in range(chunks):
        at, then = cols(chunk), cols(min(chunk + 1, chunks - 1))
        number[:, at] += starts[chunk * ext : (chunk + 1) * ext]
        total[:, at] += levels[chunk * ext : (chunk + 1) * ext]
        b0, m0 = bed[rows:, at], mann[rows:, at]
        bed_e[rows:, at] = jnp.maximum(b0, moved_left(b0, bed[rows:, then], 1))
        drag_e[rows:, at] = drag_of(m0, moved_left(m0, mann[rows:, then], 1))

        def rolled_up(ref):
            value = jnp.concatenate([ref[rows - 8 :, at], ref[:8, at]], axis=0)
            return value[:16], moved_up(value)[:16]

        s0, s1 = rolled_up(surf)
        b0, b1 = rolled_up(bed)
        m0, m1 = rolled_up(mann)
        bed_max = jnp.maximum(b0, b1)
        drag = drag_of(m0, m1)
        bed_s[rows - 8 :, at] = bed_max
        drag_s[rows - 8 :, at] = drag
        q0 = south[rows - 8 :, at]
        new_south = jnp.where(kept, q0, face(q0, s0, s1, bed_max, drag))
        south[rows - 8 :, at] = jnp.where(wall, 0.0, new_south)


def fluxes(mine, wall, before, faces, east_out, south_out=None, scale=None):
    surf, east, south = before
    bed_e, bed_s, drag_e, drag_s = faces
    chunks = surf.shape[1] // LANES
    rolled = pltpu.roll(surf[mine, cols(0)], LANES - 1, 1)
    lane = lanes_of(rolled.shape[0])
    for chunk in range(chunks):
        at = cols(chunk)
        s0 = surf[mine, at]
        rolled_then = rolled
        if chunk + 1 < chunks:
            rolled_then = pltpu.roll(surf[mine, cols(chunk + 1)], LANES - 1, 1)
        left = jnp.where(lane >= LANES - 1, rolled_then, rolled)
        rolled = rolled_then
        new_east = face(east[mine, at], s0, left, bed_e[mine, at], drag_e[mine, at])
        if scale is not None:
            new_east = scale * new_east
        east_out[mine, at] = east_walled(new_east, chunk, chunks)
        if south_out is not None:
            s0 = surf[:, at]
            new_south = face(south[:, at], s0, moved_up(s0), bed_s[:, at], drag_s[:, at])
            if scale is not None:
                new_south = scale * new_south
            south_out[:, at] = jnp.concatenate(
                [new_south[:-16], jnp.where(wall, 0.0, new_south[-16:])], axis=0
            )


def settled(mine, surf, east, south, keep, sums, spread=SPREAD * SLOPE):
    ext, columns = surf.shape
    rolled = 0.0
    for chunk in range(columns // LANES):
        at = cols(chunk)
        new_east = east[mine, at]
        new_south = south[:, at]
        lane = lanes_of(new_east.shape[0])
        rolled_before, rolled = rolled, pltpu.roll(new_east, 1, 1)
        west = jnp.where(lane < 1, rolled_before, rolled)
        north = pltpu.roll(new_south, 1, 0)[mine]
        inflow = west + north
        s0 = surf[mine, at]
        outflow = new_east + new_south[mine]
        yield chunk, keep[mine, at] * s0 + (spread * (inflow - outflow) + sums[chunk])


def exchange(corridor, mine, surf, total, count, total_out, windows=None):
    chunks = surf.shape[1] // LANES
    sums = window_sums([total[mine, cols(chunk)] for chunk in range(chunks)], corridor, False)
    if total_out is not None:
        if windows is None:
            windows = window_sums(
                [surf[mine, cols(chunk)] for chunk in range(chunks)], corridor, True
            )
        for chunk in range(chunks):
            at = cols(chunk)
            kept = (1.0 - corridor * DRAIN) * total[mine, at]
            total_out[mine, at] = kept + count[mine, at] * windows[chunk]
    return sums


def give(corridor, step, surf, before, after):
    rows, columns = after.shape
    weight = DRAIN * (1.0 - corridor * DRAIN) ** (STEPS - 1 - step)
    for chunk in range(columns // LANES):
        at = cols(chunk)
        value = weight * surf[:rows, at]
        after[:, at] = value if before is None else before[:, at] + value


def first_kernel(corridor, surf, east, south, number, total, windows, *refs):
    surf_1, total_1, count, keep, total_0 = refs
    rows = surf.shape[0] - 2 * HALO
    chunks = surf.shape[1] // LANES
    own = slice(0, rows)
    covering = window_sums([number[own, cols(chunk)] for chunk in range(chunks)], corridor, False)
    for chunk in range(chunks):
        at = cols(chunk)
        count[own, at] = (FEED * DRAIN) * number[own, at]
        keep[own, at] = 1.0 - FEED * covering[chunk]
        total_0[own, at] = FEED * total[own, at]
    windows = [windows[:, cols(chunk)] for chunk in range(chunks)]
    sums = exchange(corridor, own, surf, total_0, count, total_1, windows)
    for chunk, new_surf in settled(own, surf, east, south, keep, sums):
        surf_1[own, cols(chunk)] = new_surf


def second_kernel(corridor, tiles, far, surf, east, south, *refs):
    faces = refs[:4]
    number, total, given_1 = refs[4:7]
    surf_1, total_1, count, keep = refs[11:15]
    surf_2, east_2, south_2, total_2, given_2, total_0 = refs[15:]
    ext, columns = surf.shape
    rows = ext - 2 * HALO
    chunks = columns // LANES
    position = lax.axis_index("gy")
    tail = slice(rows, ext)

    valid, node_row, node_chunk, node_lane = located(far[1:2, :], position, rows, ext, columns)
    key = jnp.where(valid & (node_row >= rows), node_chunk * 8 + (node_row - rows), -1)
    starts, levels = scattered(far[0:1, :], key, node_lane, chunks * 8)
    starting = [
        number[tail, cols(chunk)] + starts[chunk * 8 : chunk * 8 + 8] for chunk in range(chunks)
    ]
    covering = window_sums(starting, corridor, False)
    for chunk in range(chunks):
        at = cols(chunk)
        count[tail, at] = (FEED * DRAIN) * starting[chunk]
        keep[tail, at] = 1.0 - FEED * covering[chunk]
        total_0[tail, at] = FEED * (total[tail, at] + levels[chunk * 8 : chunk * 8 + 8])
    sums = exchange(corridor, tail, surf, total_0, count, total_1)
    for chunk, new_surf in settled(tail, surf, east, south, keep, sums):
        surf_1[tail, cols(chunk)] = new_surf

    every = slice(0, ext)
    sums = exchange(corridor, every, surf_1, total_1, count, total_2)
    fluxes(every, wall_of(ext, tiles), (surf_1, east, south), faces, east_2, south_2)
    for chunk, new_surf in settled(every, surf_1, east_2, south_2, keep, sums):
        surf_2[:, cols(chunk)] = new_surf
    give(corridor, 1, surf_1, given_1, given_2)


def third_kernel(corridor, tiles, surf, east, south, *refs):
    faces = refs[:4]
    total, keep, count, given_2, surf_3, east_3, south_3, total_3, given_3 = refs[4:]
    ext = surf.shape[0]
    own = slice(0, ext - 2 * HALO)
    sums = exchange(corridor, own, surf, total, count, total_3)
    fluxes(own, wall_of(ext, tiles), (surf, east, south), faces, east_3, south_3)
    for chunk, new_surf in settled(own, surf, east_3, south_3, keep, sums):
        surf_3[own, cols(chunk)] = new_surf
    give(corridor, 2, surf, given_2, given_3)


def terms_kernel(corridor, own, surf, given_3, *refs):
    takes, masks, takes_near, masks_near, own_term, partner_term, other_term = refs
    rows, columns = given_3.shape
    owned = own.shape[1]
    chunks = columns // LANES
    levels = [
        given_3[:, cols(chunk)] + DRAIN * surf[:rows, cols(chunk)] for chunk in range(chunks)
    ]
    spare = takes.shape[2] - chunks * rows
    if spare:
        levels.append(jnp.zeros((spare, LANES), jnp.float32))
    levels = jnp.concatenate(levels, axis=0)
    high = levels.astype(jnp.bfloat16)
    low = (levels - high.astype(jnp.float32)).astype(jnp.bfloat16)
    picked = jnp.dot(
        jnp.concatenate([takes[0], takes_near[0], takes[1], takes_near[1]], axis=0),
        jnp.concatenate([high, low], axis=1),
        preferred_element_type=jnp.float32,
    )
    hit = jnp.concatenate([masks[0], masks_near[0], masks[1], masks_near[1]], axis=0)
    picked = (picked * jnp.concatenate([hit, hit], axis=1)).astype(jnp.bfloat16)
    picked = jnp.concatenate([picked[: 3 * owned], picked[3 * owned :]], axis=1)
    terms = lax.dot_general(
        jnp.ones((8, 4 * LANES), jnp.bfloat16),
        picked,
        (((1,), (1,)), ((), ())),
        preferred_element_type=jnp.float32,
    )[0:1]
    own_term[...] = (1.0 - corridor * DRAIN) ** STEPS * own[0:1, :] + terms[:, :owned]
    partner_term[...] = terms[:, owned : 2 * owned]
    other_term[...] = terms[:, 2 * owned :]


def last_kernel(corridor, tiles, surf_2, east_2, south_3, *refs):
    faces = refs[:4]
    total_2, total_3, keep, bed, _, east_3 = refs[4:10]
    surf_3, depth_out, east_out, south_out, depth_4, east_4, south_4, east_tail, sems = refs[10:]
    ext, columns = surf_2.shape
    rows = ext - 2 * HALO
    chunks = columns // LANES
    own, tail = slice(0, rows), slice(rows, ext)
    sums = exchange(corridor, tail, surf_2, total_2, None, None)
    fluxes(tail, None, (surf_2, east_2, None), faces, east_tail)
    for chunk, new_surf in settled(tail, surf_2, east_tail, south_3, keep, sums):
        surf_3[tail, cols(chunk)] = new_surf

    def copy(slot, source, target, first, last):
        part = pl.ds(first * LANES, (last - first) * LANES)
        return pltpu.make_async_copy(
            source.at[pl.ds(0, rows), part], target.at[:, part], sems.at[slot]
        )

    fluxes(
        own, wall_of(ext, tiles), (surf_3, east_3, south_3), faces, east_4, south_4, scale=SLOPE
    )
    copies = [copy(0, east_4, east_out, 0, chunks), copy(1, south_4, south_out, 0, chunks)]
    for one in copies:
        one.start()
    sums = exchange(corridor, own, surf_3, total_3, None, None)
    group = 5
    for chunk, new_surf in settled(own, surf_3, east_4, south_4, keep, sums, spread=SPREAD):
        at = cols(chunk)
        depth_4[:, at] = new_surf - bed[own, at]
        if (chunk + 1) % group == 0 or chunk + 1 == chunks:
            first = chunk // group
            copies.append(copy(2 + first, depth_4, depth_out, first * group, chunk + 1))
            copies[-1].start()
    for one in copies:
        one.wait()


def local(
    depth, flux_east, flux_south, river_section, bed_level, rough_class, manning_table, bank_cell
):
    rows, columns = depth.shape
    owned = river_section.shape[0]
    corridor = bank_cell.shape[0]
    tiles = lax.axis_size("gy")
    ext = rows + 2 * HALO
    chunks = columns // LANES
    partner_section = swapped(river_section, 0).reshape(1, owned)
    partner_cells = swapped(bank_cell, 0)

    def held(value):
        return pltpu.with_memory_space_constraint(value, pltpu.VMEM)

    def far(value):
        return pltpu.with_memory_space_constraint(value, pltpu.HBM)

    params = pltpu.CompilerParams(vmem_limit_bytes=VMEM_LIMIT)
    halo = pltpu.VMEM((4 * chunks, HALO, LANES), jnp.float32)
    wide = pltpu.VMEM((4 * chunks + 1, HALO, LANES), jnp.float32)
    field = pltpu.VMEM((ext, columns), jnp.float32)
    small = pltpu.VMEM((rows, columns), jnp.float32)
    term = pltpu.VMEM((1, owned), jnp.float32)
    pair = pltpu.VMEM((2, owned), jnp.float32)
    result = pltpu.HBM((rows, columns), jnp.float32)
    cells = -(-chunks * rows // LANES) * LANES

    def call(kernel, name, outs, values, scratch=(), aliases=None):
        return pl.pallas_call(
            kernel,
            out_shape=outs,
            in_specs=[VMEM_SPEC] * len(values),
            out_specs=[HBM_SPEC if out is result else VMEM_SPEC for out in outs],
            scratch_shapes=scratch,
            input_output_aliases=aliases or {},
            compiler_params=params,
            name=name,
        )(*[held(value) for value in values])

    def picks(nodes):
        return [
            pltpu.VMEM((2, nodes, cells), jnp.bfloat16),
            pltpu.VMEM((2, nodes, LANES), jnp.float32),
        ]

    classes = manning_table.shape[0]
    table = far(manning_table.reshape(1, classes))
    table_held = pltpu.VMEM((1, classes), jnp.float32)
    to_other, own = pl.pallas_call(
        pack_kernel,
        out_shape=[wide, pair],
        in_specs=[HBM_SPEC] * 8,
        out_specs=[VMEM_SPEC] * 2,
        scratch_shapes=[
            pltpu.VMEM((4, 8, columns), jnp.float32),
            pltpu.VMEM((8, columns), jnp.int32),
            pltpu.VMEM((corridor, owned), jnp.int32),
            table_held,
            pltpu.SemaphoreType.DMA((8,)),
        ],
        compiler_params=params,
        name="pack",
    )(
        *[far(value) for value in (depth, bed_level, rough_class, flux_east, flux_south)],
        far(river_section.reshape(1, owned)),
        far(bank_cell),
        table,
    )
    (to_other,) = call(
        join_kernel,
        "join",
        [wide],
        (to_other, partner_section, partner_cells),
        aliases={0: 0},
    )
    by_other = swapped(to_other, 1)
    *loaded, rough, table_rows = pl.pallas_call(
        load_kernel,
        out_shape=[field] * 4
        + [pltpu.VMEM((rows, columns), jnp.int32), pltpu.VMEM((classes, LANES), jnp.float32)],
        in_specs=[HBM_SPEC] * 6,
        out_specs=[VMEM_SPEC] * 6,
        scratch_shapes=[table_held, pltpu.SemaphoreType.DMA((6,))],
        compiler_params=params,
        name="load",
    )(
        *[far(value) for value in (depth, flux_east, flux_south, bed_level, rough_class)],
        table,
    )
    *fields, to_partner = call(
        prepare_kernel,
        "prepare",
        [field] * 9 + [halo],
        (table_rows, rough, *loaded),
        aliases={2 + slot: slot for slot in range(4)},
    )
    by_partner = swapped(to_partner, 0)
    number, total, takes, masks, windows, given_1 = call(
        functools.partial(nodes_kernel, corridor),
        "nodes",
        [field] * 2 + picks(2 * owned) + [small] * 2,
        (fields[0], own, partner_section, partner_cells),
    )
    (near,) = call(relay_kernel, "relay", [pair], (by_other, masks))
    from_far = swapped(near, 0)
    *fields, takes_near, masks_near = call(
        functools.partial(border_kernel, corridor, tiles),
        "border",
        [field] * 11 + picks(owned),
        (by_partner, by_other, table_rows, near, *fields, number, total),
        aliases={4 + slot: slot for slot in range(11)},
    )
    surf, east, south, bed, _, *faces, number, total = fields
    surf_1, total_1, count, keep = call(
        functools.partial(first_kernel, corridor),
        "first",
        [field] * 4,
        (surf, east, south, number, total, windows),
        scratch=[field],
    )
    surf_1, total_1, count, keep, surf_2, east_2, south_2, total_2, given_2 = call(
        functools.partial(second_kernel, corridor, tiles),
        "second",
        [field] * 8 + [small],
        (
            *(from_far, surf, east, south, *faces, number, total, given_1),
            *(surf_1, total_1, count, keep),
        ),
        scratch=[field],
        aliases={11 + slot: slot for slot in range(4)},
    )
    surf_3, east_3, south_3, total_3, given_3 = call(
        functools.partial(third_kernel, corridor, tiles),
        "third",
        [field] * 4 + [small],
        (surf_2, east_2, south_2, *faces, total_2, keep, count, given_2),
    )
    own_term, partner_term, other_term = call(
        functools.partial(terms_kernel, corridor),
        "terms",
        [term] * 3,
        (own, surf_3, given_3, takes, masks, takes_near, masks_near),
    )
    from_other = swapped(other_term.reshape(owned), 1)
    from_partner = swapped(partner_term.reshape(owned), 0)
    _, depth, flux_east, flux_south = call(
        functools.partial(last_kernel, corridor, tiles),
        "last",
        [field, result, result, result],
        (surf_2, east_2, south_3, *faces, total_2, total_3, keep, bed, surf_3, east_3),
        scratch=[small, small, field, field, pltpu.SemaphoreType.DMA((2 + -(-chunks // 5),))],
        aliases={11: 0},
    )
    river_section = own_term.reshape(owned) + from_other + from_partner
    return (depth, flux_east, flux_south, river_section)


def solution(mesh):
    return jax.shard_map(
        local,
        mesh=mesh,
        in_specs=(
            P(("runs", "gy"), None),
            P(("runs", "gy"), None),
            P(("runs", "gy"), None),
            P(("runs", "gy")),
            P("gy", None),
            P("gy", None),
            P(),
            P(None, "gy"),
        ),
        out_specs=(
            P(("runs", "gy"), None),
            P(("runs", "gy"), None),
            P(("runs", "gy"), None),
            P(("runs", "gy")),
        ),
        check_vma=False,
    )
```

```python
import functools

import jax
import jax.numpy as jnp
from jax import lax
from jax.experimental import pallas as pl
from jax.experimental.pallas import tpu as pltpu
from jax.sharding import PartitionSpec as P

STEPS = 4

GRAV = 9.81
TSTEP = 8.0
CELL = 90.0
FLOOR = 0.05
BANK_COEF = 200.0
CELL_AREA = 8100.0
NODE_AREA = 20000.0

LANES = 128
HALO = 4
SLOPE = GRAV * TSTEP / CELL
SPREAD = TSTEP / CELL
FEED = TSTEP * BANK_COEF / CELL_AREA
DRAIN = TSTEP * BANK_COEF / NODE_AREA
VMEM_LIMIT = 32 * 1024 * 1024

VMEM_SPEC = pl.BlockSpec(memory_space=pltpu.VMEM)
HBM_SPEC = pl.BlockSpec(memory_space=pltpu.HBM)


def swapped(value, first):
    count = lax.axis_size("gy")
    pairs = []
    for low in range(first, count - 1, 2):
        pairs += [(low, low + 1), (low + 1, low)]
    return lax.ppermute(value, "gy", pairs)


def cols(chunk):
    return slice(chunk * LANES, (chunk + 1) * LANES)


def lanes_of(rows):
    return lax.broadcasted_iota(jnp.int32, (rows, LANES), 1)


def moved_left(value, following, by):
    return jnp.where(
        lanes_of(value.shape[0]) >= LANES - by,
        pltpu.roll(following, LANES - by, 1),
        pltpu.roll(value, LANES - by, 1),
    )


def moved_up(value):
    return pltpu.roll(value, value.shape[0] - 1, 0)


def split3(value):
    high = value.astype(jnp.bfloat16)
    rest = value - high.astype(jnp.float32)
    middle = rest.astype(jnp.bfloat16)
    low = (rest - middle.astype(jnp.float32)).astype(jnp.bfloat16)
    return high, middle, low


def one_hot(count, key):
    rows = lax.broadcasted_iota(jnp.int32, (count, key.shape[1]), 0)
    return jnp.where(rows == key, 1.0, 0.0)


def drag_of(mann_a, mann_b):
    pair = mann_a + mann_b
    return (0.25 * GRAV * TSTEP * SLOPE) * (pair * pair)


def looked_up(klass, entries):
    value = jnp.broadcast_to(entries[0], klass.shape)
    for k in range(1, len(entries)):
        value = jnp.where(klass == k, entries[k], value)
    return value


def face(flux, surf_a, surf_b, bed_max, drag):
    flow_depth = jnp.maximum(jnp.maximum(surf_a, surf_b) - bed_max, FLOOR)
    power = jnp.exp2((-7.0 / 3.0) * jnp.log2(flow_depth))
    driven = flux - flow_depth * (surf_b - surf_a)
    damping = 1.0 + drag * jnp.abs(flux) * power
    return driven * pl.reciprocal(damping, approx=True)


def window_sums(blocks, reach, forward):
    height = blocks[0].shape[0]
    count = len(blocks)
    spare = -(count * height) % 16
    whole = blocks + ([jnp.zeros((spare, LANES), jnp.float32)] if spare else [])
    whole = jnp.concatenate(whole, axis=0)
    high = whole.astype(jnp.bfloat16)
    low = (whole - high.astype(jnp.float32)).astype(jnp.bfloat16)
    source = lax.broadcasted_iota(jnp.int32, (2 * LANES, 2 * LANES), 0) % LANES
    target = lax.broadcasted_iota(jnp.int32, (2 * LANES, 2 * LANES), 1)
    spill = target >= LANES
    target = target % LANES
    if forward:
        ahead = source - target + jnp.where(spill, LANES, 0)
    else:
        ahead = target - source + jnp.where(spill, LANES, 0)
    band = jnp.where((ahead >= 0) & (ahead < reach), 1.0, 0.0).astype(jnp.bfloat16)
    sums = jnp.dot(
        jnp.concatenate([high, low], axis=1), band, preferred_element_type=jnp.float32
    )
    results = []
    for block in range(count):
        result = sums[block * height : (block + 1) * height, :LANES]
        beside = block + 1 if forward else block - 1
        if 0 <= beside < count:
            result = result + sums[beside * height : (beside + 1) * height, LANES:]
        results.append(result)
    return results


def east_walled(value, chunk, chunks):
    if chunk + 1 < chunks:
        return value
    return jnp.where(lanes_of(value.shape[0]) == LANES - 1, 0.0, value)


def located(cell, position, rows, ext, columns):
    base = ((position * rows - HALO) * columns + 1).astype(jnp.float32)
    offset = cell - base
    valid = (cell > 0.0) & (offset >= 0.0) & (offset < float(ext * columns))
    offset = jnp.where(valid, offset, 0.0)
    row = jnp.floor((offset + 0.5) * (1.0 / columns))
    column = (offset - row * float(columns)).astype(jnp.int32)
    row = row.astype(jnp.int32) - HALO
    row = jnp.where(row < 0, row + ext, row)
    chunk = column // LANES
    return valid, row, chunk, column - chunk * LANES


def scattered(section, key, lane, count):
    at_lane = one_hot(LANES, lane)
    parts = [at_lane] + [at_lane * part.astype(jnp.float32) for part in split3(section)]
    grid = lax.dot_general(
        one_hot(-(-count // 16) * 16, key).astype(jnp.bfloat16),
        jnp.concatenate(parts, axis=0).astype(jnp.bfloat16),
        (((1,), (1,)), ((), ())),
        preferred_element_type=jnp.float32,
    )
    number = grid[:, :LANES]
    total = (grid[:, LANES : 2 * LANES] + grid[:, 2 * LANES : 3 * LANES]) + grid[:, 3 * LANES :]
    return number, total


def border_rows(of_first, fields, south):
    outer = lax.broadcasted_iota(jnp.int32, (HALO, LANES), 0) == jnp.where(of_first, HALO - 1, 0)
    flux = jnp.where(of_first, south[:HALO], south[HALO:])
    return [
        jnp.where(outer, flux[slot : slot + 1], jnp.where(of_first, value[:HALO], value[HALO:]))
        for slot, value in enumerate(fields)
    ]


def pack_kernel(
    depth, bed, rough, east, south, section, cells, table_in, to_other, own, *refs
):
    held, held_rough, held_cells, table, sems = refs
    rows, columns = depth.shape
    chunks = columns // LANES
    even = lax.axis_index("gy") % 2 == 0
    start = pl.multiple_of(jnp.where(even, 0, rows - 8), 8)
    near = pl.ds(start, 8)
    copies = [
        pltpu.make_async_copy(source, target, sems.at[slot])
        for slot, (source, target) in enumerate(
            (
                (rough.at[near, :], held_rough),
                (bed.at[near, :], held.at[1]),
                (depth.at[near, :], held.at[0]),
                (east.at[near, :], held.at[2]),
                (south.at[near, :], held.at[3]),
                (section, own.at[pl.ds(0, 1), :]),
                (cells, held_cells),
                (table_in, table),
            )
        )
    ]
    for copy in copies:
        copy.start()
    for copy in copies:
        copy.wait()
    own[1:2, :] = (held_cells[0:1, :] + 1).astype(jnp.float32)
    entries = [
        jnp.broadcast_to(table[:, k : k + 1], (1, LANES)) for k in range(table.shape[1])
    ]
    manns = [looked_up(held_rough[:, cols(chunk)], entries) for chunk in range(chunks)]
    row = lax.broadcasted_iota(jnp.int32, (8, LANES), 0)
    beds = [held[1, :, cols(chunk)] for chunk in range(chunks)]
    surfs = [held[0, :, cols(chunk)] + beds[chunk] for chunk in range(chunks)]

    def moved(values):
        rolled = [pltpu.roll(value, LANES - 1, 1) for value in values]
        rolled.append(rolled[-1])
        edge = lanes_of(8) == LANES - 1
        return [jnp.where(edge, rolled[c + 1], rolled[c]) for c in range(chunks)]

    beds_left, surfs_left, manns_left = moved(beds), moved(surfs), moved(manns)
    for chunk in range(chunks):
        at = cols(chunk)
        m0, b0, s0 = manns[chunk], beds[chunk], surfs[chunk]
        bed_max = jnp.maximum(b0, beds_left[chunk])
        drag = drag_of(m0, manns_left[chunk])
        q0 = (1.0 / SLOPE) * held[2, :, at]
        new_east = face(q0, s0, surfs_left[chunk], bed_max, drag)
        new_east = east_walled(new_east, chunk, chunks)
        bed_max = jnp.maximum(b0, moved_up(b0))
        drag = drag_of(m0, moved_up(m0))
        q0 = (1.0 / SLOPE) * held[3, :, at]
        new_south = jnp.where(row == 7, q0, face(q0, s0, moved_up(s0), bed_max, drag))
        fields = (s0, b0, held_rough[:, at].astype(jnp.float32), new_east)
        for slot, block in enumerate(border_rows(even, fields, new_south)):
            to_other[slot * chunks + chunk] = block
    to_other[4 * chunks, 0:2, :] = own[...]


def join_kernel(before, section, cells, to_other):
    nodes = to_other.shape[0] - 1
    to_other[nodes, 2:3, :] = section[...]
    to_other[nodes, 3:4, :] = (cells[0:1, :] + 1).astype(jnp.float32)


def relay_kernel(by_other, prepared, near):
    del prepared
    near[...] = by_other[by_other.shape[0] - 1, 0:2, :]


def picking(reach, rows, key, lane, takes, masks):
    for block in range(key.shape[1] // LANES):
        mine = slice(block * LANES, (block + 1) * LANES)

        def column(row):
            wide = jnp.broadcast_to(row[:, mine].astype(jnp.float32), (LANES, LANES))
            return jnp.transpose(wide).astype(jnp.int32)

        spread = lanes_of(LANES)
        at = column(key)
        after = jnp.where(at < 0, at, at + rows)
        for first in range(0, takes.shape[2], LANES):
            for half, place in enumerate((at, after)):
                hit = jnp.where(spread + first == place, 1.0, 0.0)
                takes[half, mine, first : first + LANES] = hit.astype(jnp.bfloat16)
        ahead = spread - column(lane)
        masks[0, mine, :] = jnp.where((ahead >= 0) & (ahead < reach), 1.0, 0.0)
        masks[1, mine, :] = jnp.where(ahead + LANES < reach, 1.0, 0.0)


def load_kernel(
    depth_in, east_in, south_in, bed_in, rough_in, table_in, *refs
):
    surf, east, south, bed, rough, table_rows, table, sems = refs
    rows, columns = depth_in.shape
    own = pl.ds(0, rows)
    copies = [
        pltpu.make_async_copy(source, target.at[own, :], sems.at[slot])
        for slot, (source, target) in enumerate(
            (
                (depth_in, surf),
                (bed_in, bed),
                (rough_in, rough),
                (east_in, east),
                (south_in, south),
            )
        )
    ]
    copies.append(pltpu.make_async_copy(table_in, table, sems.at[5]))
    for copy in copies:
        copy.start()
    copies[5].wait()
    for k in range(table_rows.shape[0]):
        table_rows[k : k + 1, :] = jnp.broadcast_to(table[:, k : k + 1], (1, LANES))
    for copy in copies[:5]:
        copy.wait()


def prepare_kernel(table_rows, rough, *refs):
    surf, east, south, bed = refs[4:8]
    mann, bed_e, bed_s, drag_e, drag_s, to_partner = refs[8:]
    ext, columns = surf.shape
    rows = ext - 2 * HALO
    chunks = columns // LANES
    even = lax.axis_index("gy") % 2 == 0
    entries = [table_rows[k : k + 1, :] for k in range(table_rows.shape[0])]
    for chunk in range(chunks):
        at = cols(chunk)
        mann[:rows, at] = looked_up(rough[:, at], entries)
        surf[:rows, at] = surf[:rows, at] + bed[:rows, at]

    kept = lax.broadcasted_iota(jnp.int32, (rows, LANES), 0) == rows - 1
    for chunk in range(chunks):
        at, then = cols(chunk), cols(min(chunk + 1, chunks - 1))
        s0, b0, m0 = surf[:rows, at], bed[:rows, at], mann[:rows, at]
        bed_max = jnp.maximum(b0, moved_left(b0, bed[:rows, then], 1))
        drag = drag_of(m0, moved_left(m0, mann[:rows, then], 1))
        bed_e[:rows, at] = bed_max
        drag_e[:rows, at] = drag
        q0 = (1.0 / SLOPE) * east[:rows, at]
        new_east = face(q0, s0, moved_left(s0, surf[:rows, then], 1), bed_max, drag)
        new_east = east_walled(new_east, chunk, chunks)
        east[:rows, at] = new_east
        bed_max = jnp.maximum(b0, moved_up(b0))
        drag = drag_of(m0, moved_up(m0))
        bed_s[:rows, at] = bed_max
        drag_s[:rows, at] = drag
        q0 = (1.0 / SLOPE) * south[:rows, at]
        new_south = jnp.where(kept, q0, face(q0, s0, moved_up(s0), bed_max, drag))
        south[:rows, at] = new_south

        def ends(value):
            return jnp.where(even, value[rows - 8 :], value[:8])

        fields = (ends(s0), ends(b0), ends(rough[:, at].astype(jnp.float32)), ends(new_east))
        blocks = border_rows(jnp.logical_not(even), fields, ends(new_south))
        for slot, block in enumerate(blocks):
            to_partner[slot * chunks + chunk] = block


def nodes_kernel(reach, surf, own, partner_section, partner_cells, *refs):
    number, total, takes, masks, windows, given_1 = refs
    rows = surf.shape[0] - 2 * HALO
    ext, columns = number.shape
    chunks = columns // LANES
    tiles = lax.axis_size("gy")
    position = lax.axis_index("gy")
    side = jnp.where(position % 2 == 0, 1, -1)
    partner = jnp.where(position + side < tiles, partner_cells[0:1, :] + 1, 0).astype(jnp.float32)
    section = jnp.concatenate([own[0:1, :], partner_section[...]], axis=1)
    cell = jnp.concatenate([own[1:2, :], partner], axis=1)
    valid, node_row, node_chunk, node_lane = located(cell, position, rows, ext, columns)
    key = jnp.where(valid, node_chunk * ext + node_row, -1)
    starts, levels = scattered(section, key, node_lane, chunks * ext)
    for chunk in range(chunks):
        at = cols(chunk)
        number[:, at] = starts[chunk * ext : (chunk + 1) * ext]
        total[:, at] = levels[chunk * ext : (chunk + 1) * ext]
    key = jnp.where(valid & (node_row < rows), node_chunk * rows + node_row, -1)
    picking(reach, rows, key, node_lane, takes, masks)
    sums = window_sums([surf[:rows, cols(chunk)] for chunk in range(chunks)], reach, True)
    for chunk in range(chunks):
        windows[:, cols(chunk)] = sums[chunk]
    give(reach, 0, surf, None, given_1)


def wall_of(ext, tiles):
    position = lax.axis_index("gy")
    rows = ext - 2 * HALO
    row = lax.broadcasted_iota(jnp.int32, (16, LANES), 0) + (ext - 16)
    return ((row == ext - 1) & (position == 0)) | ((row == rows - 1) & (position == tiles - 1))


def border_kernel(reach, tiles, by_partner, by_other, table_rows, near, *refs):
    surf, east, south, bed, mann, bed_e, bed_s, drag_e, drag_s, number, total, takes, masks = refs[11:]
    ext, columns = surf.shape
    rows = ext - 2 * HALO
    chunks = columns // LANES
    position = lax.axis_index("gy")
    even = position % 2 == 0
    beyond = by_other[4 * chunks, 2:4, :]
    section = jnp.concatenate([near[0:1, :], beyond[0:1, :]], axis=1)
    cell = jnp.concatenate([near[1:2, :], beyond[1:2, :]], axis=1)
    valid, node_row, node_chunk, node_lane = located(cell, position, rows, ext, columns)
    key = jnp.where(valid, node_chunk * ext + node_row, -1)
    starts, levels = scattered(section, key, node_lane, chunks * ext)

    entries = [table_rows[k : k + 1, :] for k in range(table_rows.shape[0])]
    row = lax.broadcasted_iota(jnp.int32, (2 * HALO, LANES), 0)
    for chunk in range(chunks):
        at = cols(chunk)
        halos = []
        flux = jnp.zeros((2 * HALO, LANES), jnp.float32)
        for slot in range(4):
            a, b = by_partner[slot * chunks + chunk], by_other[slot * chunks + chunk]
            below = jnp.where(even, a, b)
            above = jnp.where(even, b, a)
            halos.append(jnp.concatenate([below, above], axis=0))
            flux = jnp.where(row == slot, below[HALO - 1 :], flux)
            flux = jnp.where(row == HALO + slot, above[:1], flux)
        surf[rows:, at] = halos[0]
        bed[rows:, at] = halos[1]
        mann[rows:, at] = looked_up(halos[2].astype(jnp.int32), entries)
        east[rows:, at] = halos[3]
        south[rows:, at] = flux

    key = jnp.where(valid & (node_row < rows), node_chunk * rows + node_row, -1)
    owned = near.shape[1]
    picking(reach, rows, key[:, :owned], node_lane[:, :owned], takes, masks)

    wall = wall_of(ext, tiles)
    kept = lax.broadcasted_iota(jnp.int32, (16, LANES), 0) % 8 < 7
    for chunk in range(chunks):
        at, then = cols(chunk), cols(min(chunk + 1, chunks - 1))
        number[:, at] += starts[chunk * ext : (chunk + 1) * ext]
        total[:, at] += levels[chunk * ext : (chunk + 1) * ext]
        b0, m0 = bed[rows:, at], mann[rows:, at]
        bed_e[rows:, at] = jnp.maximum(b0, moved_left(b0, bed[rows:, then], 1))
        drag_e[rows:, at] = drag_of(m0, moved_left(m0, mann[rows:, then], 1))

        def rolled_up(ref):
            value = jnp.concatenate([ref[rows - 8 :, at], ref[:8, at]], axis=0)
            return value[:16], moved_up(value)[:16]

        s0, s1 = rolled_up(surf)
        b0, b1 = rolled_up(bed)
        m0, m1 = rolled_up(mann)
        bed_max = jnp.maximum(b0, b1)
        drag = drag_of(m0, m1)
        bed_s[rows - 8 :, at] = bed_max
        drag_s[rows - 8 :, at] = drag
        q0 = south[rows - 8 :, at]
        new_south = jnp.where(kept, q0, face(q0, s0, s1, bed_max, drag))
        south[rows - 8 :, at] = jnp.where(wall, 0.0, new_south)


def fluxes(mine, upper, wall, before, faces, east_out, south_out, scale=None):
    surf, east, south = before
    bed_e, bed_s, drag_e, drag_s = faces
    ext, columns = surf.shape
    chunks = columns // LANES
    rolled = pltpu.roll(surf[mine, cols(0)], LANES - 1, 1)
    lane = lanes_of(rolled.shape[0])
    for chunk in range(chunks):
        at = cols(chunk)
        s0 = surf[mine, at]
        rolled_then = rolled
        if chunk + 1 < chunks:
            rolled_then = pltpu.roll(surf[mine, cols(chunk + 1)], LANES - 1, 1)
        left = jnp.where(lane >= LANES - 1, rolled_then, rolled)
        rolled = rolled_then
        new_east = face(east[mine, at], s0, left, bed_e[mine, at], drag_e[mine, at])
        if scale is not None:
            new_east = scale * new_east
        east_out[mine, at] = east_walled(new_east, chunk, chunks)
        if upper:
            s0 = surf[: upper + 8, at]
            s1 = moved_up(s0)[:upper]
            new_south = face(south[:upper, at], s0[:upper], s1, bed_s[:upper, at], drag_s[:upper, at])
            if scale is not None:
                new_south = scale * new_south
            south_out[:upper, at] = new_south
        if wall is not None:
            low = slice(ext - 16, ext)
            s0 = jnp.concatenate([surf[low, at], surf[:8, at]], axis=0)
            s1 = moved_up(s0)[:16]
            new_south = face(south[low, at], s0[:16], s1, bed_s[low, at], drag_s[low, at])
            if scale is not None:
                new_south = scale * new_south
            south_out[low, at] = jnp.where(wall, 0.0, new_south)


def settled(mine, surf, east, south, keep, sums, spread=SPREAD * SLOPE):
    ext, columns = surf.shape
    rolled = 0.0
    for chunk in range(columns // LANES):
        at = cols(chunk)
        new_east = east[mine, at]
        new_south = south[:, at]
        lane = lanes_of(new_east.shape[0])
        rolled_before, rolled = rolled, pltpu.roll(new_east, 1, 1)
        west = jnp.where(lane < 1, rolled_before, rolled)
        north = pltpu.roll(new_south, 1, 0)[mine]
        inflow = west + north
        s0 = surf[mine, at]
        outflow = new_east + new_south[mine]
        yield chunk, keep[mine, at] * s0 + (spread * (inflow - outflow) + sums[chunk])


def exchange(corridor, mine, surf, total, count, total_out, windows=None):
    chunks = surf.shape[1] // LANES
    sums = window_sums([total[mine, cols(chunk)] for chunk in range(chunks)], corridor, False)
    if total_out is not None:
        if windows is None:
            windows = window_sums(
                [surf[mine, cols(chunk)] for chunk in range(chunks)], corridor, True
            )
        for chunk in range(chunks):
            at = cols(chunk)
            kept = (1.0 - corridor * DRAIN) * total[mine, at]
            total_out[mine, at] = kept + count[mine, at] * windows[chunk]
    return sums


def give(corridor, step, surf, before, after):
    rows, columns = after.shape
    weight = DRAIN * (1.0 - corridor * DRAIN) ** (STEPS - 1 - step)
    for chunk in range(columns // LANES):
        at = cols(chunk)
        value = weight * surf[:rows, at]
        after[:, at] = value if before is None else before[:, at] + value


def first_kernel(corridor, surf, east, south, number, total, windows, *refs):
    surf_1, total_1, count, keep, total_0 = refs
    rows = surf.shape[0] - 2 * HALO
    chunks = surf.shape[1] // LANES
    own = slice(0, rows)
    covering = window_sums([number[own, cols(chunk)] for chunk in range(chunks)], corridor, False)
    for chunk in range(chunks):
        at = cols(chunk)
        count[own, at] = (FEED * DRAIN) * number[own, at]
        keep[own, at] = 1.0 - FEED * covering[chunk]
        total_0[own, at] = FEED * total[own, at]
    windows = [windows[:, cols(chunk)] for chunk in range(chunks)]
    sums = exchange(corridor, own, surf, total_0, count, total_1, windows)
    for chunk, new_surf in settled(own, surf, east, south, keep, sums):
        surf_1[own, cols(chunk)] = new_surf


def second_kernel(corridor, tiles, far, surf, east, south, *refs):
    faces = refs[:4]
    number, total, given_1 = refs[4:7]
    surf_1, total_1, count, keep = refs[11:15]
    surf_2, east_2, south_2, total_2, given_2, total_0 = refs[15:]
    ext, columns = surf.shape
    rows = ext - 2 * HALO
    chunks = columns // LANES
    position = lax.axis_index("gy")
    tail = slice(rows, ext)

    valid, node_row, node_chunk, node_lane = located(far[1:2, :], position, rows, ext, columns)
    key = jnp.where(valid & (node_row >= rows), node_chunk * 8 + (node_row - rows), -1)
    starts, levels = scattered(far[0:1, :], key, node_lane, chunks * 8)
    starting = [
        number[tail, cols(chunk)] + starts[chunk * 8 : chunk * 8 + 8] for chunk in range(chunks)
    ]
    covering = window_sums(starting, corridor, False)
    for chunk in range(chunks):
        at = cols(chunk)
        count[tail, at] = (FEED * DRAIN) * starting[chunk]
        keep[tail, at] = 1.0 - FEED * covering[chunk]
        total_0[tail, at] = FEED * (total[tail, at] + levels[chunk * 8 : chunk * 8 + 8])
    sums = exchange(corridor, tail, surf, total_0, count, total_1)

    own = slice(0, rows)
    before = (surf_1, east, south)
    fluxes(own, rows - 8, None, before, faces, east_2, south_2)
    own_sums = exchange(corridor, own, surf_1, total_1, count, total_2)
    give(corridor, 1, surf_1, given_1, given_2)

    for chunk, new_surf in settled(tail, surf, east, south, keep, sums):
        surf_1[tail, cols(chunk)] = new_surf
    tail_sums = exchange(corridor, tail, surf_1, total_1, count, total_2)
    fluxes(tail, 0, wall_of(ext, tiles), before, faces, east_2, south_2)
    for mine, sums in ((own, own_sums), (tail, tail_sums)):
        for chunk, new_surf in settled(mine, surf_1, east_2, south_2, keep, sums):
            surf_2[mine, cols(chunk)] = new_surf


def third_kernel(corridor, tiles, surf, east, south, *refs):
    faces = refs[:4]
    total, keep, count, given_2, own, takes, masks, takes_near, masks_near = refs[4:13]
    surf_3, east_3, south_3, total_3, own_term, partner_term, other_term = refs[13:]
    ext, columns = surf.shape
    rows = ext - 2 * HALO
    mine = slice(0, rows)
    owned = own.shape[1]
    chunks = columns // LANES
    sums = exchange(corridor, mine, surf, total, count, total_3)
    fluxes(
        mine, rows - 8, wall_of(ext, tiles), (surf, east, south), faces, east_3, south_3
    )
    weight = DRAIN * (1.0 - corridor * DRAIN)
    levels = []
    for chunk, new_surf in settled(mine, surf, east_3, south_3, keep, sums):
        at = cols(chunk)
        surf_3[mine, at] = new_surf
        levels.append(given_2[:, at] + weight * surf[mine, at] + DRAIN * new_surf)
    spare = takes.shape[2] - chunks * rows
    if spare:
        levels.append(jnp.zeros((spare, LANES), jnp.float32))
    levels = jnp.concatenate(levels, axis=0)
    high = levels.astype(jnp.bfloat16)
    low = (levels - high.astype(jnp.float32)).astype(jnp.bfloat16)
    picked = jnp.dot(
        jnp.concatenate([takes[0], takes_near[0], takes[1], takes_near[1]], axis=0),
        jnp.concatenate([high, low], axis=1),
        preferred_element_type=jnp.float32,
    )
    hit = jnp.concatenate([masks[0], masks_near[0], masks[1], masks_near[1]], axis=0)
    picked = (picked * jnp.concatenate([hit, hit], axis=1)).astype(jnp.bfloat16)
    picked = jnp.concatenate([picked[: 3 * owned], picked[3 * owned :]], axis=1)
    terms = lax.dot_general(
        jnp.ones((8, 4 * LANES), jnp.bfloat16),
        picked,
        (((1,), (1,)), ((), ())),
        preferred_element_type=jnp.float32,
    )[0:1]
    own_term[...] = (1.0 - corridor * DRAIN) ** STEPS * own[0:1, :] + terms[:, :owned]
    partner_term[...] = terms[:, owned : 2 * owned]
    other_term[...] = terms[:, 2 * owned :]


def last_kernel(corridor, tiles, surf_2, east_2, south_3, *refs):
    faces = refs[:4]
    total_2, total_3, keep, bed, _, east_3 = refs[4:10]
    surf_3, depth_out, east_out, south_out, depth_4, east_4, south_4, east_tail, sems = refs[10:]
    ext, columns = surf_2.shape
    rows = ext - 2 * HALO
    chunks = columns // LANES
    own, tail = slice(0, rows), slice(rows, ext)
    sums = exchange(corridor, tail, surf_2, total_2, None, None)
    fluxes(tail, 0, None, (surf_2, east_2, None), faces, east_tail, None)
    for chunk, new_surf in settled(tail, surf_2, east_tail, south_3, keep, sums):
        surf_3[tail, cols(chunk)] = new_surf

    def copy(slot, source, target, first, last):
        part = pl.ds(first * LANES, (last - first) * LANES)
        return pltpu.make_async_copy(
            source.at[pl.ds(0, rows), part], target.at[:, part], sems.at[slot]
        )

    before = (surf_3, east_3, south_3)
    fluxes(own, rows - 8, wall_of(ext, tiles), before, faces, east_4, south_4, scale=SLOPE)
    copies = [copy(0, east_4, east_out, 0, chunks), copy(1, south_4, south_out, 0, chunks)]
    for one in copies:
        one.start()
    sums = exchange(corridor, own, surf_3, total_3, None, None)
    group = 5
    for chunk, new_surf in settled(own, surf_3, east_4, south_4, keep, sums, spread=SPREAD):
        at = cols(chunk)
        depth_4[:, at] = new_surf - bed[own, at]
        if (chunk + 1) % group == 0 or chunk + 1 == chunks:
            first = chunk // group
            copies.append(copy(2 + first, depth_4, depth_out, first * group, chunk + 1))
            copies[-1].start()
    for one in copies:
        one.wait()


def local(
    depth, flux_east, flux_south, river_section, bed_level, rough_class, manning_table, bank_cell
):
    rows, columns = depth.shape
    owned = river_section.shape[0]
    corridor = bank_cell.shape[0]
    tiles = lax.axis_size("gy")
    ext = rows + 2 * HALO
    chunks = columns // LANES
    partner_section = swapped(river_section, 0).reshape(1, owned)
    partner_cells = swapped(bank_cell, 0)

    def held(value):
        return pltpu.with_memory_space_constraint(value, pltpu.VMEM)

    def far(value):
        return pltpu.with_memory_space_constraint(value, pltpu.HBM)

    params = pltpu.CompilerParams(vmem_limit_bytes=VMEM_LIMIT)
    halo = pltpu.VMEM((4 * chunks, HALO, LANES), jnp.float32)
    wide = pltpu.VMEM((4 * chunks + 1, HALO, LANES), jnp.float32)
    field = pltpu.VMEM((ext, columns), jnp.float32)
    small = pltpu.VMEM((rows, columns), jnp.float32)
    term = pltpu.VMEM((1, owned), jnp.float32)
    pair = pltpu.VMEM((2, owned), jnp.float32)
    result = pltpu.HBM((rows, columns), jnp.float32)
    cells = -(-chunks * rows // LANES) * LANES

    def call(kernel, name, outs, values, scratch=(), aliases=None):
        return pl.pallas_call(
            kernel,
            out_shape=outs,
            in_specs=[VMEM_SPEC] * len(values),
            out_specs=[HBM_SPEC if out is result else VMEM_SPEC for out in outs],
            scratch_shapes=scratch,
            input_output_aliases=aliases or {},
            compiler_params=params,
            name=name,
        )(*[held(value) for value in values])

    def picks(nodes):
        return [
            pltpu.VMEM((2, nodes, cells), jnp.bfloat16),
            pltpu.VMEM((2, nodes, LANES), jnp.float32),
        ]

    classes = manning_table.shape[0]
    table = far(manning_table.reshape(1, classes))
    table_held = pltpu.VMEM((1, classes), jnp.float32)
    to_other, own = pl.pallas_call(
        pack_kernel,
        out_shape=[wide, pair],
        in_specs=[HBM_SPEC] * 8,
        out_specs=[VMEM_SPEC] * 2,
        scratch_shapes=[
            pltpu.VMEM((4, 8, columns), jnp.float32),
            pltpu.VMEM((8, columns), jnp.int32),
            pltpu.VMEM((corridor, owned), jnp.int32),
            table_held,
            pltpu.SemaphoreType.DMA((8,)),
        ],
        compiler_params=params,
        name="pack",
    )(
        *[far(value) for value in (depth, bed_level, rough_class, flux_east, flux_south)],
        far(river_section.reshape(1, owned)),
        far(bank_cell),
        table,
    )
    (to_other,) = call(
        join_kernel,
        "join",
        [wide],
        (to_other, partner_section, partner_cells),
        aliases={0: 0},
    )
    by_other = swapped(to_other, 1)
    *loaded, rough, table_rows = pl.pallas_call(
        load_kernel,
        out_shape=[field] * 4
        + [pltpu.VMEM((rows, columns), jnp.int32), pltpu.VMEM((classes, LANES), jnp.float32)],
        in_specs=[HBM_SPEC] * 6,
        out_specs=[VMEM_SPEC] * 6,
        scratch_shapes=[table_held, pltpu.SemaphoreType.DMA((6,))],
        compiler_params=params,
        name="load",
    )(
        *[far(value) for value in (depth, flux_east, flux_south, bed_level, rough_class)],
        table,
    )
    *fields, to_partner = call(
        prepare_kernel,
        "prepare",
        [field] * 9 + [halo],
        (table_rows, rough, *loaded),
        aliases={2 + slot: slot for slot in range(4)},
    )
    by_partner = swapped(to_partner, 0)
    number, total, takes, masks, windows, given_1 = call(
        functools.partial(nodes_kernel, corridor),
        "nodes",
        [field] * 2 + picks(2 * owned) + [small] * 2,
        (fields[0], own, partner_section, partner_cells),
    )
    (near,) = call(relay_kernel, "relay", [pair], (by_other, masks))
    from_far = swapped(near, 0)
    *fields, takes_near, masks_near = call(
        functools.partial(border_kernel, corridor, tiles),
        "border",
        [field] * 11 + picks(owned),
        (by_partner, by_other, table_rows, near, *fields, number, total),
        aliases={4 + slot: slot for slot in range(11)},
    )
    surf, east, south, bed, _, *faces, number, total = fields
    surf_1, total_1, count, keep = call(
        functools.partial(first_kernel, corridor),
        "first",
        [field] * 4,
        (surf, east, south, number, total, windows),
        scratch=[field],
    )
    surf_1, total_1, count, keep, surf_2, east_2, south_2, total_2, given_2 = call(
        functools.partial(second_kernel, corridor, tiles),
        "second",
        [field] * 8 + [small],
        (
            *(from_far, surf, east, south, *faces, number, total, given_1),
            *(surf_1, total_1, count, keep),
        ),
        scratch=[field],
        aliases={11 + slot: slot for slot in range(4)},
    )
    surf_3, east_3, south_3, total_3, own_term, partner_term, other_term = call(
        functools.partial(third_kernel, corridor, tiles),
        "third",
        [field] * 4 + [term] * 3,
        (
            *(surf_2, east_2, south_2, *faces, total_2, keep, count, given_2),
            *(own, takes, masks, takes_near, masks_near),
        ),
    )
    from_other = swapped(other_term.reshape(owned), 1)
    from_partner = swapped(partner_term.reshape(owned), 0)
    _, depth, flux_east, flux_south = call(
        functools.partial(last_kernel, corridor, tiles),
        "last",
        [field, result, result, result],
        (surf_2, east_2, south_3, *faces, total_2, total_3, keep, bed, surf_3, east_3),
        scratch=[small, small, field, field, pltpu.SemaphoreType.DMA((2 + -(-chunks // 5),))],
        aliases={11: 0},
    )
    river_section = own_term.reshape(owned) + from_other + from_partner
    return (depth, flux_east, flux_south, river_section)


def solution(mesh):
    return jax.shard_map(
        local,
        mesh=mesh,
        in_specs=(
            P(("runs", "gy"), None),
            P(("runs", "gy"), None),
            P(("runs", "gy"), None),
            P(("runs", "gy")),
            P("gy", None),
            P("gy", None),
            P(),
            P(None, "gy"),
        ),
        out_specs=(
            P(("runs", "gy"), None),
            P(("runs", "gy"), None),
            P(("runs", "gy"), None),
            P(("runs", "gy")),
        ),
        check_vma=False,
    )
```

```python
import functools

import jax
import jax.numpy as jnp
from jax import lax
from jax.experimental import pallas as pl
from jax.experimental.pallas import tpu as pltpu
from jax.sharding import PartitionSpec as P

STEPS = 4

GRAV = 9.81
TSTEP = 8.0
CELL = 90.0
FLOOR = 0.05
BANK_COEF = 200.0
CELL_AREA = 8100.0
NODE_AREA = 20000.0

LANES = 128
HALO = 4
SLOPE = GRAV * TSTEP / CELL
SPREAD = TSTEP / CELL
FEED = TSTEP * BANK_COEF / CELL_AREA
DRAIN = TSTEP * BANK_COEF / NODE_AREA
VMEM_LIMIT = 32 * 1024 * 1024

VMEM_SPEC = pl.BlockSpec(memory_space=pltpu.VMEM)
HBM_SPEC = pl.BlockSpec(memory_space=pltpu.HBM)


def swapped(value, first):
    count = lax.axis_size("gy")
    pairs = []
    for low in range(first, count - 1, 2):
        pairs += [(low, low + 1), (low + 1, low)]
    return lax.ppermute(value, "gy", pairs)


def cols(chunk):
    return slice(chunk * LANES, (chunk + 1) * LANES)


def lanes_of(rows):
    return lax.broadcasted_iota(jnp.int32, (rows, LANES), 1)


def moved_left(value, following, by):
    return jnp.where(
        lanes_of(value.shape[0]) >= LANES - by,
        pltpu.roll(following, LANES - by, 1),
        pltpu.roll(value, LANES - by, 1),
    )


def moved_up(value):
    return pltpu.roll(value, value.shape[0] - 1, 0)


def split3(value):
    high = value.astype(jnp.bfloat16)
    rest = value - high.astype(jnp.float32)
    middle = rest.astype(jnp.bfloat16)
    low = (rest - middle.astype(jnp.float32)).astype(jnp.bfloat16)
    return high, middle, low


def one_hot(count, key):
    rows = lax.broadcasted_iota(jnp.int32, (count, key.shape[1]), 0)
    return jnp.where(rows == key, 1.0, 0.0)


def drag_of(mann_a, mann_b):
    pair = mann_a + mann_b
    return (0.25 * GRAV * TSTEP * SLOPE) * (pair * pair)


def looked_up(klass, entries):
    value = jnp.broadcast_to(entries[0], klass.shape)
    for k in range(1, len(entries)):
        value = jnp.where(klass == k, entries[k], value)
    return value


def face(flux, surf_a, surf_b, bed_max, drag):
    flow_depth = jnp.maximum(jnp.maximum(surf_a, surf_b) - bed_max, FLOOR)
    power = jnp.exp2((-7.0 / 3.0) * jnp.log2(flow_depth))
    driven = flux - flow_depth * (surf_b - surf_a)
    damping = 1.0 + drag * jnp.abs(flux) * power
    return driven * pl.reciprocal(damping, approx=True)


def window_sums(blocks, reach, forward):
    height = blocks[0].shape[0]
    count = len(blocks)
    spare = -(count * height) % 16
    whole = blocks + ([jnp.zeros((spare, LANES), jnp.float32)] if spare else [])
    whole = jnp.concatenate(whole, axis=0)
    high = whole.astype(jnp.bfloat16)
    low = (whole - high.astype(jnp.float32)).astype(jnp.bfloat16)
    source = lax.broadcasted_iota(jnp.int32, (2 * LANES, 2 * LANES), 0) % LANES
    target = lax.broadcasted_iota(jnp.int32, (2 * LANES, 2 * LANES), 1)
    spill = target >= LANES
    target = target % LANES
    if forward:
        ahead = source - target + jnp.where(spill, LANES, 0)
    else:
        ahead = target - source + jnp.where(spill, LANES, 0)
    band = jnp.where((ahead >= 0) & (ahead < reach), 1.0, 0.0).astype(jnp.bfloat16)
    sums = jnp.dot(
        jnp.concatenate([high, low], axis=1), band, preferred_element_type=jnp.float32
    )
    results = []
    for block in range(count):
        result = sums[block * height : (block + 1) * height, :LANES]
        beside = block + 1 if forward else block - 1
        if 0 <= beside < count:
            result = result + sums[beside * height : (beside + 1) * height, LANES:]
        results.append(result)
    return results


def east_walled(value, chunk, chunks):
    if chunk + 1 < chunks:
        return value
    return jnp.where(lanes_of(value.shape[0]) == LANES - 1, 0.0, value)


def located(cell, position, rows, ext, columns):
    base = ((position * rows - HALO) * columns + 1).astype(jnp.float32)
    offset = cell - base
    valid = (cell > 0.0) & (offset >= 0.0) & (offset < float(ext * columns))
    offset = jnp.where(valid, offset, 0.0)
    row = jnp.floor((offset + 0.5) * (1.0 / columns))
    column = (offset - row * float(columns)).astype(jnp.int32)
    row = row.astype(jnp.int32) - HALO
    row = jnp.where(row < 0, row + ext, row)
    chunk = column // LANES
    return valid, row, chunk, column - chunk * LANES


def scattered(section, key, lane, count):
    at_lane = one_hot(LANES, lane)
    parts = [at_lane] + [at_lane * part.astype(jnp.float32) for part in split3(section)]
    grid = lax.dot_general(
        one_hot(-(-count // 16) * 16, key).astype(jnp.bfloat16),
        jnp.concatenate(parts, axis=0).astype(jnp.bfloat16),
        (((1,), (1,)), ((), ())),
        preferred_element_type=jnp.float32,
    )
    number = grid[:, :LANES]
    total = (grid[:, LANES : 2 * LANES] + grid[:, 2 * LANES : 3 * LANES]) + grid[:, 3 * LANES :]
    return number, total


def border_rows(of_first, fields, south):
    outer = lax.broadcasted_iota(jnp.int32, (HALO, LANES), 0) == jnp.where(of_first, HALO - 1, 0)
    flux = jnp.where(of_first, south[:HALO], south[HALO:])
    return [
        jnp.where(outer, flux[slot : slot + 1], jnp.where(of_first, value[:HALO], value[HALO:]))
        for slot, value in enumerate(fields)
    ]


def pack_kernel(
    depth, bed, rough, east, south, section, cells, table_in, to_other, own, *refs
):
    held, held_rough, held_cells, table, sems = refs
    rows, columns = depth.shape
    chunks = columns // LANES
    even = lax.axis_index("gy") % 2 == 0
    start = pl.multiple_of(jnp.where(even, 0, rows - 8), 8)
    near = pl.ds(start, 8)
    copies = [
        pltpu.make_async_copy(source, target, sems.at[slot])
        for slot, (source, target) in enumerate(
            (
                (rough.at[near, :], held_rough),
                (bed.at[near, :], held.at[1]),
                (depth.at[near, :], held.at[0]),
                (east.at[near, :], held.at[2]),
                (south.at[near, :], held.at[3]),
                (section, own.at[pl.ds(0, 1), :]),
                (cells, held_cells),
                (table_in, table),
            )
        )
    ]
    for copy in copies:
        copy.start()
    for copy in copies:
        copy.wait()
    own[1:2, :] = (held_cells[0:1, :] + 1).astype(jnp.float32)
    entries = [
        jnp.broadcast_to(table[:, k : k + 1], (1, LANES)) for k in range(table.shape[1])
    ]
    manns = [looked_up(held_rough[:, cols(chunk)], entries) for chunk in range(chunks)]
    row = lax.broadcasted_iota(jnp.int32, (8, LANES), 0)
    beds = [held[1, :, cols(chunk)] for chunk in range(chunks)]
    surfs = [held[0, :, cols(chunk)] + beds[chunk] for chunk in range(chunks)]

    def moved(values):
        rolled = [pltpu.roll(value, LANES - 1, 1) for value in values]
        rolled.append(rolled[-1])
        edge = lanes_of(8) == LANES - 1
        return [jnp.where(edge, rolled[c + 1], rolled[c]) for c in range(chunks)]

    beds_left, surfs_left, manns_left = moved(beds), moved(surfs), moved(manns)
    for chunk in range(chunks):
        at = cols(chunk)
        m0, b0, s0 = manns[chunk], beds[chunk], surfs[chunk]
        bed_max = jnp.maximum(b0, beds_left[chunk])
        drag = drag_of(m0, manns_left[chunk])
        q0 = (1.0 / SLOPE) * held[2, :, at]
        new_east = face(q0, s0, surfs_left[chunk], bed_max, drag)
        new_east = east_walled(new_east, chunk, chunks)
        bed_max = jnp.maximum(b0, moved_up(b0))
        drag = drag_of(m0, moved_up(m0))
        q0 = (1.0 / SLOPE) * held[3, :, at]
        new_south = jnp.where(row == 7, q0, face(q0, s0, moved_up(s0), bed_max, drag))
        fields = (s0, b0, held_rough[:, at].astype(jnp.float32), new_east)
        for slot, block in enumerate(border_rows(even, fields, new_south)):
            to_other[slot * chunks + chunk] = block
    to_other[4 * chunks, 0:2, :] = own[...]


def join_kernel(before, section, cells, to_other):
    nodes = to_other.shape[0] - 1
    to_other[nodes, 2:3, :] = section[...]
    to_other[nodes, 3:4, :] = (cells[0:1, :] + 1).astype(jnp.float32)


def relay_kernel(by_other, prepared, near):
    del prepared
    near[...] = by_other[by_other.shape[0] - 1, 0:2, :]


def picking(reach, rows, key, lane, takes, masks):
    for block in range(key.shape[1] // LANES):
        mine = slice(block * LANES, (block + 1) * LANES)

        def column(row):
            wide = jnp.broadcast_to(row[:, mine].astype(jnp.float32), (LANES, LANES))
            return jnp.transpose(wide).astype(jnp.int32)

        spread = lanes_of(LANES)
        at = column(key)
        after = jnp.where(at < 0, at, at + rows)
        for first in range(0, takes.shape[2], LANES):
            for half, place in enumerate((at, after)):
                hit = jnp.where(spread + first == place, 1.0, 0.0)
                takes[half, mine, first : first + LANES] = hit.astype(jnp.bfloat16)
        ahead = spread - column(lane)
        masks[0, mine, :] = jnp.where((ahead >= 0) & (ahead < reach), 1.0, 0.0)
        masks[1, mine, :] = jnp.where(ahead + LANES < reach, 1.0, 0.0)


def load_kernel(
    depth_in, east_in, south_in, bed_in, rough_in, table_in, *refs
):
    surf, east, south, bed, rough, table_rows, table, sems = refs
    rows, columns = depth_in.shape
    own = pl.ds(0, rows)
    copies = [
        pltpu.make_async_copy(source, target.at[own, :], sems.at[slot])
        for slot, (source, target) in enumerate(
            (
                (depth_in, surf),
                (bed_in, bed),
                (rough_in, rough),
                (east_in, east),
                (south_in, south),
            )
        )
    ]
    copies.append(pltpu.make_async_copy(table_in, table, sems.at[5]))
    for copy in copies:
        copy.start()
    copies[5].wait()
    for k in range(table_rows.shape[0]):
        table_rows[k : k + 1, :] = jnp.broadcast_to(table[:, k : k + 1], (1, LANES))
    for copy in copies[:5]:
        copy.wait()


def prepare_kernel(table_rows, rough, *refs):
    surf, east, south, bed = refs[4:8]
    mann, bed_e, bed_s, drag_e, drag_s, to_partner = refs[8:]
    ext, columns = surf.shape
    rows = ext - 2 * HALO
    chunks = columns // LANES
    even = lax.axis_index("gy") % 2 == 0
    entries = [table_rows[k : k + 1, :] for k in range(table_rows.shape[0])]
    for chunk in range(chunks):
        at = cols(chunk)
        mann[:rows, at] = looked_up(rough[:, at], entries)
        surf[:rows, at] = surf[:rows, at] + bed[:rows, at]

    kept = lax.broadcasted_iota(jnp.int32, (rows, LANES), 0) == rows - 1
    for chunk in range(chunks):
        at, then = cols(chunk), cols(min(chunk + 1, chunks - 1))
        s0, b0, m0 = surf[:rows, at], bed[:rows, at], mann[:rows, at]
        bed_max = jnp.maximum(b0, moved_left(b0, bed[:rows, then], 1))
        drag = drag_of(m0, moved_left(m0, mann[:rows, then], 1))
        bed_e[:rows, at] = bed_max
        drag_e[:rows, at] = drag
        q0 = (1.0 / SLOPE) * east[:rows, at]
        new_east = face(q0, s0, moved_left(s0, surf[:rows, then], 1), bed_max, drag)
        new_east = east_walled(new_east, chunk, chunks)
        east[:rows, at] = new_east
        bed_max = jnp.maximum(b0, moved_up(b0))
        drag = drag_of(m0, moved_up(m0))
        bed_s[:rows, at] = bed_max
        drag_s[:rows, at] = drag
        q0 = (1.0 / SLOPE) * south[:rows, at]
        new_south = jnp.where(kept, q0, face(q0, s0, moved_up(s0), bed_max, drag))
        south[:rows, at] = new_south

        def ends(value):
            return jnp.where(even, value[rows - 8 :], value[:8])

        fields = (ends(s0), ends(b0), ends(rough[:, at].astype(jnp.float32)), ends(new_east))
        blocks = border_rows(jnp.logical_not(even), fields, ends(new_south))
        for slot, block in enumerate(blocks):
            to_partner[slot * chunks + chunk] = block


def nodes_kernel(reach, surf, own, partner_section, partner_cells, *refs):
    number, total, takes, masks, windows, given_1 = refs
    rows = surf.shape[0] - 2 * HALO
    ext, columns = number.shape
    chunks = columns // LANES
    tiles = lax.axis_size("gy")
    position = lax.axis_index("gy")
    side = jnp.where(position % 2 == 0, 1, -1)
    partner = jnp.where(position + side < tiles, partner_cells[0:1, :] + 1, 0).astype(jnp.float32)
    section = jnp.concatenate([own[0:1, :], partner_section[...]], axis=1)
    cell = jnp.concatenate([own[1:2, :], partner], axis=1)
    valid, node_row, node_chunk, node_lane = located(cell, position, rows, ext, columns)
    key = jnp.where(valid, node_chunk * ext + node_row, -1)
    starts, levels = scattered(section, key, node_lane, chunks * ext)
    for chunk in range(chunks):
        at = cols(chunk)
        number[:, at] = starts[chunk * ext : (chunk + 1) * ext]
        total[:, at] = levels[chunk * ext : (chunk + 1) * ext]
    key = jnp.where(valid & (node_row < rows), node_chunk * rows + node_row, -1)
    picking(reach, rows, key, node_lane, takes, masks)
    sums = window_sums([surf[:rows, cols(chunk)] for chunk in range(chunks)], reach, True)
    for chunk in range(chunks):
        windows[:, cols(chunk)] = sums[chunk]
    give(reach, 0, surf, None, given_1)


def wall_of(ext, tiles):
    position = lax.axis_index("gy")
    rows = ext - 2 * HALO
    row = lax.broadcasted_iota(jnp.int32, (16, LANES), 0) + (ext - 16)
    return ((row == ext - 1) & (position == 0)) | ((row == rows - 1) & (position == tiles - 1))


def border_kernel(reach, tiles, by_partner, by_other, table_rows, near, *refs):
    surf, east, south, bed, mann, bed_e, bed_s, drag_e, drag_s, number, total, takes, masks = refs[11:]
    ext, columns = surf.shape
    rows = ext - 2 * HALO
    chunks = columns // LANES
    position = lax.axis_index("gy")
    even = position % 2 == 0
    beyond = by_other[4 * chunks, 2:4, :]
    section = jnp.concatenate([near[0:1, :], beyond[0:1, :]], axis=1)
    cell = jnp.concatenate([near[1:2, :], beyond[1:2, :]], axis=1)
    valid, node_row, node_chunk, node_lane = located(cell, position, rows, ext, columns)
    key = jnp.where(valid, node_chunk * ext + node_row, -1)
    starts, levels = scattered(section, key, node_lane, chunks * ext)

    entries = [table_rows[k : k + 1, :] for k in range(table_rows.shape[0])]
    row = lax.broadcasted_iota(jnp.int32, (2 * HALO, LANES), 0)
    for chunk in range(chunks):
        at = cols(chunk)
        halos = []
        flux = jnp.zeros((2 * HALO, LANES), jnp.float32)
        for slot in range(4):
            a, b = by_partner[slot * chunks + chunk], by_other[slot * chunks + chunk]
            below = jnp.where(even, a, b)
            above = jnp.where(even, b, a)
            halos.append(jnp.concatenate([below, above], axis=0))
            flux = jnp.where(row == slot, below[HALO - 1 :], flux)
            flux = jnp.where(row == HALO + slot, above[:1], flux)
        surf[rows:, at] = halos[0]
        bed[rows:, at] = halos[1]
        mann[rows:, at] = looked_up(halos[2].astype(jnp.int32), entries)
        east[rows:, at] = halos[3]
        south[rows:, at] = flux

    key = jnp.where(valid & (node_row < rows), node_chunk * rows + node_row, -1)
    owned = near.shape[1]
    picking(reach, rows, key[:, :owned], node_lane[:, :owned], takes, masks)

    wall = wall_of(ext, tiles)
    kept = lax.broadcasted_iota(jnp.int32, (16, LANES), 0) % 8 < 7
    for chunk in range(chunks):
        at, then = cols(chunk), cols(min(chunk + 1, chunks - 1))
        number[:, at] += starts[chunk * ext : (chunk + 1) * ext]
        total[:, at] += levels[chunk * ext : (chunk + 1) * ext]
        b0, m0 = bed[rows:, at], mann[rows:, at]
        bed_e[rows:, at] = jnp.maximum(b0, moved_left(b0, bed[rows:, then], 1))
        drag_e[rows:, at] = drag_of(m0, moved_left(m0, mann[rows:, then], 1))

        def rolled_up(ref):
            value = jnp.concatenate([ref[rows - 8 :, at], ref[:8, at]], axis=0)
            return value[:16], moved_up(value)[:16]

        s0, s1 = rolled_up(surf)
        b0, b1 = rolled_up(bed)
        m0, m1 = rolled_up(mann)
        bed_max = jnp.maximum(b0, b1)
        drag = drag_of(m0, m1)
        bed_s[rows - 8 :, at] = bed_max
        drag_s[rows - 8 :, at] = drag
        q0 = south[rows - 8 :, at]
        new_south = jnp.where(kept, q0, face(q0, s0, s1, bed_max, drag))
        south[rows - 8 :, at] = jnp.where(wall, 0.0, new_south)


def fluxes(mine, upper, wall, before, faces, east_out, south_out, scale=None):
    surf, east, south = before
    bed_e, bed_s, drag_e, drag_s = faces
    ext, columns = surf.shape
    chunks = columns // LANES
    rolled = pltpu.roll(surf[mine, cols(0)], LANES - 1, 1)
    lane = lanes_of(rolled.shape[0])
    for chunk in range(chunks):
        at = cols(chunk)
        s0 = surf[mine, at]
        rolled_then = rolled
        if chunk + 1 < chunks:
            rolled_then = pltpu.roll(surf[mine, cols(chunk + 1)], LANES - 1, 1)
        left = jnp.where(lane >= LANES - 1, rolled_then, rolled)
        rolled = rolled_then
        new_east = face(east[mine, at], s0, left, bed_e[mine, at], drag_e[mine, at])
        if scale is not None:
            new_east = scale * new_east
        east_out[mine, at] = east_walled(new_east, chunk, chunks)
        if upper:
            s0 = surf[: upper + 8, at]
            s1 = moved_up(s0)[:upper]
            new_south = face(south[:upper, at], s0[:upper], s1, bed_s[:upper, at], drag_s[:upper, at])
            if scale is not None:
                new_south = scale * new_south
            south_out[:upper, at] = new_south
        if wall is not None:
            low = slice(ext - 16, ext)
            s0 = jnp.concatenate([surf[low, at], surf[:8, at]], axis=0)
            s1 = moved_up(s0)[:16]
            new_south = face(south[low, at], s0[:16], s1, bed_s[low, at], drag_s[low, at])
            if scale is not None:
                new_south = scale * new_south
            south_out[low, at] = jnp.where(wall, 0.0, new_south)


def settled(mine, surf, east, south, keep, sums, spread=SPREAD * SLOPE):
    ext, columns = surf.shape
    rolled = 0.0
    for chunk in range(columns // LANES):
        at = cols(chunk)
        new_east = east[mine, at]
        new_south = south[:, at]
        lane = lanes_of(new_east.shape[0])
        rolled_before, rolled = rolled, pltpu.roll(new_east, 1, 1)
        west = jnp.where(lane < 1, rolled_before, rolled)
        north = pltpu.roll(new_south, 1, 0)[mine]
        inflow = west + north
        s0 = surf[mine, at]
        outflow = new_east + new_south[mine]
        yield chunk, keep[mine, at] * s0 + (spread * (inflow - outflow) + sums[chunk])


def exchange(corridor, mine, surf, total, count, total_out, windows=None):
    chunks = surf.shape[1] // LANES
    sums = window_sums([total[mine, cols(chunk)] for chunk in range(chunks)], corridor, False)
    if total_out is not None:
        if windows is None:
            windows = window_sums(
                [surf[mine, cols(chunk)] for chunk in range(chunks)], corridor, True
            )
        for chunk in range(chunks):
            at = cols(chunk)
            kept = (1.0 - corridor * DRAIN) * total[mine, at]
            total_out[mine, at] = kept + count[mine, at] * windows[chunk]
    return sums


def give(corridor, step, surf, before, after):
    rows, columns = after.shape
    weight = DRAIN * (1.0 - corridor * DRAIN) ** (STEPS - 1 - step)
    for chunk in range(columns // LANES):
        at = cols(chunk)
        value = weight * surf[:rows, at]
        after[:, at] = value if before is None else before[:, at] + value


def first_kernel(corridor, surf, east, south, number, total, windows, *refs):
    surf_1, total_1, count, keep, total_0 = refs
    rows = surf.shape[0] - 2 * HALO
    chunks = surf.shape[1] // LANES
    own = slice(0, rows)
    covering = window_sums([number[own, cols(chunk)] for chunk in range(chunks)], corridor, False)
    for chunk in range(chunks):
        at = cols(chunk)
        count[own, at] = (FEED * DRAIN) * number[own, at]
        keep[own, at] = 1.0 - FEED * covering[chunk]
        total_0[own, at] = FEED * total[own, at]
    windows = [windows[:, cols(chunk)] for chunk in range(chunks)]
    sums = exchange(corridor, own, surf, total_0, count, total_1, windows)
    for chunk, new_surf in settled(own, surf, east, south, keep, sums):
        surf_1[own, cols(chunk)] = new_surf


def second_kernel(corridor, tiles, far, surf, east, south, *refs):
    faces = refs[:4]
    number, total, given_1 = refs[4:7]
    surf_1, total_1, count, keep = refs[11:15]
    surf_2, east_2, south_2, total_2, given_2, total_0 = refs[15:]
    ext, columns = surf.shape
    rows = ext - 2 * HALO
    chunks = columns // LANES
    position = lax.axis_index("gy")
    tail = slice(rows, ext)

    valid, node_row, node_chunk, node_lane = located(far[1:2, :], position, rows, ext, columns)
    key = jnp.where(valid & (node_row >= rows), node_chunk * 8 + (node_row - rows), -1)
    starts, levels = scattered(far[0:1, :], key, node_lane, chunks * 8)
    starting = [
        number[tail, cols(chunk)] + starts[chunk * 8 : chunk * 8 + 8] for chunk in range(chunks)
    ]
    covering = window_sums(starting, corridor, False)
    for chunk in range(chunks):
        at = cols(chunk)
        count[tail, at] = (FEED * DRAIN) * starting[chunk]
        keep[tail, at] = 1.0 - FEED * covering[chunk]
        total_0[tail, at] = FEED * (total[tail, at] + levels[chunk * 8 : chunk * 8 + 8])
    sums = exchange(corridor, tail, surf, total_0, count, total_1)

    own = slice(0, rows)
    before = (surf_1, east, south)
    fluxes(own, rows - 8, None, before, faces, east_2, south_2)
    own_sums = exchange(corridor, own, surf_1, total_1, count, total_2)
    give(corridor, 1, surf_1, given_1, given_2)

    for chunk, new_surf in settled(tail, surf, east, south, keep, sums):
        surf_1[tail, cols(chunk)] = new_surf
    tail_sums = exchange(corridor, tail, surf_1, total_1, count, total_2)
    fluxes(tail, 0, wall_of(ext, tiles), before, faces, east_2, south_2)
    for mine, sums in ((own, own_sums), (tail, tail_sums)):
        for chunk, new_surf in settled(mine, surf_1, east_2, south_2, keep, sums):
            surf_2[mine, cols(chunk)] = new_surf


def third_kernel(corridor, tiles, surf, east, south, *refs):
    faces = refs[:4]
    total, keep, count, given_2, own, takes, masks, takes_near, masks_near = refs[4:13]
    surf_3, east_3, south_3, total_3, own_term, sent = refs[13:]
    ext, columns = surf.shape
    rows = ext - 2 * HALO
    mine = slice(0, rows)
    owned = own.shape[1]
    chunks = columns // LANES
    sums = exchange(corridor, mine, surf, total, count, total_3)
    fluxes(
        mine, rows - 8, wall_of(ext, tiles), (surf, east, south), faces, east_3, south_3
    )
    weight = DRAIN * (1.0 - corridor * DRAIN)
    levels = []
    for chunk, new_surf in settled(mine, surf, east_3, south_3, keep, sums):
        at = cols(chunk)
        surf_3[mine, at] = new_surf
        levels.append(given_2[:, at] + weight * surf[mine, at] + DRAIN * new_surf)
    spare = takes.shape[2] - chunks * rows
    if spare:
        levels.append(jnp.zeros((spare, LANES), jnp.float32))
    levels = jnp.concatenate(levels, axis=0)
    high = levels.astype(jnp.bfloat16)
    low = (levels - high.astype(jnp.float32)).astype(jnp.bfloat16)
    picked = jnp.dot(
        jnp.concatenate([takes[0], takes_near[0], takes[1], takes_near[1]], axis=0),
        jnp.concatenate([high, low], axis=1),
        preferred_element_type=jnp.float32,
    )
    hit = jnp.concatenate([masks[0], masks_near[0], masks[1], masks_near[1]], axis=0)
    picked = (picked * jnp.concatenate([hit, hit], axis=1)).astype(jnp.bfloat16)
    picked = jnp.concatenate([picked[: 3 * owned], picked[3 * owned :]], axis=1)
    terms = lax.dot_general(
        jnp.ones((8, 4 * LANES), jnp.bfloat16),
        picked,
        (((1,), (1,)), ((), ())),
        preferred_element_type=jnp.float32,
    )[0:1]
    own_term[...] = (1.0 - corridor * DRAIN) ** STEPS * own[0:1, :] + terms[:, :owned]
    position = lax.axis_index("gy")
    side = jnp.where(position % 2 == 0, 1, -1)
    tile = lax.broadcasted_iota(jnp.int32, (tiles, owned), 0)
    sent[...] = jnp.where(tile == position + side, terms[:, owned : 2 * owned], 0.0) + jnp.where(
        tile == position - side, terms[:, 2 * owned :], 0.0
    )


def last_kernel(corridor, tiles, surf_2, east_2, south_3, *refs):
    faces = refs[:4]
    total_2, total_3, keep, bed, _, east_3 = refs[4:10]
    surf_3, depth_out, east_out, south_out, depth_4, east_4, south_4, east_tail, sems = refs[10:]
    ext, columns = surf_2.shape
    rows = ext - 2 * HALO
    chunks = columns // LANES
    own, tail = slice(0, rows), slice(rows, ext)
    sums = exchange(corridor, tail, surf_2, total_2, None, None)
    fluxes(tail, 0, None, (surf_2, east_2, None), faces, east_tail, None)
    for chunk, new_surf in settled(tail, surf_2, east_tail, south_3, keep, sums):
        surf_3[tail, cols(chunk)] = new_surf

    def copy(slot, source, target, first, last):
        part = pl.ds(first * LANES, (last - first) * LANES)
        return pltpu.make_async_copy(
            source.at[pl.ds(0, rows), part], target.at[:, part], sems.at[slot]
        )

    before = (surf_3, east_3, south_3)
    fluxes(own, rows - 8, wall_of(ext, tiles), before, faces, east_4, south_4, scale=SLOPE)
    copies = [copy(0, east_4, east_out, 0, chunks), copy(1, south_4, south_out, 0, chunks)]
    for one in copies:
        one.start()
    sums = exchange(corridor, own, surf_3, total_3, None, None)
    group = 5
    for chunk, new_surf in settled(own, surf_3, east_4, south_4, keep, sums, spread=SPREAD):
        at = cols(chunk)
        depth_4[:, at] = new_surf - bed[own, at]
        if (chunk + 1) % group == 0 or chunk + 1 == chunks:
            first = chunk // group
            copies.append(copy(2 + first, depth_4, depth_out, first * group, chunk + 1))
            copies[-1].start()
    for one in copies:
        one.wait()


def local(
    depth, flux_east, flux_south, river_section, bed_level, rough_class, manning_table, bank_cell
):
    rows, columns = depth.shape
    owned = river_section.shape[0]
    corridor = bank_cell.shape[0]
    tiles = lax.axis_size("gy")
    ext = rows + 2 * HALO
    chunks = columns // LANES
    partner_section = swapped(river_section, 0).reshape(1, owned)
    partner_cells = swapped(bank_cell, 0)

    def held(value):
        return pltpu.with_memory_space_constraint(value, pltpu.VMEM)

    def far(value):
        return pltpu.with_memory_space_constraint(value, pltpu.HBM)

    params = pltpu.CompilerParams(vmem_limit_bytes=VMEM_LIMIT)
    halo = pltpu.VMEM((4 * chunks, HALO, LANES), jnp.float32)
    wide = pltpu.VMEM((4 * chunks + 1, HALO, LANES), jnp.float32)
    field = pltpu.VMEM((ext, columns), jnp.float32)
    small = pltpu.VMEM((rows, columns), jnp.float32)
    term = pltpu.VMEM((1, owned), jnp.float32)
    pair = pltpu.VMEM((2, owned), jnp.float32)
    result = pltpu.HBM((rows, columns), jnp.float32)
    cells = -(-chunks * rows // LANES) * LANES

    def call(kernel, name, outs, values, scratch=(), aliases=None):
        return pl.pallas_call(
            kernel,
            out_shape=outs,
            in_specs=[VMEM_SPEC] * len(values),
            out_specs=[HBM_SPEC if out is result else VMEM_SPEC for out in outs],
            scratch_shapes=scratch,
            input_output_aliases=aliases or {},
            compiler_params=params,
            name=name,
        )(*[held(value) for value in values])

    def picks(nodes):
        return [
            pltpu.VMEM((2, nodes, cells), jnp.bfloat16),
            pltpu.VMEM((2, nodes, LANES), jnp.float32),
        ]

    classes = manning_table.shape[0]
    table = far(manning_table.reshape(1, classes))
    table_held = pltpu.VMEM((1, classes), jnp.float32)
    to_other, own = pl.pallas_call(
        pack_kernel,
        out_shape=[wide, pair],
        in_specs=[HBM_SPEC] * 8,
        out_specs=[VMEM_SPEC] * 2,
        scratch_shapes=[
            pltpu.VMEM((4, 8, columns), jnp.float32),
            pltpu.VMEM((8, columns), jnp.int32),
            pltpu.VMEM((corridor, owned), jnp.int32),
            table_held,
            pltpu.SemaphoreType.DMA((8,)),
        ],
        compiler_params=params,
        name="pack",
    )(
        *[far(value) for value in (depth, bed_level, rough_class, flux_east, flux_south)],
        far(river_section.reshape(1, owned)),
        far(bank_cell),
        table,
    )
    (to_other,) = call(
        join_kernel,
        "join",
        [wide],
        (to_other, partner_section, partner_cells),
        aliases={0: 0},
    )
    by_other = swapped(to_other, 1)
    *loaded, rough, table_rows = pl.pallas_call(
        load_kernel,
        out_shape=[field] * 4
        + [pltpu.VMEM((rows, columns), jnp.int32), pltpu.VMEM((classes, LANES), jnp.float32)],
        in_specs=[HBM_SPEC] * 6,
        out_specs=[VMEM_SPEC] * 6,
        scratch_shapes=[table_held, pltpu.SemaphoreType.DMA((6,))],
        compiler_params=params,
        name="load",
    )(
        *[far(value) for value in (depth, flux_east, flux_south, bed_level, rough_class)],
        table,
    )
    *fields, to_partner = call(
        prepare_kernel,
        "prepare",
        [field] * 9 + [halo],
        (table_rows, rough, *loaded),
        aliases={2 + slot: slot for slot in range(4)},
    )
    by_partner = swapped(to_partner, 0)
    number, total, takes, masks, windows, given_1 = call(
        functools.partial(nodes_kernel, corridor),
        "nodes",
        [field] * 2 + picks(2 * owned) + [small] * 2,
        (fields[0], own, partner_section, partner_cells),
    )
    (near,) = call(relay_kernel, "relay", [pair], (by_other, masks))
    from_far = swapped(near, 0)
    *fields, takes_near, masks_near = call(
        functools.partial(border_kernel, corridor, tiles),
        "border",
        [field] * 11 + picks(owned),
        (by_partner, by_other, table_rows, near, *fields, number, total),
        aliases={4 + slot: slot for slot in range(11)},
    )
    surf, east, south, bed, _, *faces, number, total = fields
    surf_1, total_1, count, keep = call(
        functools.partial(first_kernel, corridor),
        "first",
        [field] * 4,
        (surf, east, south, number, total, windows),
        scratch=[field],
    )
    surf_1, total_1, count, keep, surf_2, east_2, south_2, total_2, given_2 = call(
        functools.partial(second_kernel, corridor, tiles),
        "second",
        [field] * 8 + [small],
        (
            *(from_far, surf, east, south, *faces, number, total, given_1),
            *(surf_1, total_1, count, keep),
        ),
        scratch=[field],
        aliases={11 + slot: slot for slot in range(4)},
    )
    surf_3, east_3, south_3, total_3, own_term, sent = call(
        functools.partial(third_kernel, corridor, tiles),
        "third",
        [field] * 4 + [term, pltpu.VMEM((tiles, owned), jnp.float32)],
        (
            *(surf_2, east_2, south_2, *faces, total_2, keep, count, given_2),
            *(own, takes, masks, takes_near, masks_near),
        ),
    )
    received = lax.all_to_all(sent, "gy", 0, 0, tiled=True)
    _, depth, flux_east, flux_south = call(
        functools.partial(last_kernel, corridor, tiles),
        "last",
        [field, result, result, result],
        (surf_2, east_2, south_3, *faces, total_2, total_3, keep, bed, surf_3, east_3),
        scratch=[small, small, field, field, pltpu.SemaphoreType.DMA((2 + -(-chunks // 5),))],
        aliases={11: 0},
    )
    river_section = own_term.reshape(owned) + jnp.sum(received, axis=0)
    return (depth, flux_east, flux_south, river_section)


def solution(mesh):
    return jax.shard_map(
        local,
        mesh=mesh,
        in_specs=(
            P(("runs", "gy"), None),
            P(("runs", "gy"), None),
            P(("runs", "gy"), None),
            P(("runs", "gy")),
            P("gy", None),
            P("gy", None),
            P(),
            P(None, "gy"),
        ),
        out_specs=(
            P(("runs", "gy"), None),
            P(("runs", "gy"), None),
            P(("runs", "gy"), None),
            P(("runs", "gy")),
        ),
        check_vma=False,
    )
```

```python
import functools

import jax
import jax.numpy as jnp
from jax import lax
from jax.experimental import pallas as pl
from jax.experimental.pallas import tpu as pltpu
from jax.sharding import PartitionSpec as P

STEPS = 4

GRAV = 9.81
TSTEP = 8.0
CELL = 90.0
FLOOR = 0.05
BANK_COEF = 200.0
CELL_AREA = 8100.0
NODE_AREA = 20000.0

LANES = 128
HALO = 4
SLOPE = GRAV * TSTEP / CELL
SPREAD = TSTEP / CELL
FEED = TSTEP * BANK_COEF / CELL_AREA
DRAIN = TSTEP * BANK_COEF / NODE_AREA
VMEM_LIMIT = 32 * 1024 * 1024

VMEM_SPEC = pl.BlockSpec(memory_space=pltpu.VMEM)
HBM_SPEC = pl.BlockSpec(memory_space=pltpu.HBM)


def swapped(value, first):
    count = lax.axis_size("gy")
    pairs = []
    for low in range(first, count - 1, 2):
        pairs += [(low, low + 1), (low + 1, low)]
    return lax.ppermute(value, "gy", pairs)


def cols(chunk):
    return slice(chunk * LANES, (chunk + 1) * LANES)


def lanes_of(rows):
    return lax.broadcasted_iota(jnp.int32, (rows, LANES), 1)


def moved_left(value, following, by):
    return jnp.where(
        lanes_of(value.shape[0]) >= LANES - by,
        pltpu.roll(following, LANES - by, 1),
        pltpu.roll(value, LANES - by, 1),
    )


def moved_up(value):
    return pltpu.roll(value, value.shape[0] - 1, 0)


def split3(value):
    high = value.astype(jnp.bfloat16)
    rest = value - high.astype(jnp.float32)
    middle = rest.astype(jnp.bfloat16)
    low = (rest - middle.astype(jnp.float32)).astype(jnp.bfloat16)
    return high, middle, low


def one_hot(count, key):
    rows = lax.broadcasted_iota(jnp.int32, (count, key.shape[1]), 0)
    return jnp.where(rows == key, 1.0, 0.0)


def drag_of(mann_a, mann_b):
    pair = mann_a + mann_b
    return (0.25 * GRAV * TSTEP * SLOPE) * (pair * pair)


def looked_up(klass, entries):
    value = jnp.broadcast_to(entries[0], klass.shape)
    for k in range(1, len(entries)):
        value = jnp.where(klass == k, entries[k], value)
    return value


def face(flux, surf_a, surf_b, bed_max, drag):
    flow_depth = jnp.maximum(jnp.maximum(surf_a, surf_b) - bed_max, FLOOR)
    power = jnp.exp2((-7.0 / 3.0) * jnp.log2(flow_depth))
    driven = flux - flow_depth * (surf_b - surf_a)
    damping = 1.0 + drag * jnp.abs(flux) * power
    return driven * pl.reciprocal(damping, approx=True)


def window_sums(blocks, reach, forward):
    height = blocks[0].shape[0]
    count = len(blocks)
    spare = -(count * height) % 16
    whole = blocks + ([jnp.zeros((spare, LANES), jnp.float32)] if spare else [])
    whole = jnp.concatenate(whole, axis=0)
    high = whole.astype(jnp.bfloat16)
    low = (whole - high.astype(jnp.float32)).astype(jnp.bfloat16)
    source = lax.broadcasted_iota(jnp.int32, (2 * LANES, 2 * LANES), 0) % LANES
    target = lax.broadcasted_iota(jnp.int32, (2 * LANES, 2 * LANES), 1)
    spill = target >= LANES
    target = target % LANES
    if forward:
        ahead = source - target + jnp.where(spill, LANES, 0)
    else:
        ahead = target - source + jnp.where(spill, LANES, 0)
    band = jnp.where((ahead >= 0) & (ahead < reach), 1.0, 0.0).astype(jnp.bfloat16)
    sums = jnp.dot(
        jnp.concatenate([high, low], axis=1), band, preferred_element_type=jnp.float32
    )
    results = []
    for block in range(count):
        result = sums[block * height : (block + 1) * height, :LANES]
        beside = block + 1 if forward else block - 1
        if 0 <= beside < count:
            result = result + sums[beside * height : (beside + 1) * height, LANES:]
        results.append(result)
    return results


def east_walled(value, chunk, chunks):
    if chunk + 1 < chunks:
        return value
    return jnp.where(lanes_of(value.shape[0]) == LANES - 1, 0.0, value)


def located(cell, position, rows, ext, columns):
    base = ((position * rows - HALO) * columns + 1).astype(jnp.float32)
    offset = cell - base
    valid = (cell > 0.0) & (offset >= 0.0) & (offset < float(ext * columns))
    offset = jnp.where(valid, offset, 0.0)
    row = jnp.floor((offset + 0.5) * (1.0 / columns))
    column = (offset - row * float(columns)).astype(jnp.int32)
    row = row.astype(jnp.int32) - HALO
    row = jnp.where(row < 0, row + ext, row)
    chunk = column // LANES
    return valid, row, chunk, column - chunk * LANES


def scattered(section, key, lane, count):
    at_lane = one_hot(LANES, lane)
    parts = [at_lane] + [at_lane * part.astype(jnp.float32) for part in split3(section)]
    grid = lax.dot_general(
        one_hot(-(-count // 16) * 16, key).astype(jnp.bfloat16),
        jnp.concatenate(parts, axis=0).astype(jnp.bfloat16),
        (((1,), (1,)), ((), ())),
        preferred_element_type=jnp.float32,
    )
    number = grid[:, :LANES]
    total = (grid[:, LANES : 2 * LANES] + grid[:, 2 * LANES : 3 * LANES]) + grid[:, 3 * LANES :]
    return number, total


def border_rows(of_first, fields, south):
    outer = lax.broadcasted_iota(jnp.int32, (HALO, LANES), 0) == jnp.where(of_first, HALO - 1, 0)
    flux = jnp.where(of_first, south[:HALO], south[HALO:])
    return [
        jnp.where(outer, flux[slot : slot + 1], jnp.where(of_first, value[:HALO], value[HALO:]))
        for slot, value in enumerate(fields)
    ]


def pack_kernel(
    depth, bed, rough, east, south, section, cells, table_in, to_other, own, *refs
):
    held, held_rough, held_cells, table, sems = refs
    rows, columns = depth.shape
    chunks = columns // LANES
    even = lax.axis_index("gy") % 2 == 0
    start = pl.multiple_of(jnp.where(even, 0, rows - 8), 8)
    near = pl.ds(start, 8)
    copies = [
        pltpu.make_async_copy(source, target, sems.at[slot])
        for slot, (source, target) in enumerate(
            (
                (table_in, table),
                (rough.at[near, :], held_rough),
                (bed.at[near, :], held.at[1]),
                (depth.at[near, :], held.at[0]),
                (east.at[near, :], held.at[2]),
                (south.at[near, :], held.at[3]),
                (section, own.at[pl.ds(0, 1), :]),
                (cells, held_cells),
            )
        )
    ]
    for copy in copies:
        copy.start()
    copies[0].wait()
    copies[1].wait()
    entries = [
        jnp.broadcast_to(table[:, k : k + 1], (1, LANES)) for k in range(table.shape[1])
    ]
    manns = [looked_up(held_rough[:, cols(chunk)], entries) for chunk in range(chunks)]
    row = lax.broadcasted_iota(jnp.int32, (8, LANES), 0)
    copies[2].wait()
    beds = [held[1, :, cols(chunk)] for chunk in range(chunks)]
    copies[3].wait()
    surfs = [held[0, :, cols(chunk)] + beds[chunk] for chunk in range(chunks)]

    def moved(values):
        rolled = [pltpu.roll(value, LANES - 1, 1) for value in values]
        rolled.append(rolled[-1])
        edge = lanes_of(8) == LANES - 1
        return [jnp.where(edge, rolled[c + 1], rolled[c]) for c in range(chunks)]

    beds_left, surfs_left, manns_left = moved(beds), moved(surfs), moved(manns)
    for copy in copies[4:]:
        copy.wait()
    own[1:2, :] = (held_cells[0:1, :] + 1).astype(jnp.float32)
    for chunk in range(chunks):
        at = cols(chunk)
        m0, b0, s0 = manns[chunk], beds[chunk], surfs[chunk]
        bed_max = jnp.maximum(b0, beds_left[chunk])
        drag = drag_of(m0, manns_left[chunk])
        q0 = (1.0 / SLOPE) * held[2, :, at]
        new_east = face(q0, s0, surfs_left[chunk], bed_max, drag)
        new_east = east_walled(new_east, chunk, chunks)
        bed_max = jnp.maximum(b0, moved_up(b0))
        drag = drag_of(m0, moved_up(m0))
        q0 = (1.0 / SLOPE) * held[3, :, at]
        new_south = jnp.where(row == 7, q0, face(q0, s0, moved_up(s0), bed_max, drag))
        fields = (s0, b0, held_rough[:, at].astype(jnp.float32), new_east)
        for slot, block in enumerate(border_rows(even, fields, new_south)):
            to_other[slot * chunks + chunk] = block
    to_other[4 * chunks, 0:2, :] = own[...]


def join_kernel(before, section, cells, to_other):
    nodes = to_other.shape[0] - 1
    to_other[nodes, 2:3, :] = section[...]
    to_other[nodes, 3:4, :] = (cells[0:1, :] + 1).astype(jnp.float32)


def relay_kernel(by_other, prepared, near, nodes):
    del prepared
    near[...] = by_other[by_other.shape[0] - 1, 0:2, :]
    nodes[...] = by_other[by_other.shape[0] - 1]


def picking(reach, rows, key, lane, takes, masks):
    for block in range(key.shape[1] // LANES):
        mine = slice(block * LANES, (block + 1) * LANES)

        def column(row):
            wide = jnp.broadcast_to(row[:, mine].astype(jnp.float32), (LANES, LANES))
            return jnp.transpose(wide).astype(jnp.int32)

        spread = lanes_of(LANES)
        at = column(key)
        after = jnp.where(at < 0, at, at + rows)
        for first in range(0, takes.shape[2], LANES):
            for half, place in enumerate((at, after)):
                hit = jnp.where(spread + first == place, 1.0, 0.0)
                takes[half, mine, first : first + LANES] = hit.astype(jnp.bfloat16)
        ahead = spread - column(lane)
        masks[0, mine, :] = jnp.where((ahead >= 0) & (ahead < reach), 1.0, 0.0)
        masks[1, mine, :] = jnp.where(ahead + LANES < reach, 1.0, 0.0)


def load_kernel(
    depth_in, east_in, south_in, bed_in, rough_in, table_in, *refs
):
    surf, east, south, bed, rough, table_rows, table, sems = refs
    rows, columns = depth_in.shape
    own = pl.ds(0, rows)
    copies = [
        pltpu.make_async_copy(source, target.at[own, :], sems.at[slot])
        for slot, (source, target) in enumerate(
            (
                (depth_in, surf),
                (bed_in, bed),
                (rough_in, rough),
                (east_in, east),
                (south_in, south),
            )
        )
    ]
    copies.append(pltpu.make_async_copy(table_in, table, sems.at[5]))
    for copy in copies:
        copy.start()
    copies[5].wait()
    for k in range(table_rows.shape[0]):
        table_rows[k : k + 1, :] = jnp.broadcast_to(table[:, k : k + 1], (1, LANES))
    for copy in copies[:5]:
        copy.wait()


def prepare_kernel(table_rows, rough, *refs):
    surf, east, south, bed = refs[4:8]
    mann, bed_e, bed_s, drag_e, drag_s, to_partner = refs[8:]
    ext, columns = surf.shape
    rows = ext - 2 * HALO
    chunks = columns // LANES
    even = lax.axis_index("gy") % 2 == 0
    entries = [table_rows[k : k + 1, :] for k in range(table_rows.shape[0])]
    for chunk in range(chunks):
        at = cols(chunk)
        mann[:rows, at] = looked_up(rough[:, at], entries)
        surf[:rows, at] = surf[:rows, at] + bed[:rows, at]

    kept = lax.broadcasted_iota(jnp.int32, (rows, LANES), 0) == rows - 1
    for chunk in range(chunks):
        at, then = cols(chunk), cols(min(chunk + 1, chunks - 1))
        s0, b0, m0 = surf[:rows, at], bed[:rows, at], mann[:rows, at]
        bed_max = jnp.maximum(b0, moved_left(b0, bed[:rows, then], 1))
        drag = drag_of(m0, moved_left(m0, mann[:rows, then], 1))
        bed_e[:rows, at] = bed_max
        drag_e[:rows, at] = drag
        q0 = (1.0 / SLOPE) * east[:rows, at]
        new_east = face(q0, s0, moved_left(s0, surf[:rows, then], 1), bed_max, drag)
        new_east = east_walled(new_east, chunk, chunks)
        east[:rows, at] = new_east
        bed_max = jnp.maximum(b0, moved_up(b0))
        drag = drag_of(m0, moved_up(m0))
        bed_s[:rows, at] = bed_max
        drag_s[:rows, at] = drag
        q0 = (1.0 / SLOPE) * south[:rows, at]
        new_south = jnp.where(kept, q0, face(q0, s0, moved_up(s0), bed_max, drag))
        south[:rows, at] = new_south

        def ends(value):
            return jnp.where(even, value[rows - 8 :], value[:8])

        fields = (ends(s0), ends(b0), ends(rough[:, at].astype(jnp.float32)), ends(new_east))
        blocks = border_rows(jnp.logical_not(even), fields, ends(new_south))
        for slot, block in enumerate(blocks):
            to_partner[slot * chunks + chunk] = block


def nodes_kernel(reach, surf, own, partner_section, partner_cells, *refs):
    number, total, takes, masks, windows, given_1 = refs
    rows = surf.shape[0] - 2 * HALO
    ext, columns = number.shape
    chunks = columns // LANES
    tiles = lax.axis_size("gy")
    position = lax.axis_index("gy")
    side = jnp.where(position % 2 == 0, 1, -1)
    partner = jnp.where(position + side < tiles, partner_cells[0:1, :] + 1, 0).astype(jnp.float32)
    section = jnp.concatenate([own[0:1, :], partner_section[...]], axis=1)
    cell = jnp.concatenate([own[1:2, :], partner], axis=1)
    valid, node_row, node_chunk, node_lane = located(cell, position, rows, ext, columns)
    key = jnp.where(valid, node_chunk * ext + node_row, -1)
    starts, levels = scattered(section, key, node_lane, chunks * ext)
    for chunk in range(chunks):
        at = cols(chunk)
        number[:, at] = starts[chunk * ext : (chunk + 1) * ext]
        total[:, at] = levels[chunk * ext : (chunk + 1) * ext]
    key = jnp.where(valid & (node_row < rows), node_chunk * rows + node_row, -1)
    picking(reach, rows, key, node_lane, takes, masks)
    sums = window_sums([surf[:rows, cols(chunk)] for chunk in range(chunks)], reach, True)
    for chunk in range(chunks):
        windows[:, cols(chunk)] = sums[chunk]
    give(reach, 0, surf, None, given_1)


def wall_of(ext, tiles):
    position = lax.axis_index("gy")
    rows = ext - 2 * HALO
    row = lax.broadcasted_iota(jnp.int32, (16, LANES), 0) + (ext - 16)
    return ((row == ext - 1) & (position == 0)) | ((row == rows - 1) & (position == tiles - 1))


def border_kernel(reach, tiles, by_partner, by_other, table_rows, near, *refs):
    surf, east, south, bed, mann, bed_e, bed_s, drag_e, drag_s, number, total, takes, masks = refs[11:]
    ext, columns = surf.shape
    rows = ext - 2 * HALO
    chunks = columns // LANES
    position = lax.axis_index("gy")
    even = position % 2 == 0
    valid, node_row, node_chunk, node_lane = located(near[1:2, :], position, rows, ext, columns)
    key = jnp.where(valid, node_chunk * ext + node_row, -1)
    starts, levels = scattered(near[0:1, :], key, node_lane, chunks * ext)

    entries = [table_rows[k : k + 1, :] for k in range(table_rows.shape[0])]
    row = lax.broadcasted_iota(jnp.int32, (2 * HALO, LANES), 0)
    for chunk in range(chunks):
        at = cols(chunk)
        halos = []
        flux = jnp.zeros((2 * HALO, LANES), jnp.float32)
        for slot in range(4):
            a, b = by_partner[slot * chunks + chunk], by_other[slot * chunks + chunk]
            below = jnp.where(even, a, b)
            above = jnp.where(even, b, a)
            halos.append(jnp.concatenate([below, above], axis=0))
            flux = jnp.where(row == slot, below[HALO - 1 :], flux)
            flux = jnp.where(row == HALO + slot, above[:1], flux)
        surf[rows:, at] = halos[0]
        bed[rows:, at] = halos[1]
        mann[rows:, at] = looked_up(halos[2].astype(jnp.int32), entries)
        east[rows:, at] = halos[3]
        south[rows:, at] = flux

    key = jnp.where(valid & (node_row < rows), node_chunk * rows + node_row, -1)
    picking(reach, rows, key, node_lane, takes, masks)

    wall = wall_of(ext, tiles)
    kept = lax.broadcasted_iota(jnp.int32, (16, LANES), 0) % 8 < 7
    for chunk in range(chunks):
        at, then = cols(chunk), cols(min(chunk + 1, chunks - 1))
        number[:, at] += starts[chunk * ext : (chunk + 1) * ext]
        total[:, at] += levels[chunk * ext : (chunk + 1) * ext]
        b0, m0 = bed[rows:, at], mann[rows:, at]
        bed_e[rows:, at] = jnp.maximum(b0, moved_left(b0, bed[rows:, then], 1))
        drag_e[rows:, at] = drag_of(m0, moved_left(m0, mann[rows:, then], 1))

        def rolled_up(ref):
            value = jnp.concatenate([ref[rows - 8 :, at], ref[:8, at]], axis=0)
            return value[:16], moved_up(value)[:16]

        s0, s1 = rolled_up(surf)
        b0, b1 = rolled_up(bed)
        m0, m1 = rolled_up(mann)
        bed_max = jnp.maximum(b0, b1)
        drag = drag_of(m0, m1)
        bed_s[rows - 8 :, at] = bed_max
        drag_s[rows - 8 :, at] = drag
        q0 = south[rows - 8 :, at]
        new_south = jnp.where(kept, q0, face(q0, s0, s1, bed_max, drag))
        south[rows - 8 :, at] = jnp.where(wall, 0.0, new_south)


def fluxes(mine, upper, wall, before, faces, east_out, south_out, scale=None):
    surf, east, south = before
    bed_e, bed_s, drag_e, drag_s = faces
    ext, columns = surf.shape
    chunks = columns // LANES
    rolled = pltpu.roll(surf[mine, cols(0)], LANES - 1, 1)
    lane = lanes_of(rolled.shape[0])
    for chunk in range(chunks):
        at = cols(chunk)
        s0 = surf[mine, at]
        rolled_then = rolled
        if chunk + 1 < chunks:
            rolled_then = pltpu.roll(surf[mine, cols(chunk + 1)], LANES - 1, 1)
        left = jnp.where(lane >= LANES - 1, rolled_then, rolled)
        rolled = rolled_then
        new_east = face(east[mine, at], s0, left, bed_e[mine, at], drag_e[mine, at])
        if scale is not None:
            new_east = scale * new_east
        east_out[mine, at] = east_walled(new_east, chunk, chunks)
        if upper:
            s0 = surf[: upper + 8, at]
            s1 = moved_up(s0)[:upper]
            new_south = face(south[:upper, at], s0[:upper], s1, bed_s[:upper, at], drag_s[:upper, at])
            if scale is not None:
                new_south = scale * new_south
            south_out[:upper, at] = new_south
        if wall is not None:
            low = slice(ext - 16, ext)
            s0 = jnp.concatenate([surf[low, at], surf[:8, at]], axis=0)
            s1 = moved_up(s0)[:16]
            new_south = face(south[low, at], s0[:16], s1, bed_s[low, at], drag_s[low, at])
            if scale is not None:
                new_south = scale * new_south
            south_out[low, at] = jnp.where(wall, 0.0, new_south)


def settled(mine, surf, east, south, keep, sums, spread=SPREAD * SLOPE):
    ext, columns = surf.shape
    rolled = 0.0
    for chunk in range(columns // LANES):
        at = cols(chunk)
        new_east = east[mine, at]
        new_south = south[:, at]
        lane = lanes_of(new_east.shape[0])
        rolled_before, rolled = rolled, pltpu.roll(new_east, 1, 1)
        west = jnp.where(lane < 1, rolled_before, rolled)
        north = pltpu.roll(new_south, 1, 0)[mine]
        inflow = west + north
        s0 = surf[mine, at]
        outflow = new_east + new_south[mine]
        yield chunk, keep[mine, at] * s0 + (spread * (inflow - outflow) + sums[chunk])


def exchange(corridor, mine, surf, total, count, total_out, windows=None):
    chunks = surf.shape[1] // LANES
    sums = window_sums([total[mine, cols(chunk)] for chunk in range(chunks)], corridor, False)
    if total_out is not None:
        if windows is None:
            windows = window_sums(
                [surf[mine, cols(chunk)] for chunk in range(chunks)], corridor, True
            )
        for chunk in range(chunks):
            at = cols(chunk)
            kept = (1.0 - corridor * DRAIN) * total[mine, at]
            total_out[mine, at] = kept + count[mine, at] * windows[chunk]
    return sums


def give(corridor, step, surf, before, after):
    rows, columns = after.shape
    weight = DRAIN * (1.0 - corridor * DRAIN) ** (STEPS - 1 - step)
    for chunk in range(columns // LANES):
        at = cols(chunk)
        value = weight * surf[:rows, at]
        after[:, at] = value if before is None else before[:, at] + value


def first_kernel(corridor, surf, east, south, number, total, windows, *refs):
    surf_1, total_1, count, keep, total_0 = refs
    rows = surf.shape[0] - 2 * HALO
    chunks = surf.shape[1] // LANES
    own = slice(0, rows)
    covering = window_sums([number[own, cols(chunk)] for chunk in range(chunks)], corridor, False)
    for chunk in range(chunks):
        at = cols(chunk)
        count[own, at] = (FEED * DRAIN) * number[own, at]
        keep[own, at] = 1.0 - FEED * covering[chunk]
        total_0[own, at] = FEED * total[own, at]
    windows = [windows[:, cols(chunk)] for chunk in range(chunks)]
    sums = exchange(corridor, own, surf, total_0, count, total_1, windows)
    for chunk, new_surf in settled(own, surf, east, south, keep, sums):
        surf_1[own, cols(chunk)] = new_surf


def ahead_kernel(corridor, surf_1, east, south, *refs):
    faces = refs[:4]
    total_1, count, given_1, east_2, south_2, total_2, given_2, sums_2 = refs[4:]
    ext, columns = surf_1.shape
    rows = ext - 2 * HALO
    own = slice(0, rows)
    sums = exchange(corridor, own, surf_1, total_1, count, total_2)
    fluxes(own, rows - 8, None, (surf_1, east, south), faces, east_2, south_2)
    for chunk in range(columns // LANES):
        sums_2[:, cols(chunk)] = sums[chunk]
    give(corridor, 1, surf_1, given_1, given_2)


def second_kernel(corridor, tiles, far, beyond, surf, east, south, *refs):
    faces = refs[:4]
    number, total, sums_2 = refs[4:7]
    surf_1, total_1, count, keep, east_2, south_2, total_2, surf_2, total_0 = refs[14:]
    ext, columns = surf.shape
    rows = ext - 2 * HALO
    chunks = columns // LANES
    position = lax.axis_index("gy")
    own, tail = slice(0, rows), slice(rows, ext)

    section = jnp.concatenate([far[0:1, :], beyond[2:3, :]], axis=1)
    cell = jnp.concatenate([far[1:2, :], beyond[3:4, :]], axis=1)
    valid, node_row, node_chunk, node_lane = located(cell, position, rows, ext, columns)
    key = jnp.where(valid & (node_row >= rows), node_chunk * 8 + (node_row - rows), -1)
    starts, levels = scattered(section, key, node_lane, chunks * 8)
    starting = [
        number[tail, cols(chunk)] + starts[chunk * 8 : chunk * 8 + 8] for chunk in range(chunks)
    ]
    covering = window_sums(starting, corridor, False)
    for chunk in range(chunks):
        at = cols(chunk)
        count[tail, at] = (FEED * DRAIN) * starting[chunk]
        keep[tail, at] = 1.0 - FEED * covering[chunk]
        total_0[tail, at] = FEED * (total[tail, at] + levels[chunk * 8 : chunk * 8 + 8])
    sums = exchange(corridor, tail, surf, total_0, count, total_1)
    for chunk, new_surf in settled(tail, surf, east, south, keep, sums):
        surf_1[tail, cols(chunk)] = new_surf
    tail_sums = exchange(corridor, tail, surf_1, total_1, count, total_2)
    fluxes(tail, 0, wall_of(ext, tiles), (surf_1, east, south), faces, east_2, south_2)
    own_sums = [sums_2[:, cols(chunk)] for chunk in range(chunks)]
    for mine, sums in ((own, own_sums), (tail, tail_sums)):
        for chunk, new_surf in settled(mine, surf_1, east_2, south_2, keep, sums):
            surf_2[mine, cols(chunk)] = new_surf


def third_kernel(corridor, tiles, surf, east, south, *refs):
    faces = refs[:4]
    total, keep, count, given_2, own, takes, masks, takes_near, masks_near = refs[4:13]
    surf_3, east_3, south_3, total_3, own_term, partner_term, other_term = refs[13:]
    ext, columns = surf.shape
    rows = ext - 2 * HALO
    mine = slice(0, rows)
    owned = own.shape[1]
    chunks = columns // LANES
    sums = exchange(corridor, mine, surf, total, count, total_3)
    fluxes(
        mine, rows - 8, wall_of(ext, tiles), (surf, east, south), faces, east_3, south_3
    )
    weight = DRAIN * (1.0 - corridor * DRAIN)
    levels = []
    for chunk, new_surf in settled(mine, surf, east_3, south_3, keep, sums):
        at = cols(chunk)
        surf_3[mine, at] = new_surf
        levels.append(given_2[:, at] + weight * surf[mine, at] + DRAIN * new_surf)
    spare = takes.shape[2] - chunks * rows
    if spare:
        levels.append(jnp.zeros((spare, LANES), jnp.float32))
    levels = jnp.concatenate(levels, axis=0)
    high = levels.astype(jnp.bfloat16)
    low = (levels - high.astype(jnp.float32)).astype(jnp.bfloat16)
    picked = jnp.dot(
        jnp.concatenate([takes[0], takes_near[0], takes[1], takes_near[1]], axis=0),
        jnp.concatenate([high, low], axis=1),
        preferred_element_type=jnp.float32,
    )
    hit = jnp.concatenate([masks[0], masks_near[0], masks[1], masks_near[1]], axis=0)
    picked = (picked * jnp.concatenate([hit, hit], axis=1)).astype(jnp.bfloat16)
    picked = jnp.concatenate([picked[: 3 * owned], picked[3 * owned :]], axis=1)
    terms = lax.dot_general(
        jnp.ones((8, 4 * LANES), jnp.bfloat16),
        picked,
        (((1,), (1,)), ((), ())),
        preferred_element_type=jnp.float32,
    )[0:1]
    own_term[...] = (1.0 - corridor * DRAIN) ** STEPS * own[0:1, :] + terms[:, :owned]
    partner_term[...] = terms[:, owned : 2 * owned]
    other_term[...] = terms[:, 2 * owned :]


def last_kernel(corridor, tiles, surf_2, east_2, south_3, *refs):
    faces = refs[:4]
    total_2, total_3, keep, bed, _, east_3 = refs[4:10]
    surf_3, depth_out, east_out, south_out, depth_4, east_4, south_4, east_tail, sems = refs[10:]
    ext, columns = surf_2.shape
    rows = ext - 2 * HALO
    chunks = columns // LANES
    own, tail = slice(0, rows), slice(rows, ext)
    sums = exchange(corridor, tail, surf_2, total_2, None, None)
    fluxes(tail, 0, None, (surf_2, east_2, None), faces, east_tail, None)
    for chunk, new_surf in settled(tail, surf_2, east_tail, south_3, keep, sums):
        surf_3[tail, cols(chunk)] = new_surf

    def copy(slot, source, target, first, last):
        part = pl.ds(first * LANES, (last - first) * LANES)
        return pltpu.make_async_copy(
            source.at[pl.ds(0, rows), part], target.at[:, part], sems.at[slot]
        )

    before = (surf_3, east_3, south_3)
    fluxes(own, rows - 8, wall_of(ext, tiles), before, faces, east_4, south_4, scale=SLOPE)
    copies = [copy(0, east_4, east_out, 0, chunks), copy(1, south_4, south_out, 0, chunks)]
    for one in copies:
        one.start()
    sums = exchange(corridor, own, surf_3, total_3, None, None)
    group = 5
    for chunk, new_surf in settled(own, surf_3, east_4, south_4, keep, sums, spread=SPREAD):
        at = cols(chunk)
        depth_4[:, at] = new_surf - bed[own, at]
        if (chunk + 1) % group == 0 or chunk + 1 == chunks:
            first = chunk // group
            copies.append(copy(2 + first, depth_4, depth_out, first * group, chunk + 1))
            copies[-1].start()
    for one in copies:
        one.wait()


def local(
    depth, flux_east, flux_south, river_section, bed_level, rough_class, manning_table, bank_cell
):
    rows, columns = depth.shape
    owned = river_section.shape[0]
    corridor = bank_cell.shape[0]
    tiles = lax.axis_size("gy")
    ext = rows + 2 * HALO
    chunks = columns // LANES
    partner_section = swapped(river_section, 0).reshape(1, owned)
    partner_cells = swapped(bank_cell, 0)

    def held(value):
        return pltpu.with_memory_space_constraint(value, pltpu.VMEM)

    def far(value):
        return pltpu.with_memory_space_constraint(value, pltpu.HBM)

    params = pltpu.CompilerParams(vmem_limit_bytes=VMEM_LIMIT)
    halo = pltpu.VMEM((4 * chunks, HALO, LANES), jnp.float32)
    wide = pltpu.VMEM((4 * chunks + 1, HALO, LANES), jnp.float32)
    field = pltpu.VMEM((ext, columns), jnp.float32)
    small = pltpu.VMEM((rows, columns), jnp.float32)
    term = pltpu.VMEM((1, owned), jnp.float32)
    pair = pltpu.VMEM((2, owned), jnp.float32)
    result = pltpu.HBM((rows, columns), jnp.float32)
    cells = -(-chunks * rows // LANES) * LANES

    def call(kernel, name, outs, values, scratch=(), aliases=None):
        return pl.pallas_call(
            kernel,
            out_shape=outs,
            in_specs=[VMEM_SPEC] * len(values),
            out_specs=[HBM_SPEC if out is result else VMEM_SPEC for out in outs],
            scratch_shapes=scratch,
            input_output_aliases=aliases or {},
            compiler_params=params,
            name=name,
        )(*[held(value) for value in values])

    def picks(nodes):
        return [
            pltpu.VMEM((2, nodes, cells), jnp.bfloat16),
            pltpu.VMEM((2, nodes, LANES), jnp.float32),
        ]

    classes = manning_table.shape[0]
    table = far(manning_table.reshape(1, classes))
    table_held = pltpu.VMEM((1, classes), jnp.float32)
    to_other, own = pl.pallas_call(
        pack_kernel,
        out_shape=[wide, pair],
        in_specs=[HBM_SPEC] * 8,
        out_specs=[VMEM_SPEC] * 2,
        scratch_shapes=[
            pltpu.VMEM((4, 8, columns), jnp.float32),
            pltpu.VMEM((8, columns), jnp.int32),
            pltpu.VMEM((corridor, owned), jnp.int32),
            table_held,
            pltpu.SemaphoreType.DMA((8,)),
        ],
        compiler_params=params,
        name="pack",
    )(
        *[far(value) for value in (depth, bed_level, rough_class, flux_east, flux_south)],
        far(river_section.reshape(1, owned)),
        far(bank_cell),
        table,
    )
    (to_other,) = call(
        join_kernel,
        "join",
        [wide],
        (to_other, partner_section, partner_cells),
        aliases={0: 0},
    )
    by_other = swapped(to_other, 1)
    *loaded, rough, table_rows = pl.pallas_call(
        load_kernel,
        out_shape=[field] * 4
        + [pltpu.VMEM((rows, columns), jnp.int32), pltpu.VMEM((classes, LANES), jnp.float32)],
        in_specs=[HBM_SPEC] * 6,
        out_specs=[VMEM_SPEC] * 6,
        scratch_shapes=[table_held, pltpu.SemaphoreType.DMA((6,))],
        compiler_params=params,
        name="load",
    )(
        *[far(value) for value in (depth, flux_east, flux_south, bed_level, rough_class)],
        table,
    )
    *fields, to_partner = call(
        prepare_kernel,
        "prepare",
        [field] * 9 + [halo],
        (table_rows, rough, *loaded),
        aliases={2 + slot: slot for slot in range(4)},
    )
    by_partner = swapped(to_partner, 0)
    number, total, takes, masks, windows, given_1 = call(
        functools.partial(nodes_kernel, corridor),
        "nodes",
        [field] * 2 + picks(2 * owned) + [small] * 2,
        (fields[0], own, partner_section, partner_cells),
    )
    near, beyond = call(
        relay_kernel,
        "relay",
        [pair, pltpu.VMEM((HALO, LANES), jnp.float32)],
        (by_other, masks),
    )
    from_far = swapped(near, 0)
    *fields, takes_near, masks_near = call(
        functools.partial(border_kernel, corridor, tiles),
        "border",
        [field] * 11 + picks(owned),
        (by_partner, by_other, table_rows, near, *fields, number, total),
        aliases={4 + slot: slot for slot in range(11)},
    )
    surf, east, south, bed, _, *faces, number, total = fields
    surf_1, total_1, count, keep = call(
        functools.partial(first_kernel, corridor),
        "first",
        [field] * 4,
        (surf, east, south, number, total, windows),
        scratch=[field],
    )
    east_2, south_2, total_2, given_2, sums_2 = call(
        functools.partial(ahead_kernel, corridor),
        "ahead",
        [field] * 3 + [small] * 2,
        (surf_1, east, south, *faces, total_1, count, given_1),
    )
    surf_1, total_1, count, keep, east_2, south_2, total_2, surf_2 = call(
        functools.partial(second_kernel, corridor, tiles),
        "second",
        [field] * 8,
        (
            *(from_far, beyond, surf, east, south, *faces, number, total, sums_2),
            *(surf_1, total_1, count, keep, east_2, south_2, total_2),
        ),
        scratch=[field],
        aliases={12 + slot: slot for slot in range(7)},
    )
    surf_3, east_3, south_3, total_3, own_term, partner_term, other_term = call(
        functools.partial(third_kernel, corridor, tiles),
        "third",
        [field] * 4 + [term] * 3,
        (
            *(surf_2, east_2, south_2, *faces, total_2, keep, count, given_2),
            *(own, takes, masks, takes_near, masks_near),
        ),
    )
    from_other = swapped(other_term.reshape(owned), 1)
    from_partner = swapped(partner_term.reshape(owned), 0)
    _, depth, flux_east, flux_south = call(
        functools.partial(last_kernel, corridor, tiles),
        "last",
        [field, result, result, result],
        (surf_2, east_2, south_3, *faces, total_2, total_3, keep, bed, surf_3, east_3),
        scratch=[small, small, field, field, pltpu.SemaphoreType.DMA((2 + -(-chunks // 5),))],
        aliases={11: 0},
    )
    river_section = own_term.reshape(owned) + from_other + from_partner
    return (depth, flux_east, flux_south, river_section)


def solution(mesh):
    return jax.shard_map(
        local,
        mesh=mesh,
        in_specs=(
            P(("runs", "gy"), None),
            P(("runs", "gy"), None),
            P(("runs", "gy"), None),
            P(("runs", "gy")),
            P("gy", None),
            P("gy", None),
            P(),
            P(None, "gy"),
        ),
        out_specs=(
            P(("runs", "gy"), None),
            P(("runs", "gy"), None),
            P(("runs", "gy"), None),
            P(("runs", "gy")),
        ),
        check_vma=False,
    )
```

```python
import functools

import jax
import jax.numpy as jnp
from jax import lax
from jax.experimental import pallas as pl
from jax.experimental.pallas import tpu as pltpu
from jax.sharding import PartitionSpec as P

STEPS = 4

GRAV = 9.81
TSTEP = 8.0
CELL = 90.0
FLOOR = 0.05
BANK_COEF = 200.0
CELL_AREA = 8100.0
NODE_AREA = 20000.0

LANES = 128
HALO = 4
SLOPE = GRAV * TSTEP / CELL
SPREAD = TSTEP / CELL
FEED = TSTEP * BANK_COEF / CELL_AREA
DRAIN = TSTEP * BANK_COEF / NODE_AREA
VMEM_LIMIT = 32 * 1024 * 1024

VMEM_SPEC = pl.BlockSpec(memory_space=pltpu.VMEM)
HBM_SPEC = pl.BlockSpec(memory_space=pltpu.HBM)


def swapped(value, first):
    count = lax.axis_size("gy")
    pairs = []
    for low in range(first, count - 1, 2):
        pairs += [(low, low + 1), (low + 1, low)]
    return lax.ppermute(value, "gy", pairs)


def cols(chunk):
    return slice(chunk * LANES, (chunk + 1) * LANES)


def lanes_of(rows):
    return lax.broadcasted_iota(jnp.int32, (rows, LANES), 1)


def moved_left(value, following, by):
    return jnp.where(
        lanes_of(value.shape[0]) >= LANES - by,
        pltpu.roll(following, LANES - by, 1),
        pltpu.roll(value, LANES - by, 1),
    )


def moved_up(value):
    return pltpu.roll(value, value.shape[0] - 1, 0)


def split3(value):
    high = value.astype(jnp.bfloat16)
    rest = value - high.astype(jnp.float32)
    middle = rest.astype(jnp.bfloat16)
    low = (rest - middle.astype(jnp.float32)).astype(jnp.bfloat16)
    return high, middle, low


def one_hot(count, key):
    rows = lax.broadcasted_iota(jnp.int32, (count, key.shape[1]), 0)
    return jnp.where(rows == key, 1.0, 0.0)


def drag_of(mann_a, mann_b):
    pair = mann_a + mann_b
    return (0.25 * GRAV * TSTEP * SLOPE) * (pair * pair)


def looked_up(klass, entries):
    value = jnp.broadcast_to(entries[0], klass.shape)
    for k in range(1, len(entries)):
        value = jnp.where(klass == k, entries[k], value)
    return value


def face(flux, surf_a, surf_b, bed_max, drag):
    flow_depth = jnp.maximum(jnp.maximum(surf_a, surf_b) - bed_max, FLOOR)
    power = jnp.exp2((-7.0 / 3.0) * jnp.log2(flow_depth))
    driven = flux - flow_depth * (surf_b - surf_a)
    damping = 1.0 + drag * jnp.abs(flux) * power
    return driven * pl.reciprocal(damping, approx=True)


def window_sums(blocks, reach, forward):
    height = blocks[0].shape[0]
    count = len(blocks)
    spare = -(count * height) % 16
    whole = blocks + ([jnp.zeros((spare, LANES), jnp.float32)] if spare else [])
    whole = jnp.concatenate(whole, axis=0)
    high = whole.astype(jnp.bfloat16)
    low = (whole - high.astype(jnp.float32)).astype(jnp.bfloat16)
    source = lax.broadcasted_iota(jnp.int32, (2 * LANES, 2 * LANES), 0) % LANES
    target = lax.broadcasted_iota(jnp.int32, (2 * LANES, 2 * LANES), 1)
    spill = target >= LANES
    target = target % LANES
    if forward:
        ahead = source - target + jnp.where(spill, LANES, 0)
    else:
        ahead = target - source + jnp.where(spill, LANES, 0)
    band = jnp.where((ahead >= 0) & (ahead < reach), 1.0, 0.0).astype(jnp.bfloat16)
    sums = jnp.dot(
        jnp.concatenate([high, low], axis=1), band, preferred_element_type=jnp.float32
    )
    results = []
    for block in range(count):
        result = sums[block * height : (block + 1) * height, :LANES]
        beside = block + 1 if forward else block - 1
        if 0 <= beside < count:
            result = result + sums[beside * height : (beside + 1) * height, LANES:]
        results.append(result)
    return results


def east_walled(value, chunk, chunks):
    if chunk + 1 < chunks:
        return value
    return jnp.where(lanes_of(value.shape[0]) == LANES - 1, 0.0, value)


def located(cell, position, rows, ext, columns):
    base = ((position * rows - HALO) * columns + 1).astype(jnp.float32)
    offset = cell - base
    valid = (cell > 0.0) & (offset >= 0.0) & (offset < float(ext * columns))
    offset = jnp.where(valid, offset, 0.0)
    row = jnp.floor((offset + 0.5) * (1.0 / columns))
    column = (offset - row * float(columns)).astype(jnp.int32)
    row = row.astype(jnp.int32) - HALO
    row = jnp.where(row < 0, row + ext, row)
    chunk = column // LANES
    return valid, row, chunk, column - chunk * LANES


def scattered(section, key, lane, count):
    at_lane = one_hot(LANES, lane)
    parts = [at_lane] + [at_lane * part.astype(jnp.float32) for part in split3(section)]
    grid = lax.dot_general(
        one_hot(-(-count // 16) * 16, key).astype(jnp.bfloat16),
        jnp.concatenate(parts, axis=0).astype(jnp.bfloat16),
        (((1,), (1,)), ((), ())),
        preferred_element_type=jnp.float32,
    )
    number = grid[:, :LANES]
    total = (grid[:, LANES : 2 * LANES] + grid[:, 2 * LANES : 3 * LANES]) + grid[:, 3 * LANES :]
    return number, total


def border_rows(of_first, fields, south):
    outer = lax.broadcasted_iota(jnp.int32, (HALO, LANES), 0) == jnp.where(of_first, HALO - 1, 0)
    flux = jnp.where(of_first, south[:HALO], south[HALO:])
    return [
        jnp.where(outer, flux[slot : slot + 1], jnp.where(of_first, value[:HALO], value[HALO:]))
        for slot, value in enumerate(fields)
    ]


def pack_kernel(
    depth, bed, rough, east, south, section, cells, table_in, to_other, own, *refs
):
    held, held_rough, held_cells, table, sems = refs
    rows, columns = depth.shape
    chunks = columns // LANES
    even = lax.axis_index("gy") % 2 == 0
    start = pl.multiple_of(jnp.where(even, 0, rows - 8), 8)
    near = pl.ds(start, 8)
    copies = [
        pltpu.make_async_copy(source, target, sems.at[slot])
        for slot, (source, target) in enumerate(
            (
                (rough.at[near, :], held_rough),
                (bed.at[near, :], held.at[1]),
                (depth.at[near, :], held.at[0]),
                (east.at[near, :], held.at[2]),
                (south.at[near, :], held.at[3]),
                (section, own.at[pl.ds(0, 1), :]),
                (cells, held_cells),
                (table_in, table),
            )
        )
    ]
    for copy in copies:
        copy.start()
    for copy in copies:
        copy.wait()
    own[1:2, :] = (held_cells[0:1, :] + 1).astype(jnp.float32)
    entries = [
        jnp.broadcast_to(table[:, k : k + 1], (1, LANES)) for k in range(table.shape[1])
    ]
    manns = [looked_up(held_rough[:, cols(chunk)], entries) for chunk in range(chunks)]
    row = lax.broadcasted_iota(jnp.int32, (8, LANES), 0)
    beds = [held[1, :, cols(chunk)] for chunk in range(chunks)]
    surfs = [held[0, :, cols(chunk)] + beds[chunk] for chunk in range(chunks)]

    def moved(values):
        rolled = [pltpu.roll(value, LANES - 1, 1) for value in values]
        rolled.append(rolled[-1])
        edge = lanes_of(8) == LANES - 1
        return [jnp.where(edge, rolled[c + 1], rolled[c]) for c in range(chunks)]

    beds_left, surfs_left, manns_left = moved(beds), moved(surfs), moved(manns)
    for chunk in range(chunks):
        at = cols(chunk)
        m0, b0, s0 = manns[chunk], beds[chunk], surfs[chunk]
        bed_max = jnp.maximum(b0, beds_left[chunk])
        drag = drag_of(m0, manns_left[chunk])
        q0 = (1.0 / SLOPE) * held[2, :, at]
        new_east = face(q0, s0, surfs_left[chunk], bed_max, drag)
        new_east = east_walled(new_east, chunk, chunks)
        bed_max = jnp.maximum(b0, moved_up(b0))
        drag = drag_of(m0, moved_up(m0))
        q0 = (1.0 / SLOPE) * held[3, :, at]
        new_south = jnp.where(row == 7, q0, face(q0, s0, moved_up(s0), bed_max, drag))
        fields = (s0, b0, held_rough[:, at].astype(jnp.float32), new_east)
        for slot, block in enumerate(border_rows(even, fields, new_south)):
            to_other[slot * chunks + chunk] = block
    to_other[4 * chunks, 0:2, :] = own[...]


def join_kernel(before, section, cells, to_other):
    nodes = to_other.shape[0] - 1
    to_other[nodes, 2:3, :] = section[...]
    to_other[nodes, 3:4, :] = (cells[0:1, :] + 1).astype(jnp.float32)


def relay_kernel(by_other, prepared, near, beyond):
    del prepared
    nodes = by_other.shape[0] - 1
    near[...] = by_other[nodes, 0:2, :]
    beyond[...] = by_other[nodes, 2:4, :]


def picking(reach, rows, key, lane, takes, masks):
    for block in range(key.shape[1] // LANES):
        mine = slice(block * LANES, (block + 1) * LANES)

        def column(row):
            wide = jnp.broadcast_to(row[:, mine].astype(jnp.float32), (LANES, LANES))
            return jnp.transpose(wide).astype(jnp.int32)

        spread = lanes_of(LANES)
        at = column(key)
        after = jnp.where(at < 0, at, at + rows)
        for first in range(0, takes.shape[2], LANES):
            for half, place in enumerate((at, after)):
                hit = jnp.where(spread + first == place, 1.0, 0.0)
                takes[half, mine, first : first + LANES] = hit.astype(jnp.bfloat16)
        ahead = spread - column(lane)
        masks[0, mine, :] = jnp.where((ahead >= 0) & (ahead < reach), 1.0, 0.0)
        masks[1, mine, :] = jnp.where(ahead + LANES < reach, 1.0, 0.0)


def load_kernel(
    depth_in, east_in, south_in, bed_in, rough_in, table_in, *refs
):
    surf, east, south, bed, rough, table_rows, table, sems = refs
    rows, columns = depth_in.shape
    own = pl.ds(0, rows)
    copies = [
        pltpu.make_async_copy(source, target.at[own, :], sems.at[slot])
        for slot, (source, target) in enumerate(
            (
                (depth_in, surf),
                (bed_in, bed),
                (rough_in, rough),
                (east_in, east),
                (south_in, south),
            )
        )
    ]
    copies.append(pltpu.make_async_copy(table_in, table, sems.at[5]))
    for copy in copies:
        copy.start()
    copies[5].wait()
    for k in range(table_rows.shape[0]):
        table_rows[k : k + 1, :] = jnp.broadcast_to(table[:, k : k + 1], (1, LANES))
    for copy in copies[:5]:
        copy.wait()


def prepare_kernel(table_rows, rough, *refs):
    surf, east, south, bed = refs[4:8]
    mann, bed_e, bed_s, drag_e, drag_s, to_partner = refs[8:]
    ext, columns = surf.shape
    rows = ext - 2 * HALO
    chunks = columns // LANES
    even = lax.axis_index("gy") % 2 == 0
    entries = [table_rows[k : k + 1, :] for k in range(table_rows.shape[0])]
    for chunk in range(chunks):
        at = cols(chunk)
        mann[:rows, at] = looked_up(rough[:, at], entries)
        surf[:rows, at] = surf[:rows, at] + bed[:rows, at]

    kept = lax.broadcasted_iota(jnp.int32, (rows, LANES), 0) == rows - 1
    for chunk in range(chunks):
        at, then = cols(chunk), cols(min(chunk + 1, chunks - 1))
        s0, b0, m0 = surf[:rows, at], bed[:rows, at], mann[:rows, at]
        bed_max = jnp.maximum(b0, moved_left(b0, bed[:rows, then], 1))
        drag = drag_of(m0, moved_left(m0, mann[:rows, then], 1))
        bed_e[:rows, at] = bed_max
        drag_e[:rows, at] = drag
        q0 = (1.0 / SLOPE) * east[:rows, at]
        new_east = face(q0, s0, moved_left(s0, surf[:rows, then], 1), bed_max, drag)
        new_east = east_walled(new_east, chunk, chunks)
        east[:rows, at] = new_east
        bed_max = jnp.maximum(b0, moved_up(b0))
        drag = drag_of(m0, moved_up(m0))
        bed_s[:rows, at] = bed_max
        drag_s[:rows, at] = drag
        q0 = (1.0 / SLOPE) * south[:rows, at]
        new_south = jnp.where(kept, q0, face(q0, s0, moved_up(s0), bed_max, drag))
        south[:rows, at] = new_south

        def ends(value):
            return jnp.where(even, value[rows - 8 :], value[:8])

        fields = (ends(s0), ends(b0), ends(rough[:, at].astype(jnp.float32)), ends(new_east))
        blocks = border_rows(jnp.logical_not(even), fields, ends(new_south))
        for slot, block in enumerate(blocks):
            to_partner[slot * chunks + chunk] = block


def nodes_kernel(reach, surf, own, partner_section, partner_cells, *refs):
    number, total, takes, masks, windows, given_1 = refs
    rows = surf.shape[0] - 2 * HALO
    ext, columns = number.shape
    chunks = columns // LANES
    tiles = lax.axis_size("gy")
    position = lax.axis_index("gy")
    side = jnp.where(position % 2 == 0, 1, -1)
    partner = jnp.where(position + side < tiles, partner_cells[0:1, :] + 1, 0).astype(jnp.float32)
    section = jnp.concatenate([own[0:1, :], partner_section[...]], axis=1)
    cell = jnp.concatenate([own[1:2, :], partner], axis=1)
    valid, node_row, node_chunk, node_lane = located(cell, position, rows, ext, columns)
    key = jnp.where(valid, node_chunk * ext + node_row, -1)
    starts, levels = scattered(section, key, node_lane, chunks * ext)
    for chunk in range(chunks):
        at = cols(chunk)
        number[:, at] = starts[chunk * ext : (chunk + 1) * ext]
        total[:, at] = levels[chunk * ext : (chunk + 1) * ext]
    key = jnp.where(valid & (node_row < rows), node_chunk * rows + node_row, -1)
    picking(reach, rows, key, node_lane, takes, masks)
    sums = window_sums([surf[:rows, cols(chunk)] for chunk in range(chunks)], reach, True)
    for chunk in range(chunks):
        windows[:, cols(chunk)] = sums[chunk]
    give(reach, 0, surf, None, given_1)


def wall_of(ext, tiles):
    position = lax.axis_index("gy")
    rows = ext - 2 * HALO
    row = lax.broadcasted_iota(jnp.int32, (16, LANES), 0) + (ext - 16)
    return ((row == ext - 1) & (position == 0)) | ((row == rows - 1) & (position == tiles - 1))


def border_kernel(reach, tiles, by_partner, by_other, table_rows, near, *refs):
    surf, east, south, bed, mann, bed_e, bed_s, drag_e, drag_s, number, total, takes, masks = refs[11:]
    ext, columns = surf.shape
    rows = ext - 2 * HALO
    chunks = columns // LANES
    position = lax.axis_index("gy")
    even = position % 2 == 0
    valid, node_row, node_chunk, node_lane = located(near[1:2, :], position, rows, ext, columns)
    key = jnp.where(valid, node_chunk * ext + node_row, -1)
    starts, levels = scattered(near[0:1, :], key, node_lane, chunks * ext)

    entries = [table_rows[k : k + 1, :] for k in range(table_rows.shape[0])]
    row = lax.broadcasted_iota(jnp.int32, (2 * HALO, LANES), 0)
    for chunk in range(chunks):
        at = cols(chunk)
        halos = []
        flux = jnp.zeros((2 * HALO, LANES), jnp.float32)
        for slot in range(4):
            a, b = by_partner[slot * chunks + chunk], by_other[slot * chunks + chunk]
            below = jnp.where(even, a, b)
            above = jnp.where(even, b, a)
            halos.append(jnp.concatenate([below, above], axis=0))
            flux = jnp.where(row == slot, below[HALO - 1 :], flux)
            flux = jnp.where(row == HALO + slot, above[:1], flux)
        surf[rows:, at] = halos[0]
        bed[rows:, at] = halos[1]
        mann[rows:, at] = looked_up(halos[2].astype(jnp.int32), entries)
        east[rows:, at] = halos[3]
        south[rows:, at] = flux

    key = jnp.where(valid & (node_row < rows), node_chunk * rows + node_row, -1)
    picking(reach, rows, key, node_lane, takes, masks)

    wall = wall_of(ext, tiles)
    kept = lax.broadcasted_iota(jnp.int32, (16, LANES), 0) % 8 < 7
    for chunk in range(chunks):
        at, then = cols(chunk), cols(min(chunk + 1, chunks - 1))
        number[:, at] += starts[chunk * ext : (chunk + 1) * ext]
        total[:, at] += levels[chunk * ext : (chunk + 1) * ext]
        b0, m0 = bed[rows:, at], mann[rows:, at]
        bed_e[rows:, at] = jnp.maximum(b0, moved_left(b0, bed[rows:, then], 1))
        drag_e[rows:, at] = drag_of(m0, moved_left(m0, mann[rows:, then], 1))

        def rolled_up(ref):
            value = jnp.concatenate([ref[rows - 8 :, at], ref[:8, at]], axis=0)
            return value[:16], moved_up(value)[:16]

        s0, s1 = rolled_up(surf)
        b0, b1 = rolled_up(bed)
        m0, m1 = rolled_up(mann)
        bed_max = jnp.maximum(b0, b1)
        drag = drag_of(m0, m1)
        bed_s[rows - 8 :, at] = bed_max
        drag_s[rows - 8 :, at] = drag
        q0 = south[rows - 8 :, at]
        new_south = jnp.where(kept, q0, face(q0, s0, s1, bed_max, drag))
        south[rows - 8 :, at] = jnp.where(wall, 0.0, new_south)


def fluxes(mine, upper, wall, before, faces, east_out, south_out, scale=None):
    surf, east, south = before
    bed_e, bed_s, drag_e, drag_s = faces
    ext, columns = surf.shape
    chunks = columns // LANES
    rolled = lane = None
    if east_out is not None:
        rolled = pltpu.roll(surf[mine, cols(0)], LANES - 1, 1)
        lane = lanes_of(rolled.shape[0])
    for chunk in range(chunks):
        at = cols(chunk)
        if east_out is not None:
            s0 = surf[mine, at]
            rolled_then = rolled
            if chunk + 1 < chunks:
                rolled_then = pltpu.roll(surf[mine, cols(chunk + 1)], LANES - 1, 1)
            left = jnp.where(lane >= LANES - 1, rolled_then, rolled)
            rolled = rolled_then
            new_east = face(east[mine, at], s0, left, bed_e[mine, at], drag_e[mine, at])
            if scale is not None:
                new_east = scale * new_east
            east_out[mine, at] = east_walled(new_east, chunk, chunks)
        if upper:
            s0 = surf[: upper + 8, at]
            s1 = moved_up(s0)[:upper]
            new_south = face(south[:upper, at], s0[:upper], s1, bed_s[:upper, at], drag_s[:upper, at])
            if scale is not None:
                new_south = scale * new_south
            south_out[:upper, at] = new_south
        if wall is not None:
            low = slice(ext - 16, ext)
            s0 = jnp.concatenate([surf[low, at], surf[:8, at]], axis=0)
            s1 = moved_up(s0)[:16]
            new_south = face(south[low, at], s0[:16], s1, bed_s[low, at], drag_s[low, at])
            if scale is not None:
                new_south = scale * new_south
            south_out[low, at] = jnp.where(wall, 0.0, new_south)


def settled(mine, surf, east, south, keep, sums, spread=SPREAD * SLOPE):
    ext, columns = surf.shape
    rolled = 0.0
    for chunk in range(columns // LANES):
        at = cols(chunk)
        new_east = east[mine, at]
        new_south = south[:, at]
        lane = lanes_of(new_east.shape[0])
        rolled_before, rolled = rolled, pltpu.roll(new_east, 1, 1)
        west = jnp.where(lane < 1, rolled_before, rolled)
        north = pltpu.roll(new_south, 1, 0)[mine]
        inflow = west + north
        s0 = surf[mine, at]
        outflow = new_east + new_south[mine]
        yield chunk, keep[mine, at] * s0 + (spread * (inflow - outflow) + sums[chunk])


def refill(corridor, mine, surf, total, count, total_out, windows=None):
    chunks = surf.shape[1] // LANES
    if windows is None:
        windows = window_sums([surf[mine, cols(chunk)] for chunk in range(chunks)], corridor, True)
    for chunk in range(chunks):
        at = cols(chunk)
        kept = (1.0 - corridor * DRAIN) * total[mine, at]
        total_out[mine, at] = kept + count[mine, at] * windows[chunk]


def summed(corridor, mine, total):
    chunks = total.shape[1] // LANES
    return window_sums([total[mine, cols(chunk)] for chunk in range(chunks)], corridor, False)


def exchange(corridor, mine, surf, total, count, total_out, windows=None):
    sums = summed(corridor, mine, total)
    refill(corridor, mine, surf, total, count, total_out, windows)
    return sums


def give(corridor, step, surf, before, after):
    rows, columns = after.shape
    weight = DRAIN * (1.0 - corridor * DRAIN) ** (STEPS - 1 - step)
    for chunk in range(columns // LANES):
        at = cols(chunk)
        value = weight * surf[:rows, at]
        after[:, at] = value if before is None else before[:, at] + value


def first_kernel(corridor, surf, east, south, number, total, windows, *refs):
    surf_1, total_1, count, keep, total_0 = refs
    rows = surf.shape[0] - 2 * HALO
    chunks = surf.shape[1] // LANES
    own = slice(0, rows)
    covering = window_sums([number[own, cols(chunk)] for chunk in range(chunks)], corridor, False)
    for chunk in range(chunks):
        at = cols(chunk)
        count[own, at] = (FEED * DRAIN) * number[own, at]
        keep[own, at] = 1.0 - FEED * covering[chunk]
        total_0[own, at] = FEED * total[own, at]
    windows = [windows[:, cols(chunk)] for chunk in range(chunks)]
    sums = exchange(corridor, own, surf, total_0, count, total_1, windows)
    for chunk, new_surf in settled(own, surf, east, south, keep, sums):
        surf_1[own, cols(chunk)] = new_surf


def second_kernel(corridor, tiles, far, beyond, surf, east, south, *refs):
    faces = refs[:4]
    number, total, given_1 = refs[4:7]
    surf_1, total_1, count, keep = refs[11:15]
    surf_2, east_2, south_2, total_2, given_2, total_0 = refs[15:]
    ext, columns = surf.shape
    rows = ext - 2 * HALO
    chunks = columns // LANES
    position = lax.axis_index("gy")
    tail = slice(rows, ext)

    section = jnp.concatenate([far[0:1, :], beyond[0:1, :]], axis=1)
    cell = jnp.concatenate([far[1:2, :], beyond[1:2, :]], axis=1)
    valid, node_row, node_chunk, node_lane = located(cell, position, rows, ext, columns)
    key = jnp.where(valid & (node_row >= rows), node_chunk * 8 + (node_row - rows), -1)
    starts, levels = scattered(section, key, node_lane, chunks * 8)
    starting = [
        number[tail, cols(chunk)] + starts[chunk * 8 : chunk * 8 + 8] for chunk in range(chunks)
    ]
    covering = window_sums(starting, corridor, False)
    for chunk in range(chunks):
        at = cols(chunk)
        count[tail, at] = (FEED * DRAIN) * starting[chunk]
        keep[tail, at] = 1.0 - FEED * covering[chunk]
        total_0[tail, at] = FEED * (total[tail, at] + levels[chunk * 8 : chunk * 8 + 8])
    sums = exchange(corridor, tail, surf, total_0, count, total_1)

    own = slice(0, rows)
    before = (surf_1, east, south)
    fluxes(own, rows - 8, None, before, faces, east_2, south_2)
    own_sums = exchange(corridor, own, surf_1, total_1, count, total_2)
    give(corridor, 1, surf_1, given_1, given_2)

    for chunk, new_surf in settled(tail, surf, east, south, keep, sums):
        surf_1[tail, cols(chunk)] = new_surf
    tail_sums = exchange(corridor, tail, surf_1, total_1, count, total_2)
    fluxes(tail, 0, wall_of(ext, tiles), before, faces, east_2, south_2)
    for mine, sums in ((own, own_sums), (tail, tail_sums)):
        for chunk, new_surf in settled(mine, surf_1, east_2, south_2, keep, sums):
            surf_2[mine, cols(chunk)] = new_surf


def third_kernel(corridor, tiles, surf, east, south, *refs):
    faces = refs[:4]
    total, keep, given_2, own, takes, masks, takes_near, masks_near = refs[4:12]
    surf_3, east_3, south_3, own_term, partner_term, other_term = refs[12:]
    ext, columns = surf.shape
    rows = ext - 2 * HALO
    mine = slice(0, rows)
    owned = own.shape[1]
    chunks = columns // LANES
    sums = summed(corridor, mine, total)
    fluxes(
        mine, rows - 8, wall_of(ext, tiles), (surf, east, south), faces, east_3, south_3
    )
    weight = DRAIN * (1.0 - corridor * DRAIN)
    levels = []
    for chunk, new_surf in settled(mine, surf, east_3, south_3, keep, sums):
        at = cols(chunk)
        surf_3[mine, at] = new_surf
        levels.append(given_2[:, at] + weight * surf[mine, at] + DRAIN * new_surf)
    spare = takes.shape[2] - chunks * rows
    if spare:
        levels.append(jnp.zeros((spare, LANES), jnp.float32))
    levels = jnp.concatenate(levels, axis=0)
    high = levels.astype(jnp.bfloat16)
    low = (levels - high.astype(jnp.float32)).astype(jnp.bfloat16)
    picked = jnp.dot(
        jnp.concatenate([takes[0], takes_near[0], takes[1], takes_near[1]], axis=0),
        jnp.concatenate([high, low], axis=1),
        preferred_element_type=jnp.float32,
    )
    hit = jnp.concatenate([masks[0], masks_near[0], masks[1], masks_near[1]], axis=0)
    picked = (picked * jnp.concatenate([hit, hit], axis=1)).astype(jnp.bfloat16)
    picked = jnp.concatenate([picked[: 3 * owned], picked[3 * owned :]], axis=1)
    terms = lax.dot_general(
        jnp.ones((8, 4 * LANES), jnp.bfloat16),
        picked,
        (((1,), (1,)), ((), ())),
        preferred_element_type=jnp.float32,
    )[0:1]
    own_term[...] = (1.0 - corridor * DRAIN) ** STEPS * own[0:1, :] + terms[:, :owned]
    partner_term[...] = terms[:, owned : 2 * owned]
    other_term[...] = terms[:, 2 * owned :]


def last_kernel(corridor, tiles, surf_2, east_2, south_3, *refs):
    faces = refs[:4]
    total_2, count, keep, bed, _, east_3 = refs[4:10]
    surf_3, depth_out, east_out, south_out = refs[10:14]
    depth_4, east_4, south_4, east_tail, total_3, sems = refs[14:]
    ext, columns = surf_2.shape
    rows = ext - 2 * HALO
    chunks = columns // LANES
    own, tail = slice(0, rows), slice(rows, ext)

    def copy(slot, source, target, first, last):
        part = pl.ds(first * LANES, (last - first) * LANES)
        return pltpu.make_async_copy(
            source.at[pl.ds(0, rows), part], target.at[:, part], sems.at[slot]
        )

    before = (surf_3, east_3, south_3)
    tail_sums = summed(corridor, tail, total_2)
    refill(corridor, own, surf_2, total_2, count, total_3)
    fluxes(own, rows - 8, None, before, faces, east_4, south_4, scale=SLOPE)
    copies = [copy(0, east_4, east_out, 0, chunks)]
    copies[0].start()
    fluxes(tail, 0, None, (surf_2, east_2, None), faces, east_tail, None)
    for chunk, new_surf in settled(tail, surf_2, east_tail, south_3, keep, tail_sums):
        surf_3[tail, cols(chunk)] = new_surf
    sums = summed(corridor, own, total_3)
    fluxes(slice(0, 0), 0, wall_of(ext, tiles), before, faces, None, south_4, scale=SLOPE)
    copies.append(copy(1, south_4, south_out, 0, chunks))
    copies[1].start()
    group = 5
    for chunk, new_surf in settled(own, surf_3, east_4, south_4, keep, sums, spread=SPREAD):
        at = cols(chunk)
        depth_4[:, at] = new_surf - bed[own, at]
        if (chunk + 1) % group == 0 or chunk + 1 == chunks:
            first = chunk // group
            copies.append(copy(2 + first, depth_4, depth_out, first * group, chunk + 1))
            copies[-1].start()
    for one in copies:
        one.wait()


def local(
    depth, flux_east, flux_south, river_section, bed_level, rough_class, manning_table, bank_cell
):
    rows, columns = depth.shape
    owned = river_section.shape[0]
    corridor = bank_cell.shape[0]
    tiles = lax.axis_size("gy")
    ext = rows + 2 * HALO
    chunks = columns // LANES
    partner_section = swapped(river_section, 0).reshape(1, owned)
    partner_cells = swapped(bank_cell, 0)

    def held(value):
        return pltpu.with_memory_space_constraint(value, pltpu.VMEM)

    def far(value):
        return pltpu.with_memory_space_constraint(value, pltpu.HBM)

    params = pltpu.CompilerParams(vmem_limit_bytes=VMEM_LIMIT)
    halo = pltpu.VMEM((4 * chunks, HALO, LANES), jnp.float32)
    wide = pltpu.VMEM((4 * chunks + 1, HALO, LANES), jnp.float32)
    field = pltpu.VMEM((ext, columns), jnp.float32)
    small = pltpu.VMEM((rows, columns), jnp.float32)
    term = pltpu.VMEM((1, owned), jnp.float32)
    pair = pltpu.VMEM((2, owned), jnp.float32)
    result = pltpu.HBM((rows, columns), jnp.float32)
    cells = -(-chunks * rows // LANES) * LANES

    def call(kernel, name, outs, values, scratch=(), aliases=None):
        return pl.pallas_call(
            kernel,
            out_shape=outs,
            in_specs=[VMEM_SPEC] * len(values),
            out_specs=[HBM_SPEC if out is result else VMEM_SPEC for out in outs],
            scratch_shapes=scratch,
            input_output_aliases=aliases or {},
            compiler_params=params,
            name=name,
        )(*[held(value) for value in values])

    def picks(nodes):
        return [
            pltpu.VMEM((2, nodes, cells), jnp.bfloat16),
            pltpu.VMEM((2, nodes, LANES), jnp.float32),
        ]

    classes = manning_table.shape[0]
    table = far(manning_table.reshape(1, classes))
    table_held = pltpu.VMEM((1, classes), jnp.float32)
    to_other, own = pl.pallas_call(
        pack_kernel,
        out_shape=[wide, pair],
        in_specs=[HBM_SPEC] * 8,
        out_specs=[VMEM_SPEC] * 2,
        scratch_shapes=[
            pltpu.VMEM((4, 8, columns), jnp.float32),
            pltpu.VMEM((8, columns), jnp.int32),
            pltpu.VMEM((corridor, owned), jnp.int32),
            table_held,
            pltpu.SemaphoreType.DMA((8,)),
        ],
        compiler_params=params,
        name="pack",
    )(
        *[far(value) for value in (depth, bed_level, rough_class, flux_east, flux_south)],
        far(river_section.reshape(1, owned)),
        far(bank_cell),
        table,
    )
    (to_other,) = call(
        join_kernel,
        "join",
        [wide],
        (to_other, partner_section, partner_cells),
        aliases={0: 0},
    )
    by_other = swapped(to_other, 1)
    *loaded, rough, table_rows = pl.pallas_call(
        load_kernel,
        out_shape=[field] * 4
        + [pltpu.VMEM((rows, columns), jnp.int32), pltpu.VMEM((classes, LANES), jnp.float32)],
        in_specs=[HBM_SPEC] * 6,
        out_specs=[VMEM_SPEC] * 6,
        scratch_shapes=[table_held, pltpu.SemaphoreType.DMA((6,))],
        compiler_params=params,
        name="load",
    )(
        *[far(value) for value in (depth, flux_east, flux_south, bed_level, rough_class)],
        table,
    )
    *fields, to_partner = call(
        prepare_kernel,
        "prepare",
        [field] * 9 + [halo],
        (table_rows, rough, *loaded),
        aliases={2 + slot: slot for slot in range(4)},
    )
    by_partner = swapped(to_partner, 0)
    number, total, takes, masks, windows, given_1 = call(
        functools.partial(nodes_kernel, corridor),
        "nodes",
        [field] * 2 + picks(2 * owned) + [small] * 2,
        (fields[0], own, partner_section, partner_cells),
    )
    near, beyond = call(relay_kernel, "relay", [pair, pair], (by_other, masks))
    from_far = swapped(near, 0)
    *fields, takes_near, masks_near = call(
        functools.partial(border_kernel, corridor, tiles),
        "border",
        [field] * 11 + picks(owned),
        (by_partner, by_other, table_rows, near, *fields, number, total),
        aliases={4 + slot: slot for slot in range(11)},
    )
    surf, east, south, bed, _, *faces, number, total = fields
    surf_1, total_1, count, keep = call(
        functools.partial(first_kernel, corridor),
        "first",
        [field] * 4,
        (surf, east, south, number, total, windows),
        scratch=[field],
    )
    surf_1, total_1, count, keep, surf_2, east_2, south_2, total_2, given_2 = call(
        functools.partial(second_kernel, corridor, tiles),
        "second",
        [field] * 8 + [small],
        (
            *(from_far, beyond, surf, east, south, *faces, number, total, given_1),
            *(surf_1, total_1, count, keep),
        ),
        scratch=[field],
        aliases={12 + slot: slot for slot in range(4)},
    )
    surf_3, east_3, south_3, own_term, partner_term, other_term = call(
        functools.partial(third_kernel, corridor, tiles),
        "third",
        [field] * 3 + [term] * 3,
        (
            *(surf_2, east_2, south_2, *faces, total_2, keep, given_2),
            *(own, takes, masks, takes_near, masks_near),
        ),
    )
    from_other = swapped(other_term.reshape(owned), 1)
    from_partner = swapped(partner_term.reshape(owned), 0)
    _, depth, flux_east, flux_south = call(
        functools.partial(last_kernel, corridor, tiles),
        "last",
        [field, result, result, result],
        (surf_2, east_2, south_3, *faces, total_2, count, keep, bed, surf_3, east_3),
        scratch=[small, small, field, field, small, pltpu.SemaphoreType.DMA((2 + -(-chunks // 5),))],
        aliases={11: 0},
    )
    river_section = own_term.reshape(owned) + from_other + from_partner
    return (depth, flux_east, flux_south, river_section)


def solution(mesh):
    return jax.shard_map(
        local,
        mesh=mesh,
        in_specs=(
            P(("runs", "gy"), None),
            P(("runs", "gy"), None),
            P(("runs", "gy"), None),
            P(("runs", "gy")),
            P("gy", None),
            P("gy", None),
            P(),
            P(None, "gy"),
        ),
        out_specs=(
            P(("runs", "gy"), None),
            P(("runs", "gy"), None),
            P(("runs", "gy"), None),
            P(("runs", "gy")),
        ),
        check_vma=False,
    )
```

```python
import functools

import jax
import jax.numpy as jnp
from jax import lax
from jax.experimental import pallas as pl
from jax.experimental.pallas import tpu as pltpu
from jax.sharding import PartitionSpec as P

STEPS = 4

GRAV = 9.81
TSTEP = 8.0
CELL = 90.0
FLOOR = 0.05
BANK_COEF = 200.0
CELL_AREA = 8100.0
NODE_AREA = 20000.0

LANES = 128
HALO = 4
SLOPE = GRAV * TSTEP / CELL
SPREAD = TSTEP / CELL
FEED = TSTEP * BANK_COEF / CELL_AREA
DRAIN = TSTEP * BANK_COEF / NODE_AREA
VMEM_LIMIT = 32 * 1024 * 1024

VMEM_SPEC = pl.BlockSpec(memory_space=pltpu.VMEM)
HBM_SPEC = pl.BlockSpec(memory_space=pltpu.HBM)


def swapped(value, first):
    count = lax.axis_size("gy")
    pairs = []
    for low in range(first, count - 1, 2):
        pairs += [(low, low + 1), (low + 1, low)]
    return lax.ppermute(value, "gy", pairs)


def cols(chunk):
    return slice(chunk * LANES, (chunk + 1) * LANES)


def lanes_of(rows):
    return lax.broadcasted_iota(jnp.int32, (rows, LANES), 1)


def moved_left(value, following, by):
    return jnp.where(
        lanes_of(value.shape[0]) >= LANES - by,
        pltpu.roll(following, LANES - by, 1),
        pltpu.roll(value, LANES - by, 1),
    )


def moved_up(value):
    return pltpu.roll(value, value.shape[0] - 1, 0)


def split3(value):
    high = value.astype(jnp.bfloat16)
    rest = value - high.astype(jnp.float32)
    middle = rest.astype(jnp.bfloat16)
    low = (rest - middle.astype(jnp.float32)).astype(jnp.bfloat16)
    return high, middle, low


def one_hot(count, key):
    rows = lax.broadcasted_iota(jnp.int32, (count, key.shape[1]), 0)
    return jnp.where(rows == key, 1.0, 0.0)


def drag_of(mann_a, mann_b):
    pair = mann_a + mann_b
    return (0.25 * GRAV * TSTEP * SLOPE) * (pair * pair)


def looked_up(klass, entries):
    value = jnp.broadcast_to(entries[0], klass.shape)
    for k in range(1, len(entries)):
        value = jnp.where(klass == k, entries[k], value)
    return value


def face(flux, surf_a, surf_b, bed_max, drag):
    flow_depth = jnp.maximum(jnp.maximum(surf_a, surf_b) - bed_max, FLOOR)
    power = jnp.exp2((-7.0 / 3.0) * jnp.log2(flow_depth))
    driven = flux - flow_depth * (surf_b - surf_a)
    damping = 1.0 + drag * jnp.abs(flux) * power
    return driven * pl.reciprocal(damping, approx=True)


def window_sums(blocks, reach, forward):
    height = blocks[0].shape[0]
    count = len(blocks)
    spare = -(count * height) % 16
    whole = blocks + ([jnp.zeros((spare, LANES), jnp.float32)] if spare else [])
    whole = jnp.concatenate(whole, axis=0)
    high = whole.astype(jnp.bfloat16)
    low = (whole - high.astype(jnp.float32)).astype(jnp.bfloat16)
    source = lax.broadcasted_iota(jnp.int32, (2 * LANES, 2 * LANES), 0) % LANES
    target = lax.broadcasted_iota(jnp.int32, (2 * LANES, 2 * LANES), 1)
    spill = target >= LANES
    target = target % LANES
    if forward:
        ahead = source - target + jnp.where(spill, LANES, 0)
    else:
        ahead = target - source + jnp.where(spill, LANES, 0)
    band = jnp.where((ahead >= 0) & (ahead < reach), 1.0, 0.0).astype(jnp.bfloat16)
    sums = jnp.dot(
        jnp.concatenate([high, low], axis=1), band, preferred_element_type=jnp.float32
    )
    results = []
    for block in range(count):
        result = sums[block * height : (block + 1) * height, :LANES]
        beside = block + 1 if forward else block - 1
        if 0 <= beside < count:
            result = result + sums[beside * height : (beside + 1) * height, LANES:]
        results.append(result)
    return results


def east_walled(value, chunk, chunks):
    if chunk + 1 < chunks:
        return value
    return jnp.where(lanes_of(value.shape[0]) == LANES - 1, 0.0, value)


def located(cell, position, rows, ext, columns):
    base = ((position * rows - HALO) * columns + 1).astype(jnp.float32)
    offset = cell - base
    valid = (cell > 0.0) & (offset >= 0.0) & (offset < float(ext * columns))
    offset = jnp.where(valid, offset, 0.0)
    row = jnp.floor((offset + 0.5) * (1.0 / columns))
    column = (offset - row * float(columns)).astype(jnp.int32)
    row = row.astype(jnp.int32) - HALO
    row = jnp.where(row < 0, row + ext, row)
    chunk = column // LANES
    return valid, row, chunk, column - chunk * LANES


def scattered(section, key, lane, count):
    at_lane = one_hot(LANES, lane)
    parts = [at_lane] + [at_lane * part.astype(jnp.float32) for part in split3(section)]
    grid = lax.dot_general(
        one_hot(-(-count // 16) * 16, key).astype(jnp.bfloat16),
        jnp.concatenate(parts, axis=0).astype(jnp.bfloat16),
        (((1,), (1,)), ((), ())),
        preferred_element_type=jnp.float32,
    )
    number = grid[:, :LANES]
    total = (grid[:, LANES : 2 * LANES] + grid[:, 2 * LANES : 3 * LANES]) + grid[:, 3 * LANES :]
    return number, total


def border_rows(of_first, fields, south):
    outer = lax.broadcasted_iota(jnp.int32, (HALO, LANES), 0) == jnp.where(of_first, HALO - 1, 0)
    flux = jnp.where(of_first, south[:HALO], south[HALO:])
    return [
        jnp.where(outer, flux[slot : slot + 1], jnp.where(of_first, value[:HALO], value[HALO:]))
        for slot, value in enumerate(fields)
    ]


def pack_kernel(
    depth, bed, rough, east, south, section, cells, table_in, to_other, own, *refs
):
    held, held_rough, held_cells, table, sems = refs
    rows, columns = depth.shape
    chunks = columns // LANES
    even = lax.axis_index("gy") % 2 == 0
    start = pl.multiple_of(jnp.where(even, 0, rows - 8), 8)
    near = pl.ds(start, 8)
    copies = [
        pltpu.make_async_copy(source, target, sems.at[slot])
        for slot, (source, target) in enumerate(
            (
                (rough.at[near, :], held_rough),
                (bed.at[near, :], held.at[1]),
                (depth.at[near, :], held.at[0]),
                (east.at[near, :], held.at[2]),
                (south.at[near, :], held.at[3]),
                (section, own.at[pl.ds(0, 1), :]),
                (cells, held_cells),
                (table_in, table),
            )
        )
    ]
    for copy in copies:
        copy.start()
    for copy in copies:
        copy.wait()
    own[1:2, :] = (held_cells[0:1, :] + 1).astype(jnp.float32)
    entries = [
        jnp.broadcast_to(table[:, k : k + 1], (1, LANES)) for k in range(table.shape[1])
    ]
    manns = [looked_up(held_rough[:, cols(chunk)], entries) for chunk in range(chunks)]
    row = lax.broadcasted_iota(jnp.int32, (8, LANES), 0)
    beds = [held[1, :, cols(chunk)] for chunk in range(chunks)]
    surfs = [held[0, :, cols(chunk)] + beds[chunk] for chunk in range(chunks)]

    def moved(values):
        rolled = [pltpu.roll(value, LANES - 1, 1) for value in values]
        rolled.append(rolled[-1])
        edge = lanes_of(8) == LANES - 1
        return [jnp.where(edge, rolled[c + 1], rolled[c]) for c in range(chunks)]

    beds_left, surfs_left, manns_left = moved(beds), moved(surfs), moved(manns)
    for chunk in range(chunks):
        at = cols(chunk)
        m0, b0, s0 = manns[chunk], beds[chunk], surfs[chunk]
        bed_max = jnp.maximum(b0, beds_left[chunk])
        drag = drag_of(m0, manns_left[chunk])
        q0 = (1.0 / SLOPE) * held[2, :, at]
        new_east = face(q0, s0, surfs_left[chunk], bed_max, drag)
        new_east = east_walled(new_east, chunk, chunks)
        bed_max = jnp.maximum(b0, moved_up(b0))
        drag = drag_of(m0, moved_up(m0))
        q0 = (1.0 / SLOPE) * held[3, :, at]
        new_south = jnp.where(row == 7, q0, face(q0, s0, moved_up(s0), bed_max, drag))
        fields = (s0, b0, held_rough[:, at].astype(jnp.float32), new_east)
        for slot, block in enumerate(border_rows(even, fields, new_south)):
            to_other[slot * chunks + chunk] = block
    to_other[4 * chunks, 0:2, :] = own[...]


def join_kernel(before, section, cells, to_other):
    nodes = to_other.shape[0] - 1
    to_other[nodes, 2:3, :] = section[...]
    to_other[nodes, 3:4, :] = (cells[0:1, :] + 1).astype(jnp.float32)


def relay_kernel(by_other, prepared, near, beyond):
    del prepared
    nodes = by_other.shape[0] - 1
    near[...] = by_other[nodes, 0:2, :]
    beyond[...] = by_other[nodes, 2:4, :]


def picking(reach, rows, key, lane, takes, masks):
    for block in range(key.shape[1] // LANES):
        mine = slice(block * LANES, (block + 1) * LANES)

        def column(row):
            wide = jnp.broadcast_to(row[:, mine].astype(jnp.float32), (LANES, LANES))
            return jnp.transpose(wide).astype(jnp.int32)

        spread = lanes_of(LANES)
        at = column(key)
        after = jnp.where(at < 0, at, at + rows)
        for first in range(0, takes.shape[2], LANES):
            for half, place in enumerate((at, after)):
                hit = jnp.where(spread + first == place, 1.0, 0.0)
                takes[half, mine, first : first + LANES] = hit.astype(jnp.bfloat16)
        ahead = spread - column(lane)
        masks[0, mine, :] = jnp.where((ahead >= 0) & (ahead < reach), 1.0, 0.0)
        masks[1, mine, :] = jnp.where(ahead + LANES < reach, 1.0, 0.0)


def load_kernel(
    depth_in, east_in, south_in, bed_in, rough_in, table_in, *refs
):
    surf, east, south, bed, rough, table_rows, table, sems = refs
    rows, columns = depth_in.shape
    own = pl.ds(0, rows)
    copies = [
        pltpu.make_async_copy(source, target.at[own, :], sems.at[slot])
        for slot, (source, target) in enumerate(
            (
                (depth_in, surf),
                (bed_in, bed),
                (rough_in, rough),
                (east_in, east),
                (south_in, south),
            )
        )
    ]
    copies.append(pltpu.make_async_copy(table_in, table, sems.at[5]))
    for copy in copies:
        copy.start()
    copies[5].wait()
    for k in range(table_rows.shape[0]):
        table_rows[k : k + 1, :] = jnp.broadcast_to(table[:, k : k + 1], (1, LANES))
    for copy in copies[:5]:
        copy.wait()


def prepare_kernel(table_rows, rough, *refs):
    surf, east, south, bed = refs[4:8]
    mann, bed_e, bed_s, drag_e, drag_s, to_partner = refs[8:]
    ext, columns = surf.shape
    rows = ext - 2 * HALO
    chunks = columns // LANES
    even = lax.axis_index("gy") % 2 == 0
    entries = [table_rows[k : k + 1, :] for k in range(table_rows.shape[0])]
    for chunk in range(chunks):
        at = cols(chunk)
        mann[:rows, at] = looked_up(rough[:, at], entries)
        surf[:rows, at] = surf[:rows, at] + bed[:rows, at]

    kept = lax.broadcasted_iota(jnp.int32, (rows, LANES), 0) == rows - 1
    for chunk in range(chunks):
        at, then = cols(chunk), cols(min(chunk + 1, chunks - 1))
        s0, b0, m0 = surf[:rows, at], bed[:rows, at], mann[:rows, at]
        bed_max = jnp.maximum(b0, moved_left(b0, bed[:rows, then], 1))
        drag = drag_of(m0, moved_left(m0, mann[:rows, then], 1))
        bed_e[:rows, at] = bed_max
        drag_e[:rows, at] = drag
        q0 = (1.0 / SLOPE) * east[:rows, at]
        new_east = face(q0, s0, moved_left(s0, surf[:rows, then], 1), bed_max, drag)
        new_east = east_walled(new_east, chunk, chunks)
        east[:rows, at] = new_east
        bed_max = jnp.maximum(b0, moved_up(b0))
        drag = drag_of(m0, moved_up(m0))
        bed_s[:rows, at] = bed_max
        drag_s[:rows, at] = drag
        q0 = (1.0 / SLOPE) * south[:rows, at]
        new_south = jnp.where(kept, q0, face(q0, s0, moved_up(s0), bed_max, drag))
        south[:rows, at] = new_south

        def ends(value):
            return jnp.where(even, value[rows - 8 :], value[:8])

        fields = (ends(s0), ends(b0), ends(rough[:, at].astype(jnp.float32)), ends(new_east))
        blocks = border_rows(jnp.logical_not(even), fields, ends(new_south))
        for slot, block in enumerate(blocks):
            to_partner[slot * chunks + chunk] = block


def nodes_kernel(reach, surf, own, partner_section, partner_cells, *refs):
    number, total, takes, masks, windows, given_1 = refs
    rows = surf.shape[0] - 2 * HALO
    ext, columns = number.shape
    chunks = columns // LANES
    tiles = lax.axis_size("gy")
    position = lax.axis_index("gy")
    side = jnp.where(position % 2 == 0, 1, -1)
    partner = jnp.where(position + side < tiles, partner_cells[0:1, :] + 1, 0).astype(jnp.float32)
    section = jnp.concatenate([own[0:1, :], partner_section[...]], axis=1)
    cell = jnp.concatenate([own[1:2, :], partner], axis=1)
    valid, node_row, node_chunk, node_lane = located(cell, position, rows, ext, columns)
    key = jnp.where(valid, node_chunk * ext + node_row, -1)
    starts, levels = scattered(section, key, node_lane, chunks * ext)
    for chunk in range(chunks):
        at = cols(chunk)
        number[:, at] = starts[chunk * ext : (chunk + 1) * ext]
        total[:, at] = levels[chunk * ext : (chunk + 1) * ext]
    key = jnp.where(valid & (node_row < rows), node_chunk * rows + node_row, -1)
    picking(reach, rows, key, node_lane, takes, masks)
    sums = window_sums([surf[:rows, cols(chunk)] for chunk in range(chunks)], reach, True)
    for chunk in range(chunks):
        windows[:, cols(chunk)] = sums[chunk]
    give(reach, 0, surf, None, given_1)


def wall_of(ext, tiles):
    position = lax.axis_index("gy")
    rows = ext - 2 * HALO
    row = lax.broadcasted_iota(jnp.int32, (16, LANES), 0) + (ext - 16)
    return ((row == ext - 1) & (position == 0)) | ((row == rows - 1) & (position == tiles - 1))


def border_kernel(reach, tiles, by_partner, by_other, table_rows, near, *refs):
    surf, east, south, bed, mann, bed_e, bed_s, drag_e, drag_s, number, total, takes, masks = refs[11:]
    ext, columns = surf.shape
    rows = ext - 2 * HALO
    chunks = columns // LANES
    position = lax.axis_index("gy")
    even = position % 2 == 0
    valid, node_row, node_chunk, node_lane = located(near[1:2, :], position, rows, ext, columns)
    key = jnp.where(valid, node_chunk * ext + node_row, -1)
    starts, levels = scattered(near[0:1, :], key, node_lane, chunks * ext)

    entries = [table_rows[k : k + 1, :] for k in range(table_rows.shape[0])]
    row = lax.broadcasted_iota(jnp.int32, (2 * HALO, LANES), 0)
    for chunk in range(chunks):
        at = cols(chunk)
        halos = []
        flux = jnp.zeros((2 * HALO, LANES), jnp.float32)
        for slot in range(4):
            a, b = by_partner[slot * chunks + chunk], by_other[slot * chunks + chunk]
            below = jnp.where(even, a, b)
            above = jnp.where(even, b, a)
            halos.append(jnp.concatenate([below, above], axis=0))
            flux = jnp.where(row == slot, below[HALO - 1 :], flux)
            flux = jnp.where(row == HALO + slot, above[:1], flux)
        surf[rows:, at] = halos[0]
        bed[rows:, at] = halos[1]
        mann[rows:, at] = looked_up(halos[2].astype(jnp.int32), entries)
        east[rows:, at] = halos[3]
        south[rows:, at] = flux

    key = jnp.where(valid & (node_row < rows), node_chunk * rows + node_row, -1)
    picking(reach, rows, key, node_lane, takes, masks)

    wall = wall_of(ext, tiles)
    kept = lax.broadcasted_iota(jnp.int32, (16, LANES), 0) % 8 < 7
    for chunk in range(chunks):
        at, then = cols(chunk), cols(min(chunk + 1, chunks - 1))
        number[:, at] += starts[chunk * ext : (chunk + 1) * ext]
        total[:, at] += levels[chunk * ext : (chunk + 1) * ext]
        b0, m0 = bed[rows:, at], mann[rows:, at]
        bed_e[rows:, at] = jnp.maximum(b0, moved_left(b0, bed[rows:, then], 1))
        drag_e[rows:, at] = drag_of(m0, moved_left(m0, mann[rows:, then], 1))

        def rolled_up(ref):
            value = jnp.concatenate([ref[rows - 8 :, at], ref[:8, at]], axis=0)
            return value[:16], moved_up(value)[:16]

        s0, s1 = rolled_up(surf)
        b0, b1 = rolled_up(bed)
        m0, m1 = rolled_up(mann)
        bed_max = jnp.maximum(b0, b1)
        drag = drag_of(m0, m1)
        bed_s[rows - 8 :, at] = bed_max
        drag_s[rows - 8 :, at] = drag
        q0 = south[rows - 8 :, at]
        new_south = jnp.where(kept, q0, face(q0, s0, s1, bed_max, drag))
        south[rows - 8 :, at] = jnp.where(wall, 0.0, new_south)


def fluxes(mine, upper, wall, before, faces, east_out, south_out, scale=None):
    surf, east, south = before
    bed_e, bed_s, drag_e, drag_s = faces
    ext, columns = surf.shape
    chunks = columns // LANES
    rolled = lane = None
    if east_out is not None:
        rolled = pltpu.roll(surf[mine, cols(0)], LANES - 1, 1)
        lane = lanes_of(rolled.shape[0])
    for chunk in range(chunks):
        at = cols(chunk)
        if east_out is not None:
            s0 = surf[mine, at]
            rolled_then = rolled
            if chunk + 1 < chunks:
                rolled_then = pltpu.roll(surf[mine, cols(chunk + 1)], LANES - 1, 1)
            left = jnp.where(lane >= LANES - 1, rolled_then, rolled)
            rolled = rolled_then
            new_east = face(east[mine, at], s0, left, bed_e[mine, at], drag_e[mine, at])
            if scale is not None:
                new_east = scale * new_east
            east_out[mine, at] = east_walled(new_east, chunk, chunks)
        if upper:
            s0 = surf[: upper + 8, at]
            s1 = moved_up(s0)[:upper]
            new_south = face(south[:upper, at], s0[:upper], s1, bed_s[:upper, at], drag_s[:upper, at])
            if scale is not None:
                new_south = scale * new_south
            south_out[:upper, at] = new_south
        if wall is not None:
            low = slice(ext - 16, ext)
            s0 = jnp.concatenate([surf[low, at], surf[:8, at]], axis=0)
            s1 = moved_up(s0)[:16]
            new_south = face(south[low, at], s0[:16], s1, bed_s[low, at], drag_s[low, at])
            if scale is not None:
                new_south = scale * new_south
            south_out[low, at] = jnp.where(wall, 0.0, new_south)


def settled(mine, surf, east, south, keep, sums, spread=SPREAD * SLOPE):
    ext, columns = surf.shape
    rolled = 0.0
    for chunk in range(columns // LANES):
        at = cols(chunk)
        new_east = east[mine, at]
        new_south = south[:, at]
        lane = lanes_of(new_east.shape[0])
        rolled_before, rolled = rolled, pltpu.roll(new_east, 1, 1)
        west = jnp.where(lane < 1, rolled_before, rolled)
        north = pltpu.roll(new_south, 1, 0)[mine]
        inflow = west + north
        s0 = surf[mine, at]
        outflow = new_east + new_south[mine]
        yield chunk, keep[mine, at] * s0 + (spread * (inflow - outflow) + sums[chunk])


def refill(corridor, mine, surf, total, count, total_out, windows=None):
    chunks = surf.shape[1] // LANES
    if windows is None:
        windows = window_sums([surf[mine, cols(chunk)] for chunk in range(chunks)], corridor, True)
    for chunk in range(chunks):
        at = cols(chunk)
        kept = (1.0 - corridor * DRAIN) * total[mine, at]
        total_out[mine, at] = kept + count[mine, at] * windows[chunk]


def summed(corridor, mine, total):
    chunks = total.shape[1] // LANES
    return window_sums([total[mine, cols(chunk)] for chunk in range(chunks)], corridor, False)


def exchange(corridor, mine, surf, total, count, total_out, windows=None):
    sums = summed(corridor, mine, total)
    refill(corridor, mine, surf, total, count, total_out, windows)
    return sums


def give(corridor, step, surf, before, after):
    rows, columns = after.shape
    weight = DRAIN * (1.0 - corridor * DRAIN) ** (STEPS - 1 - step)
    for chunk in range(columns // LANES):
        at = cols(chunk)
        value = weight * surf[:rows, at]
        after[:, at] = value if before is None else before[:, at] + value


def first_kernel(corridor, surf, east, south, number, total, windows, *refs):
    surf_1, total_1, count, keep, total_0 = refs
    rows = surf.shape[0] - 2 * HALO
    chunks = surf.shape[1] // LANES
    own = slice(0, rows)
    covering = window_sums([number[own, cols(chunk)] for chunk in range(chunks)], corridor, False)
    for chunk in range(chunks):
        at = cols(chunk)
        count[own, at] = (FEED * DRAIN) * number[own, at]
        keep[own, at] = 1.0 - FEED * covering[chunk]
        total_0[own, at] = FEED * total[own, at]
    windows = [windows[:, cols(chunk)] for chunk in range(chunks)]
    sums = exchange(corridor, own, surf, total_0, count, total_1, windows)
    for chunk, new_surf in settled(own, surf, east, south, keep, sums):
        surf_1[own, cols(chunk)] = new_surf


def second_kernel(corridor, tiles, far, beyond, surf, east, south, *refs):
    faces = refs[:4]
    number, total, given_1 = refs[4:7]
    surf_1, total_1, count, keep = refs[11:15]
    surf_2, east_2, south_2, total_2, given_2, total_0 = refs[15:]
    ext, columns = surf.shape
    rows = ext - 2 * HALO
    chunks = columns // LANES
    position = lax.axis_index("gy")
    tail = slice(rows, ext)

    section = jnp.concatenate([far[0:1, :], beyond[0:1, :]], axis=1)
    cell = jnp.concatenate([far[1:2, :], beyond[1:2, :]], axis=1)
    valid, node_row, node_chunk, node_lane = located(cell, position, rows, ext, columns)
    key = jnp.where(valid & (node_row >= rows), node_chunk * 8 + (node_row - rows), -1)
    starts, levels = scattered(section, key, node_lane, chunks * 8)
    starting = [
        number[tail, cols(chunk)] + starts[chunk * 8 : chunk * 8 + 8] for chunk in range(chunks)
    ]
    covering = window_sums(starting, corridor, False)
    for chunk in range(chunks):
        at = cols(chunk)
        count[tail, at] = (FEED * DRAIN) * starting[chunk]
        keep[tail, at] = 1.0 - FEED * covering[chunk]
        total_0[tail, at] = FEED * (total[tail, at] + levels[chunk * 8 : chunk * 8 + 8])
    sums = exchange(corridor, tail, surf, total_0, count, total_1)

    own = slice(0, rows)
    before = (surf_1, east, south)
    fluxes(own, rows - 8, None, before, faces, east_2, south_2)
    own_sums = exchange(corridor, own, surf_1, total_1, count, total_2)
    give(corridor, 1, surf_1, given_1, given_2)

    for chunk, new_surf in settled(tail, surf, east, south, keep, sums):
        surf_1[tail, cols(chunk)] = new_surf
    tail_sums = exchange(corridor, tail, surf_1, total_1, count, total_2)
    fluxes(tail, 0, wall_of(ext, tiles), before, faces, east_2, south_2)
    for mine, sums in ((own, own_sums), (tail, tail_sums)):
        for chunk, new_surf in settled(mine, surf_1, east_2, south_2, keep, sums):
            surf_2[mine, cols(chunk)] = new_surf


def third_kernel(corridor, tiles, surf, east, south, *refs):
    faces = refs[:4]
    total, keep, given_2, own, takes, masks, takes_near, masks_near = refs[4:12]
    surf_3, east_3, south_3, own_term, partner_term, other_term = refs[12:]
    ext, columns = surf.shape
    rows = ext - 2 * HALO
    mine = slice(0, rows)
    owned = own.shape[1]
    chunks = columns // LANES
    sums = summed(corridor, mine, total)
    fluxes(
        mine, rows - 8, wall_of(ext, tiles), (surf, east, south), faces, east_3, south_3
    )
    weight = DRAIN * (1.0 - corridor * DRAIN)
    levels = []
    for chunk, new_surf in settled(mine, surf, east_3, south_3, keep, sums):
        at = cols(chunk)
        surf_3[mine, at] = new_surf
        levels.append(given_2[:, at] + weight * surf[mine, at] + DRAIN * new_surf)
    spare = takes.shape[2] - chunks * rows
    if spare:
        levels.append(jnp.zeros((spare, LANES), jnp.float32))
    levels = jnp.concatenate(levels, axis=0)
    high = levels.astype(jnp.bfloat16)
    low = (levels - high.astype(jnp.float32)).astype(jnp.bfloat16)
    picked = jnp.dot(
        jnp.concatenate([takes[0], takes_near[0], takes[1], takes_near[1]], axis=0),
        jnp.concatenate([high, low], axis=1),
        preferred_element_type=jnp.float32,
    )
    hit = jnp.concatenate([masks[0], masks_near[0], masks[1], masks_near[1]], axis=0)
    picked = (picked * jnp.concatenate([hit, hit], axis=1)).astype(jnp.bfloat16)
    picked = jnp.concatenate([picked[: 3 * owned], picked[3 * owned :]], axis=1)
    terms = lax.dot_general(
        jnp.ones((8, 4 * LANES), jnp.bfloat16),
        picked,
        (((1,), (1,)), ((), ())),
        preferred_element_type=jnp.float32,
    )[0:1]
    own_term[...] = (1.0 - corridor * DRAIN) ** STEPS * own[0:1, :] + terms[:, :owned]
    partner_term[...] = terms[:, owned : 2 * owned]
    other_term[...] = terms[:, 2 * owned :]


def last_kernel(corridor, tiles, early, *refs):
    inputs, outputs, scratch = refs[:13], refs[15:19], refs[21:]
    if early:
        refs[19][...] = refs[13][...]
        refs[20][...] = refs[14][...]
    else:
        outputs, scratch = refs[16:20], refs[20:]
    position = lax.axis_index("gy")
    at_edge = (position == 0) | (position == tiles - 1)

    @pl.when(at_edge if early else jnp.logical_not(at_edge))
    def _():
        last_substep(corridor, tiles, *inputs, *outputs, *scratch)


def last_substep(corridor, tiles, surf_2, east_2, south_3, *refs):
    faces = refs[:4]
    total_2, count, keep, bed, _, east_3 = refs[4:10]
    surf_3, depth_out, east_out, south_out = refs[10:14]
    depth_4, east_4, south_4, east_tail, total_3, sems = refs[14:]
    ext, columns = surf_2.shape
    rows = ext - 2 * HALO
    chunks = columns // LANES
    own, tail = slice(0, rows), slice(rows, ext)

    def copy(slot, source, target, first, last):
        part = pl.ds(first * LANES, (last - first) * LANES)
        return pltpu.make_async_copy(
            source.at[pl.ds(0, rows), part], target.at[:, part], sems.at[slot]
        )

    before = (surf_3, east_3, south_3)
    tail_sums = summed(corridor, tail, total_2)
    refill(corridor, own, surf_2, total_2, count, total_3)
    fluxes(own, rows - 8, None, before, faces, east_4, south_4, scale=SLOPE)
    copies = [copy(0, east_4, east_out, 0, chunks)]
    copies[0].start()
    fluxes(tail, 0, None, (surf_2, east_2, None), faces, east_tail, None)
    for chunk, new_surf in settled(tail, surf_2, east_tail, south_3, keep, tail_sums):
        surf_3[tail, cols(chunk)] = new_surf
    sums = summed(corridor, own, total_3)
    fluxes(slice(0, 0), 0, wall_of(ext, tiles), before, faces, None, south_4, scale=SLOPE)
    copies.append(copy(1, south_4, south_out, 0, chunks))
    copies[1].start()
    group = 5
    for chunk, new_surf in settled(own, surf_3, east_4, south_4, keep, sums, spread=SPREAD):
        at = cols(chunk)
        depth_4[:, at] = new_surf - bed[own, at]
        if (chunk + 1) % group == 0 or chunk + 1 == chunks:
            first = chunk // group
            copies.append(copy(2 + first, depth_4, depth_out, first * group, chunk + 1))
            copies[-1].start()
    for one in copies:
        one.wait()


def local(
    depth, flux_east, flux_south, river_section, bed_level, rough_class, manning_table, bank_cell
):
    rows, columns = depth.shape
    owned = river_section.shape[0]
    corridor = bank_cell.shape[0]
    tiles = lax.axis_size("gy")
    ext = rows + 2 * HALO
    chunks = columns // LANES
    partner_section = swapped(river_section, 0).reshape(1, owned)
    partner_cells = swapped(bank_cell, 0)

    def held(value):
        return pltpu.with_memory_space_constraint(value, pltpu.VMEM)

    def far(value):
        return pltpu.with_memory_space_constraint(value, pltpu.HBM)

    params = pltpu.CompilerParams(vmem_limit_bytes=VMEM_LIMIT)
    halo = pltpu.VMEM((4 * chunks, HALO, LANES), jnp.float32)
    wide = pltpu.VMEM((4 * chunks + 1, HALO, LANES), jnp.float32)
    field = pltpu.VMEM((ext, columns), jnp.float32)
    small = pltpu.VMEM((rows, columns), jnp.float32)
    term = pltpu.VMEM((1, owned), jnp.float32)
    pair = pltpu.VMEM((2, owned), jnp.float32)
    result = pltpu.HBM((rows, columns), jnp.float32)
    cells = -(-chunks * rows // LANES) * LANES

    def call(kernel, name, outs, values, scratch=(), aliases=None):
        return pl.pallas_call(
            kernel,
            out_shape=outs,
            in_specs=[VMEM_SPEC] * len(values),
            out_specs=[HBM_SPEC if out is result else VMEM_SPEC for out in outs],
            scratch_shapes=scratch,
            input_output_aliases=aliases or {},
            compiler_params=params,
            name=name,
        )(*[held(value) for value in values])

    def picks(nodes):
        return [
            pltpu.VMEM((2, nodes, cells), jnp.bfloat16),
            pltpu.VMEM((2, nodes, LANES), jnp.float32),
        ]

    classes = manning_table.shape[0]
    table = far(manning_table.reshape(1, classes))
    table_held = pltpu.VMEM((1, classes), jnp.float32)
    to_other, own = pl.pallas_call(
        pack_kernel,
        out_shape=[wide, pair],
        in_specs=[HBM_SPEC] * 8,
        out_specs=[VMEM_SPEC] * 2,
        scratch_shapes=[
            pltpu.VMEM((4, 8, columns), jnp.float32),
            pltpu.VMEM((8, columns), jnp.int32),
            pltpu.VMEM((corridor, owned), jnp.int32),
            table_held,
            pltpu.SemaphoreType.DMA((8,)),
        ],
        compiler_params=params,
        name="pack",
    )(
        *[far(value) for value in (depth, bed_level, rough_class, flux_east, flux_south)],
        far(river_section.reshape(1, owned)),
        far(bank_cell),
        table,
    )
    (to_other,) = call(
        join_kernel,
        "join",
        [wide],
        (to_other, partner_section, partner_cells),
        aliases={0: 0},
    )
    by_other = swapped(to_other, 1)
    *loaded, rough, table_rows = pl.pallas_call(
        load_kernel,
        out_shape=[field] * 4
        + [pltpu.VMEM((rows, columns), jnp.int32), pltpu.VMEM((classes, LANES), jnp.float32)],
        in_specs=[HBM_SPEC] * 6,
        out_specs=[VMEM_SPEC] * 6,
        scratch_shapes=[table_held, pltpu.SemaphoreType.DMA((6,))],
        compiler_params=params,
        name="load",
    )(
        *[far(value) for value in (depth, flux_east, flux_south, bed_level, rough_class)],
        table,
    )
    *fields, to_partner = call(
        prepare_kernel,
        "prepare",
        [field] * 9 + [halo],
        (table_rows, rough, *loaded),
        aliases={2 + slot: slot for slot in range(4)},
    )
    by_partner = swapped(to_partner, 0)
    number, total, takes, masks, windows, given_1 = call(
        functools.partial(nodes_kernel, corridor),
        "nodes",
        [field] * 2 + picks(2 * owned) + [small] * 2,
        (fields[0], own, partner_section, partner_cells),
    )
    near, beyond = call(relay_kernel, "relay", [pair, pair], (by_other, masks))
    from_far = swapped(near, 0)
    *fields, takes_near, masks_near = call(
        functools.partial(border_kernel, corridor, tiles),
        "border",
        [field] * 11 + picks(owned),
        (by_partner, by_other, table_rows, near, *fields, number, total),
        aliases={4 + slot: slot for slot in range(11)},
    )
    surf, east, south, bed, _, *faces, number, total = fields
    surf_1, total_1, count, keep = call(
        functools.partial(first_kernel, corridor),
        "first",
        [field] * 4,
        (surf, east, south, number, total, windows),
        scratch=[field],
    )
    surf_1, total_1, count, keep, surf_2, east_2, south_2, total_2, given_2 = call(
        functools.partial(second_kernel, corridor, tiles),
        "second",
        [field] * 8 + [small],
        (
            *(from_far, beyond, surf, east, south, *faces, number, total, given_1),
            *(surf_1, total_1, count, keep),
        ),
        scratch=[field],
        aliases={12 + slot: slot for slot in range(4)},
    )
    surf_3, east_3, south_3, own_term, partner_term, other_term = call(
        functools.partial(third_kernel, corridor, tiles),
        "third",
        [field] * 3 + [term] * 3,
        (
            *(surf_2, east_2, south_2, *faces, total_2, keep, given_2),
            *(own, takes, masks, takes_near, masks_near),
        ),
    )
    last_in = [
        held(value)
        for value in (surf_2, east_2, south_3, *faces, total_2, count, keep, bed, surf_3, east_3)
    ]
    last_scratch = [small, small, field, field, small]
    last_scratch.append(pltpu.SemaphoreType.DMA((2 + -(-chunks // 5),)))
    surf_3, *results, partner_term, other_term = pl.pallas_call(
        functools.partial(last_kernel, corridor, tiles, True),
        out_shape=[field] + [result] * 3 + [term] * 2,
        in_specs=[VMEM_SPEC] * 15,
        out_specs=[VMEM_SPEC] + [HBM_SPEC] * 3 + [VMEM_SPEC] * 2,
        scratch_shapes=last_scratch,
        input_output_aliases={11: 0},
        compiler_params=params,
        name="last_early",
    )(*last_in, held(partner_term), held(other_term))
    from_other = swapped(other_term.reshape(owned), 1)
    from_partner = swapped(partner_term.reshape(owned), 0)
    last_in[11] = held(surf_3)
    _, depth, flux_east, flux_south = pl.pallas_call(
        functools.partial(last_kernel, corridor, tiles, False),
        out_shape=[field] + [result] * 3,
        in_specs=[VMEM_SPEC] * 13 + [HBM_SPEC] * 3,
        out_specs=[VMEM_SPEC] + [HBM_SPEC] * 3,
        scratch_shapes=last_scratch,
        input_output_aliases={11: 0, 13: 1, 14: 2, 15: 3},
        compiler_params=params,
        name="last",
    )(*last_in, *[far(value) for value in results])
    river_section = own_term.reshape(owned) + from_other + from_partner
    return (depth, flux_east, flux_south, river_section)


def solution(mesh):
    return jax.shard_map(
        local,
        mesh=mesh,
        in_specs=(
            P(("runs", "gy"), None),
            P(("runs", "gy"), None),
            P(("runs", "gy"), None),
            P(("runs", "gy")),
            P("gy", None),
            P("gy", None),
            P(),
            P(None, "gy"),
        ),
        out_specs=(
            P(("runs", "gy"), None),
            P(("runs", "gy"), None),
            P(("runs", "gy"), None),
            P(("runs", "gy")),
        ),
        check_vma=False,
    )
```

```python
import functools

import jax
import jax.numpy as jnp
from jax import lax
from jax.experimental import pallas as pl
from jax.experimental.pallas import tpu as pltpu
from jax.sharding import PartitionSpec as P

STEPS = 4

GRAV = 9.81
TSTEP = 8.0
CELL = 90.0
FLOOR = 0.05
BANK_COEF = 200.0
CELL_AREA = 8100.0
NODE_AREA = 20000.0

LANES = 128
HALO = 4
SLOPE = GRAV * TSTEP / CELL
SPREAD = TSTEP / CELL
FEED = TSTEP * BANK_COEF / CELL_AREA
DRAIN = TSTEP * BANK_COEF / NODE_AREA
VMEM_LIMIT = 32 * 1024 * 1024

VMEM_SPEC = pl.BlockSpec(memory_space=pltpu.VMEM)
HBM_SPEC = pl.BlockSpec(memory_space=pltpu.HBM)


def swapped(value, first):
    count = lax.axis_size("gy")
    pairs = []
    for low in range(first, count - 1, 2):
        pairs += [(low, low + 1), (low + 1, low)]
    return lax.ppermute(value, "gy", pairs)


def cols(chunk):
    return slice(chunk * LANES, (chunk + 1) * LANES)


def lanes_of(rows):
    return lax.broadcasted_iota(jnp.int32, (rows, LANES), 1)


def moved_left(value, following, by):
    return jnp.where(
        lanes_of(value.shape[0]) >= LANES - by,
        pltpu.roll(following, LANES - by, 1),
        pltpu.roll(value, LANES - by, 1),
    )


def moved_up(value):
    return pltpu.roll(value, value.shape[0] - 1, 0)


def split3(value):
    high = value.astype(jnp.bfloat16)
    rest = value - high.astype(jnp.float32)
    middle = rest.astype(jnp.bfloat16)
    low = (rest - middle.astype(jnp.float32)).astype(jnp.bfloat16)
    return high, middle, low


def one_hot(count, key):
    rows = lax.broadcasted_iota(jnp.int32, (count, key.shape[1]), 0)
    return jnp.where(rows == key, 1.0, 0.0)


def drag_of(mann_a, mann_b):
    pair = mann_a + mann_b
    return (0.25 * GRAV * TSTEP * SLOPE) * (pair * pair)


def looked_up(klass, entries):
    value = jnp.broadcast_to(entries[0], klass.shape)
    for k in range(1, len(entries)):
        value = jnp.where(klass == k, entries[k], value)
    return value


def face(flux, surf_a, surf_b, bed_max, drag):
    flow_depth = jnp.maximum(jnp.maximum(surf_a, surf_b) - bed_max, FLOOR)
    power = jnp.exp2((-7.0 / 3.0) * jnp.log2(flow_depth))
    driven = flux - flow_depth * (surf_b - surf_a)
    damping = 1.0 + drag * jnp.abs(flux) * power
    return driven * pl.reciprocal(damping, approx=True)


def window_sums(blocks, reach, forward):
    height = blocks[0].shape[0]
    count = len(blocks)
    spare = -(count * height) % 16
    whole = blocks + ([jnp.zeros((spare, LANES), jnp.float32)] if spare else [])
    whole = jnp.concatenate(whole, axis=0)
    high = whole.astype(jnp.bfloat16)
    low = (whole - high.astype(jnp.float32)).astype(jnp.bfloat16)
    source = lax.broadcasted_iota(jnp.int32, (2 * LANES, 2 * LANES), 0) % LANES
    target = lax.broadcasted_iota(jnp.int32, (2 * LANES, 2 * LANES), 1)
    spill = target >= LANES
    target = target % LANES
    if forward:
        ahead = source - target + jnp.where(spill, LANES, 0)
    else:
        ahead = target - source + jnp.where(spill, LANES, 0)
    band = jnp.where((ahead >= 0) & (ahead < reach), 1.0, 0.0).astype(jnp.bfloat16)
    sums = jnp.dot(
        jnp.concatenate([high, low], axis=1), band, preferred_element_type=jnp.float32
    )
    results = []
    for block in range(count):
        result = sums[block * height : (block + 1) * height, :LANES]
        beside = block + 1 if forward else block - 1
        if 0 <= beside < count:
            result = result + sums[beside * height : (beside + 1) * height, LANES:]
        results.append(result)
    return results


def east_walled(value, chunk, chunks):
    if chunk + 1 < chunks:
        return value
    return jnp.where(lanes_of(value.shape[0]) == LANES - 1, 0.0, value)


def located(cell, position, rows, ext, columns):
    base = ((position * rows - HALO) * columns + 1).astype(jnp.float32)
    offset = cell - base
    valid = (cell > 0.0) & (offset >= 0.0) & (offset < float(ext * columns))
    offset = jnp.where(valid, offset, 0.0)
    row = jnp.floor((offset + 0.5) * (1.0 / columns))
    column = (offset - row * float(columns)).astype(jnp.int32)
    row = row.astype(jnp.int32) - HALO
    row = jnp.where(row < 0, row + ext, row)
    chunk = column // LANES
    return valid, row, chunk, column - chunk * LANES


def scattered(section, key, lane, count):
    at_lane = one_hot(LANES, lane)
    parts = [at_lane] + [at_lane * part.astype(jnp.float32) for part in split3(section)]
    grid = lax.dot_general(
        one_hot(-(-count // 16) * 16, key).astype(jnp.bfloat16),
        jnp.concatenate(parts, axis=0).astype(jnp.bfloat16),
        (((1,), (1,)), ((), ())),
        preferred_element_type=jnp.float32,
    )
    number = grid[:, :LANES]
    total = (grid[:, LANES : 2 * LANES] + grid[:, 2 * LANES : 3 * LANES]) + grid[:, 3 * LANES :]
    return number, total


def border_rows(of_first, fields, south):
    outer = lax.broadcasted_iota(jnp.int32, (HALO, LANES), 0) == jnp.where(of_first, HALO - 1, 0)
    flux = jnp.where(of_first, south[:HALO], south[HALO:])
    return [
        jnp.where(outer, flux[slot : slot + 1], jnp.where(of_first, value[:HALO], value[HALO:]))
        for slot, value in enumerate(fields)
    ]


def pack_kernel(
    depth, bed, rough, east, south, section, cells, table_in, to_other, own, *refs
):
    held, held_rough, held_cells, table, sems = refs
    rows, columns = depth.shape
    chunks = columns // LANES
    even = lax.axis_index("gy") % 2 == 0
    start = pl.multiple_of(jnp.where(even, 0, rows - 8), 8)
    near = pl.ds(start, 8)
    copies = [
        pltpu.make_async_copy(source, target, sems.at[slot])
        for slot, (source, target) in enumerate(
            (
                (rough.at[near, :], held_rough),
                (bed.at[near, :], held.at[1]),
                (depth.at[near, :], held.at[0]),
                (east.at[near, :], held.at[2]),
                (south.at[near, :], held.at[3]),
                (section, own.at[pl.ds(0, 1), :]),
                (cells, held_cells),
                (table_in, table),
            )
        )
    ]
    for copy in copies:
        copy.start()
    for copy in copies:
        copy.wait()
    own[1:2, :] = (held_cells[0:1, :] + 1).astype(jnp.float32)
    entries = [
        jnp.broadcast_to(table[:, k : k + 1], (1, LANES)) for k in range(table.shape[1])
    ]
    manns = [looked_up(held_rough[:, cols(chunk)], entries) for chunk in range(chunks)]
    row = lax.broadcasted_iota(jnp.int32, (8, LANES), 0)
    beds = [held[1, :, cols(chunk)] for chunk in range(chunks)]
    surfs = [held[0, :, cols(chunk)] + beds[chunk] for chunk in range(chunks)]

    def moved(values):
        rolled = [pltpu.roll(value, LANES - 1, 1) for value in values]
        rolled.append(rolled[-1])
        edge = lanes_of(8) == LANES - 1
        return [jnp.where(edge, rolled[c + 1], rolled[c]) for c in range(chunks)]

    beds_left, surfs_left, manns_left = moved(beds), moved(surfs), moved(manns)
    for chunk in range(chunks):
        at = cols(chunk)
        m0, b0, s0 = manns[chunk], beds[chunk], surfs[chunk]
        bed_max = jnp.maximum(b0, beds_left[chunk])
        drag = drag_of(m0, manns_left[chunk])
        q0 = (1.0 / SLOPE) * held[2, :, at]
        new_east = face(q0, s0, surfs_left[chunk], bed_max, drag)
        new_east = east_walled(new_east, chunk, chunks)
        bed_max = jnp.maximum(b0, moved_up(b0))
        drag = drag_of(m0, moved_up(m0))
        q0 = (1.0 / SLOPE) * held[3, :, at]
        new_south = jnp.where(row == 7, q0, face(q0, s0, moved_up(s0), bed_max, drag))
        fields = (s0, b0, held_rough[:, at].astype(jnp.float32), new_east)
        for slot, block in enumerate(border_rows(even, fields, new_south)):
            to_other[slot * chunks + chunk] = block
    to_other[4 * chunks, 0:2, :] = own[...]


def join_kernel(before, section, cells, to_other):
    nodes = to_other.shape[0] - 1
    to_other[nodes, 2:3, :] = section[...]
    to_other[nodes, 3:4, :] = (cells[0:1, :] + 1).astype(jnp.float32)


def relay_kernel(by_other, prepared, near, beyond):
    del prepared
    nodes = by_other.shape[0] - 1
    near[...] = by_other[nodes, 0:2, :]
    beyond[...] = by_other[nodes, 2:4, :]


def picking(reach, rows, key, lane, takes, masks):
    for block in range(key.shape[1] // LANES):
        mine = slice(block * LANES, (block + 1) * LANES)

        def column(row):
            wide = jnp.broadcast_to(row[:, mine].astype(jnp.float32), (LANES, LANES))
            return jnp.transpose(wide).astype(jnp.int32)

        spread = lanes_of(LANES)
        at = column(key)
        after = jnp.where(at < 0, at, at + rows)
        for first in range(0, takes.shape[2], LANES):
            for half, place in enumerate((at, after)):
                hit = jnp.where(spread + first == place, 1.0, 0.0)
                takes[half, mine, first : first + LANES] = hit.astype(jnp.bfloat16)
        ahead = spread - column(lane)
        masks[0, mine, :] = jnp.where((ahead >= 0) & (ahead < reach), 1.0, 0.0)
        masks[1, mine, :] = jnp.where(ahead + LANES < reach, 1.0, 0.0)


def load_kernel(
    depth_in, east_in, south_in, bed_in, rough_in, table_in, *refs
):
    surf, east, south, bed, rough, table_rows, table, sems = refs
    rows, columns = depth_in.shape
    own = pl.ds(0, rows)
    copies = [
        pltpu.make_async_copy(source, target.at[own, :], sems.at[slot])
        for slot, (source, target) in enumerate(
            (
                (depth_in, surf),
                (bed_in, bed),
                (rough_in, rough),
                (east_in, east),
                (south_in, south),
            )
        )
    ]
    copies.append(pltpu.make_async_copy(table_in, table, sems.at[5]))
    for copy in copies:
        copy.start()
    copies[5].wait()
    for k in range(table_rows.shape[0]):
        table_rows[k : k + 1, :] = jnp.broadcast_to(table[:, k : k + 1], (1, LANES))
    for copy in copies[:5]:
        copy.wait()


def prepare_kernel(table_rows, rough, *refs):
    surf, east, south, bed = refs[4:8]
    mann, bed_e, bed_s, drag_e, drag_s, to_partner = refs[8:]
    ext, columns = surf.shape
    rows = ext - 2 * HALO
    chunks = columns // LANES
    even = lax.axis_index("gy") % 2 == 0
    entries = [table_rows[k : k + 1, :] for k in range(table_rows.shape[0])]
    for chunk in range(chunks):
        at = cols(chunk)
        mann[:rows, at] = looked_up(rough[:, at], entries)
        surf[:rows, at] = surf[:rows, at] + bed[:rows, at]

    kept = lax.broadcasted_iota(jnp.int32, (rows, LANES), 0) == rows - 1
    for chunk in range(chunks):
        at, then = cols(chunk), cols(min(chunk + 1, chunks - 1))
        s0, b0, m0 = surf[:rows, at], bed[:rows, at], mann[:rows, at]
        bed_max = jnp.maximum(b0, moved_left(b0, bed[:rows, then], 1))
        drag = drag_of(m0, moved_left(m0, mann[:rows, then], 1))
        bed_e[:rows, at] = bed_max
        drag_e[:rows, at] = drag
        q0 = (1.0 / SLOPE) * east[:rows, at]
        new_east = face(q0, s0, moved_left(s0, surf[:rows, then], 1), bed_max, drag)
        new_east = east_walled(new_east, chunk, chunks)
        east[:rows, at] = new_east
        bed_max = jnp.maximum(b0, moved_up(b0))
        drag = drag_of(m0, moved_up(m0))
        bed_s[:rows, at] = bed_max
        drag_s[:rows, at] = drag
        q0 = (1.0 / SLOPE) * south[:rows, at]
        new_south = jnp.where(kept, q0, face(q0, s0, moved_up(s0), bed_max, drag))
        south[:rows, at] = new_south

        def ends(value):
            return jnp.where(even, value[rows - 8 :], value[:8])

        fields = (ends(s0), ends(b0), ends(rough[:, at].astype(jnp.float32)), ends(new_east))
        blocks = border_rows(jnp.logical_not(even), fields, ends(new_south))
        for slot, block in enumerate(blocks):
            to_partner[slot * chunks + chunk] = block


def nodes_kernel(reach, surf, own, partner_section, partner_cells, *refs):
    number, total, takes, masks, windows, given_1 = refs
    rows = surf.shape[0] - 2 * HALO
    ext, columns = number.shape
    chunks = columns // LANES
    tiles = lax.axis_size("gy")
    position = lax.axis_index("gy")
    side = jnp.where(position % 2 == 0, 1, -1)
    partner = jnp.where(position + side < tiles, partner_cells[0:1, :] + 1, 0).astype(jnp.float32)
    section = jnp.concatenate([own[0:1, :], partner_section[...]], axis=1)
    cell = jnp.concatenate([own[1:2, :], partner], axis=1)
    valid, node_row, node_chunk, node_lane = located(cell, position, rows, ext, columns)
    key = jnp.where(valid, node_chunk * ext + node_row, -1)
    starts, levels = scattered(section, key, node_lane, chunks * ext)
    for chunk in range(chunks):
        at = cols(chunk)
        number[:, at] = starts[chunk * ext : (chunk + 1) * ext]
        total[:, at] = levels[chunk * ext : (chunk + 1) * ext]
    key = jnp.where(valid & (node_row < rows), node_chunk * rows + node_row, -1)
    picking(reach, rows, key, node_lane, takes, masks)
    sums = window_sums([surf[:rows, cols(chunk)] for chunk in range(chunks)], reach, True)
    for chunk in range(chunks):
        windows[:, cols(chunk)] = sums[chunk]
    give(reach, 0, surf, None, given_1)


def wall_of(ext, tiles):
    position = lax.axis_index("gy")
    rows = ext - 2 * HALO
    row = lax.broadcasted_iota(jnp.int32, (16, LANES), 0) + (ext - 16)
    return ((row == ext - 1) & (position == 0)) | ((row == rows - 1) & (position == tiles - 1))


def border_kernel(reach, tiles, by_partner, by_other, table_rows, near, *refs):
    surf, east, south, bed, mann, bed_e, bed_s, drag_e, drag_s, number, total, takes, masks = refs[11:]
    ext, columns = surf.shape
    rows = ext - 2 * HALO
    chunks = columns // LANES
    position = lax.axis_index("gy")
    even = position % 2 == 0
    valid, node_row, node_chunk, node_lane = located(near[1:2, :], position, rows, ext, columns)
    key = jnp.where(valid, node_chunk * ext + node_row, -1)
    starts, levels = scattered(near[0:1, :], key, node_lane, chunks * ext)

    entries = [table_rows[k : k + 1, :] for k in range(table_rows.shape[0])]
    row = lax.broadcasted_iota(jnp.int32, (2 * HALO, LANES), 0)
    for chunk in range(chunks):
        at = cols(chunk)
        halos = []
        flux = jnp.zeros((2 * HALO, LANES), jnp.float32)
        for slot in range(4):
            a, b = by_partner[slot * chunks + chunk], by_other[slot * chunks + chunk]
            below = jnp.where(even, a, b)
            above = jnp.where(even, b, a)
            halos.append(jnp.concatenate([below, above], axis=0))
            flux = jnp.where(row == slot, below[HALO - 1 :], flux)
            flux = jnp.where(row == HALO + slot, above[:1], flux)
        surf[rows:, at] = halos[0]
        bed[rows:, at] = halos[1]
        mann[rows:, at] = looked_up(halos[2].astype(jnp.int32), entries)
        east[rows:, at] = halos[3]
        south[rows:, at] = flux

    key = jnp.where(valid & (node_row < rows), node_chunk * rows + node_row, -1)
    picking(reach, rows, key, node_lane, takes, masks)

    wall = wall_of(ext, tiles)
    kept = lax.broadcasted_iota(jnp.int32, (16, LANES), 0) % 8 < 7
    for chunk in range(chunks):
        at, then = cols(chunk), cols(min(chunk + 1, chunks - 1))
        number[:, at] += starts[chunk * ext : (chunk + 1) * ext]
        total[:, at] += levels[chunk * ext : (chunk + 1) * ext]
        b0, m0 = bed[rows:, at], mann[rows:, at]
        bed_e[rows:, at] = jnp.maximum(b0, moved_left(b0, bed[rows:, then], 1))
        drag_e[rows:, at] = drag_of(m0, moved_left(m0, mann[rows:, then], 1))

        def rolled_up(ref):
            value = jnp.concatenate([ref[rows - 8 :, at], ref[:8, at]], axis=0)
            return value[:16], moved_up(value)[:16]

        s0, s1 = rolled_up(surf)
        b0, b1 = rolled_up(bed)
        m0, m1 = rolled_up(mann)
        bed_max = jnp.maximum(b0, b1)
        drag = drag_of(m0, m1)
        bed_s[rows - 8 :, at] = bed_max
        drag_s[rows - 8 :, at] = drag
        q0 = south[rows - 8 :, at]
        new_south = jnp.where(kept, q0, face(q0, s0, s1, bed_max, drag))
        south[rows - 8 :, at] = jnp.where(wall, 0.0, new_south)


def fluxes(mine, upper, wall, before, faces, east_out, south_out, scale=None):
    surf, east, south = before
    bed_e, bed_s, drag_e, drag_s = faces
    ext, columns = surf.shape
    chunks = columns // LANES
    rolled = lane = None
    if east_out is not None:
        rolled = pltpu.roll(surf[mine, cols(0)], LANES - 1, 1)
        lane = lanes_of(rolled.shape[0])
    for chunk in range(chunks):
        at = cols(chunk)
        if east_out is not None:
            s0 = surf[mine, at]
            rolled_then = rolled
            if chunk + 1 < chunks:
                rolled_then = pltpu.roll(surf[mine, cols(chunk + 1)], LANES - 1, 1)
            left = jnp.where(lane >= LANES - 1, rolled_then, rolled)
            rolled = rolled_then
            new_east = face(east[mine, at], s0, left, bed_e[mine, at], drag_e[mine, at])
            if scale is not None:
                new_east = scale * new_east
            east_out[mine, at] = east_walled(new_east, chunk, chunks)
        if upper:
            s0 = surf[: upper + 8, at]
            s1 = moved_up(s0)[:upper]
            new_south = face(south[:upper, at], s0[:upper], s1, bed_s[:upper, at], drag_s[:upper, at])
            if scale is not None:
                new_south = scale * new_south
            south_out[:upper, at] = new_south
        if wall is not None:
            low = slice(ext - 16, ext)
            s0 = jnp.concatenate([surf[low, at], surf[:8, at]], axis=0)
            s1 = moved_up(s0)[:16]
            new_south = face(south[low, at], s0[:16], s1, bed_s[low, at], drag_s[low, at])
            if scale is not None:
                new_south = scale * new_south
            south_out[low, at] = jnp.where(wall, 0.0, new_south)


def settled(mine, surf, east, south, keep, sums, spread=SPREAD * SLOPE):
    ext, columns = surf.shape
    rolled = 0.0
    for chunk in range(columns // LANES):
        at = cols(chunk)
        new_east = east[mine, at]
        new_south = south[:, at]
        lane = lanes_of(new_east.shape[0])
        rolled_before, rolled = rolled, pltpu.roll(new_east, 1, 1)
        west = jnp.where(lane < 1, rolled_before, rolled)
        north = pltpu.roll(new_south, 1, 0)[mine]
        inflow = west + north
        s0 = surf[mine, at]
        outflow = new_east + new_south[mine]
        yield chunk, keep[mine, at] * s0 + (spread * (inflow - outflow) + sums[chunk])


def refill(corridor, mine, surf, total, count, total_out, windows=None):
    chunks = surf.shape[1] // LANES
    if windows is None:
        windows = window_sums([surf[mine, cols(chunk)] for chunk in range(chunks)], corridor, True)
    for chunk in range(chunks):
        at = cols(chunk)
        kept = (1.0 - corridor * DRAIN) * total[mine, at]
        total_out[mine, at] = kept + count[mine, at] * windows[chunk]


def summed(corridor, mine, total):
    chunks = total.shape[1] // LANES
    return window_sums([total[mine, cols(chunk)] for chunk in range(chunks)], corridor, False)


def exchange(corridor, mine, surf, total, count, total_out, windows=None):
    sums = summed(corridor, mine, total)
    refill(corridor, mine, surf, total, count, total_out, windows)
    return sums


def give(corridor, step, surf, before, after):
    rows, columns = after.shape
    weight = DRAIN * (1.0 - corridor * DRAIN) ** (STEPS - 1 - step)
    for chunk in range(columns // LANES):
        at = cols(chunk)
        value = weight * surf[:rows, at]
        after[:, at] = value if before is None else before[:, at] + value


def first_kernel(corridor, surf, east, south, number, total, windows, *refs):
    surf_1, total_1, count, keep, total_0 = refs
    rows = surf.shape[0] - 2 * HALO
    chunks = surf.shape[1] // LANES
    own = slice(0, rows)
    covering = window_sums([number[own, cols(chunk)] for chunk in range(chunks)], corridor, False)
    for chunk in range(chunks):
        at = cols(chunk)
        count[own, at] = (FEED * DRAIN) * number[own, at]
        keep[own, at] = 1.0 - FEED * covering[chunk]
        total_0[own, at] = FEED * total[own, at]
    windows = [windows[:, cols(chunk)] for chunk in range(chunks)]
    sums = exchange(corridor, own, surf, total_0, count, total_1, windows)
    for chunk, new_surf in settled(own, surf, east, south, keep, sums):
        surf_1[own, cols(chunk)] = new_surf


def second_kernel(corridor, tiles, far, beyond, surf, east, south, *refs):
    faces = refs[:4]
    number, total, given_1 = refs[4:7]
    surf_1, total_1, count, keep = refs[11:15]
    surf_2, east_2, south_2, total_2, given_2, total_0 = refs[15:]
    ext, columns = surf.shape
    rows = ext - 2 * HALO
    chunks = columns // LANES
    position = lax.axis_index("gy")
    tail = slice(rows, ext)

    section = jnp.concatenate([far[0:1, :], beyond[0:1, :]], axis=1)
    cell = jnp.concatenate([far[1:2, :], beyond[1:2, :]], axis=1)
    valid, node_row, node_chunk, node_lane = located(cell, position, rows, ext, columns)
    key = jnp.where(valid & (node_row >= rows), node_chunk * 8 + (node_row - rows), -1)
    starts, levels = scattered(section, key, node_lane, chunks * 8)
    starting = [
        number[tail, cols(chunk)] + starts[chunk * 8 : chunk * 8 + 8] for chunk in range(chunks)
    ]
    covering = window_sums(starting, corridor, False)
    for chunk in range(chunks):
        at = cols(chunk)
        count[tail, at] = (FEED * DRAIN) * starting[chunk]
        keep[tail, at] = 1.0 - FEED * covering[chunk]
        total_0[tail, at] = FEED * (total[tail, at] + levels[chunk * 8 : chunk * 8 + 8])
    sums = exchange(corridor, tail, surf, total_0, count, total_1)

    own = slice(0, rows)
    before = (surf_1, east, south)
    fluxes(own, rows - 8, None, before, faces, east_2, south_2)
    own_sums = exchange(corridor, own, surf_1, total_1, count, total_2)
    give(corridor, 1, surf_1, given_1, given_2)

    for chunk, new_surf in settled(tail, surf, east, south, keep, sums):
        surf_1[tail, cols(chunk)] = new_surf
    tail_sums = exchange(corridor, tail, surf_1, total_1, count, total_2)
    fluxes(tail, 0, wall_of(ext, tiles), before, faces, east_2, south_2)
    for mine, sums in ((own, own_sums), (tail, tail_sums)):
        for chunk, new_surf in settled(mine, surf_1, east_2, south_2, keep, sums):
            surf_2[mine, cols(chunk)] = new_surf


def third_kernel(corridor, tiles, surf, east, south, *refs):
    faces = refs[:4]
    total, keep, given_2, own, takes, masks, takes_near, masks_near, count, bed = refs[4:14]
    surf_3, east_3, south_3, own_term, partner_term, other_term = refs[14:20]
    ext, columns = surf.shape
    rows = ext - 2 * HALO
    mine = slice(0, rows)
    owned = own.shape[1]
    chunks = columns // LANES
    sums = summed(corridor, mine, total)
    fluxes(
        mine, rows - 8, wall_of(ext, tiles), (surf, east, south), faces, east_3, south_3
    )
    weight = DRAIN * (1.0 - corridor * DRAIN)
    levels = []
    for chunk, new_surf in settled(mine, surf, east_3, south_3, keep, sums):
        at = cols(chunk)
        surf_3[mine, at] = new_surf
        levels.append(given_2[:, at] + weight * surf[mine, at] + DRAIN * new_surf)
    spare = takes.shape[2] - chunks * rows
    if spare:
        levels.append(jnp.zeros((spare, LANES), jnp.float32))
    levels = jnp.concatenate(levels, axis=0)
    high = levels.astype(jnp.bfloat16)
    low = (levels - high.astype(jnp.float32)).astype(jnp.bfloat16)
    picked = jnp.dot(
        jnp.concatenate([takes[0], takes_near[0], takes[1], takes_near[1]], axis=0),
        jnp.concatenate([high, low], axis=1),
        preferred_element_type=jnp.float32,
    )
    hit = jnp.concatenate([masks[0], masks_near[0], masks[1], masks_near[1]], axis=0)
    picked = (picked * jnp.concatenate([hit, hit], axis=1)).astype(jnp.bfloat16)
    picked = jnp.concatenate([picked[: 3 * owned], picked[3 * owned :]], axis=1)
    terms = lax.dot_general(
        jnp.ones((8, 4 * LANES), jnp.bfloat16),
        picked,
        (((1,), (1,)), ((), ())),
        preferred_element_type=jnp.float32,
    )[0:1]
    own_term[...] = (1.0 - corridor * DRAIN) ** STEPS * own[0:1, :] + terms[:, :owned]
    partner_term[...] = terms[:, owned : 2 * owned]
    other_term[...] = terms[:, 2 * owned :]

    @pl.when(is_edge(tiles))
    def _():
        last_substep(
            *(corridor, tiles, surf, east, south_3, *faces, total, count, keep, bed),
            *(None, east_3, surf_3, *refs[20:]),
        )


def is_edge(tiles):
    position = lax.axis_index("gy")
    return (position == 0) | (position == tiles - 1)


def last_kernel(corridor, tiles, *refs):
    @pl.when(jnp.logical_not(is_edge(tiles)))
    def _():
        last_substep(corridor, tiles, *refs[:13], *refs[16:])


def last_substep(corridor, tiles, surf_2, east_2, south_3, *refs):
    faces = refs[:4]
    total_2, count, keep, bed, _, east_3 = refs[4:10]
    surf_3, depth_out, east_out, south_out = refs[10:14]
    depth_4, east_4, south_4, east_tail, total_3, sems = refs[14:]
    ext, columns = surf_2.shape
    rows = ext - 2 * HALO
    chunks = columns // LANES
    own, tail = slice(0, rows), slice(rows, ext)

    def copy(slot, source, target, first, last):
        part = pl.ds(first * LANES, (last - first) * LANES)
        return pltpu.make_async_copy(
            source.at[pl.ds(0, rows), part], target.at[:, part], sems.at[slot]
        )

    before = (surf_3, east_3, south_3)
    tail_sums = summed(corridor, tail, total_2)
    refill(corridor, own, surf_2, total_2, count, total_3)
    fluxes(own, rows - 8, None, before, faces, east_4, south_4, scale=SLOPE)
    copies = [copy(0, east_4, east_out, 0, chunks)]
    copies[0].start()
    fluxes(tail, 0, None, (surf_2, east_2, None), faces, east_tail, None)
    for chunk, new_surf in settled(tail, surf_2, east_tail, south_3, keep, tail_sums):
        surf_3[tail, cols(chunk)] = new_surf
    sums = summed(corridor, own, total_3)
    fluxes(slice(0, 0), 0, wall_of(ext, tiles), before, faces, None, south_4, scale=SLOPE)
    copies.append(copy(1, south_4, south_out, 0, chunks))
    copies[1].start()
    group = 5
    for chunk, new_surf in settled(own, surf_3, east_4, south_4, keep, sums, spread=SPREAD):
        at = cols(chunk)
        depth_4[:, at] = new_surf - bed[own, at]
        if (chunk + 1) % group == 0 or chunk + 1 == chunks:
            first = chunk // group
            copies.append(copy(2 + first, depth_4, depth_out, first * group, chunk + 1))
            copies[-1].start()
    for one in copies:
        one.wait()


def local(
    depth, flux_east, flux_south, river_section, bed_level, rough_class, manning_table, bank_cell
):
    rows, columns = depth.shape
    owned = river_section.shape[0]
    corridor = bank_cell.shape[0]
    tiles = lax.axis_size("gy")
    ext = rows + 2 * HALO
    chunks = columns // LANES
    partner_section = swapped(river_section, 0).reshape(1, owned)
    partner_cells = swapped(bank_cell, 0)

    def held(value):
        return pltpu.with_memory_space_constraint(value, pltpu.VMEM)

    def far(value):
        return pltpu.with_memory_space_constraint(value, pltpu.HBM)

    params = pltpu.CompilerParams(vmem_limit_bytes=VMEM_LIMIT)
    halo = pltpu.VMEM((4 * chunks, HALO, LANES), jnp.float32)
    wide = pltpu.VMEM((4 * chunks + 1, HALO, LANES), jnp.float32)
    field = pltpu.VMEM((ext, columns), jnp.float32)
    small = pltpu.VMEM((rows, columns), jnp.float32)
    term = pltpu.VMEM((1, owned), jnp.float32)
    pair = pltpu.VMEM((2, owned), jnp.float32)
    result = pltpu.HBM((rows, columns), jnp.float32)
    cells = -(-chunks * rows // LANES) * LANES

    def call(kernel, name, outs, values, scratch=(), aliases=None):
        return pl.pallas_call(
            kernel,
            out_shape=outs,
            in_specs=[VMEM_SPEC] * len(values),
            out_specs=[HBM_SPEC if out is result else VMEM_SPEC for out in outs],
            scratch_shapes=scratch,
            input_output_aliases=aliases or {},
            compiler_params=params,
            name=name,
        )(*[held(value) for value in values])

    def picks(nodes):
        return [
            pltpu.VMEM((2, nodes, cells), jnp.bfloat16),
            pltpu.VMEM((2, nodes, LANES), jnp.float32),
        ]

    classes = manning_table.shape[0]
    table = far(manning_table.reshape(1, classes))
    table_held = pltpu.VMEM((1, classes), jnp.float32)
    to_other, own = pl.pallas_call(
        pack_kernel,
        out_shape=[wide, pair],
        in_specs=[HBM_SPEC] * 8,
        out_specs=[VMEM_SPEC] * 2,
        scratch_shapes=[
            pltpu.VMEM((4, 8, columns), jnp.float32),
            pltpu.VMEM((8, columns), jnp.int32),
            pltpu.VMEM((corridor, owned), jnp.int32),
            table_held,
            pltpu.SemaphoreType.DMA((8,)),
        ],
        compiler_params=params,
        name="pack",
    )(
        *[far(value) for value in (depth, bed_level, rough_class, flux_east, flux_south)],
        far(river_section.reshape(1, owned)),
        far(bank_cell),
        table,
    )
    (to_other,) = call(
        join_kernel,
        "join",
        [wide],
        (to_other, partner_section, partner_cells),
        aliases={0: 0},
    )
    by_other = swapped(to_other, 1)
    *loaded, rough, table_rows = pl.pallas_call(
        load_kernel,
        out_shape=[field] * 4
        + [pltpu.VMEM((rows, columns), jnp.int32), pltpu.VMEM((classes, LANES), jnp.float32)],
        in_specs=[HBM_SPEC] * 6,
        out_specs=[VMEM_SPEC] * 6,
        scratch_shapes=[table_held, pltpu.SemaphoreType.DMA((6,))],
        compiler_params=params,
        name="load",
    )(
        *[far(value) for value in (depth, flux_east, flux_south, bed_level, rough_class)],
        table,
    )
    *fields, to_partner = call(
        prepare_kernel,
        "prepare",
        [field] * 9 + [halo],
        (table_rows, rough, *loaded),
        aliases={2 + slot: slot for slot in range(4)},
    )
    by_partner = swapped(to_partner, 0)
    number, total, takes, masks, windows, given_1 = call(
        functools.partial(nodes_kernel, corridor),
        "nodes",
        [field] * 2 + picks(2 * owned) + [small] * 2,
        (fields[0], own, partner_section, partner_cells),
    )
    near, beyond = call(relay_kernel, "relay", [pair, pair], (by_other, masks))
    from_far = swapped(near, 0)
    *fields, takes_near, masks_near = call(
        functools.partial(border_kernel, corridor, tiles),
        "border",
        [field] * 11 + picks(owned),
        (by_partner, by_other, table_rows, near, *fields, number, total),
        aliases={4 + slot: slot for slot in range(11)},
    )
    surf, east, south, bed, _, *faces, number, total = fields
    surf_1, total_1, count, keep = call(
        functools.partial(first_kernel, corridor),
        "first",
        [field] * 4,
        (surf, east, south, number, total, windows),
        scratch=[field],
    )
    surf_1, total_1, count, keep, surf_2, east_2, south_2, total_2, given_2 = call(
        functools.partial(second_kernel, corridor, tiles),
        "second",
        [field] * 8 + [small],
        (
            *(from_far, beyond, surf, east, south, *faces, number, total, given_1),
            *(surf_1, total_1, count, keep),
        ),
        scratch=[field],
        aliases={12 + slot: slot for slot in range(4)},
    )
    last_scratch = [small, small, field, field, small]
    last_scratch.append(pltpu.SemaphoreType.DMA((2 + -(-chunks // 5),)))
    surf_3, east_3, south_3, own_term, partner_term, other_term, *results = call(
        functools.partial(third_kernel, corridor, tiles),
        "third",
        [field] * 3 + [term] * 3 + [result] * 3,
        (
            *(surf_2, east_2, south_2, *faces, total_2, keep, given_2),
            *(own, takes, masks, takes_near, masks_near, count, bed),
        ),
        scratch=last_scratch,
    )
    from_other = swapped(other_term.reshape(owned), 1)
    from_partner = swapped(partner_term.reshape(owned), 0)
    last_in = (surf_2, east_2, south_3, *faces, total_2, count, keep, bed, surf_3, east_3)
    _, depth, flux_east, flux_south = pl.pallas_call(
        functools.partial(last_kernel, corridor, tiles),
        out_shape=[field] + [result] * 3,
        in_specs=[VMEM_SPEC] * 13 + [HBM_SPEC] * 3,
        out_specs=[VMEM_SPEC] + [HBM_SPEC] * 3,
        scratch_shapes=last_scratch,
        input_output_aliases={11: 0, 13: 1, 14: 2, 15: 3},
        compiler_params=params,
        name="last",
    )(*[held(value) for value in last_in], *[far(value) for value in results])
    river_section = own_term.reshape(owned) + from_other + from_partner
    return (depth, flux_east, flux_south, river_section)


def solution(mesh):
    return jax.shard_map(
        local,
        mesh=mesh,
        in_specs=(
            P(("runs", "gy"), None),
            P(("runs", "gy"), None),
            P(("runs", "gy"), None),
            P(("runs", "gy")),
            P("gy", None),
            P("gy", None),
            P(),
            P(None, "gy"),
        ),
        out_specs=(
            P(("runs", "gy"), None),
            P(("runs", "gy"), None),
            P(("runs", "gy"), None),
            P(("runs", "gy")),
        ),
        check_vma=False,
    )
```

```python
import functools

import jax
import jax.numpy as jnp
from jax import lax
from jax.experimental import pallas as pl
from jax.experimental.pallas import tpu as pltpu
from jax.sharding import PartitionSpec as P

STEPS = 4

GRAV = 9.81
TSTEP = 8.0
CELL = 90.0
FLOOR = 0.05
BANK_COEF = 200.0
CELL_AREA = 8100.0
NODE_AREA = 20000.0

LANES = 128
HALO = 4
SLOPE = GRAV * TSTEP / CELL
SPREAD = TSTEP / CELL
FEED = TSTEP * BANK_COEF / CELL_AREA
DRAIN = TSTEP * BANK_COEF / NODE_AREA
VMEM_LIMIT = 32 * 1024 * 1024

VMEM_SPEC = pl.BlockSpec(memory_space=pltpu.VMEM)
HBM_SPEC = pl.BlockSpec(memory_space=pltpu.HBM)


def swapped(value, first):
    count = lax.axis_size("gy")
    pairs = []
    for low in range(first, count - 1, 2):
        pairs += [(low, low + 1), (low + 1, low)]
    return lax.ppermute(value, "gy", pairs)


def cols(chunk):
    return slice(chunk * LANES, (chunk + 1) * LANES)


def lanes_of(rows):
    return lax.broadcasted_iota(jnp.int32, (rows, LANES), 1)


def moved_left(value, following, by):
    return jnp.where(
        lanes_of(value.shape[0]) >= LANES - by,
        pltpu.roll(following, LANES - by, 1),
        pltpu.roll(value, LANES - by, 1),
    )


def moved_up(value):
    return pltpu.roll(value, value.shape[0] - 1, 0)


def split3(value):
    high = value.astype(jnp.bfloat16)
    rest = value - high.astype(jnp.float32)
    middle = rest.astype(jnp.bfloat16)
    low = (rest - middle.astype(jnp.float32)).astype(jnp.bfloat16)
    return high, middle, low


def one_hot(count, key):
    rows = lax.broadcasted_iota(jnp.int32, (count, key.shape[1]), 0)
    return jnp.where(rows == key, 1.0, 0.0)


def drag_of(mann_a, mann_b):
    pair = mann_a + mann_b
    return (0.25 * GRAV * TSTEP * SLOPE) * (pair * pair)


def looked_up(klass, entries):
    value = jnp.broadcast_to(entries[0], klass.shape)
    for k in range(1, len(entries)):
        value = jnp.where(klass == k, entries[k], value)
    return value


def face(flux, surf_a, surf_b, bed_max, drag):
    flow_depth = jnp.maximum(jnp.maximum(surf_a, surf_b) - bed_max, FLOOR)
    power = jnp.exp2((-7.0 / 3.0) * jnp.log2(flow_depth))
    driven = flux - flow_depth * (surf_b - surf_a)
    damping = 1.0 + drag * jnp.abs(flux) * power
    return driven * pl.reciprocal(damping, approx=True)


def window_sums(blocks, reach, forward):
    height = blocks[0].shape[0]
    count = len(blocks)
    spare = -(count * height) % 16
    whole = blocks + ([jnp.zeros((spare, LANES), jnp.float32)] if spare else [])
    whole = jnp.concatenate(whole, axis=0)
    high = whole.astype(jnp.bfloat16)
    low = (whole - high.astype(jnp.float32)).astype(jnp.bfloat16)
    source = lax.broadcasted_iota(jnp.int32, (2 * LANES, 2 * LANES), 0) % LANES
    target = lax.broadcasted_iota(jnp.int32, (2 * LANES, 2 * LANES), 1)
    spill = target >= LANES
    target = target % LANES
    if forward:
        ahead = source - target + jnp.where(spill, LANES, 0)
    else:
        ahead = target - source + jnp.where(spill, LANES, 0)
    band = jnp.where((ahead >= 0) & (ahead < reach), 1.0, 0.0).astype(jnp.bfloat16)
    sums = jnp.dot(
        jnp.concatenate([high, low], axis=1), band, preferred_element_type=jnp.float32
    )
    results = []
    for block in range(count):
        result = sums[block * height : (block + 1) * height, :LANES]
        beside = block + 1 if forward else block - 1
        if 0 <= beside < count:
            result = result + sums[beside * height : (beside + 1) * height, LANES:]
        results.append(result)
    return results


def east_walled(value, chunk, chunks):
    if chunk + 1 < chunks:
        return value
    return jnp.where(lanes_of(value.shape[0]) == LANES - 1, 0.0, value)


def located(cell, position, rows, ext, columns):
    base = ((position * rows - HALO) * columns + 1).astype(jnp.float32)
    offset = cell - base
    valid = (cell > 0.0) & (offset >= 0.0) & (offset < float(ext * columns))
    offset = jnp.where(valid, offset, 0.0)
    row = jnp.floor((offset + 0.5) * (1.0 / columns))
    column = (offset - row * float(columns)).astype(jnp.int32)
    row = row.astype(jnp.int32) - HALO
    row = jnp.where(row < 0, row + ext, row)
    chunk = column // LANES
    return valid, row, chunk, column - chunk * LANES


def scattered(section, key, lane, count):
    at_lane = one_hot(LANES, lane)
    parts = [at_lane] + [at_lane * part.astype(jnp.float32) for part in split3(section)]
    grid = lax.dot_general(
        one_hot(-(-count // 16) * 16, key).astype(jnp.bfloat16),
        jnp.concatenate(parts, axis=0).astype(jnp.bfloat16),
        (((1,), (1,)), ((), ())),
        preferred_element_type=jnp.float32,
    )
    number = grid[:, :LANES]
    total = (grid[:, LANES : 2 * LANES] + grid[:, 2 * LANES : 3 * LANES]) + grid[:, 3 * LANES :]
    return number, total


def border_rows(of_first, fields, south):
    outer = lax.broadcasted_iota(jnp.int32, (HALO, LANES), 0) == jnp.where(of_first, HALO - 1, 0)
    flux = jnp.where(of_first, south[:HALO], south[HALO:])
    return [
        jnp.where(outer, flux[slot : slot + 1], jnp.where(of_first, value[:HALO], value[HALO:]))
        for slot, value in enumerate(fields)
    ]


def pack_kernel(
    depth, bed, rough, east, south, section, cells, table_in, to_other, own, *refs
):
    held, held_rough, held_cells, table, sems = refs
    rows, columns = depth.shape
    chunks = columns // LANES
    even = lax.axis_index("gy") % 2 == 0
    start = pl.multiple_of(jnp.where(even, 0, rows - 8), 8)
    near = pl.ds(start, 8)
    copies = [
        pltpu.make_async_copy(source, target, sems.at[slot])
        for slot, (source, target) in enumerate(
            (
                (rough.at[near, :], held_rough),
                (bed.at[near, :], held.at[1]),
                (depth.at[near, :], held.at[0]),
                (east.at[near, :], held.at[2]),
                (south.at[near, :], held.at[3]),
                (section, own.at[pl.ds(0, 1), :]),
                (cells, held_cells),
                (table_in, table),
            )
        )
    ]
    for copy in copies:
        copy.start()
    for copy in copies:
        copy.wait()
    own[1:2, :] = (held_cells[0:1, :] + 1).astype(jnp.float32)
    entries = [
        jnp.broadcast_to(table[:, k : k + 1], (1, LANES)) for k in range(table.shape[1])
    ]
    manns = [looked_up(held_rough[:, cols(chunk)], entries) for chunk in range(chunks)]
    row = lax.broadcasted_iota(jnp.int32, (8, LANES), 0)
    beds = [held[1, :, cols(chunk)] for chunk in range(chunks)]
    surfs = [held[0, :, cols(chunk)] + beds[chunk] for chunk in range(chunks)]

    def moved(values):
        rolled = [pltpu.roll(value, LANES - 1, 1) for value in values]
        rolled.append(rolled[-1])
        edge = lanes_of(8) == LANES - 1
        return [jnp.where(edge, rolled[c + 1], rolled[c]) for c in range(chunks)]

    beds_left, surfs_left, manns_left = moved(beds), moved(surfs), moved(manns)
    for chunk in range(chunks):
        at = cols(chunk)
        m0, b0, s0 = manns[chunk], beds[chunk], surfs[chunk]
        bed_max = jnp.maximum(b0, beds_left[chunk])
        drag = drag_of(m0, manns_left[chunk])
        q0 = (1.0 / SLOPE) * held[2, :, at]
        new_east = face(q0, s0, surfs_left[chunk], bed_max, drag)
        new_east = east_walled(new_east, chunk, chunks)
        bed_max = jnp.maximum(b0, moved_up(b0))
        drag = drag_of(m0, moved_up(m0))
        q0 = (1.0 / SLOPE) * held[3, :, at]
        new_south = jnp.where(row == 7, q0, face(q0, s0, moved_up(s0), bed_max, drag))
        fields = (s0, b0, held_rough[:, at].astype(jnp.float32), new_east)
        for slot, block in enumerate(border_rows(even, fields, new_south)):
            to_other[slot * chunks + chunk] = block
    to_other[4 * chunks, 0:2, :] = own[...]


def join_kernel(before, section, cells, to_other):
    nodes = to_other.shape[0] - 1
    to_other[nodes, 2:3, :] = section[...]
    to_other[nodes, 3:4, :] = (cells[0:1, :] + 1).astype(jnp.float32)


def relay_kernel(by_other, prepared, near, beyond):
    del prepared
    nodes = by_other.shape[0] - 1
    near[...] = by_other[nodes, 0:2, :]
    beyond[...] = by_other[nodes, 2:4, :]


def picking(reach, rows, key, lane, takes, masks):
    for block in range(key.shape[1] // LANES):
        mine = slice(block * LANES, (block + 1) * LANES)

        def column(row):
            wide = jnp.broadcast_to(row[:, mine].astype(jnp.float32), (LANES, LANES))
            return jnp.transpose(wide).astype(jnp.int32)

        spread = lanes_of(LANES)
        at = column(key)
        after = jnp.where(at < 0, at, at + rows)
        for first in range(0, takes.shape[2], LANES):
            for half, place in enumerate((at, after)):
                hit = jnp.where(spread + first == place, 1.0, 0.0)
                takes[half, mine, first : first + LANES] = hit.astype(jnp.bfloat16)
        ahead = spread - column(lane)
        masks[0, mine, :] = jnp.where((ahead >= 0) & (ahead < reach), 1.0, 0.0)
        masks[1, mine, :] = jnp.where(ahead + LANES < reach, 1.0, 0.0)


def load_kernel(
    depth_in, east_in, south_in, bed_in, rough_in, table_in, *refs
):
    surf, east, south, bed, rough, table_rows, table, sems = refs
    rows, columns = depth_in.shape
    own = pl.ds(0, rows)
    copies = [
        pltpu.make_async_copy(source, target.at[own, :], sems.at[slot])
        for slot, (source, target) in enumerate(
            (
                (depth_in, surf),
                (bed_in, bed),
                (rough_in, rough),
                (east_in, east),
                (south_in, south),
            )
        )
    ]
    copies.append(pltpu.make_async_copy(table_in, table, sems.at[5]))
    for copy in copies:
        copy.start()
    copies[5].wait()
    for k in range(table_rows.shape[0]):
        table_rows[k : k + 1, :] = jnp.broadcast_to(table[:, k : k + 1], (1, LANES))
    for copy in copies[:5]:
        copy.wait()


def prepare_kernel(table_rows, rough, *refs):
    surf, east, south, bed = refs[4:8]
    mann, bed_e, bed_s, drag_e, drag_s, to_partner = refs[8:]
    ext, columns = surf.shape
    rows = ext - 2 * HALO
    chunks = columns // LANES
    even = lax.axis_index("gy") % 2 == 0
    entries = [table_rows[k : k + 1, :] for k in range(table_rows.shape[0])]
    for chunk in range(chunks):
        at = cols(chunk)
        mann[:rows, at] = looked_up(rough[:, at], entries)
        surf[:rows, at] = surf[:rows, at] + bed[:rows, at]

    kept = lax.broadcasted_iota(jnp.int32, (rows, LANES), 0) == rows - 1
    for chunk in range(chunks):
        at, then = cols(chunk), cols(min(chunk + 1, chunks - 1))
        s0, b0, m0 = surf[:rows, at], bed[:rows, at], mann[:rows, at]
        bed_max = jnp.maximum(b0, moved_left(b0, bed[:rows, then], 1))
        drag = drag_of(m0, moved_left(m0, mann[:rows, then], 1))
        bed_e[:rows, at] = bed_max
        drag_e[:rows, at] = drag
        q0 = (1.0 / SLOPE) * east[:rows, at]
        new_east = face(q0, s0, moved_left(s0, surf[:rows, then], 1), bed_max, drag)
        new_east = east_walled(new_east, chunk, chunks)
        east[:rows, at] = new_east
        bed_max = jnp.maximum(b0, moved_up(b0))
        drag = drag_of(m0, moved_up(m0))
        bed_s[:rows, at] = bed_max
        drag_s[:rows, at] = drag
        q0 = (1.0 / SLOPE) * south[:rows, at]
        new_south = jnp.where(kept, q0, face(q0, s0, moved_up(s0), bed_max, drag))
        south[:rows, at] = new_south

        def ends(value):
            return jnp.where(even, value[rows - 8 :], value[:8])

        fields = (ends(s0), ends(b0), ends(rough[:, at].astype(jnp.float32)), ends(new_east))
        blocks = border_rows(jnp.logical_not(even), fields, ends(new_south))
        for slot, block in enumerate(blocks):
            to_partner[slot * chunks + chunk] = block


def nodes_kernel(reach, surf, own, partner_section, partner_cells, *refs):
    number, total, takes, masks, windows, given_1 = refs
    rows = surf.shape[0] - 2 * HALO
    ext, columns = number.shape
    chunks = columns // LANES
    tiles = lax.axis_size("gy")
    position = lax.axis_index("gy")
    side = jnp.where(position % 2 == 0, 1, -1)
    partner = jnp.where(position + side < tiles, partner_cells[0:1, :] + 1, 0).astype(jnp.float32)
    section = jnp.concatenate([own[0:1, :], partner_section[...]], axis=1)
    cell = jnp.concatenate([own[1:2, :], partner], axis=1)
    valid, node_row, node_chunk, node_lane = located(cell, position, rows, ext, columns)
    key = jnp.where(valid, node_chunk * ext + node_row, -1)
    starts, levels = scattered(section, key, node_lane, chunks * ext)
    for chunk in range(chunks):
        at = cols(chunk)
        number[:, at] = starts[chunk * ext : (chunk + 1) * ext]
        total[:, at] = levels[chunk * ext : (chunk + 1) * ext]
    key = jnp.where(valid & (node_row < rows), node_chunk * rows + node_row, -1)
    picking(reach, rows, key, node_lane, takes, masks)
    sums = window_sums([surf[:rows, cols(chunk)] for chunk in range(chunks)], reach, True)
    for chunk in range(chunks):
        windows[:, cols(chunk)] = sums[chunk]
    give(reach, 0, surf, None, given_1)


def wall_of(ext, tiles):
    position = lax.axis_index("gy")
    rows = ext - 2 * HALO
    row = lax.broadcasted_iota(jnp.int32, (16, LANES), 0) + (ext - 16)
    return ((row == ext - 1) & (position == 0)) | ((row == rows - 1) & (position == tiles - 1))


def border_kernel(reach, tiles, by_partner, by_other, table_rows, near, *refs):
    surf, east, south, bed, mann, bed_e, bed_s, drag_e, drag_s, number, total, takes, masks = refs[11:]
    ext, columns = surf.shape
    rows = ext - 2 * HALO
    chunks = columns // LANES
    position = lax.axis_index("gy")
    even = position % 2 == 0
    valid, node_row, node_chunk, node_lane = located(near[1:2, :], position, rows, ext, columns)
    key = jnp.where(valid, node_chunk * ext + node_row, -1)
    starts, levels = scattered(near[0:1, :], key, node_lane, chunks * ext)

    entries = [table_rows[k : k + 1, :] for k in range(table_rows.shape[0])]
    row = lax.broadcasted_iota(jnp.int32, (2 * HALO, LANES), 0)
    for chunk in range(chunks):
        at = cols(chunk)
        halos = []
        flux = jnp.zeros((2 * HALO, LANES), jnp.float32)
        for slot in range(4):
            a, b = by_partner[slot * chunks + chunk], by_other[slot * chunks + chunk]
            below = jnp.where(even, a, b)
            above = jnp.where(even, b, a)
            halos.append(jnp.concatenate([below, above], axis=0))
            flux = jnp.where(row == slot, below[HALO - 1 :], flux)
            flux = jnp.where(row == HALO + slot, above[:1], flux)
        surf[rows:, at] = halos[0]
        bed[rows:, at] = halos[1]
        mann[rows:, at] = looked_up(halos[2].astype(jnp.int32), entries)
        east[rows:, at] = halos[3]
        south[rows:, at] = flux

    key = jnp.where(valid & (node_row < rows), node_chunk * rows + node_row, -1)
    picking(reach, rows, key, node_lane, takes, masks)

    wall = wall_of(ext, tiles)
    kept = lax.broadcasted_iota(jnp.int32, (16, LANES), 0) % 8 < 7
    for chunk in range(chunks):
        at, then = cols(chunk), cols(min(chunk + 1, chunks - 1))
        number[:, at] += starts[chunk * ext : (chunk + 1) * ext]
        total[:, at] += levels[chunk * ext : (chunk + 1) * ext]
        b0, m0 = bed[rows:, at], mann[rows:, at]
        bed_e[rows:, at] = jnp.maximum(b0, moved_left(b0, bed[rows:, then], 1))
        drag_e[rows:, at] = drag_of(m0, moved_left(m0, mann[rows:, then], 1))

        def rolled_up(ref):
            value = jnp.concatenate([ref[rows - 8 :, at], ref[:8, at]], axis=0)
            return value[:16], moved_up(value)[:16]

        s0, s1 = rolled_up(surf)
        b0, b1 = rolled_up(bed)
        m0, m1 = rolled_up(mann)
        bed_max = jnp.maximum(b0, b1)
        drag = drag_of(m0, m1)
        bed_s[rows - 8 :, at] = bed_max
        drag_s[rows - 8 :, at] = drag
        q0 = south[rows - 8 :, at]
        new_south = jnp.where(kept, q0, face(q0, s0, s1, bed_max, drag))
        south[rows - 8 :, at] = jnp.where(wall, 0.0, new_south)


def fluxes(mine, upper, wall, before, faces, east_out, south_out, scale=None):
    surf, east, south = before
    bed_e, bed_s, drag_e, drag_s = faces
    ext, columns = surf.shape
    chunks = columns // LANES
    rolled = lane = None
    if east_out is not None:
        rolled = pltpu.roll(surf[mine, cols(0)], LANES - 1, 1)
        lane = lanes_of(rolled.shape[0])
    for chunk in range(chunks):
        at = cols(chunk)
        if east_out is not None:
            s0 = surf[mine, at]
            rolled_then = rolled
            if chunk + 1 < chunks:
                rolled_then = pltpu.roll(surf[mine, cols(chunk + 1)], LANES - 1, 1)
            left = jnp.where(lane >= LANES - 1, rolled_then, rolled)
            rolled = rolled_then
            new_east = face(east[mine, at], s0, left, bed_e[mine, at], drag_e[mine, at])
            if scale is not None:
                new_east = scale * new_east
            east_out[mine, at] = east_walled(new_east, chunk, chunks)
        if upper:
            s0 = surf[: upper + 8, at]
            s1 = moved_up(s0)[:upper]
            new_south = face(south[:upper, at], s0[:upper], s1, bed_s[:upper, at], drag_s[:upper, at])
            if scale is not None:
                new_south = scale * new_south
            south_out[:upper, at] = new_south
        if wall is not None:
            low = slice(ext - 16, ext)
            s0 = jnp.concatenate([surf[low, at], surf[:8, at]], axis=0)
            s1 = moved_up(s0)[:16]
            new_south = face(south[low, at], s0[:16], s1, bed_s[low, at], drag_s[low, at])
            if scale is not None:
                new_south = scale * new_south
            south_out[low, at] = jnp.where(wall, 0.0, new_south)


def settled(mine, surf, east, south, keep, sums, spread=SPREAD * SLOPE):
    ext, columns = surf.shape
    rolled = 0.0
    for chunk in range(columns // LANES):
        at = cols(chunk)
        new_east = east[mine, at]
        new_south = south[:, at]
        lane = lanes_of(new_east.shape[0])
        rolled_before, rolled = rolled, pltpu.roll(new_east, 1, 1)
        west = jnp.where(lane < 1, rolled_before, rolled)
        north = pltpu.roll(new_south, 1, 0)[mine]
        inflow = west + north
        s0 = surf[mine, at]
        outflow = new_east + new_south[mine]
        yield chunk, keep[mine, at] * s0 + (spread * (inflow - outflow) + sums[chunk])


def refill(corridor, mine, surf, total, count, total_out, windows=None):
    chunks = surf.shape[1] // LANES
    if windows is None:
        windows = window_sums([surf[mine, cols(chunk)] for chunk in range(chunks)], corridor, True)
    for chunk in range(chunks):
        at = cols(chunk)
        kept = (1.0 - corridor * DRAIN) * total[mine, at]
        total_out[mine, at] = kept + count[mine, at] * windows[chunk]


def summed(corridor, mine, total):
    chunks = total.shape[1] // LANES
    return window_sums([total[mine, cols(chunk)] for chunk in range(chunks)], corridor, False)


def exchange(corridor, mine, surf, total, count, total_out, windows=None):
    sums = summed(corridor, mine, total)
    refill(corridor, mine, surf, total, count, total_out, windows)
    return sums


def give(corridor, step, surf, before, after):
    rows, columns = after.shape
    weight = DRAIN * (1.0 - corridor * DRAIN) ** (STEPS - 1 - step)
    for chunk in range(columns // LANES):
        at = cols(chunk)
        value = weight * surf[:rows, at]
        after[:, at] = value if before is None else before[:, at] + value


def first_kernel(corridor, surf, east, south, number, total, windows, given_1, *refs):
    surf_1, total_1, count, keep, total_2, sums_2, given_2, total_0 = refs
    rows = surf.shape[0] - 2 * HALO
    chunks = surf.shape[1] // LANES
    own = slice(0, rows)
    covering = window_sums([number[own, cols(chunk)] for chunk in range(chunks)], corridor, False)
    for chunk in range(chunks):
        at = cols(chunk)
        count[own, at] = (FEED * DRAIN) * number[own, at]
        keep[own, at] = 1.0 - FEED * covering[chunk]
        total_0[own, at] = FEED * total[own, at]
    windows = [windows[:, cols(chunk)] for chunk in range(chunks)]
    sums = exchange(corridor, own, surf, total_0, count, total_1, windows)
    after = summed(corridor, own, total_1)
    for chunk, new_surf in settled(own, surf, east, south, keep, sums):
        surf_1[own, cols(chunk)] = new_surf
        sums_2[:, cols(chunk)] = after[chunk]
    refill(corridor, own, surf_1, total_1, count, total_2)
    give(corridor, 1, surf_1, given_1, given_2)


def second_kernel(corridor, tiles, far, beyond, surf, east, south, *refs):
    faces = refs[:4]
    number, total, sums_2 = refs[4:7]
    surf_1, total_1, count, keep, total_2 = refs[12:17]
    surf_2, east_2, south_2, total_0 = refs[17:]
    ext, columns = surf.shape
    rows = ext - 2 * HALO
    chunks = columns // LANES
    position = lax.axis_index("gy")
    tail = slice(rows, ext)

    section = jnp.concatenate([far[0:1, :], beyond[0:1, :]], axis=1)
    cell = jnp.concatenate([far[1:2, :], beyond[1:2, :]], axis=1)
    valid, node_row, node_chunk, node_lane = located(cell, position, rows, ext, columns)
    key = jnp.where(valid & (node_row >= rows), node_chunk * 8 + (node_row - rows), -1)
    starts, levels = scattered(section, key, node_lane, chunks * 8)
    starting = [
        number[tail, cols(chunk)] + starts[chunk * 8 : chunk * 8 + 8] for chunk in range(chunks)
    ]
    covering = window_sums(starting, corridor, False)
    for chunk in range(chunks):
        at = cols(chunk)
        count[tail, at] = (FEED * DRAIN) * starting[chunk]
        keep[tail, at] = 1.0 - FEED * covering[chunk]
        total_0[tail, at] = FEED * (total[tail, at] + levels[chunk * 8 : chunk * 8 + 8])
    sums = exchange(corridor, tail, surf, total_0, count, total_1)

    own = slice(0, rows)
    before = (surf_1, east, south)
    fluxes(own, rows - 8, None, before, faces, east_2, south_2)
    own_sums = [sums_2[:, cols(chunk)] for chunk in range(chunks)]

    for chunk, new_surf in settled(tail, surf, east, south, keep, sums):
        surf_1[tail, cols(chunk)] = new_surf
    tail_sums = exchange(corridor, tail, surf_1, total_1, count, total_2)
    fluxes(tail, 0, wall_of(ext, tiles), before, faces, east_2, south_2)
    for mine, sums in ((own, own_sums), (tail, tail_sums)):
        for chunk, new_surf in settled(mine, surf_1, east_2, south_2, keep, sums):
            surf_2[mine, cols(chunk)] = new_surf


def third_kernel(corridor, tiles, surf, east, south, *refs):
    faces = refs[:4]
    total, keep, given_2, own, takes, masks, takes_near, masks_near, count, bed = refs[4:14]
    surf_3, east_3, south_3, own_term, partner_term, other_term = refs[14:20]
    ext, columns = surf.shape
    rows = ext - 2 * HALO
    mine = slice(0, rows)
    owned = own.shape[1]
    chunks = columns // LANES
    sums = summed(corridor, mine, total)
    fluxes(
        mine, rows - 8, wall_of(ext, tiles), (surf, east, south), faces, east_3, south_3
    )
    weight = DRAIN * (1.0 - corridor * DRAIN)
    levels = []
    for chunk, new_surf in settled(mine, surf, east_3, south_3, keep, sums):
        at = cols(chunk)
        surf_3[mine, at] = new_surf
        levels.append(given_2[:, at] + weight * surf[mine, at] + DRAIN * new_surf)
    spare = takes.shape[2] - chunks * rows
    if spare:
        levels.append(jnp.zeros((spare, LANES), jnp.float32))
    levels = jnp.concatenate(levels, axis=0)
    high = levels.astype(jnp.bfloat16)
    low = (levels - high.astype(jnp.float32)).astype(jnp.bfloat16)
    picked = jnp.dot(
        jnp.concatenate([takes[0], takes_near[0], takes[1], takes_near[1]], axis=0),
        jnp.concatenate([high, low], axis=1),
        preferred_element_type=jnp.float32,
    )
    hit = jnp.concatenate([masks[0], masks_near[0], masks[1], masks_near[1]], axis=0)
    picked = (picked * jnp.concatenate([hit, hit], axis=1)).astype(jnp.bfloat16)
    picked = jnp.concatenate([picked[: 3 * owned], picked[3 * owned :]], axis=1)
    terms = lax.dot_general(
        jnp.ones((8, 4 * LANES), jnp.bfloat16),
        picked,
        (((1,), (1,)), ((), ())),
        preferred_element_type=jnp.float32,
    )[0:1]
    own_term[...] = (1.0 - corridor * DRAIN) ** STEPS * own[0:1, :] + terms[:, :owned]
    partner_term[...] = terms[:, owned : 2 * owned]
    other_term[...] = terms[:, 2 * owned :]

    @pl.when(is_edge(tiles))
    def _():
        last_substep(
            *(corridor, tiles, surf, east, south_3, *faces, total, count, keep, bed),
            *(None, east_3, surf_3, *refs[20:]),
        )


def is_edge(tiles):
    position = lax.axis_index("gy")
    return (position == 0) | (position == tiles - 1)


def last_kernel(corridor, tiles, *refs):
    @pl.when(jnp.logical_not(is_edge(tiles)))
    def _():
        last_substep(corridor, tiles, *refs[:13], *refs[16:])


def last_substep(corridor, tiles, surf_2, east_2, south_3, *refs):
    faces = refs[:4]
    total_2, count, keep, bed, _, east_3 = refs[4:10]
    surf_3, depth_out, east_out, south_out = refs[10:14]
    depth_4, east_4, south_4, east_tail, total_3, sems = refs[14:]
    ext, columns = surf_2.shape
    rows = ext - 2 * HALO
    chunks = columns // LANES
    own, tail = slice(0, rows), slice(rows, ext)

    def copy(slot, source, target, first, last):
        part = pl.ds(first * LANES, (last - first) * LANES)
        return pltpu.make_async_copy(
            source.at[pl.ds(0, rows), part], target.at[:, part], sems.at[slot]
        )

    before = (surf_3, east_3, south_3)
    tail_sums = summed(corridor, tail, total_2)
    refill(corridor, own, surf_2, total_2, count, total_3)
    fluxes(own, rows - 8, None, before, faces, east_4, south_4, scale=SLOPE)
    copies = [copy(0, east_4, east_out, 0, chunks)]
    copies[0].start()
    fluxes(tail, 0, None, (surf_2, east_2, None), faces, east_tail, None)
    for chunk, new_surf in settled(tail, surf_2, east_tail, south_3, keep, tail_sums):
        surf_3[tail, cols(chunk)] = new_surf
    sums = summed(corridor, own, total_3)
    fluxes(slice(0, 0), 0, wall_of(ext, tiles), before, faces, None, south_4, scale=SLOPE)
    copies.append(copy(1, south_4, south_out, 0, chunks))
    copies[1].start()
    group = 5
    for chunk, new_surf in settled(own, surf_3, east_4, south_4, keep, sums, spread=SPREAD):
        at = cols(chunk)
        depth_4[:, at] = new_surf - bed[own, at]
        if (chunk + 1) % group == 0 or chunk + 1 == chunks:
            first = chunk // group
            copies.append(copy(2 + first, depth_4, depth_out, first * group, chunk + 1))
            copies[-1].start()
    for one in copies:
        one.wait()


def local(
    depth, flux_east, flux_south, river_section, bed_level, rough_class, manning_table, bank_cell
):
    rows, columns = depth.shape
    owned = river_section.shape[0]
    corridor = bank_cell.shape[0]
    tiles = lax.axis_size("gy")
    ext = rows + 2 * HALO
    chunks = columns // LANES
    partner_section = swapped(river_section, 0).reshape(1, owned)
    partner_cells = swapped(bank_cell, 0)

    def held(value):
        return pltpu.with_memory_space_constraint(value, pltpu.VMEM)

    def far(value):
        return pltpu.with_memory_space_constraint(value, pltpu.HBM)

    params = pltpu.CompilerParams(vmem_limit_bytes=VMEM_LIMIT)
    halo = pltpu.VMEM((4 * chunks, HALO, LANES), jnp.float32)
    wide = pltpu.VMEM((4 * chunks + 1, HALO, LANES), jnp.float32)
    field = pltpu.VMEM((ext, columns), jnp.float32)
    small = pltpu.VMEM((rows, columns), jnp.float32)
    term = pltpu.VMEM((1, owned), jnp.float32)
    pair = pltpu.VMEM((2, owned), jnp.float32)
    result = pltpu.HBM((rows, columns), jnp.float32)
    cells = -(-chunks * rows // LANES) * LANES

    def call(kernel, name, outs, values, scratch=(), aliases=None):
        return pl.pallas_call(
            kernel,
            out_shape=outs,
            in_specs=[VMEM_SPEC] * len(values),
            out_specs=[HBM_SPEC if out is result else VMEM_SPEC for out in outs],
            scratch_shapes=scratch,
            input_output_aliases=aliases or {},
            compiler_params=params,
            name=name,
        )(*[held(value) for value in values])

    def picks(nodes):
        return [
            pltpu.VMEM((2, nodes, cells), jnp.bfloat16),
            pltpu.VMEM((2, nodes, LANES), jnp.float32),
        ]

    classes = manning_table.shape[0]
    table = far(manning_table.reshape(1, classes))
    table_held = pltpu.VMEM((1, classes), jnp.float32)
    to_other, own = pl.pallas_call(
        pack_kernel,
        out_shape=[wide, pair],
        in_specs=[HBM_SPEC] * 8,
        out_specs=[VMEM_SPEC] * 2,
        scratch_shapes=[
            pltpu.VMEM((4, 8, columns), jnp.float32),
            pltpu.VMEM((8, columns), jnp.int32),
            pltpu.VMEM((corridor, owned), jnp.int32),
            table_held,
            pltpu.SemaphoreType.DMA((8,)),
        ],
        compiler_params=params,
        name="pack",
    )(
        *[far(value) for value in (depth, bed_level, rough_class, flux_east, flux_south)],
        far(river_section.reshape(1, owned)),
        far(bank_cell),
        table,
    )
    (to_other,) = call(
        join_kernel,
        "join",
        [wide],
        (to_other, partner_section, partner_cells),
        aliases={0: 0},
    )
    by_other = swapped(to_other, 1)
    *loaded, rough, table_rows = pl.pallas_call(
        load_kernel,
        out_shape=[field] * 4
        + [pltpu.VMEM((rows, columns), jnp.int32), pltpu.VMEM((classes, LANES), jnp.float32)],
        in_specs=[HBM_SPEC] * 6,
        out_specs=[VMEM_SPEC] * 6,
        scratch_shapes=[table_held, pltpu.SemaphoreType.DMA((6,))],
        compiler_params=params,
        name="load",
    )(
        *[far(value) for value in (depth, flux_east, flux_south, bed_level, rough_class)],
        table,
    )
    *fields, to_partner = call(
        prepare_kernel,
        "prepare",
        [field] * 9 + [halo],
        (table_rows, rough, *loaded),
        aliases={2 + slot: slot for slot in range(4)},
    )
    by_partner = swapped(to_partner, 0)
    number, total, takes, masks, windows, given_1 = call(
        functools.partial(nodes_kernel, corridor),
        "nodes",
        [field] * 2 + picks(2 * owned) + [small] * 2,
        (fields[0], own, partner_section, partner_cells),
    )
    near, beyond = call(relay_kernel, "relay", [pair, pair], (by_other, masks))
    from_far = swapped(near, 0)
    *fields, takes_near, masks_near = call(
        functools.partial(border_kernel, corridor, tiles),
        "border",
        [field] * 11 + picks(owned),
        (by_partner, by_other, table_rows, near, *fields, number, total),
        aliases={4 + slot: slot for slot in range(11)},
    )
    surf, east, south, bed, _, *faces, number, total = fields
    surf_1, total_1, count, keep, total_2, sums_2, given_2 = call(
        functools.partial(first_kernel, corridor),
        "first",
        [field] * 5 + [small] * 2,
        (surf, east, south, number, total, windows, given_1),
        scratch=[field],
    )
    surf_1, total_1, count, keep, total_2, surf_2, east_2, south_2 = call(
        functools.partial(second_kernel, corridor, tiles),
        "second",
        [field] * 8,
        (
            *(from_far, beyond, surf, east, south, *faces, number, total, sums_2),
            *(surf_1, total_1, count, keep, total_2),
        ),
        scratch=[field],
        aliases={12 + slot: slot for slot in range(5)},
    )
    last_scratch = [small, small, field, field, small]
    last_scratch.append(pltpu.SemaphoreType.DMA((2 + -(-chunks // 5),)))
    surf_3, east_3, south_3, own_term, partner_term, other_term, *results = call(
        functools.partial(third_kernel, corridor, tiles),
        "third",
        [field] * 3 + [term] * 3 + [result] * 3,
        (
            *(surf_2, east_2, south_2, *faces, total_2, keep, given_2),
            *(own, takes, masks, takes_near, masks_near, count, bed),
        ),
        scratch=last_scratch,
    )
    from_other = swapped(other_term.reshape(owned), 1)
    from_partner = swapped(partner_term.reshape(owned), 0)
    last_in = (surf_2, east_2, south_3, *faces, total_2, count, keep, bed, surf_3, east_3)
    _, depth, flux_east, flux_south = pl.pallas_call(
        functools.partial(last_kernel, corridor, tiles),
        out_shape=[field] + [result] * 3,
        in_specs=[VMEM_SPEC] * 13 + [HBM_SPEC] * 3,
        out_specs=[VMEM_SPEC] + [HBM_SPEC] * 3,
        scratch_shapes=last_scratch,
        input_output_aliases={11: 0, 13: 1, 14: 2, 15: 3},
        compiler_params=params,
        name="last",
    )(*[held(value) for value in last_in], *[far(value) for value in results])
    river_section = own_term.reshape(owned) + from_other + from_partner
    return (depth, flux_east, flux_south, river_section)


def solution(mesh):
    return jax.shard_map(
        local,
        mesh=mesh,
        in_specs=(
            P(("runs", "gy"), None),
            P(("runs", "gy"), None),
            P(("runs", "gy"), None),
            P(("runs", "gy")),
            P("gy", None),
            P("gy", None),
            P(),
            P(None, "gy"),
        ),
        out_specs=(
            P(("runs", "gy"), None),
            P(("runs", "gy"), None),
            P(("runs", "gy"), None),
            P(("runs", "gy")),
        ),
        check_vma=False,
    )
```

```python
import functools

import jax
import jax.numpy as jnp
from jax import lax
from jax.experimental import pallas as pl
from jax.experimental.pallas import tpu as pltpu
from jax.sharding import PartitionSpec as P

STEPS = 4

GRAV = 9.81
TSTEP = 8.0
CELL = 90.0
FLOOR = 0.05
BANK_COEF = 200.0
CELL_AREA = 8100.0
NODE_AREA = 20000.0

LANES = 128
HALO = 4
SLOPE = GRAV * TSTEP / CELL
SPREAD = TSTEP / CELL
FEED = TSTEP * BANK_COEF / CELL_AREA
DRAIN = TSTEP * BANK_COEF / NODE_AREA
VMEM_LIMIT = 32 * 1024 * 1024

VMEM_SPEC = pl.BlockSpec(memory_space=pltpu.VMEM)
HBM_SPEC = pl.BlockSpec(memory_space=pltpu.HBM)


def swapped(value, first):
    count = lax.axis_size("gy")
    pairs = []
    for low in range(first, count - 1, 2):
        pairs += [(low, low + 1), (low + 1, low)]
    return lax.ppermute(value, "gy", pairs)


def cols(chunk):
    return slice(chunk * LANES, (chunk + 1) * LANES)


def lanes_of(rows):
    return lax.broadcasted_iota(jnp.int32, (rows, LANES), 1)


def moved_left(value, following, by):
    return jnp.where(
        lanes_of(value.shape[0]) >= LANES - by,
        pltpu.roll(following, LANES - by, 1),
        pltpu.roll(value, LANES - by, 1),
    )


def moved_up(value):
    return pltpu.roll(value, value.shape[0] - 1, 0)


def split3(value):
    high = value.astype(jnp.bfloat16)
    rest = value - high.astype(jnp.float32)
    middle = rest.astype(jnp.bfloat16)
    low = (rest - middle.astype(jnp.float32)).astype(jnp.bfloat16)
    return high, middle, low


def one_hot(count, key):
    rows = lax.broadcasted_iota(jnp.int32, (count, key.shape[1]), 0)
    return jnp.where(rows == key, 1.0, 0.0)


def drag_of(mann_a, mann_b):
    pair = mann_a + mann_b
    return (0.25 * GRAV * TSTEP * SLOPE) * (pair * pair)


def looked_up(klass, entries):
    value = jnp.broadcast_to(entries[0], klass.shape)
    for k in range(1, len(entries)):
        value = jnp.where(klass == k, entries[k], value)
    return value


def face(flux, surf_a, surf_b, bed_max, drag):
    flow_depth = jnp.maximum(jnp.maximum(surf_a, surf_b) - bed_max, FLOOR)
    power = jnp.exp2((-7.0 / 3.0) * jnp.log2(flow_depth))
    driven = flux - flow_depth * (surf_b - surf_a)
    damping = 1.0 + drag * jnp.abs(flux) * power
    return driven * pl.reciprocal(damping, approx=True)


def window_sums(blocks, reach, forward):
    height = blocks[0].shape[0]
    count = len(blocks)
    spare = -(count * height) % 16
    whole = blocks + ([jnp.zeros((spare, LANES), jnp.float32)] if spare else [])
    whole = jnp.concatenate(whole, axis=0)
    high = whole.astype(jnp.bfloat16)
    low = (whole - high.astype(jnp.float32)).astype(jnp.bfloat16)
    source = lax.broadcasted_iota(jnp.int32, (2 * LANES, 2 * LANES), 0) % LANES
    target = lax.broadcasted_iota(jnp.int32, (2 * LANES, 2 * LANES), 1)
    spill = target >= LANES
    target = target % LANES
    if forward:
        ahead = source - target + jnp.where(spill, LANES, 0)
    else:
        ahead = target - source + jnp.where(spill, LANES, 0)
    band = jnp.where((ahead >= 0) & (ahead < reach), 1.0, 0.0).astype(jnp.bfloat16)
    sums = jnp.dot(
        jnp.concatenate([high, low], axis=1), band, preferred_element_type=jnp.float32
    )
    results = []
    for block in range(count):
        result = sums[block * height : (block + 1) * height, :LANES]
        beside = block + 1 if forward else block - 1
        if 0 <= beside < count:
            result = result + sums[beside * height : (beside + 1) * height, LANES:]
        results.append(result)
    return results


def east_walled(value, chunk, chunks):
    if chunk + 1 < chunks:
        return value
    return jnp.where(lanes_of(value.shape[0]) == LANES - 1, 0.0, value)


def located(cell, position, rows, ext, columns):
    base = ((position * rows - HALO) * columns + 1).astype(jnp.float32)
    offset = cell - base
    valid = (cell > 0.0) & (offset >= 0.0) & (offset < float(ext * columns))
    offset = jnp.where(valid, offset, 0.0)
    row = jnp.floor((offset + 0.5) * (1.0 / columns))
    column = (offset - row * float(columns)).astype(jnp.int32)
    row = row.astype(jnp.int32) - HALO
    row = jnp.where(row < 0, row + ext, row)
    chunk = column // LANES
    return valid, row, chunk, column - chunk * LANES


def scattered(section, key, lane, count):
    at_lane = one_hot(LANES, lane)
    parts = [at_lane] + [at_lane * part.astype(jnp.float32) for part in split3(section)]
    grid = lax.dot_general(
        one_hot(-(-count // 16) * 16, key).astype(jnp.bfloat16),
        jnp.concatenate(parts, axis=0).astype(jnp.bfloat16),
        (((1,), (1,)), ((), ())),
        preferred_element_type=jnp.float32,
    )
    number = grid[:, :LANES]
    total = (grid[:, LANES : 2 * LANES] + grid[:, 2 * LANES : 3 * LANES]) + grid[:, 3 * LANES :]
    return number, total


def border_rows(of_first, fields, south):
    outer = lax.broadcasted_iota(jnp.int32, (HALO, LANES), 0) == jnp.where(of_first, HALO - 1, 0)
    flux = jnp.where(of_first, south[:HALO], south[HALO:])
    return [
        jnp.where(outer, flux[slot : slot + 1], jnp.where(of_first, value[:HALO], value[HALO:]))
        for slot, value in enumerate(fields)
    ]


def pack_kernel(
    depth, bed, rough, east, south, section, cells, table_in, to_other, own, *refs
):
    held, held_rough, held_cells, table, sems = refs
    rows, columns = depth.shape
    chunks = columns // LANES
    even = lax.axis_index("gy") % 2 == 0
    start = pl.multiple_of(jnp.where(even, 0, rows - 8), 8)
    near = pl.ds(start, 8)
    copies = [
        pltpu.make_async_copy(source, target, sems.at[slot])
        for slot, (source, target) in enumerate(
            (
                (rough.at[near, :], held_rough),
                (bed.at[near, :], held.at[1]),
                (depth.at[near, :], held.at[0]),
                (east.at[near, :], held.at[2]),
                (south.at[near, :], held.at[3]),
                (section, own.at[pl.ds(0, 1), :]),
                (cells, held_cells),
                (table_in, table),
            )
        )
    ]
    for copy in copies:
        copy.start()
    for copy in copies:
        copy.wait()
    own[1:2, :] = (held_cells[0:1, :] + 1).astype(jnp.float32)
    entries = [
        jnp.broadcast_to(table[:, k : k + 1], (1, LANES)) for k in range(table.shape[1])
    ]
    manns = [looked_up(held_rough[:, cols(chunk)], entries) for chunk in range(chunks)]
    row = lax.broadcasted_iota(jnp.int32, (8, LANES), 0)
    beds = [held[1, :, cols(chunk)] for chunk in range(chunks)]
    surfs = [held[0, :, cols(chunk)] + beds[chunk] for chunk in range(chunks)]

    def moved(values):
        rolled = [pltpu.roll(value, LANES - 1, 1) for value in values]
        rolled.append(rolled[-1])
        edge = lanes_of(8) == LANES - 1
        return [jnp.where(edge, rolled[c + 1], rolled[c]) for c in range(chunks)]

    beds_left, surfs_left, manns_left = moved(beds), moved(surfs), moved(manns)
    for chunk in range(chunks):
        at = cols(chunk)
        m0, b0, s0 = manns[chunk], beds[chunk], surfs[chunk]
        bed_max = jnp.maximum(b0, beds_left[chunk])
        drag = drag_of(m0, manns_left[chunk])
        q0 = (1.0 / SLOPE) * held[2, :, at]
        new_east = face(q0, s0, surfs_left[chunk], bed_max, drag)
        new_east = east_walled(new_east, chunk, chunks)
        bed_max = jnp.maximum(b0, moved_up(b0))
        drag = drag_of(m0, moved_up(m0))
        q0 = (1.0 / SLOPE) * held[3, :, at]
        new_south = jnp.where(row == 7, q0, face(q0, s0, moved_up(s0), bed_max, drag))
        fields = (s0, b0, held_rough[:, at].astype(jnp.float32), new_east)
        for slot, block in enumerate(border_rows(even, fields, new_south)):
            to_other[slot * chunks + chunk] = block
    to_other[4 * chunks, 0:2, :] = own[...]


def join_kernel(before, section, cells, to_other):
    nodes = to_other.shape[0] - 1
    to_other[nodes, 2:3, :] = section[...]
    to_other[nodes, 3:4, :] = (cells[0:1, :] + 1).astype(jnp.float32)


def relay_kernel(by_other, prepared, near, beyond):
    del prepared
    nodes = by_other.shape[0] - 1
    near[...] = by_other[nodes, 0:2, :]
    beyond[...] = by_other[nodes, 2:4, :]


def picking(reach, rows, key, lane, takes, masks):
    for block in range(key.shape[1] // LANES):
        mine = slice(block * LANES, (block + 1) * LANES)

        def column(row):
            wide = jnp.broadcast_to(row[:, mine].astype(jnp.float32), (LANES, LANES))
            return jnp.transpose(wide).astype(jnp.int32)

        spread = lanes_of(LANES)
        at = column(key)
        after = jnp.where(at < 0, at, at + rows)
        for first in range(0, takes.shape[2], LANES):
            for half, place in enumerate((at, after)):
                hit = jnp.where(spread + first == place, 1.0, 0.0)
                takes[half, mine, first : first + LANES] = hit.astype(jnp.bfloat16)
        ahead = spread - column(lane)
        masks[0, mine, :] = jnp.where((ahead >= 0) & (ahead < reach), 1.0, 0.0)
        masks[1, mine, :] = jnp.where(ahead + LANES < reach, 1.0, 0.0)


def load_kernel(
    depth_in, east_in, south_in, bed_in, rough_in, table_in, *refs
):
    surf, east, south, bed, rough, table_rows, table, sems = refs
    rows, columns = depth_in.shape
    own = pl.ds(0, rows)
    copies = [
        pltpu.make_async_copy(source, target.at[own, :], sems.at[slot])
        for slot, (source, target) in enumerate(
            (
                (depth_in, surf),
                (bed_in, bed),
                (rough_in, rough),
                (east_in, east),
                (south_in, south),
            )
        )
    ]
    copies.append(pltpu.make_async_copy(table_in, table, sems.at[5]))
    for copy in copies:
        copy.start()
    copies[5].wait()
    for k in range(table_rows.shape[0]):
        table_rows[k : k + 1, :] = jnp.broadcast_to(table[:, k : k + 1], (1, LANES))
    for copy in copies[:5]:
        copy.wait()


def prepare_kernel(table_rows, rough, *refs):
    surf, east, south, bed = refs[4:8]
    mann, bed_e, bed_s, drag_e, drag_s, to_partner = refs[8:]
    ext, columns = surf.shape
    rows = ext - 2 * HALO
    chunks = columns // LANES
    even = lax.axis_index("gy") % 2 == 0
    entries = [table_rows[k : k + 1, :] for k in range(table_rows.shape[0])]
    for chunk in range(chunks):
        at = cols(chunk)
        mann[:rows, at] = looked_up(rough[:, at], entries)
        surf[:rows, at] = surf[:rows, at] + bed[:rows, at]

    kept = lax.broadcasted_iota(jnp.int32, (rows, LANES), 0) == rows - 1
    for chunk in range(chunks):
        at, then = cols(chunk), cols(min(chunk + 1, chunks - 1))
        s0, b0, m0 = surf[:rows, at], bed[:rows, at], mann[:rows, at]
        bed_max = jnp.maximum(b0, moved_left(b0, bed[:rows, then], 1))
        drag = drag_of(m0, moved_left(m0, mann[:rows, then], 1))
        bed_e[:rows, at] = bed_max
        drag_e[:rows, at] = drag
        q0 = (1.0 / SLOPE) * east[:rows, at]
        new_east = face(q0, s0, moved_left(s0, surf[:rows, then], 1), bed_max, drag)
        new_east = east_walled(new_east, chunk, chunks)
        east[:rows, at] = new_east
        bed_max = jnp.maximum(b0, moved_up(b0))
        drag = drag_of(m0, moved_up(m0))
        bed_s[:rows, at] = bed_max
        drag_s[:rows, at] = drag
        q0 = (1.0 / SLOPE) * south[:rows, at]
        new_south = jnp.where(kept, q0, face(q0, s0, moved_up(s0), bed_max, drag))
        south[:rows, at] = new_south

        def ends(value):
            return jnp.where(even, value[rows - 8 :], value[:8])

        fields = (ends(s0), ends(b0), ends(rough[:, at].astype(jnp.float32)), ends(new_east))
        blocks = border_rows(jnp.logical_not(even), fields, ends(new_south))
        for slot, block in enumerate(blocks):
            to_partner[slot * chunks + chunk] = block


def nodes_kernel(reach, surf, own, partner_section, partner_cells, *refs):
    number, total, takes, masks, windows, given_1 = refs
    rows = surf.shape[0] - 2 * HALO
    ext, columns = number.shape
    chunks = columns // LANES
    tiles = lax.axis_size("gy")
    position = lax.axis_index("gy")
    side = jnp.where(position % 2 == 0, 1, -1)
    partner = jnp.where(position + side < tiles, partner_cells[0:1, :] + 1, 0).astype(jnp.float32)
    section = jnp.concatenate([own[0:1, :], partner_section[...]], axis=1)
    cell = jnp.concatenate([own[1:2, :], partner], axis=1)
    valid, node_row, node_chunk, node_lane = located(cell, position, rows, ext, columns)
    key = jnp.where(valid, node_chunk * ext + node_row, -1)
    starts, levels = scattered(section, key, node_lane, chunks * ext)
    for chunk in range(chunks):
        at = cols(chunk)
        number[:, at] = starts[chunk * ext : (chunk + 1) * ext]
        total[:, at] = levels[chunk * ext : (chunk + 1) * ext]
    key = jnp.where(valid & (node_row < rows), node_chunk * rows + node_row, -1)
    picking(reach, rows, key, node_lane, takes, masks)
    sums = window_sums([surf[:rows, cols(chunk)] for chunk in range(chunks)], reach, True)
    for chunk in range(chunks):
        windows[:, cols(chunk)] = sums[chunk]
    give(reach, 0, surf, None, given_1)


def wall_of(ext, tiles):
    position = lax.axis_index("gy")
    rows = ext - 2 * HALO
    row = lax.broadcasted_iota(jnp.int32, (16, LANES), 0) + (ext - 16)
    return ((row == ext - 1) & (position == 0)) | ((row == rows - 1) & (position == tiles - 1))


def near_kernel(reach, early, near, *refs):
    number, total, takes, masks = refs[-4:]
    ext, columns = number.shape
    rows = ext - 2 * HALO
    chunks = columns // LANES
    position = lax.axis_index("gy")
    if early:
        refs[2][...] = near[...]

    @pl.when((position % 4 == 3) if early else (position % 4 != 3))
    def _():
        cell = near[1:2, :]
        valid, node_row, node_chunk, node_lane = located(cell, position, rows, ext, columns)
        key = jnp.where(valid, node_chunk * ext + node_row, -1)
        starts, levels = scattered(near[0:1, :], key, node_lane, chunks * ext)
        for chunk in range(chunks):
            at = cols(chunk)
            number[:, at] += starts[chunk * ext : (chunk + 1) * ext]
            total[:, at] += levels[chunk * ext : (chunk + 1) * ext]
        key = jnp.where(valid & (node_row < rows), node_chunk * rows + node_row, -1)
        picking(reach, rows, key, node_lane, takes, masks)


def border_kernel(tiles, by_partner, by_other, table_rows, *refs):
    surf, east, south, bed, mann, bed_e, bed_s, drag_e, drag_s = refs[9:]
    ext, columns = surf.shape
    rows = ext - 2 * HALO
    chunks = columns // LANES
    position = lax.axis_index("gy")
    even = position % 2 == 0
    entries = [table_rows[k : k + 1, :] for k in range(table_rows.shape[0])]
    row = lax.broadcasted_iota(jnp.int32, (2 * HALO, LANES), 0)
    for chunk in range(chunks):
        at = cols(chunk)
        halos = []
        flux = jnp.zeros((2 * HALO, LANES), jnp.float32)
        for slot in range(4):
            a, b = by_partner[slot * chunks + chunk], by_other[slot * chunks + chunk]
            below = jnp.where(even, a, b)
            above = jnp.where(even, b, a)
            halos.append(jnp.concatenate([below, above], axis=0))
            flux = jnp.where(row == slot, below[HALO - 1 :], flux)
            flux = jnp.where(row == HALO + slot, above[:1], flux)
        surf[rows:, at] = halos[0]
        bed[rows:, at] = halos[1]
        mann[rows:, at] = looked_up(halos[2].astype(jnp.int32), entries)
        east[rows:, at] = halos[3]
        south[rows:, at] = flux

    wall = wall_of(ext, tiles)
    kept = lax.broadcasted_iota(jnp.int32, (16, LANES), 0) % 8 < 7
    for chunk in range(chunks):
        at, then = cols(chunk), cols(min(chunk + 1, chunks - 1))
        b0, m0 = bed[rows:, at], mann[rows:, at]
        bed_e[rows:, at] = jnp.maximum(b0, moved_left(b0, bed[rows:, then], 1))
        drag_e[rows:, at] = drag_of(m0, moved_left(m0, mann[rows:, then], 1))

        def rolled_up(ref):
            value = jnp.concatenate([ref[rows - 8 :, at], ref[:8, at]], axis=0)
            return value[:16], moved_up(value)[:16]

        s0, s1 = rolled_up(surf)
        b0, b1 = rolled_up(bed)
        m0, m1 = rolled_up(mann)
        bed_max = jnp.maximum(b0, b1)
        drag = drag_of(m0, m1)
        bed_s[rows - 8 :, at] = bed_max
        drag_s[rows - 8 :, at] = drag
        q0 = south[rows - 8 :, at]
        new_south = jnp.where(kept, q0, face(q0, s0, s1, bed_max, drag))
        south[rows - 8 :, at] = jnp.where(wall, 0.0, new_south)


def fluxes(mine, upper, wall, before, faces, east_out, south_out, scale=None):
    surf, east, south = before
    bed_e, bed_s, drag_e, drag_s = faces
    ext, columns = surf.shape
    chunks = columns // LANES
    rolled = lane = None
    if east_out is not None:
        rolled = pltpu.roll(surf[mine, cols(0)], LANES - 1, 1)
        lane = lanes_of(rolled.shape[0])
    for chunk in range(chunks):
        at = cols(chunk)
        if east_out is not None:
            s0 = surf[mine, at]
            rolled_then = rolled
            if chunk + 1 < chunks:
                rolled_then = pltpu.roll(surf[mine, cols(chunk + 1)], LANES - 1, 1)
            left = jnp.where(lane >= LANES - 1, rolled_then, rolled)
            rolled = rolled_then
            new_east = face(east[mine, at], s0, left, bed_e[mine, at], drag_e[mine, at])
            if scale is not None:
                new_east = scale * new_east
            east_out[mine, at] = east_walled(new_east, chunk, chunks)
        if upper:
            s0 = surf[: upper + 8, at]
            s1 = moved_up(s0)[:upper]
            new_south = face(south[:upper, at], s0[:upper], s1, bed_s[:upper, at], drag_s[:upper, at])
            if scale is not None:
                new_south = scale * new_south
            south_out[:upper, at] = new_south
        if wall is not None:
            low = slice(ext - 16, ext)
            s0 = jnp.concatenate([surf[low, at], surf[:8, at]], axis=0)
            s1 = moved_up(s0)[:16]
            new_south = face(south[low, at], s0[:16], s1, bed_s[low, at], drag_s[low, at])
            if scale is not None:
                new_south = scale * new_south
            south_out[low, at] = jnp.where(wall, 0.0, new_south)


def settled(mine, surf, east, south, keep, sums, spread=SPREAD * SLOPE):
    ext, columns = surf.shape
    rolled = 0.0
    for chunk in range(columns // LANES):
        at = cols(chunk)
        new_east = east[mine, at]
        new_south = south[:, at]
        lane = lanes_of(new_east.shape[0])
        rolled_before, rolled = rolled, pltpu.roll(new_east, 1, 1)
        west = jnp.where(lane < 1, rolled_before, rolled)
        north = pltpu.roll(new_south, 1, 0)[mine]
        inflow = west + north
        s0 = surf[mine, at]
        outflow = new_east + new_south[mine]
        yield chunk, keep[mine, at] * s0 + (spread * (inflow - outflow) + sums[chunk])


def refill(corridor, mine, surf, total, count, total_out, windows=None):
    chunks = surf.shape[1] // LANES
    if windows is None:
        windows = window_sums([surf[mine, cols(chunk)] for chunk in range(chunks)], corridor, True)
    for chunk in range(chunks):
        at = cols(chunk)
        kept = (1.0 - corridor * DRAIN) * total[mine, at]
        total_out[mine, at] = kept + count[mine, at] * windows[chunk]


def summed(corridor, mine, total):
    chunks = total.shape[1] // LANES
    return window_sums([total[mine, cols(chunk)] for chunk in range(chunks)], corridor, False)


def exchange(corridor, mine, surf, total, count, total_out, windows=None):
    sums = summed(corridor, mine, total)
    refill(corridor, mine, surf, total, count, total_out, windows)
    return sums


def give(corridor, step, surf, before, after):
    rows, columns = after.shape
    weight = DRAIN * (1.0 - corridor * DRAIN) ** (STEPS - 1 - step)
    for chunk in range(columns // LANES):
        at = cols(chunk)
        value = weight * surf[:rows, at]
        after[:, at] = value if before is None else before[:, at] + value


def first_kernel(corridor, surf, east, south, number, total, windows, given_1, *refs):
    surf_1, total_1, count, keep, total_2, sums_2, given_2, total_0 = refs
    rows = surf.shape[0] - 2 * HALO
    chunks = surf.shape[1] // LANES
    own = slice(0, rows)
    covering = window_sums([number[own, cols(chunk)] for chunk in range(chunks)], corridor, False)
    for chunk in range(chunks):
        at = cols(chunk)
        count[own, at] = (FEED * DRAIN) * number[own, at]
        keep[own, at] = 1.0 - FEED * covering[chunk]
        total_0[own, at] = FEED * total[own, at]
    windows = [windows[:, cols(chunk)] for chunk in range(chunks)]
    sums = exchange(corridor, own, surf, total_0, count, total_1, windows)
    after = summed(corridor, own, total_1)
    for chunk, new_surf in settled(own, surf, east, south, keep, sums):
        surf_1[own, cols(chunk)] = new_surf
        sums_2[:, cols(chunk)] = after[chunk]
    refill(corridor, own, surf_1, total_1, count, total_2)
    give(corridor, 1, surf_1, given_1, given_2)


def second_kernel(corridor, tiles, far, beyond, surf, east, south, *refs):
    faces = refs[:4]
    number, total, sums_2 = refs[4:7]
    surf_1, total_1, count, keep, total_2 = refs[12:17]
    surf_2, east_2, south_2, total_0 = refs[17:]
    ext, columns = surf.shape
    rows = ext - 2 * HALO
    chunks = columns // LANES
    position = lax.axis_index("gy")
    tail = slice(rows, ext)

    section = jnp.concatenate([far[0:1, :], beyond[0:1, :]], axis=1)
    cell = jnp.concatenate([far[1:2, :], beyond[1:2, :]], axis=1)
    valid, node_row, node_chunk, node_lane = located(cell, position, rows, ext, columns)
    key = jnp.where(valid & (node_row >= rows), node_chunk * 8 + (node_row - rows), -1)
    starts, levels = scattered(section, key, node_lane, chunks * 8)
    starting = [
        number[tail, cols(chunk)] + starts[chunk * 8 : chunk * 8 + 8] for chunk in range(chunks)
    ]
    covering = window_sums(starting, corridor, False)
    for chunk in range(chunks):
        at = cols(chunk)
        count[tail, at] = (FEED * DRAIN) * starting[chunk]
        keep[tail, at] = 1.0 - FEED * covering[chunk]
        total_0[tail, at] = FEED * (total[tail, at] + levels[chunk * 8 : chunk * 8 + 8])
    sums = exchange(corridor, tail, surf, total_0, count, total_1)

    own = slice(0, rows)
    before = (surf_1, east, south)
    fluxes(own, rows - 8, None, before, faces, east_2, south_2)
    own_sums = [sums_2[:, cols(chunk)] for chunk in range(chunks)]

    for chunk, new_surf in settled(tail, surf, east, south, keep, sums):
        surf_1[tail, cols(chunk)] = new_surf
    tail_sums = exchange(corridor, tail, surf_1, total_1, count, total_2)
    fluxes(tail, 0, wall_of(ext, tiles), before, faces, east_2, south_2)
    for mine, sums in ((own, own_sums), (tail, tail_sums)):
        for chunk, new_surf in settled(mine, surf_1, east_2, south_2, keep, sums):
            surf_2[mine, cols(chunk)] = new_surf


def third_kernel(corridor, tiles, surf, east, south, *refs):
    faces = refs[:4]
    total, keep, given_2, own, takes, masks, takes_near, masks_near, count, bed = refs[4:14]
    surf_3, east_3, south_3, own_term, partner_term, other_term = refs[14:20]
    ext, columns = surf.shape
    rows = ext - 2 * HALO
    mine = slice(0, rows)
    owned = own.shape[1]
    chunks = columns // LANES
    sums = summed(corridor, mine, total)
    fluxes(
        mine, rows - 8, wall_of(ext, tiles), (surf, east, south), faces, east_3, south_3
    )
    weight = DRAIN * (1.0 - corridor * DRAIN)
    levels = []
    for chunk, new_surf in settled(mine, surf, east_3, south_3, keep, sums):
        at = cols(chunk)
        surf_3[mine, at] = new_surf
        levels.append(given_2[:, at] + weight * surf[mine, at] + DRAIN * new_surf)
    spare = takes.shape[2] - chunks * rows
    if spare:
        levels.append(jnp.zeros((spare, LANES), jnp.float32))
    levels = jnp.concatenate(levels, axis=0)
    high = levels.astype(jnp.bfloat16)
    low = (levels - high.astype(jnp.float32)).astype(jnp.bfloat16)
    picked = jnp.dot(
        jnp.concatenate([takes[0], takes_near[0], takes[1], takes_near[1]], axis=0),
        jnp.concatenate([high, low], axis=1),
        preferred_element_type=jnp.float32,
    )
    hit = jnp.concatenate([masks[0], masks_near[0], masks[1], masks_near[1]], axis=0)
    picked = (picked * jnp.concatenate([hit, hit], axis=1)).astype(jnp.bfloat16)
    picked = jnp.concatenate([picked[: 3 * owned], picked[3 * owned :]], axis=1)
    terms = lax.dot_general(
        jnp.ones((8, 4 * LANES), jnp.bfloat16),
        picked,
        (((1,), (1,)), ((), ())),
        preferred_element_type=jnp.float32,
    )[0:1]
    own_term[...] = (1.0 - corridor * DRAIN) ** STEPS * own[0:1, :] + terms[:, :owned]
    partner_term[...] = terms[:, owned : 2 * owned]
    other_term[...] = terms[:, 2 * owned :]

    @pl.when(is_edge(tiles))
    def _():
        last_substep(
            *(corridor, tiles, surf, east, south_3, *faces, total, count, keep, bed),
            *(None, east_3, surf_3, *refs[20:]),
        )


def is_edge(tiles):
    position = lax.axis_index("gy")
    return (position == 0) | (position == tiles - 1)


def last_kernel(corridor, tiles, *refs):
    @pl.when(jnp.logical_not(is_edge(tiles)))
    def _():
        last_substep(corridor, tiles, *refs[:13], *refs[16:])


def last_substep(corridor, tiles, surf_2, east_2, south_3, *refs):
    faces = refs[:4]
    total_2, count, keep, bed, _, east_3 = refs[4:10]
    surf_3, depth_out, east_out, south_out = refs[10:14]
    depth_4, east_4, south_4, east_tail, total_3, sems = refs[14:]
    ext, columns = surf_2.shape
    rows = ext - 2 * HALO
    chunks = columns // LANES
    own, tail = slice(0, rows), slice(rows, ext)

    def copy(slot, source, target, first, last):
        part = pl.ds(first * LANES, (last - first) * LANES)
        return pltpu.make_async_copy(
            source.at[pl.ds(0, rows), part], target.at[:, part], sems.at[slot]
        )

    before = (surf_3, east_3, south_3)
    tail_sums = summed(corridor, tail, total_2)
    refill(corridor, own, surf_2, total_2, count, total_3)
    fluxes(own, rows - 8, None, before, faces, east_4, south_4, scale=SLOPE)
    copies = [copy(0, east_4, east_out, 0, chunks)]
    copies[0].start()
    fluxes(tail, 0, None, (surf_2, east_2, None), faces, east_tail, None)
    for chunk, new_surf in settled(tail, surf_2, east_tail, south_3, keep, tail_sums):
        surf_3[tail, cols(chunk)] = new_surf
    sums = summed(corridor, own, total_3)
    fluxes(slice(0, 0), 0, wall_of(ext, tiles), before, faces, None, south_4, scale=SLOPE)
    copies.append(copy(1, south_4, south_out, 0, chunks))
    copies[1].start()
    group = 5
    for chunk, new_surf in settled(own, surf_3, east_4, south_4, keep, sums, spread=SPREAD):
        at = cols(chunk)
        depth_4[:, at] = new_surf - bed[own, at]
        if (chunk + 1) % group == 0 or chunk + 1 == chunks:
            first = chunk // group
            copies.append(copy(2 + first, depth_4, depth_out, first * group, chunk + 1))
            copies[-1].start()
    for one in copies:
        one.wait()


def local(
    depth, flux_east, flux_south, river_section, bed_level, rough_class, manning_table, bank_cell
):
    rows, columns = depth.shape
    owned = river_section.shape[0]
    corridor = bank_cell.shape[0]
    tiles = lax.axis_size("gy")
    ext = rows + 2 * HALO
    chunks = columns // LANES
    partner_section = swapped(river_section, 0).reshape(1, owned)
    partner_cells = swapped(bank_cell, 0)

    def held(value):
        return pltpu.with_memory_space_constraint(value, pltpu.VMEM)

    def far(value):
        return pltpu.with_memory_space_constraint(value, pltpu.HBM)

    params = pltpu.CompilerParams(vmem_limit_bytes=VMEM_LIMIT)
    halo = pltpu.VMEM((4 * chunks, HALO, LANES), jnp.float32)
    wide = pltpu.VMEM((4 * chunks + 1, HALO, LANES), jnp.float32)
    field = pltpu.VMEM((ext, columns), jnp.float32)
    small = pltpu.VMEM((rows, columns), jnp.float32)
    term = pltpu.VMEM((1, owned), jnp.float32)
    pair = pltpu.VMEM((2, owned), jnp.float32)
    result = pltpu.HBM((rows, columns), jnp.float32)
    cells = -(-chunks * rows // LANES) * LANES

    def call(kernel, name, outs, values, scratch=(), aliases=None):
        return pl.pallas_call(
            kernel,
            out_shape=outs,
            in_specs=[VMEM_SPEC] * len(values),
            out_specs=[HBM_SPEC if out is result else VMEM_SPEC for out in outs],
            scratch_shapes=scratch,
            input_output_aliases=aliases or {},
            compiler_params=params,
            name=name,
        )(*[held(value) for value in values])

    def picks(nodes):
        return [
            pltpu.VMEM((2, nodes, cells), jnp.bfloat16),
            pltpu.VMEM((2, nodes, LANES), jnp.float32),
        ]

    classes = manning_table.shape[0]
    table = far(manning_table.reshape(1, classes))
    table_held = pltpu.VMEM((1, classes), jnp.float32)
    to_other, own = pl.pallas_call(
        pack_kernel,
        out_shape=[wide, pair],
        in_specs=[HBM_SPEC] * 8,
        out_specs=[VMEM_SPEC] * 2,
        scratch_shapes=[
            pltpu.VMEM((4, 8, columns), jnp.float32),
            pltpu.VMEM((8, columns), jnp.int32),
            pltpu.VMEM((corridor, owned), jnp.int32),
            table_held,
            pltpu.SemaphoreType.DMA((8,)),
        ],
        compiler_params=params,
        name="pack",
    )(
        *[far(value) for value in (depth, bed_level, rough_class, flux_east, flux_south)],
        far(river_section.reshape(1, owned)),
        far(bank_cell),
        table,
    )
    (to_other,) = call(
        join_kernel,
        "join",
        [wide],
        (to_other, partner_section, partner_cells),
        aliases={0: 0},
    )
    by_other = swapped(to_other, 1)
    *loaded, rough, table_rows = pl.pallas_call(
        load_kernel,
        out_shape=[field] * 4
        + [pltpu.VMEM((rows, columns), jnp.int32), pltpu.VMEM((classes, LANES), jnp.float32)],
        in_specs=[HBM_SPEC] * 6,
        out_specs=[VMEM_SPEC] * 6,
        scratch_shapes=[table_held, pltpu.SemaphoreType.DMA((6,))],
        compiler_params=params,
        name="load",
    )(
        *[far(value) for value in (depth, flux_east, flux_south, bed_level, rough_class)],
        table,
    )
    *fields, to_partner = call(
        prepare_kernel,
        "prepare",
        [field] * 9 + [halo],
        (table_rows, rough, *loaded),
        aliases={2 + slot: slot for slot in range(4)},
    )
    by_partner = swapped(to_partner, 0)
    number, total, takes, masks, windows, given_1 = call(
        functools.partial(nodes_kernel, corridor),
        "nodes",
        [field] * 2 + picks(2 * owned) + [small] * 2,
        (fields[0], own, partner_section, partner_cells),
    )
    near, beyond = call(relay_kernel, "relay", [pair, pair], (by_other, masks))
    near, number, total, takes_near, masks_near = call(
        functools.partial(near_kernel, corridor, True),
        "near_early",
        [pair, field, field] + picks(owned),
        (near, number, total),
        aliases={1: 1, 2: 2},
    )
    from_far = swapped(near, 0)
    number, total, takes_near, masks_near = call(
        functools.partial(near_kernel, corridor, False),
        "near",
        [field] * 2 + picks(owned),
        (near, number, total, takes_near, masks_near),
        aliases={1 + slot: slot for slot in range(4)},
    )
    fields = call(
        functools.partial(border_kernel, tiles),
        "border",
        [field] * 9,
        (by_partner, by_other, table_rows, *fields),
        aliases={3 + slot: slot for slot in range(9)},
    )
    surf, east, south, bed, _, *faces = fields
    surf_1, total_1, count, keep, total_2, sums_2, given_2 = call(
        functools.partial(first_kernel, corridor),
        "first",
        [field] * 5 + [small] * 2,
        (surf, east, south, number, total, windows, given_1),
        scratch=[field],
    )
    surf_1, total_1, count, keep, total_2, surf_2, east_2, south_2 = call(
        functools.partial(second_kernel, corridor, tiles),
        "second",
        [field] * 8,
        (
            *(from_far, beyond, surf, east, south, *faces, number, total, sums_2),
            *(surf_1, total_1, count, keep, total_2),
        ),
        scratch=[field],
        aliases={12 + slot: slot for slot in range(5)},
    )
    last_scratch = [small, small, field, field, small]
    last_scratch.append(pltpu.SemaphoreType.DMA((2 + -(-chunks // 5),)))
    surf_3, east_3, south_3, own_term, partner_term, other_term, *results = call(
        functools.partial(third_kernel, corridor, tiles),
        "third",
        [field] * 3 + [term] * 3 + [result] * 3,
        (
            *(surf_2, east_2, south_2, *faces, total_2, keep, given_2),
            *(own, takes, masks, takes_near, masks_near, count, bed),
        ),
        scratch=last_scratch,
    )
    from_other = swapped(other_term.reshape(owned), 1)
    from_partner = swapped(partner_term.reshape(owned), 0)
    last_in = (surf_2, east_2, south_3, *faces, total_2, count, keep, bed, surf_3, east_3)
    _, depth, flux_east, flux_south = pl.pallas_call(
        functools.partial(last_kernel, corridor, tiles),
        out_shape=[field] + [result] * 3,
        in_specs=[VMEM_SPEC] * 13 + [HBM_SPEC] * 3,
        out_specs=[VMEM_SPEC] + [HBM_SPEC] * 3,
        scratch_shapes=last_scratch,
        input_output_aliases={11: 0, 13: 1, 14: 2, 15: 3},
        compiler_params=params,
        name="last",
    )(*[held(value) for value in last_in], *[far(value) for value in results])
    river_section = own_term.reshape(owned) + from_other + from_partner
    return (depth, flux_east, flux_south, river_section)


def solution(mesh):
    return jax.shard_map(
        local,
        mesh=mesh,
        in_specs=(
            P(("runs", "gy"), None),
            P(("runs", "gy"), None),
            P(("runs", "gy"), None),
            P(("runs", "gy")),
            P("gy", None),
            P("gy", None),
            P(),
            P(None, "gy"),
        ),
        out_specs=(
            P(("runs", "gy"), None),
            P(("runs", "gy"), None),
            P(("runs", "gy"), None),
            P(("runs", "gy")),
        ),
        check_vma=False,
    )
```

```python
import functools

import jax
import jax.numpy as jnp
from jax import lax
from jax.experimental import pallas as pl
from jax.experimental.pallas import tpu as pltpu
from jax.sharding import PartitionSpec as P

STEPS = 4

GRAV = 9.81
TSTEP = 8.0
CELL = 90.0
FLOOR = 0.05
BANK_COEF = 200.0
CELL_AREA = 8100.0
NODE_AREA = 20000.0

LANES = 128
HALO = 4
SLOPE = GRAV * TSTEP / CELL
SPREAD = TSTEP / CELL
FEED = TSTEP * BANK_COEF / CELL_AREA
DRAIN = TSTEP * BANK_COEF / NODE_AREA
VMEM_LIMIT = 32 * 1024 * 1024

VMEM_SPEC = pl.BlockSpec(memory_space=pltpu.VMEM)
HBM_SPEC = pl.BlockSpec(memory_space=pltpu.HBM)


def swapped(value, first):
    count = lax.axis_size("gy")
    pairs = []
    for low in range(first, count - 1, 2):
        pairs += [(low, low + 1), (low + 1, low)]
    return lax.ppermute(value, "gy", pairs)


def cols(chunk):
    return slice(chunk * LANES, (chunk + 1) * LANES)


def lanes_of(rows):
    return lax.broadcasted_iota(jnp.int32, (rows, LANES), 1)


def moved_left(value, following, by):
    return jnp.where(
        lanes_of(value.shape[0]) >= LANES - by,
        pltpu.roll(following, LANES - by, 1),
        pltpu.roll(value, LANES - by, 1),
    )


def moved_up(value):
    return pltpu.roll(value, value.shape[0] - 1, 0)


def split3(value):
    high = value.astype(jnp.bfloat16)
    rest = value - high.astype(jnp.float32)
    middle = rest.astype(jnp.bfloat16)
    low = (rest - middle.astype(jnp.float32)).astype(jnp.bfloat16)
    return high, middle, low


def one_hot(count, key):
    rows = lax.broadcasted_iota(jnp.int32, (count, key.shape[1]), 0)
    return jnp.where(rows == key, 1.0, 0.0)


def drag_of(mann_a, mann_b):
    pair = mann_a + mann_b
    return (0.25 * GRAV * TSTEP * SLOPE) * (pair * pair)


def looked_up(klass, entries):
    value = jnp.broadcast_to(entries[0], klass.shape)
    for k in range(1, len(entries)):
        value = jnp.where(klass == k, entries[k], value)
    return value


def face(flux, surf_a, surf_b, bed_max, drag):
    flow_depth = jnp.maximum(jnp.maximum(surf_a, surf_b) - bed_max, FLOOR)
    power = jnp.exp2((-7.0 / 3.0) * jnp.log2(flow_depth))
    driven = flux - flow_depth * (surf_b - surf_a)
    damping = 1.0 + drag * jnp.abs(flux) * power
    return driven * pl.reciprocal(damping, approx=True)


def window_sums(blocks, reach, forward):
    height = blocks[0].shape[0]
    count = len(blocks)
    spare = -(count * height) % 16
    whole = blocks + ([jnp.zeros((spare, LANES), jnp.float32)] if spare else [])
    whole = jnp.concatenate(whole, axis=0)
    high = whole.astype(jnp.bfloat16)
    low = (whole - high.astype(jnp.float32)).astype(jnp.bfloat16)
    source = lax.broadcasted_iota(jnp.int32, (2 * LANES, 2 * LANES), 0) % LANES
    target = lax.broadcasted_iota(jnp.int32, (2 * LANES, 2 * LANES), 1)
    spill = target >= LANES
    target = target % LANES
    if forward:
        ahead = source - target + jnp.where(spill, LANES, 0)
    else:
        ahead = target - source + jnp.where(spill, LANES, 0)
    band = jnp.where((ahead >= 0) & (ahead < reach), 1.0, 0.0).astype(jnp.bfloat16)
    sums = jnp.dot(
        jnp.concatenate([high, low], axis=1), band, preferred_element_type=jnp.float32
    )
    results = []
    for block in range(count):
        result = sums[block * height : (block + 1) * height, :LANES]
        beside = block + 1 if forward else block - 1
        if 0 <= beside < count:
            result = result + sums[beside * height : (beside + 1) * height, LANES:]
        results.append(result)
    return results


def east_walled(value, chunk, chunks):
    if chunk + 1 < chunks:
        return value
    return jnp.where(lanes_of(value.shape[0]) == LANES - 1, 0.0, value)


def located(cell, position, rows, ext, columns):
    base = ((position * rows - HALO) * columns + 1).astype(jnp.float32)
    offset = cell - base
    valid = (cell > 0.0) & (offset >= 0.0) & (offset < float(ext * columns))
    offset = jnp.where(valid, offset, 0.0)
    row = jnp.floor((offset + 0.5) * (1.0 / columns))
    column = (offset - row * float(columns)).astype(jnp.int32)
    row = row.astype(jnp.int32) - HALO
    row = jnp.where(row < 0, row + ext, row)
    chunk = column // LANES
    return valid, row, chunk, column - chunk * LANES


def scattered(section, key, lane, count):
    at_lane = one_hot(LANES, lane)
    parts = [at_lane] + [at_lane * part.astype(jnp.float32) for part in split3(section)]
    grid = lax.dot_general(
        one_hot(-(-count // 16) * 16, key).astype(jnp.bfloat16),
        jnp.concatenate(parts, axis=0).astype(jnp.bfloat16),
        (((1,), (1,)), ((), ())),
        preferred_element_type=jnp.float32,
    )
    number = grid[:, :LANES]
    total = (grid[:, LANES : 2 * LANES] + grid[:, 2 * LANES : 3 * LANES]) + grid[:, 3 * LANES :]
    return number, total


def border_rows(of_first, fields, south):
    outer = lax.broadcasted_iota(jnp.int32, (HALO, LANES), 0) == jnp.where(of_first, HALO - 1, 0)
    flux = jnp.where(of_first, south[:HALO], south[HALO:])
    return [
        jnp.where(outer, flux[slot : slot + 1], jnp.where(of_first, value[:HALO], value[HALO:]))
        for slot, value in enumerate(fields)
    ]


def pack_kernel(
    depth, bed, rough, east, south, section, cells, table_in, to_other, own, *refs
):
    held, held_rough, held_cells, table, sems = refs
    rows, columns = depth.shape
    chunks = columns // LANES
    even = lax.axis_index("gy") % 2 == 0
    start = pl.multiple_of(jnp.where(even, 0, rows - 8), 8)
    near = pl.ds(start, 8)
    copies = [
        pltpu.make_async_copy(source, target, sems.at[slot])
        for slot, (source, target) in enumerate(
            (
                (rough.at[near, :], held_rough),
                (bed.at[near, :], held.at[1]),
                (depth.at[near, :], held.at[0]),
                (east.at[near, :], held.at[2]),
                (south.at[near, :], held.at[3]),
                (section, own.at[pl.ds(0, 1), :]),
                (cells, held_cells),
                (table_in, table),
            )
        )
    ]
    for copy in copies:
        copy.start()
    for copy in copies:
        copy.wait()
    own[1:2, :] = (held_cells[0:1, :] + 1).astype(jnp.float32)
    entries = [
        jnp.broadcast_to(table[:, k : k + 1], (1, LANES)) for k in range(table.shape[1])
    ]
    manns = [looked_up(held_rough[:, cols(chunk)], entries) for chunk in range(chunks)]
    row = lax.broadcasted_iota(jnp.int32, (8, LANES), 0)
    beds = [held[1, :, cols(chunk)] for chunk in range(chunks)]
    surfs = [held[0, :, cols(chunk)] + beds[chunk] for chunk in range(chunks)]

    def moved(values):
        rolled = [pltpu.roll(value, LANES - 1, 1) for value in values]
        rolled.append(rolled[-1])
        edge = lanes_of(8) == LANES - 1
        return [jnp.where(edge, rolled[c + 1], rolled[c]) for c in range(chunks)]

    beds_left, surfs_left, manns_left = moved(beds), moved(surfs), moved(manns)
    for chunk in range(chunks):
        at = cols(chunk)
        m0, b0, s0 = manns[chunk], beds[chunk], surfs[chunk]
        bed_max = jnp.maximum(b0, beds_left[chunk])
        drag = drag_of(m0, manns_left[chunk])
        q0 = (1.0 / SLOPE) * held[2, :, at]
        new_east = face(q0, s0, surfs_left[chunk], bed_max, drag)
        new_east = east_walled(new_east, chunk, chunks)
        bed_max = jnp.maximum(b0, moved_up(b0))
        drag = drag_of(m0, moved_up(m0))
        q0 = (1.0 / SLOPE) * held[3, :, at]
        new_south = jnp.where(row == 7, q0, face(q0, s0, moved_up(s0), bed_max, drag))
        fields = (s0, b0, held_rough[:, at].astype(jnp.float32), new_east)
        for slot, block in enumerate(border_rows(even, fields, new_south)):
            to_other[slot * chunks + chunk] = block
    to_other[4 * chunks, 0:2, :] = own[...]


def join_kernel(before, section, cells, to_other):
    nodes = to_other.shape[0] - 1
    to_other[nodes, 2:3, :] = section[...]
    to_other[nodes, 3:4, :] = (cells[0:1, :] + 1).astype(jnp.float32)


def relay_kernel(by_other, prepared, near, beyond):
    del prepared
    nodes = by_other.shape[0] - 1
    near[...] = by_other[nodes, 0:2, :]
    beyond[...] = by_other[nodes, 2:4, :]


def picking(reach, rows, key, lane, takes, masks):
    for block in range(key.shape[1] // LANES):
        mine = slice(block * LANES, (block + 1) * LANES)

        def column(row):
            wide = jnp.broadcast_to(row[:, mine].astype(jnp.float32), (LANES, LANES))
            return jnp.transpose(wide).astype(jnp.int32)

        spread = lanes_of(LANES)
        at = column(key)
        after = jnp.where(at < 0, at, at + rows)
        for first in range(0, takes.shape[2], LANES):
            for half, place in enumerate((at, after)):
                hit = jnp.where(spread + first == place, 1.0, 0.0)
                takes[half, mine, first : first + LANES] = hit.astype(jnp.bfloat16)
        ahead = spread - column(lane)
        masks[0, mine, :] = jnp.where((ahead >= 0) & (ahead < reach), 1.0, 0.0)
        masks[1, mine, :] = jnp.where(ahead + LANES < reach, 1.0, 0.0)


def load_kernel(
    depth_in, east_in, south_in, bed_in, rough_in, table_in, *refs
):
    surf, east, south, bed, rough, table_rows, table, sems = refs
    rows, columns = depth_in.shape
    own = pl.ds(0, rows)
    copies = [
        pltpu.make_async_copy(source, target.at[own, :], sems.at[slot])
        for slot, (source, target) in enumerate(
            (
                (depth_in, surf),
                (bed_in, bed),
                (rough_in, rough),
                (east_in, east),
                (south_in, south),
            )
        )
    ]
    copies.append(pltpu.make_async_copy(table_in, table, sems.at[5]))
    for copy in copies:
        copy.start()
    copies[5].wait()
    for k in range(table_rows.shape[0]):
        table_rows[k : k + 1, :] = jnp.broadcast_to(table[:, k : k + 1], (1, LANES))
    for copy in copies[:5]:
        copy.wait()


def prepare_kernel(table_rows, rough, *refs):
    surf, east, south, bed = refs[4:8]
    mann, bed_e, bed_s, drag_e, drag_s, to_partner = refs[8:]
    ext, columns = surf.shape
    rows = ext - 2 * HALO
    chunks = columns // LANES
    even = lax.axis_index("gy") % 2 == 0
    entries = [table_rows[k : k + 1, :] for k in range(table_rows.shape[0])]
    for chunk in range(chunks):
        at = cols(chunk)
        mann[:rows, at] = looked_up(rough[:, at], entries)
        surf[:rows, at] = surf[:rows, at] + bed[:rows, at]

    kept = lax.broadcasted_iota(jnp.int32, (rows, LANES), 0) == rows - 1
    for chunk in range(chunks):
        at, then = cols(chunk), cols(min(chunk + 1, chunks - 1))
        s0, b0, m0 = surf[:rows, at], bed[:rows, at], mann[:rows, at]
        bed_max = jnp.maximum(b0, moved_left(b0, bed[:rows, then], 1))
        drag = drag_of(m0, moved_left(m0, mann[:rows, then], 1))
        bed_e[:rows, at] = bed_max
        drag_e[:rows, at] = drag
        q0 = (1.0 / SLOPE) * east[:rows, at]
        new_east = face(q0, s0, moved_left(s0, surf[:rows, then], 1), bed_max, drag)
        new_east = east_walled(new_east, chunk, chunks)
        east[:rows, at] = new_east
        bed_max = jnp.maximum(b0, moved_up(b0))
        drag = drag_of(m0, moved_up(m0))
        bed_s[:rows, at] = bed_max
        drag_s[:rows, at] = drag
        q0 = (1.0 / SLOPE) * south[:rows, at]
        new_south = jnp.where(kept, q0, face(q0, s0, moved_up(s0), bed_max, drag))
        south[:rows, at] = new_south

        def ends(value):
            return jnp.where(even, value[rows - 8 :], value[:8])

        fields = (ends(s0), ends(b0), ends(rough[:, at].astype(jnp.float32)), ends(new_east))
        blocks = border_rows(jnp.logical_not(even), fields, ends(new_south))
        for slot, block in enumerate(blocks):
            to_partner[slot * chunks + chunk] = block


def nodes_kernel(reach, surf, own, partner_section, partner_cells, *refs):
    number, total, takes, masks, windows, given_1 = refs
    rows = surf.shape[0] - 2 * HALO
    ext, columns = number.shape
    chunks = columns // LANES
    tiles = lax.axis_size("gy")
    position = lax.axis_index("gy")
    side = jnp.where(position % 2 == 0, 1, -1)
    partner = jnp.where(position + side < tiles, partner_cells[0:1, :] + 1, 0).astype(jnp.float32)
    section = jnp.concatenate([own[0:1, :], partner_section[...]], axis=1)
    cell = jnp.concatenate([own[1:2, :], partner], axis=1)
    valid, node_row, node_chunk, node_lane = located(cell, position, rows, ext, columns)
    key = jnp.where(valid, node_chunk * ext + node_row, -1)
    starts, levels = scattered(section, key, node_lane, chunks * ext)
    for chunk in range(chunks):
        at = cols(chunk)
        number[:, at] = starts[chunk * ext : (chunk + 1) * ext]
        total[:, at] = levels[chunk * ext : (chunk + 1) * ext]
    key = jnp.where(valid & (node_row < rows), node_chunk * rows + node_row, -1)
    picking(reach, rows, key, node_lane, takes, masks)
    sums = window_sums([surf[:rows, cols(chunk)] for chunk in range(chunks)], reach, True)
    for chunk in range(chunks):
        windows[:, cols(chunk)] = sums[chunk]
    give(reach, 0, surf, None, given_1)


def wall_of(ext, tiles):
    position = lax.axis_index("gy")
    rows = ext - 2 * HALO
    row = lax.broadcasted_iota(jnp.int32, (16, LANES), 0) + (ext - 16)
    return ((row == ext - 1) & (position == 0)) | ((row == rows - 1) & (position == tiles - 1))


def near_kernel(reach, early, near, *refs):
    number, total, takes, masks = refs[-4:]
    ext, columns = number.shape
    rows = ext - 2 * HALO
    chunks = columns // LANES
    position = lax.axis_index("gy")
    if early:
        refs[2][...] = near[...]

    @pl.when((position % 4 == 3) if early else (position % 4 != 3))
    def _():
        cell = near[1:2, :]
        valid, node_row, node_chunk, node_lane = located(cell, position, rows, ext, columns)
        key = jnp.where(valid, node_chunk * ext + node_row, -1)
        starts, levels = scattered(near[0:1, :], key, node_lane, chunks * ext)
        for chunk in range(chunks):
            at = cols(chunk)
            number[:, at] += starts[chunk * ext : (chunk + 1) * ext]
            total[:, at] += levels[chunk * ext : (chunk + 1) * ext]
        key = jnp.where(valid & (node_row < rows), node_chunk * rows + node_row, -1)
        picking(reach, rows, key, node_lane, takes, masks)


def border_kernel(tiles, by_partner, by_other, table_rows, *refs):
    surf, east, south, bed, mann, bed_e, bed_s, drag_e, drag_s = refs[9:]
    ext, columns = surf.shape
    rows = ext - 2 * HALO
    chunks = columns // LANES
    position = lax.axis_index("gy")
    even = position % 2 == 0
    entries = [table_rows[k : k + 1, :] for k in range(table_rows.shape[0])]
    row = lax.broadcasted_iota(jnp.int32, (2 * HALO, LANES), 0)
    for chunk in range(chunks):
        at = cols(chunk)
        halos = []
        flux = jnp.zeros((2 * HALO, LANES), jnp.float32)
        for slot in range(4):
            a, b = by_partner[slot * chunks + chunk], by_other[slot * chunks + chunk]
            below = jnp.where(even, a, b)
            above = jnp.where(even, b, a)
            halos.append(jnp.concatenate([below, above], axis=0))
            flux = jnp.where(row == slot, below[HALO - 1 :], flux)
            flux = jnp.where(row == HALO + slot, above[:1], flux)
        surf[rows:, at] = halos[0]
        bed[rows:, at] = halos[1]
        mann[rows:, at] = looked_up(halos[2].astype(jnp.int32), entries)
        east[rows:, at] = halos[3]
        south[rows:, at] = flux

    wall = wall_of(ext, tiles)
    kept = lax.broadcasted_iota(jnp.int32, (16, LANES), 0) % 8 < 7
    for chunk in range(chunks):
        at, then = cols(chunk), cols(min(chunk + 1, chunks - 1))
        b0, m0 = bed[rows:, at], mann[rows:, at]
        bed_e[rows:, at] = jnp.maximum(b0, moved_left(b0, bed[rows:, then], 1))
        drag_e[rows:, at] = drag_of(m0, moved_left(m0, mann[rows:, then], 1))

        def rolled_up(ref):
            value = jnp.concatenate([ref[rows - 8 :, at], ref[:8, at]], axis=0)
            return value[:16], moved_up(value)[:16]

        s0, s1 = rolled_up(surf)
        b0, b1 = rolled_up(bed)
        m0, m1 = rolled_up(mann)
        bed_max = jnp.maximum(b0, b1)
        drag = drag_of(m0, m1)
        bed_s[rows - 8 :, at] = bed_max
        drag_s[rows - 8 :, at] = drag
        q0 = south[rows - 8 :, at]
        new_south = jnp.where(kept, q0, face(q0, s0, s1, bed_max, drag))
        south[rows - 8 :, at] = jnp.where(wall, 0.0, new_south)


def fluxes(mine, upper, wall, before, faces, east_out, south_out, scale=None):
    surf, east, south = before
    bed_e, bed_s, drag_e, drag_s = faces
    ext, columns = surf.shape
    chunks = columns // LANES
    rolled = lane = None
    if east_out is not None:
        rolled = pltpu.roll(surf[mine, cols(0)], LANES - 1, 1)
        lane = lanes_of(rolled.shape[0])
    for chunk in range(chunks):
        at = cols(chunk)
        if east_out is not None:
            s0 = surf[mine, at]
            rolled_then = rolled
            if chunk + 1 < chunks:
                rolled_then = pltpu.roll(surf[mine, cols(chunk + 1)], LANES - 1, 1)
            left = jnp.where(lane >= LANES - 1, rolled_then, rolled)
            rolled = rolled_then
            new_east = face(east[mine, at], s0, left, bed_e[mine, at], drag_e[mine, at])
            if scale is not None:
                new_east = scale * new_east
            east_out[mine, at] = east_walled(new_east, chunk, chunks)
        if upper:
            s0 = surf[: upper + 8, at]
            s1 = moved_up(s0)[:upper]
            new_south = face(south[:upper, at], s0[:upper], s1, bed_s[:upper, at], drag_s[:upper, at])
            if scale is not None:
                new_south = scale * new_south
            south_out[:upper, at] = new_south
        if wall is not None:
            low = slice(ext - 16, ext)
            s0 = jnp.concatenate([surf[low, at], surf[:8, at]], axis=0)
            s1 = moved_up(s0)[:16]
            new_south = face(south[low, at], s0[:16], s1, bed_s[low, at], drag_s[low, at])
            if scale is not None:
                new_south = scale * new_south
            south_out[low, at] = jnp.where(wall, 0.0, new_south)


def settled(mine, surf, east, south, keep, sums, spread=SPREAD * SLOPE):
    ext, columns = surf.shape
    rolled = 0.0
    for chunk in range(columns // LANES):
        at = cols(chunk)
        new_east = east[mine, at]
        new_south = south[:, at]
        lane = lanes_of(new_east.shape[0])
        rolled_before, rolled = rolled, pltpu.roll(new_east, 1, 1)
        west = jnp.where(lane < 1, rolled_before, rolled)
        north = pltpu.roll(new_south, 1, 0)[mine]
        inflow = west + north
        s0 = surf[mine, at]
        outflow = new_east + new_south[mine]
        yield chunk, keep[mine, at] * s0 + (spread * (inflow - outflow) + sums[chunk])


def refill(corridor, mine, surf, total, count, total_out, windows=None):
    chunks = surf.shape[1] // LANES
    if windows is None:
        windows = window_sums([surf[mine, cols(chunk)] for chunk in range(chunks)], corridor, True)
    for chunk in range(chunks):
        at = cols(chunk)
        kept = (1.0 - corridor * DRAIN) * total[mine, at]
        total_out[mine, at] = kept + count[mine, at] * windows[chunk]


def summed(corridor, mine, total):
    chunks = total.shape[1] // LANES
    return window_sums([total[mine, cols(chunk)] for chunk in range(chunks)], corridor, False)


def exchange(corridor, mine, surf, total, count, total_out, windows=None):
    sums = summed(corridor, mine, total)
    refill(corridor, mine, surf, total, count, total_out, windows)
    return sums


def give(corridor, step, surf, before, after):
    rows, columns = after.shape
    weight = DRAIN * (1.0 - corridor * DRAIN) ** (STEPS - 1 - step)
    for chunk in range(columns // LANES):
        at = cols(chunk)
        value = weight * surf[:rows, at]
        after[:, at] = value if before is None else before[:, at] + value


def first_kernel(corridor, surf, east, south, number, total, windows, given_1, *refs):
    surf_1, total_1, count, keep, total_2, sums_2, given_2, total_0 = refs
    rows = surf.shape[0] - 2 * HALO
    chunks = surf.shape[1] // LANES
    own = slice(0, rows)
    covering = window_sums([number[own, cols(chunk)] for chunk in range(chunks)], corridor, False)
    for chunk in range(chunks):
        at = cols(chunk)
        count[own, at] = (FEED * DRAIN) * number[own, at]
        keep[own, at] = 1.0 - FEED * covering[chunk]
        total_0[own, at] = FEED * total[own, at]
    windows = [windows[:, cols(chunk)] for chunk in range(chunks)]
    sums = exchange(corridor, own, surf, total_0, count, total_1, windows)
    after = summed(corridor, own, total_1)
    for chunk, new_surf in settled(own, surf, east, south, keep, sums):
        surf_1[own, cols(chunk)] = new_surf
        sums_2[:, cols(chunk)] = after[chunk]
    refill(corridor, own, surf_1, total_1, count, total_2)
    give(corridor, 1, surf_1, given_1, given_2)


def second_kernel(corridor, tiles, far, beyond, surf, east, south, *refs):
    faces = refs[:4]
    number, total, sums_2 = refs[4:7]
    surf_1, total_1, count, keep, total_2 = refs[12:17]
    surf_2, east_2, south_2, total_0 = refs[17:]
    ext, columns = surf.shape
    rows = ext - 2 * HALO
    chunks = columns // LANES
    position = lax.axis_index("gy")
    tail = slice(rows, ext)

    section = jnp.concatenate([far[0:1, :], beyond[0:1, :]], axis=1)
    cell = jnp.concatenate([far[1:2, :], beyond[1:2, :]], axis=1)
    valid, node_row, node_chunk, node_lane = located(cell, position, rows, ext, columns)
    key = jnp.where(valid & (node_row >= rows), node_chunk * 8 + (node_row - rows), -1)
    starts, levels = scattered(section, key, node_lane, chunks * 8)
    starting = [
        number[tail, cols(chunk)] + starts[chunk * 8 : chunk * 8 + 8] for chunk in range(chunks)
    ]
    covering = window_sums(starting, corridor, False)
    for chunk in range(chunks):
        at = cols(chunk)
        count[tail, at] = (FEED * DRAIN) * starting[chunk]
        keep[tail, at] = 1.0 - FEED * covering[chunk]
        total_0[tail, at] = FEED * (total[tail, at] + levels[chunk * 8 : chunk * 8 + 8])
    sums = exchange(corridor, tail, surf, total_0, count, total_1)

    own = slice(0, rows)
    before = (surf_1, east, south)
    fluxes(own, rows - 8, None, before, faces, east_2, south_2)
    own_sums = [sums_2[:, cols(chunk)] for chunk in range(chunks)]

    for chunk, new_surf in settled(tail, surf, east, south, keep, sums):
        surf_1[tail, cols(chunk)] = new_surf
    tail_sums = exchange(corridor, tail, surf_1, total_1, count, total_2)
    fluxes(tail, 0, wall_of(ext, tiles), before, faces, east_2, south_2)
    for mine, sums in ((own, own_sums), (tail, tail_sums)):
        for chunk, new_surf in settled(mine, surf_1, east_2, south_2, keep, sums):
            surf_2[mine, cols(chunk)] = new_surf


def third_kernel(corridor, tiles, surf, east, south, *refs):
    faces = refs[:4]
    total, keep, given_2, own, takes, masks, takes_near, masks_near, count, bed = refs[4:14]
    surf_3, east_3, south_3, own_term, partner_term, other_term = refs[14:20]
    ext, columns = surf.shape
    rows = ext - 2 * HALO
    mine = slice(0, rows)
    owned = own.shape[1]
    chunks = columns // LANES
    sums = summed(corridor, mine, total)
    fluxes(
        mine, rows - 8, wall_of(ext, tiles), (surf, east, south), faces, east_3, south_3
    )
    weight = DRAIN * (1.0 - corridor * DRAIN)
    levels = []
    for chunk, new_surf in settled(mine, surf, east_3, south_3, keep, sums):
        at = cols(chunk)
        surf_3[mine, at] = new_surf
        levels.append(given_2[:, at] + weight * surf[mine, at] + DRAIN * new_surf)
    spare = takes.shape[2] - chunks * rows
    if spare:
        levels.append(jnp.zeros((spare, LANES), jnp.float32))
    levels = jnp.concatenate(levels, axis=0)
    high = levels.astype(jnp.bfloat16)
    low = (levels - high.astype(jnp.float32)).astype(jnp.bfloat16)
    picked = jnp.dot(
        jnp.concatenate([takes[0], takes_near[0], takes[1], takes_near[1]], axis=0),
        jnp.concatenate([high, low], axis=1),
        preferred_element_type=jnp.float32,
    )
    hit = jnp.concatenate([masks[0], masks_near[0], masks[1], masks_near[1]], axis=0)
    picked = (picked * jnp.concatenate([hit, hit], axis=1)).astype(jnp.bfloat16)
    picked = jnp.concatenate([picked[: 3 * owned], picked[3 * owned :]], axis=1)
    terms = lax.dot_general(
        jnp.ones((8, 4 * LANES), jnp.bfloat16),
        picked,
        (((1,), (1,)), ((), ())),
        preferred_element_type=jnp.float32,
    )[0:1]
    own_term[...] = (1.0 - corridor * DRAIN) ** STEPS * own[0:1, :] + terms[:, :owned]
    partner_term[...] = terms[:, owned : 2 * owned]
    other_term[...] = terms[:, 2 * owned :]

    @pl.when(is_edge(tiles))
    def _():
        last_substep(
            *(corridor, tiles, surf, east, south_3, *faces, total, count, keep, bed),
            *(None, east_3, surf_3, *refs[20:]),
        )


def is_edge(tiles):
    position = lax.axis_index("gy")
    return (position == 0) | (position == tiles - 1)


def last_kernel(corridor, tiles, *refs):
    @pl.when(jnp.logical_not(is_edge(tiles)))
    def _():
        last_substep(corridor, tiles, *refs[:13], *refs[16:])


def last_substep(corridor, tiles, surf_2, east_2, south_3, *refs):
    faces = refs[:4]
    total_2, count, keep, bed, _, east_3 = refs[4:10]
    surf_3, depth_out, east_out, south_out = refs[10:14]
    depth_4, east_4, south_4, east_tail, total_3, sems = refs[14:]
    ext, columns = surf_2.shape
    rows = ext - 2 * HALO
    chunks = columns // LANES
    own, tail = slice(0, rows), slice(rows, ext)

    def copy(slot, source, target, first=0, last=chunks, top=0, bottom=rows):
        part = pl.ds(first * LANES, (last - first) * LANES)
        lines = pl.ds(top, bottom - top)
        return pltpu.make_async_copy(
            source.at[lines, part], target.at[lines, part], sems.at[slot]
        )

    before = (surf_3, east_3, south_3)
    tail_sums = summed(corridor, tail, total_2)
    refill(corridor, own, surf_2, total_2, count, total_3)
    fluxes(own, rows - 8, None, before, faces, east_4, south_4, scale=SLOPE)
    copies = [copy(0, east_4, east_out), copy(1, south_4, south_out, bottom=rows - 8)]
    copies[0].start()
    copies[1].start()
    fluxes(tail, 0, None, (surf_2, east_2, None), faces, east_tail, None)
    for chunk, new_surf in settled(tail, surf_2, east_tail, south_3, keep, tail_sums):
        surf_3[tail, cols(chunk)] = new_surf
    sums = summed(corridor, own, total_3)
    fluxes(slice(0, 0), 0, wall_of(ext, tiles), before, faces, None, south_4, scale=SLOPE)
    copies.append(copy(2, south_4, south_out, top=rows - 8))
    copies[2].start()
    group = 3
    for chunk, new_surf in settled(own, surf_3, east_4, south_4, keep, sums, spread=SPREAD):
        at = cols(chunk)
        depth_4[:, at] = new_surf - bed[own, at]
        if (chunk + 1) % group == 0 or chunk + 1 == chunks:
            first = chunk // group
            copies.append(copy(3 + first, depth_4, depth_out, first * group, chunk + 1))
            copies[-1].start()
    for one in copies:
        one.wait()


def local(
    depth, flux_east, flux_south, river_section, bed_level, rough_class, manning_table, bank_cell
):
    rows, columns = depth.shape
    owned = river_section.shape[0]
    corridor = bank_cell.shape[0]
    tiles = lax.axis_size("gy")
    ext = rows + 2 * HALO
    chunks = columns // LANES
    partner_section = swapped(river_section, 0).reshape(1, owned)
    partner_cells = swapped(bank_cell, 0)

    def held(value):
        return pltpu.with_memory_space_constraint(value, pltpu.VMEM)

    def far(value):
        return pltpu.with_memory_space_constraint(value, pltpu.HBM)

    params = pltpu.CompilerParams(vmem_limit_bytes=VMEM_LIMIT)
    halo = pltpu.VMEM((4 * chunks, HALO, LANES), jnp.float32)
    wide = pltpu.VMEM((4 * chunks + 1, HALO, LANES), jnp.float32)
    field = pltpu.VMEM((ext, columns), jnp.float32)
    small = pltpu.VMEM((rows, columns), jnp.float32)
    term = pltpu.VMEM((1, owned), jnp.float32)
    pair = pltpu.VMEM((2, owned), jnp.float32)
    result = pltpu.HBM((rows, columns), jnp.float32)
    cells = -(-chunks * rows // LANES) * LANES

    def call(kernel, name, outs, values, scratch=(), aliases=None):
        return pl.pallas_call(
            kernel,
            out_shape=outs,
            in_specs=[VMEM_SPEC] * len(values),
            out_specs=[HBM_SPEC if out is result else VMEM_SPEC for out in outs],
            scratch_shapes=scratch,
            input_output_aliases=aliases or {},
            compiler_params=params,
            name=name,
        )(*[held(value) for value in values])

    def picks(nodes):
        return [
            pltpu.VMEM((2, nodes, cells), jnp.bfloat16),
            pltpu.VMEM((2, nodes, LANES), jnp.float32),
        ]

    classes = manning_table.shape[0]
    table = far(manning_table.reshape(1, classes))
    table_held = pltpu.VMEM((1, classes), jnp.float32)
    to_other, own = pl.pallas_call(
        pack_kernel,
        out_shape=[wide, pair],
        in_specs=[HBM_SPEC] * 8,
        out_specs=[VMEM_SPEC] * 2,
        scratch_shapes=[
            pltpu.VMEM((4, 8, columns), jnp.float32),
            pltpu.VMEM((8, columns), jnp.int32),
            pltpu.VMEM((corridor, owned), jnp.int32),
            table_held,
            pltpu.SemaphoreType.DMA((8,)),
        ],
        compiler_params=params,
        name="pack",
    )(
        *[far(value) for value in (depth, bed_level, rough_class, flux_east, flux_south)],
        far(river_section.reshape(1, owned)),
        far(bank_cell),
        table,
    )
    (to_other,) = call(
        join_kernel,
        "join",
        [wide],
        (to_other, partner_section, partner_cells),
        aliases={0: 0},
    )
    by_other = swapped(to_other, 1)
    *loaded, rough, table_rows = pl.pallas_call(
        load_kernel,
        out_shape=[field] * 4
        + [pltpu.VMEM((rows, columns), jnp.int32), pltpu.VMEM((classes, LANES), jnp.float32)],
        in_specs=[HBM_SPEC] * 6,
        out_specs=[VMEM_SPEC] * 6,
        scratch_shapes=[table_held, pltpu.SemaphoreType.DMA((6,))],
        compiler_params=params,
        name="load",
    )(
        *[far(value) for value in (depth, flux_east, flux_south, bed_level, rough_class)],
        table,
    )
    *fields, to_partner = call(
        prepare_kernel,
        "prepare",
        [field] * 9 + [halo],
        (table_rows, rough, *loaded),
        aliases={2 + slot: slot for slot in range(4)},
    )
    by_partner = swapped(to_partner, 0)
    number, total, takes, masks, windows, given_1 = call(
        functools.partial(nodes_kernel, corridor),
        "nodes",
        [field] * 2 + picks(2 * owned) + [small] * 2,
        (fields[0], own, partner_section, partner_cells),
    )
    near, beyond = call(relay_kernel, "relay", [pair, pair], (by_other, masks))
    near, number, total, takes_near, masks_near = call(
        functools.partial(near_kernel, corridor, True),
        "near_early",
        [pair, field, field] + picks(owned),
        (near, number, total),
        aliases={1: 1, 2: 2},
    )
    from_far = swapped(near, 0)
    number, total, takes_near, masks_near = call(
        functools.partial(near_kernel, corridor, False),
        "near",
        [field] * 2 + picks(owned),
        (near, number, total, takes_near, masks_near),
        aliases={1 + slot: slot for slot in range(4)},
    )
    fields = call(
        functools.partial(border_kernel, tiles),
        "border",
        [field] * 9,
        (by_partner, by_other, table_rows, *fields),
        aliases={3 + slot: slot for slot in range(9)},
    )
    surf, east, south, bed, _, *faces = fields
    surf_1, total_1, count, keep, total_2, sums_2, given_2 = call(
        functools.partial(first_kernel, corridor),
        "first",
        [field] * 5 + [small] * 2,
        (surf, east, south, number, total, windows, given_1),
        scratch=[field],
    )
    surf_1, total_1, count, keep, total_2, surf_2, east_2, south_2 = call(
        functools.partial(second_kernel, corridor, tiles),
        "second",
        [field] * 8,
        (
            *(from_far, beyond, surf, east, south, *faces, number, total, sums_2),
            *(surf_1, total_1, count, keep, total_2),
        ),
        scratch=[field],
        aliases={12 + slot: slot for slot in range(5)},
    )
    last_scratch = [small, small, field, field, small]
    last_scratch.append(pltpu.SemaphoreType.DMA((3 + -(-chunks // 3),)))
    surf_3, east_3, south_3, own_term, partner_term, other_term, *results = call(
        functools.partial(third_kernel, corridor, tiles),
        "third",
        [field] * 3 + [term] * 3 + [result] * 3,
        (
            *(surf_2, east_2, south_2, *faces, total_2, keep, given_2),
            *(own, takes, masks, takes_near, masks_near, count, bed),
        ),
        scratch=last_scratch,
    )
    from_other = swapped(other_term.reshape(owned), 1)
    from_partner = swapped(partner_term.reshape(owned), 0)
    last_in = (surf_2, east_2, south_3, *faces, total_2, count, keep, bed, surf_3, east_3)
    _, depth, flux_east, flux_south = pl.pallas_call(
        functools.partial(last_kernel, corridor, tiles),
        out_shape=[field] + [result] * 3,
        in_specs=[VMEM_SPEC] * 13 + [HBM_SPEC] * 3,
        out_specs=[VMEM_SPEC] + [HBM_SPEC] * 3,
        scratch_shapes=last_scratch,
        input_output_aliases={11: 0, 13: 1, 14: 2, 15: 3},
        compiler_params=params,
        name="last",
    )(*[held(value) for value in last_in], *[far(value) for value in results])
    river_section = own_term.reshape(owned) + from_other + from_partner
    return (depth, flux_east, flux_south, river_section)


def solution(mesh):
    return jax.shard_map(
        local,
        mesh=mesh,
        in_specs=(
            P(("runs", "gy"), None),
            P(("runs", "gy"), None),
            P(("runs", "gy"), None),
            P(("runs", "gy")),
            P("gy", None),
            P("gy", None),
            P(),
            P(None, "gy"),
        ),
        out_specs=(
            P(("runs", "gy"), None),
            P(("runs", "gy"), None),
            P(("runs", "gy"), None),
            P(("runs", "gy")),
        ),
        check_vma=False,
    )
```
